32 devices in a mesh: tm: 4 (over x, core), slot: 8 (over z, y).
Axes of the slice: x: 2, y: 2, z: 4, core: 2. Of those that a mesh axis runs over, the one named last changes fastest.
Arguments:
- inputs: bfloat16 [8, 1536, 512], P('slot', 'tm'), may hold values from -6 to 6
- cotangent: bfloat16 [8, 1536, 512], P('slot', 'tm'), may hold values from -6 to 6
- lengths: int32 [8], P('slot'), may hold values from 48 to 1512, as said below
- weight_noise: bfloat16 [32, 196608], P(('tm', 'slot')), may hold values from -0.25 to 0.25
- ffn1_in: bfloat16 [512, 2048], replicated, may hold values from -0.25 to 0.25
- ffn1_out: bfloat16 [2048, 512], replicated, may hold values from -0.125 to 0.125
- query_w: bfloat16 [512, 512], replicated, may hold values from -0.25 to 0.25
- key_w: bfloat16 [512, 512], replicated, may hold values from -0.25 to 0.25
- value_w: bfloat16 [512, 512], replicated, may hold values from -0.25 to 0.25
- pos_w: bfloat16 [512, 512], replicated, may hold values from -0.25 to 0.25
- out_w: bfloat16 [512, 512], replicated, may hold values from -2 to 2
- conv_in: bfloat16 [512, 1024], replicated, may hold values from -0.25 to 0.25
- conv_out: bfloat16 [512, 512], replicated, may hold values from -0.25 to 0.25
- ffn2_in: bfloat16 [512, 2048], replicated, may hold values from -0.25 to 0.25
- ffn2_out: bfloat16 [2048, 512], replicated, may hold values from -0.125 to 0.125
- conv_kernel: float32 [32, 512], replicated, may hold values from -1 to 1
- ffn1_gain: float32 [512], replicated, may hold values from 0.5 to 1.5
- attn_gain: float32 [512], replicated, may hold values from 0.5 to 1.5
- conv_gain: float32 [512], replicated, may hold values from 0.5 to 1.5
- ffn2_gain: float32 [512], replicated, may hold values from 0.5 to 1.5
- final_gain: float32 [512], replicated, may hold values from 0.5 to 1.5
- bn_gain: float32 [512], replicated, may hold values from 0.5 to 1.5
- bn_bias: float32 [512], replicated, may hold values from -3 to 3
- pos_u: float32 [512], replicated, may hold values from -3 to 3
- pos_v: float32 [512], replicated, may hold values from -3 to 3
Outputs:
- output: bfloat16 [8, 1536, 512], P('slot', 'tm')
- input_grad: bfloat16 [8, 1536, 512], P('slot', 'tm')
- ffn1_in_grad: float32 [512, 2048], replicated
- ffn1_out_grad: float32 [2048, 512], replicated
- query_grad: float32 [512, 512], replicated
- key_grad: float32 [512, 512], replicated
- value_grad: float32 [512, 512], replicated
- pos_grad: float32 [512, 512], replicated
- out_grad: float32 [512, 512], replicated
- conv_in_grad: float32 [512, 1024], replicated
- conv_out_grad: float32 [512, 512], replicated
- ffn2_in_grad: float32 [512, 2048], replicated
- ffn2_out_grad: float32 [2048, 512], replicated
- kernel_grad: float32 [32, 512], replicated
- ffn1_gain_grad: float32 [512], replicated
- attn_gain_grad: float32 [512], replicated
- conv_gain_grad: float32 [512], replicated
- ffn2_gain_grad: float32 [512], replicated
- final_gain_grad: float32 [512], replicated
- bn_gain_grad: float32 [512], replicated
- bn_bias_grad: float32 [512], replicated
- pos_u_grad: float32 [512], replicated
- pos_v_grad: float32 [512], replicated
The draws below stay inside these ranges and needn't reach their ends.
Inputs may be any that keep to these rules, and one draw needn't show every extreme that they name: `lengths`: among the 1 slots of each index of slot, one, drawn from the seed, has the largest length 1512.
All inputs are finite; a program needn't handle non-finite values.
Results may differ from the reference program's by a relative error of at most 0.029.
Values may be sent and summed in bfloat16 or wider, within the bound.
A program may use at most 256 MiB of HBM per device.

```python
import math
from functools import partial
import jax
import jax.numpy as jnp
from jax import lax

D = 512
FF = 2048
H = 8
HD = 64
KERNEL = 32
FRAMES = 1536
SEQ_DEV = 1
SLOTS = 8
NOISE_COLS = 196608
DEVICES = 32


def draw_lengths(key, part):
    key = jax.random.fold_in(key, 11)
    first_key, second_key = jax.random.split(key)
    shortest = FRAMES // 32
    longest = FRAMES - FRAMES // 64
    sampled = jax.random.randint(first_key, (SLOTS,), shortest, longest + 1)
    chosen = jax.random.randint(second_key, (SLOTS // SEQ_DEV,), 0, SEQ_DEV)
    member = jnp.arange(SLOTS, dtype=jnp.int32) % SEQ_DEV
    marked = member == jnp.repeat(chosen, SEQ_DEV)
    return jnp.where(marked, longest, sampled).astype(jnp.int32)


def shard_levels(rng, shape, cuts, low, largest):
    def one(position, shards_of):
        draws = jax.random.uniform(jax.random.fold_in(jax.random.fold_in(rng, 6), position), (shards_of,), jnp.float32, low / len(cuts), largest / len(cuts))
        return jnp.repeat(jnp.exp(draws), shape[position] // shards_of).reshape((-1,) + (1,) * (len(shape) - position - 1))

    factor_of = one(*cuts[0])
    for cut in cuts[1:]:
        factor_of = factor_of * one(*cut)
    return factor_of


def noise(key, dims, deviation, most, pieces=(), kind=jnp.bfloat16):
    values = jax.random.normal(key, dims, jnp.float32) * deviation
    if len(pieces) > 0:
        values = shard_levels(key, dims, pieces, -0.22, 0.18) * values
    return jnp.clip(values, min=-most, max=most).astype(kind)


def setup_inputs(seed: int = 0) -> dict:
    arg_keys = jax.random.split(jax.random.key(seed), 26)
    return {
        "inputs": noise(arg_keys[0], (SLOTS, FRAMES, D), 1.0, 6.0, ((0, 8), (1, 4))),
        "cotangent": noise(arg_keys[1], (SLOTS, FRAMES, D), 1.0, 6.0, ((0, 8), (1, 4))),
        "lengths": draw_lengths(jax.random.fold_in(arg_keys[25], 71), 0),
        "weight_noise": noise(arg_keys[3], (DEVICES, NOISE_COLS), D ** -0.5, 0.25, ((0, 32),)),
        "ffn1_in": noise(arg_keys[4], (D, FF), D ** -0.5, 0.25),
        "ffn1_out": noise(arg_keys[5], (FF, D), FF ** -0.5, 0.125),
        "query_w": noise(arg_keys[6], (D, D), D ** -0.5, 0.25),
        "key_w": noise(arg_keys[7], (D, D), D ** -0.5, 0.25),
        "value_w": noise(arg_keys[8], (D, D), D ** -0.5, 0.25),
        "pos_w": noise(arg_keys[9], (D, D), D ** -0.5, 0.25),
        "out_w": noise(arg_keys[10], (D, D), (max(D // 64, 1)) ** -0.5, 2.0),
        "conv_in": noise(arg_keys[11], (D, 2 * D), D ** -0.5, 0.25),
        "conv_out": noise(arg_keys[12], (D, D), D ** -0.5, 0.25),
        "ffn2_in": noise(arg_keys[13], (D, FF), D ** -0.5, 0.25),
        "ffn2_out": noise(arg_keys[14], (FF, D), FF ** -0.5, 0.125),
        "conv_kernel": noise(arg_keys[15], (KERNEL, D), KERNEL ** -0.5, 1.0, (), jnp.float32),
        "ffn1_gain": jnp.clip(1.0 + 0.1 * jax.random.normal(arg_keys[16], (D,), jnp.float32), 0.5, 1.5),
        "attn_gain": jnp.clip(1.0 + 0.1 * jax.random.normal(arg_keys[17], (D,), jnp.float32), 0.5, 1.5),
        "conv_gain": jnp.clip(1.0 + 0.1 * jax.random.normal(arg_keys[18], (D,), jnp.float32), 0.5, 1.5),
        "ffn2_gain": jnp.clip(1.0 + 0.1 * jax.random.normal(arg_keys[19], (D,), jnp.float32), 0.5, 1.5),
        "final_gain": jnp.clip(1.0 + 0.1 * jax.random.normal(arg_keys[20], (D,), jnp.float32), 0.5, 1.5),
        "bn_gain": jnp.clip(1.0 + 0.1 * jax.random.normal(arg_keys[21], (D,), jnp.float32), 0.5, 1.5),
        "bn_bias": noise(arg_keys[22], (D,), 0.5, 3.0, (), jnp.float32),
        "pos_u": noise(arg_keys[23], (D,), 0.5, 3.0, (), jnp.float32),
        "pos_v": noise(arg_keys[24], (D,), 0.5, 3.0, (), jnp.float32),
    }


@jax.custom_vjp
def low(v):
    return lax.optimization_barrier(v.astype(jnp.bfloat16)).astype(jnp.float32)

@jax.custom_vjp
def low_back(v):
    return v

def low_keep(v):
    return (low(v), None)

def low_pass(kept, grad):
    return (grad,)

def back_keep(v):
    return (v, None)

def back_low(kept, grad):
    return (low(grad),)
low.defvjp(low_keep, low_pass)
low_back.defvjp(back_keep, back_low)
eps_small = 1e-05
mask_fill = -1e+30
highest = lax.Precision.HIGHEST

def layer_norm(values, norm_gain):
    average = lax.optimization_barrier(jnp.mean(values, axis=-1, keepdims=True))
    centred = values - average
    spread = lax.optimization_barrier(jnp.mean(centred * centred, axis=-1, keepdims=True))
    return centred * lax.rsqrt(spread + eps_small) * norm_gain

def swish(values):
    return values * jax.nn.sigmoid(values)

def project(left_in, right_in):
    return jnp.einsum('bld,df->blf', left_in, right_in, precision=highest)

def rel_table(row_count, top_distance, model_width):
    distance = top_distance - jnp.arange(row_count, dtype=jnp.float32)
    half_width = model_width // 2
    freq_rates = jnp.exp(jnp.arange(half_width, dtype=jnp.float32) * (-2.0 * math.log(10000.0) / model_width))
    angles = distance[:, None] * freq_rates[None, :]
    return jnp.concatenate([jnp.sin(angles), jnp.cos(angles)], axis=1)

def skew(pos_band, band_rows, key_count):
    lead_dims = pos_band.shape[:-2]
    band_width = pos_band.shape[-1]
    flat_view = pos_band.reshape(lead_dims + (band_rows * band_width,))
    flat_view = flat_view[..., band_rows - 1:band_rows - 1 + band_rows * (band_width - 1)]
    return flat_view.reshape(lead_dims + (band_rows, band_width - 1))[..., :key_count]

def depthwise(extended, kernel):
    return lax.conv_general_dilated(extended, kernel[:, None, :], (1,), 'VALID', dimension_numbers=('NWC', 'WIO', 'NWC'), feature_group_count=extended.shape[-1], precision=highest)

def feed_forward(values, norm_gain, w_in, w_out):
    normed = low(layer_norm(values, norm_gain))
    hidden_pre = low_back(project(normed, w_in))
    hidden = low(swish(hidden_pre))
    return values + 0.5 * low_back(project(hidden, w_out))

def attend(prow_heads, att_item):
    query_u, query_v, keys_in, values_in, key_ok = att_item
    direct = jnp.einsum('qhd,khd->hqk', query_u, keys_in, precision=highest)
    pos_band = jnp.einsum('qhd,rhd->hqr', query_v, prow_heads, precision=highest)
    raw_scores = low_back(direct + skew(pos_band, FRAMES, FRAMES))
    scores = jnp.where(key_ok[None, None, :], raw_scores * HD ** (-0.5), mask_fill)
    att_probs = jax.nn.softmax(scores, axis=-1)
    att_mixed = jnp.einsum('hqk,khd->qhd', low(att_probs), values_in, precision=highest)
    return att_mixed.reshape(FRAMES, H * HD)

def reference(inputs, cotangent, lengths, weight_noise, ffn1_in, ffn1_out, query_w, key_w, value_w, pos_w, out_w, conv_in, conv_out, ffn2_in, ffn2_out, conv_kernel, ffn1_gain, attn_gain, conv_gain, ffn2_gain, final_gain, bn_gain, bn_bias, pos_u, pos_v):
    slot_count = inputs.shape[0]
    positions = jnp.arange(FRAMES, dtype=jnp.int32)
    valid_rows = (positions[None, :] < lengths[:, None]).astype(jnp.float32)[..., None]
    key_ok = positions[None, :] < lengths[:, None]
    noise_flat = weight_noise.astype(jnp.float32).reshape(-1)
    matrices = tuple((matrix.astype(jnp.float32) for matrix in (ffn1_in, ffn1_out, query_w, key_w, value_w, pos_w, out_w, conv_in, conv_out, ffn2_in, ffn2_out)))
    norm_gains = (ffn1_gain, attn_gain, conv_gain, ffn2_gain, final_gain)

    def forward(states, matrices, kernel, norm_gains, batch_gain, batch_bias, bias_u, bias_v):
        noisy_list = []
        offset = 0
        for matrix in matrices:
            amount = matrix.shape[0] * matrix.shape[1]
            noisy_list.append(low(matrix + noise_flat[offset:offset + amount].reshape(matrix.shape)))
            offset = offset + amount
        w_ffn1_in, w_ffn1_out, w_query, w_key, w_value, w_pos, w_out, w_conv_in, w_conv_out, w_ffn2_in, w_ffn2_out = noisy_list
        after_ffn1 = feed_forward(states, norm_gains[0], w_ffn1_in, w_ffn1_out)
        normed_att = low(layer_norm(after_ffn1, norm_gains[1]))
        query_full = low_back(project(normed_att, w_query))
        keys_low = low(low_back(project(normed_att, w_key)))
        values_low = low(low_back(project(normed_att, w_value)))
        query_u = low(query_full + bias_u)
        query_v = low(query_full + bias_v)
        pos_table = low(rel_table(2 * FRAMES - 1, FRAMES - 1, H * HD))
        prows = low(jnp.dot(pos_table, w_pos, precision=highest))
        prow_heads = prows.reshape(2 * FRAMES - 1, H, HD)
        head_shape = (slot_count, FRAMES, H, HD)
        att_items = (query_u.reshape(head_shape), query_v.reshape(head_shape), keys_low.reshape(head_shape), values_low.reshape(head_shape), key_ok)
        att_mixed = lax.map(jax.checkpoint(partial(attend, prow_heads)), att_items)
        att_mixed = low(low_back(att_mixed))
        after_att = after_ffn1 + low_back(project(att_mixed, w_out))
        normed_conv = low(layer_norm(after_att, norm_gains[2]))
        gate_pre = low_back(project(normed_conv, w_conv_in))
        width_half = gate_pre.shape[-1] // 2
        gated = low(gate_pre[..., :width_half] * jax.nn.sigmoid(gate_pre[..., width_half:]) * valid_rows)
        padded = jnp.pad(gated, ((0, 0), (KERNEL - 1, 0), (0, 0)))
        conv_raw = low_back(depthwise(padded, kernel))
        frame_total = jnp.sum(valid_rows)
        col_mean = lax.optimization_barrier(jnp.sum(conv_raw * valid_rows, axis=(0, 1))) / frame_total
        col_square = lax.optimization_barrier(jnp.sum(conv_raw * conv_raw * valid_rows, axis=(0, 1))) / frame_total
        variance = col_square - col_mean * col_mean
        batch_out = (conv_raw - col_mean) * lax.rsqrt(variance + eps_small) * batch_gain + batch_bias
        activated = low(swish(batch_out))
        after_conv = after_att + low_back(project(activated, w_conv_out))
        after_ffn2 = feed_forward(after_conv, norm_gains[3], w_ffn2_in, w_ffn2_out)
        return layer_norm(after_ffn2, norm_gains[4])
    result, puller = jax.vjp(forward, inputs.astype(jnp.float32), matrices, conv_kernel, norm_gains, bn_gain, bn_bias, pos_u, pos_v)
    grad_states, grad_mats, grad_kernel, grad_norms, grad_bgain, grad_bbias, grad_u, grad_v = puller(cotangent.astype(jnp.float32))
    return (result.astype(jnp.bfloat16), grad_states.astype(jnp.bfloat16), grad_mats[0], grad_mats[1], grad_mats[2], grad_mats[3], grad_mats[4], grad_mats[5], grad_mats[6], grad_mats[7], grad_mats[8], grad_mats[9], grad_mats[10], grad_kernel, grad_norms[0], grad_norms[1], grad_norms[2], grad_norms[3], grad_norms[4], grad_bgain, grad_bbias, grad_u, grad_v)
```

```python
import math

import jax
import jax.numpy as jnp
from jax import lax
from jax.experimental import pallas as pl
from jax.experimental.pallas import tpu as pltpu
from jax.sharding import PartitionSpec as P

H = 8
HD = 64
LANE = 128
F32 = jnp.float32
BF = jnp.bfloat16
EPS = 1e-05
FILL = -1e30
VMEM_LIMIT = 60 * 2**20


def dot(a, b):
    return lax.dot_general(a, b, (((1,), (0,)), ((), ())), preferred_element_type=F32)


def dot_nt(a, b):
    return lax.dot_general(a, b, (((1,), (1,)), ((), ())), preferred_element_type=F32)


def dot_tn(a, b):
    return lax.dot_general(a, b, (((0,), (0,)), ((), ())), preferred_element_type=F32)


def norm_parts(v):
    mean = jnp.mean(v, axis=-1, keepdims=True)
    cen = v - mean
    r = lax.rsqrt(jnp.mean(cen * cen, axis=-1, keepdims=True) + EPS)
    return cen * r, r


def norm(v, gain):
    u, _ = norm_parts(v)
    return u * gain


def norm_back(v, gain, e):
    u, r = norm_parts(v)
    eg = e * gain
    back = r * (eg - jnp.mean(eg, axis=-1, keepdims=True) - u * jnp.mean(eg * u, axis=-1, keepdims=True))
    return back, jnp.sum(e * u, axis=0, keepdims=True)


def sigmoid(v):
    return 1.0 / (1.0 + jnp.exp(-v))


def swish_and_slope(v):
    s = sigmoid(v)
    sv = s * v
    return sv, s + sv * (1.0 - s)


def cols(p, width=LANE):
    return pl.ds(pl.multiple_of(p * width, width), width)


def lane_half(e):
    lane = lax.broadcasted_iota(jnp.int32, (1, LANE), 1)
    return (lane < HD) if e == 0 else (lane >= HD)


def call(body, outs, ins, scratch=(), name=None):
    return pl.pallas_call(
        body,
        out_shape=[jax.ShapeDtypeStruct(s, d) for s, d in outs],
        in_specs=[
            pl.BlockSpec(memory_space=pltpu.SMEM) if x.dtype == jnp.int32 else pl.BlockSpec(memory_space=pltpu.VMEM)
            for x in ins
        ],
        out_specs=[pl.BlockSpec(memory_space=pltpu.VMEM) for _ in outs],
        scratch_shapes=list(scratch),
        compiler_params=pltpu.CompilerParams(vmem_limit_bytes=VMEM_LIMIT),
        name=name,
    )(*ins)


def noisy_body(noise, *refs):
    n = (len(refs) - 1) // 2
    raws, outs, scr = refs[:n], refs[n : 2 * n], refs[2 * n]
    base = 0
    for raw, out in zip(raws, outs):
        rows, width = raw.shape
        fold = width // 512
        step = 256 // fold

        def one(i, carry, raw=raw, out=out, base=base, fold=fold, step=step):
            src = pl.ds(pl.multiple_of(base + i * 256, 256), 256)
            dst = pl.ds(pl.multiple_of(i * step, step), step)
            if fold == 1:
                out[dst, :] = (raw[dst, :].astype(F32) + noise[src, :].astype(F32)).astype(BF)
            else:
                part = noise[src, :].astype(F32)
                for c in range(512 // LANE):
                    scr[c] = part[:, c * LANE : (c + 1) * LANE]
                for c in range(512 // LANE):
                    for j in range(fold):
                        at = pl.ds(j * 512 + c * LANE, LANE)
                        part = scr[c, pl.ds(j, step, stride=fold), :]
                        out[dst, at] = (raw[dst, at].astype(F32) + part).astype(BF)
            return carry

        lax.fori_loop(0, rows * fold // 256, one, 0)
        base += rows * fold


def ffn_forward(normed, w_in, w_out, pre_ref, hid_ref):
    width = w_in.shape[1]

    def one(c, acc):
        at = cols(c, 512)
        pre = dot(normed, w_in[:, at])
        pre_ref[:, at] = pre
        hid = (pre * sigmoid(pre)).astype(BF)
        if hid_ref is not None:
            hid_ref[:, at] = hid
        return acc + dot(hid, w_out[pl.ds(pl.multiple_of(c * 512, 512), 512), :])

    return lax.fori_loop(0, width // 512, one, jnp.zeros((normed.shape[0], w_out.shape[1]), F32))


def ffn_backward(g_low, normed, w_in, w_out, pre_ref, gin_ref, gout_ref):
    width = w_in.shape[1]
    normed_t = normed.T

    def one(c, acc):
        at = cols(c, 512)
        rows = pl.ds(pl.multiple_of(c * 512, 512), 512)
        sw, slope = swish_and_slope(pre_ref[:, at])
        hid = sw.astype(BF)
        gout_ref[rows, :] = dot_tn(hid, g_low).astype(gout_ref.dtype)
        dpre = (dot_nt(g_low, w_out[rows, :]) * slope).astype(BF)
        gin_ref[:, at] = dot(normed_t, dpre).astype(gin_ref.dtype)
        return acc + dot_nt(dpre, w_in[:, at])

    return lax.fori_loop(0, width // 512, one, jnp.zeros(g_low.shape, F32))


def fwd1_body(x_ref, w_in, w_out, w_q, w_k, w_v, gain1, gain2, pos_u, pos_v, x1_ref, pre_ref, a2_ref, qu_ref, qv_ref, k_ref, v_ref):
    x = x_ref[...].astype(F32)
    a1 = norm(x, gain1[...]).astype(BF)
    x1 = x + 0.5 * ffn_forward(a1, w_in, w_out, pre_ref, None)
    x1_ref[...] = x1
    a2 = norm(x1, gain2[...]).astype(BF)
    a2_ref[...] = a2
    q = dot(a2, w_q[...])
    scale = HD**-0.5
    qu_ref[...] = ((q + pos_u[...]).astype(BF).astype(F32) * scale).astype(BF)
    qv_ref[...] = ((q + pos_v[...]).astype(BF).astype(F32) * scale).astype(BF)
    k_ref[...] = dot(a2, w_k[...]).astype(BF)
    v_ref[...] = dot(a2, w_v[...]).astype(BF)


def att_fwd_body(lens, qu, qv, k, v, w_pos, trig, sin, cos, att_ref, p_ref, s_scr):
    rows, frames = qu.shape[0], k.shape[0]
    half = sin.shape[1]
    ok = lax.broadcasted_iota(jnp.int32, (1, frames), 1) < lens[0]

    def pair(p, carry):
        at = cols(p)
        mixed = None
        for e in range(2):
            mine = lane_half(e)
            qve = jnp.where(mine, qv[:, at], jnp.zeros((), BF))
            que = jnp.where(mine, qu[:, at], jnp.zeros((), BF))
            a_s = dot_nt(qve, w_pos[pl.ds(0, half), at])
            a_c = dot_nt(qve, w_pos[pl.ds(half, half), at])
            b_c = (a_s * sin[...] + a_c * cos[...]).astype(BF)
            b_s = (a_c * sin[...] - a_s * cos[...]).astype(BF)
            s = dot_nt(b_s, trig[:, pl.ds(0, half)]) + dot_nt(b_c, trig[:, pl.ds(half, half)]) + dot_nt(que, k[:, at])
            s = jnp.where(ok, s, FILL)
            m = jnp.max(s, axis=-1, keepdims=True)
            ex = jnp.exp(s - m)
            tot = jnp.sum(ex, axis=-1, keepdims=True)
            low = (ex * (1.0 / tot)).astype(BF)
            p_ref[2 * p + e] = low
            part = dot(low, v[:, at])
            mixed = part if e == 0 else jnp.where(mine, part, mixed)
        att_ref[:, at] = mixed.astype(BF)
        return carry

    lax.fori_loop(0, H // 2, pair, 0)


def att_bwd_body(qu, qv, k, v, w_pos, trig, sin, cos, p_ref, datt, att, dq_ref, dkt_ref, dvt_ref, gpos_ref, gu_ref, gv_ref, qut, qvt, datt_t, gpost):
    half = sin.shape[1]
    qut[...] = qu[...].T
    qvt[...] = qv[...].T
    datt_t[...] = datt[...].T

    def pair(p, carry):
        at = cols(p)
        dqu = dqv = None
        for e in range(2):
            mine = lane_half(e)
            rows = pl.ds(pl.multiple_of(p * LANE + e * HD, HD), HD)
            dm = jnp.where(mine, datt[:, at], jnp.zeros((), BF))
            inner = jnp.sum(dm.astype(F32) * att[:, at].astype(F32), axis=-1, keepdims=True)
            low = p_ref[2 * p + e]
            dp = dot_nt(dm, v[:, at])
            ds = (low.astype(F32) * (dp - inner)).astype(BF)
            dkt_ref[rows, :] = dot(qut[rows, :], ds).astype(BF)
            dvt_ref[rows, :] = dot(datt_t[rows, :], low).astype(BF)
            db_s = dot(ds, trig[:, pl.ds(0, half)])
            db_c = dot(ds, trig[:, pl.ds(half, half)])
            da_s = (db_c * sin[...] - db_s * cos[...]).astype(BF)
            da_c = (db_c * cos[...] + db_s * sin[...]).astype(BF)
            gpost[rows, pl.ds(0, half)] = dot(qvt[rows, :], da_s)
            gpost[rows, pl.ds(half, half)] = dot(qvt[rows, :], da_c)
            part_v = dot(da_s, w_pos[pl.ds(0, half), at]) + dot(da_c, w_pos[pl.ds(half, half), at])
            part_u = dot(ds, k[:, at])
            dqu = part_u if e == 0 else jnp.where(mine, part_u, dqu)
            dqv = part_v if e == 0 else jnp.where(mine, part_v, dqv)
        scale = HD**-0.5
        dqu = dqu * scale
        dqv = dqv * scale
        dq_ref[:, at] = (dqu + dqv).astype(BF)
        gu_ref[:, at] = jnp.sum(dqu, axis=0, keepdims=True)
        gv_ref[:, at] = jnp.sum(dqv, axis=0, keepdims=True)
        return carry

    lax.fori_loop(0, H // 2, pair, 0)
    gpos_ref[...] = gpost[...].T.astype(gpos_ref.dtype)


def conv_in_body(lens, att, x1_ref, w_out, w_cin, gain, x2_ref, a3_ref, z_ref, gm_ref):
    rows, width = x1_ref.shape
    x2 = x1_ref[...] + dot(att[...], w_out[...])
    x2_ref[...] = x2
    a3 = norm(x2, gain[...]).astype(BF)
    a3_ref[...] = a3
    z1 = dot(a3, w_cin[:, pl.ds(0, width)])
    z2 = dot(a3, w_cin[:, pl.ds(width, width)])
    z_ref[:, pl.ds(0, width)] = z1
    z_ref[:, pl.ds(width, width)] = z2
    gm_ref[...] = (z1 * sigmoid(z2) * valid_rows(lens, rows)).astype(BF)


def valid_rows(lens, rows):
    first = lax.axis_index("tm") * rows
    return ((first + lax.broadcasted_iota(jnp.int32, (rows, 1), 0)) < lens[0]).astype(F32)


def spread(ext, start, value):
    value = value.astype(F32)
    for b in range(ext.shape[0]):
        ext[b, pl.ds(start, value.shape[0]), :] = value[:, b * LANE : (b + 1) * LANE]


def tap_sum(ext, taps, out_ref, offset):
    count = taps.shape[0]
    rows = out_ref.shape[0]
    block = 64 if rows % 64 == 0 else 16

    def one(i, carry):
        for b in range(ext.shape[0]):
            at = pl.ds(b * LANE, LANE)
            acc = jnp.zeros((block, LANE), F32)
            for k in range(count):
                acc = acc + taps[pl.ds(k, 1), at] * ext[b, pl.ds(i * block + offset(k), block), :]
            out_ref[pl.ds(pl.multiple_of(i * block, block), block), at] = acc
        return carry

    lax.fori_loop(0, rows // block, one, 0)


def conv_body(lens, early, gm, taps, dwo_ref, sums_ref, ext):
    rows = gm.shape[0]
    count = taps.shape[0]
    spread(ext, 0, early[...])
    spread(ext, count, gm[...])
    tap_sum(ext, taps, dwo_ref, lambda k: k + 1)
    ok = valid_rows(lens, rows)
    dwo = dwo_ref[...] * ok
    sums_ref[0:1, :] = jnp.sum(dwo, axis=0, keepdims=True)
    sums_ref[1:2, :] = jnp.sum(dwo * dwo, axis=0, keepdims=True)
    sums_ref[2:3, :] = jnp.zeros((1, dwo.shape[1]), F32) + jnp.sum(ok, axis=0, keepdims=True)
    sums_ref[3:8, :] = jnp.zeros((5, dwo.shape[1]), F32)


def bn_stats(sums):
    total = sums[2:3, :]
    mu = sums[0:1, :] / total
    var = sums[1:2, :] / total - mu * mu
    return mu, lax.rsqrt(var + EPS), total


def mid_body(
    dwo_ref, sums, x2_ref, cot, w_cout, w_in, w_out, bn_gain, bn_bias, gain4, gain5,
    out_ref, dx3_ref, dbn_ref, gin_ref, gout_ref, gcout_ref, sums2_ref, smalls_ref, pre_ref,
):
    mu, inv, _ = bn_stats(sums)
    xhat = (dwo_ref[...] - mu) * inv
    sw, slope = swish_and_slope(xhat * bn_gain[...] + bn_bias[...])
    sw = sw.astype(BF)
    x3 = x2_ref[...] + dot(sw, w_cout[...])
    a4 = norm(x3, gain4[...]).astype(BF)
    x4 = x3 + 0.5 * ffn_forward(a4, w_in, w_out, pre_ref, None)
    out_ref[...] = norm(x4, gain5[...]).astype(BF)
    dx4, gg5 = norm_back(x4, gain5[...], cot[...].astype(F32))
    g4 = (0.5 * dx4).astype(BF)
    da4 = ffn_backward(g4, a4, w_in, w_out, pre_ref, gin_ref, gout_ref)
    back, gg4 = norm_back(x3, gain4[...], da4)
    dx3 = dx4 + back
    dx3_ref[...] = dx3
    g3 = dx3.astype(BF)
    gcout_ref[...] = dot_tn(sw, g3).astype(gcout_ref.dtype)
    dbn = dot_nt(g3, w_cout[...]) * slope
    dbn_ref[...] = dbn
    sums2_ref[0:1, :] = jnp.sum(dbn * xhat, axis=0, keepdims=True)
    sums2_ref[1:2, :] = jnp.sum(dbn, axis=0, keepdims=True)
    sums2_ref[2:8, :] = jnp.zeros((6, dbn.shape[1]), F32)
    smalls_ref[0:1, :] = gg4
    smalls_ref[1:2, :] = gg5


def bn_back_body(lens, dwo_ref, sums, sums2, dbn_ref, bn_gain, ddwo_ref):
    rows = dwo_ref.shape[0]
    mu, inv, total = bn_stats(sums)
    xhat = (dwo_ref[...] - mu) * inv
    ok = valid_rows(lens, rows)
    ddwo_ref[...] = (bn_gain[...] * inv * (dbn_ref[...] - ok * (sums2[1:2, :] + xhat * sums2[0:1, :]) / total)).astype(BF)


def conv_back_body(
    lens, ddwo, late, early, gm, taps, z_ref, a3, x2_ref, dx3_ref, att, w_cin, w_out, gain3,
    dx2_ref, datt_ref, gcin_ref, gout_ref, gtaps_ref, gg3_ref, ext, ext2, dgm_ref, acc,
):
    rows, width = x2_ref.shape
    count = taps.shape[0]
    spread(ext2, 0, ddwo[...])
    spread(ext2, rows, late[...])
    spread(ext, 0, early[...])
    spread(ext, count, gm[...])
    tap_sum(ext2, taps, dgm_ref, lambda k: count - 1 - k)
    block = 64 if rows % 64 == 0 else 16
    for b in range(ext.shape[0]):
        acc[...] = jnp.zeros(acc.shape, F32)

        def one(i, carry, b=b):
            mine = ext2[b, pl.ds(pl.multiple_of(i * block, block), block), :]
            for k in range(count):
                prod = mine * ext[b, pl.ds(i * block + k + 1, block), :]
                acc[k] = acc[k] + jnp.sum(prod.reshape(block // 8, 8, LANE), axis=0)
            return carry

        lax.fori_loop(0, rows // block, one, 0)
        gtaps_ref[:, pl.ds(b * LANE, LANE)] = jnp.sum(acc[...], axis=1)
    z1 = z_ref[:, pl.ds(0, width)]
    sg = sigmoid(z_ref[:, pl.ds(width, width)])
    dg = dgm_ref[...] * valid_rows(lens, rows)
    dz1 = (dg * sg).astype(BF)
    dz2 = (dg * z1 * sg * (1.0 - sg)).astype(BF)
    a3t = a3[...].T
    gcin_ref[:, pl.ds(0, width)] = dot(a3t, dz1).astype(gcin_ref.dtype)
    gcin_ref[:, pl.ds(width, width)] = dot(a3t, dz2).astype(gcin_ref.dtype)
    da3 = dot_nt(dz1, w_cin[:, pl.ds(0, width)]) + dot_nt(dz2, w_cin[:, pl.ds(width, width)])
    back, gg3 = norm_back(x2_ref[...], gain3[...], da3)
    gg3_ref[...] = gg3
    dx2 = dx3_ref[...] + back
    dx2_ref[...] = dx2
    g2 = dx2.astype(BF)
    gout_ref[...] = dot_tn(att[...], g2).astype(gout_ref.dtype)
    datt_ref[...] = dot_nt(g2, w_out[...]).astype(BF)


def bwd3_body(
    dq, dkt, dvt, a2, x1_ref, dx2_ref, x_ref, pre_ref, w_q, w_k, w_v, w_in, w_out, gain2, gain1,
    dx0_ref, gq_ref, gk_ref, gv_ref, gin_ref, gout_ref, gg_ref,
):
    a2t = a2[...].T
    gq_ref[...] = dot(a2t, dq[...]).astype(gq_ref.dtype)
    gk_ref[...] = dot_nt(a2t, dkt[...]).astype(gk_ref.dtype)
    gv_ref[...] = dot_nt(a2t, dvt[...]).astype(gv_ref.dtype)
    da2 = dot_nt(dq[...], w_q[...]) + dot_nt(dkt[...].T, w_k[...]) + dot_nt(dvt[...].T, w_v[...])
    back, gg2 = norm_back(x1_ref[...], gain2[...], da2)
    dx1 = dx2_ref[...] + back
    g1 = (0.5 * dx1).astype(BF)
    x = x_ref[...].astype(F32)
    a1 = norm(x, gain1[...]).astype(BF)
    da1 = ffn_backward(g1, a1, w_in, w_out, pre_ref, gin_ref, gout_ref)
    back, gg1 = norm_back(x, gain1[...], da1)
    dx0_ref[...] = (dx1 + back).astype(BF)
    gg_ref[0:1, :] = gg1
    gg_ref[1:2, :] = gg2


def passed_along(value, axis, steps):
    count = lax.axis_size(axis)
    first, last = max(0, -steps), min(count, count - steps)
    return lax.ppermute(value, axis, [(s, s + steps) for s in range(first, last)])


def local(
    inputs, cotangent, lengths, weight_noise, ffn1_in, ffn1_out, query_w, key_w, value_w, pos_w, out_w,
    conv_in, conv_out, ffn2_in, ffn2_out, conv_kernel, ffn1_gain, attn_gain, conv_gain, ffn2_gain,
    final_gain, bn_gain, bn_bias, pos_u, pos_v,
):
    _, rows, width = inputs.shape
    tm = lax.axis_size("tm")
    frames = rows * tm
    count = conv_kernel.shape[0]
    axes = ("tm", "slot")
    devices = tm * lax.axis_size("slot")
    x = inputs[0]
    cot = cotangent[0]
    gains = [g.reshape(1, -1) for g in (ffn1_gain, attn_gain, conv_gain, ffn2_gain, final_gain)]
    bng, bnb, pu, pv = (g.reshape(1, -1) for g in (bn_gain, bn_bias, pos_u, pos_v))
    raws = (ffn1_in, ffn1_out, query_w, key_w, value_w, pos_w, out_w, conv_in, conv_out, ffn2_in, ffn2_out)
    noise = lax.all_gather(weight_noise.reshape(-1, width), axes, axis=0, tiled=True)
    w = call(noisy_body, [(r.shape, BF) for r in raws], (noise,) + raws, [pltpu.VMEM((512 // LANE, 256, LANE), F32)], name="noisy")
    w_f1i, w_f1o, w_q, w_k, w_v, w_p, w_o, w_ci, w_co, w_f2i, w_f2o = w

    half = width // 2
    rates = jnp.exp(jnp.arange(half, dtype=F32) * (-2.0 * math.log(10000.0) / width))
    angles = jnp.arange(frames, dtype=F32)[:, None] * rates[None, :]
    sin_all, cos_all = jnp.sin(angles), jnp.cos(angles)
    trig = jnp.concatenate([sin_all, cos_all], axis=1).astype(BF)
    first = lax.axis_index("tm") * rows
    sin = lax.dynamic_slice_in_dim(sin_all, first, rows, 0)
    cos = lax.dynamic_slice_in_dim(cos_all, first, rows, 0)

    act, actb = ((rows, width), F32), ((rows, width), BF)
    hidden = w_f1i.shape[1]
    x1, pre1, a2, qu, qv, k, v = call(
        fwd1_body,
        [act, ((rows, hidden), F32), actb, actb, actb, actb, actb],
        (x, w_f1i, w_f1o, w_q, w_k, w_v, gains[0], gains[1], pu, pv),
        name="fwd1",
    )
    k_all = lax.all_gather(k, "tm", axis=0, tiled=True)
    v_all = lax.all_gather(v, "tm", axis=0, tiled=True)
    att, probs = call(
        att_fwd_body,
        [actb, ((H, rows, frames), BF)],
        (lengths, qu, qv, k_all, v_all, w_p, trig, sin, cos),
        [pltpu.VMEM((8, LANE), F32)],
        name="att_fwd",
    )
    x2, a3, z, gm = call(
        conv_in_body, [act, actb, ((rows, 2 * width), F32), actb], (lengths, att, x1, w_o, w_ci, gains[2]), name="conv_in"
    )
    early = passed_along(gm[rows - count :], "tm", 1)
    ext_shape = pltpu.VMEM((width // LANE, rows + count, LANE), F32)
    sums_shape = ((8, width), F32)
    dwo, sums = call(conv_body, [act, sums_shape], (lengths, early, gm, conv_kernel), [ext_shape], name="conv")
    sums = lax.psum(sums, axes)
    output, dx3, dbn, g_f2i, g_f2o, g_co, sums2, smalls45 = call(
        mid_body,
        [actb, act, act, (w_f2i.shape, BF), (w_f2o.shape, BF), (w_co.shape, BF), sums_shape, ((2, width), F32)],
        (dwo, sums, x2, cot, w_co, w_f2i, w_f2o, bng, bnb, gains[3], gains[4]),
        [pltpu.VMEM((rows, hidden), F32)],
        name="mid",
    )
    sums2 = lax.psum(sums2, axes)
    (ddwo,) = call(bn_back_body, [actb], (lengths, dwo, sums, sums2, dbn, bng), name="bn_back")
    late = passed_along(ddwo[:count], "tm", -1)
    dx2, datt, g_ci, g_o, g_taps, gg3 = call(
        conv_back_body,
        [act, actb, (w_ci.shape, BF), (w_o.shape, BF), (conv_kernel.shape, F32), ((1, width), F32)],
        (lengths, ddwo, late, early, gm, conv_kernel, z, a3, x2, dx3, att, w_ci, w_o, gains[2]),
        [ext_shape, ext_shape, pltpu.VMEM((rows, width), F32), pltpu.VMEM((count, 8, LANE), F32)],
        name="conv_back",
    )
    wide = ((width, frames), BF)
    vec = ((1, width), F32)
    dq, dkt, dvt, g_p, gu, gv = call(
        att_bwd_body,
        [actb, wide, wide, (w_p.shape, BF), vec, vec],
        (qu, qv, k_all, v_all, w_p, trig, sin, cos, probs, datt, att),
        [pltpu.VMEM((width, rows), BF)] * 3 + [pltpu.VMEM((width, width), F32)],
        name="att_bwd",
    )
    dkt = lax.psum_scatter(dkt, "tm", scatter_dimension=1, tiled=True)
    dvt = lax.psum_scatter(dvt, "tm", scatter_dimension=1, tiled=True)
    dx0, g_q, g_k, g_v, g_f1i, g_f1o, gg12 = call(
        bwd3_body,
        [actb, (w_q.shape, BF), (w_k.shape, BF), (w_v.shape, BF), (w_f1i.shape, BF), (w_f1o.shape, BF), ((2, width), F32)],
        (dq, dkt, dvt, a2, x1, dx2, x, pre1, w_q, w_k, w_v, w_f1i, w_f1o, gains[1], gains[0]),
        name="bwd3",
    )
    grads = (g_f1i, g_f1o, g_q, g_k, g_v, g_p, g_o, g_ci, g_co, g_f2i, g_f2o)
    big = tuple(lax.psum(g, axes).astype(F32) for g in grads)
    gg12, smalls45, g_taps, gu, gv, gg3 = lax.psum((gg12, smalls45, g_taps, gu, gv, gg3), axes)
    return (output[None], dx0[None]) + big + (
        g_taps, gg12[0], gg12[1], gg3[0], smalls45[0], smalls45[1], sums2[0], sums2[1], gu[0], gv[0],
    )


def solution(mesh):
    split = P("slot", "tm", None)
    in_specs = (split, split, P("slot"), P(("tm", "slot"), None)) + (P(),) * 21
    out_specs = (split, split) + (P(),) * 21
    return jax.shard_map(local, mesh=mesh, in_specs=in_specs, out_specs=out_specs, check_vma=False)
```

```python
import math

import jax
import jax.numpy as jnp
from jax import lax
from jax.experimental import pallas as pl
from jax.experimental.pallas import tpu as pltpu
from jax.sharding import PartitionSpec as P

H = 8
HD = 64
LANE = 128
F32 = jnp.float32
BF = jnp.bfloat16
EPS = 1e-05
FILL = -1e30
VMEM_LIMIT = 60 * 2**20


def dot(a, b):
    return lax.dot_general(a, b, (((1,), (0,)), ((), ())), preferred_element_type=F32)


def dot_nt(a, b):
    return lax.dot_general(a, b, (((1,), (1,)), ((), ())), preferred_element_type=F32)


def dot_tn(a, b):
    return lax.dot_general(a, b, (((0,), (0,)), ((), ())), preferred_element_type=F32)


def norm_parts(v):
    mean = jnp.mean(v, axis=-1, keepdims=True)
    cen = v - mean
    r = lax.rsqrt(jnp.mean(cen * cen, axis=-1, keepdims=True) + EPS)
    return cen * r, r


def norm(v, gain):
    u, _ = norm_parts(v)
    return u * gain


def norm_back(v, gain, e):
    u, r = norm_parts(v)
    eg = e * gain
    back = r * (eg - jnp.mean(eg, axis=-1, keepdims=True) - u * jnp.mean(eg * u, axis=-1, keepdims=True))
    return back, jnp.sum(e * u, axis=0, keepdims=True)


def sigmoid(v):
    return 1.0 / (1.0 + jnp.exp(-v))


def swish_and_slope(v):
    s = sigmoid(v)
    sv = s * v
    return sv, s + sv * (1.0 - s)


def cols(p, width=LANE):
    return pl.ds(pl.multiple_of(p * width, width), width)


def lane_half(e):
    lane = lax.broadcasted_iota(jnp.int32, (1, LANE), 1)
    return (lane < HD) if e == 0 else (lane >= HD)


def call(body, outs, ins, scratch=(), name=None):
    return pl.pallas_call(
        body,
        out_shape=[jax.ShapeDtypeStruct(s, d) for s, d in outs],
        in_specs=[
            pl.BlockSpec(memory_space=pltpu.SMEM) if x.dtype == jnp.int32 else pl.BlockSpec(memory_space=pltpu.VMEM)
            for x in ins
        ],
        out_specs=[pl.BlockSpec(memory_space=pltpu.VMEM) for _ in outs],
        scratch_shapes=list(scratch),
        compiler_params=pltpu.CompilerParams(vmem_limit_bytes=VMEM_LIMIT),
        name=name,
    )(*ins)


MESH = pl.DeviceIdType.MESH


class Place:
    def __init__(self):
        tms, slots = lax.axis_size("tm"), lax.axis_size("slot")
        wide = 1 << ((slots.bit_length() - 1) // 2)
        self.size = {"c": 2, "x": tms // 2, "y": wide, "z": slots // wide}
        self.tm, self.slot = lax.axis_index("tm"), lax.axis_index("slot")
        self.at = {
            "c": lax.rem(self.tm, 2),
            "x": lax.div(self.tm, 2),
            "y": lax.rem(self.slot, wide),
            "z": lax.div(self.slot, wide),
        }

    def peer(self, axis, off):
        pos = dict(self.at)
        pos[axis] = lax.rem(pos[axis] + off, self.size[axis])
        return (pos["x"] * 2 + pos["c"], pos["z"] * self.size["y"] + pos["y"]), pos[axis]

    def peers(self, axis):
        return [(off,) + self.peer(axis, off) for off in range(1, self.size[axis])]

    def greet(self, axes):
        bar = pltpu.get_barrier_semaphore()
        count = 0
        for axis in axes:
            for _, dev, _ in self.peers(axis):
                pl.semaphore_signal(bar, inc=1, device_id=dev, device_id_type=MESH)
                count += 1
        pl.semaphore_wait(bar, count)


def rows_at(start, size):
    return pl.ds(pl.multiple_of(start, 16), size)


def add_into(dst, start, lanes, terms, size):
    step = 64 if size % 64 == 0 else 16

    def one(i, carry):
        off = pl.multiple_of(i * step, step)
        total = terms[0](off, step).astype(F32)
        for term in terms[1:]:
            total = total + term(off, step).astype(F32)
        dst[pl.ds(pl.multiple_of(start + off, 16), step), lanes] = total.astype(dst.dtype)
        return carry

    lax.fori_loop(0, size // step, one, 0)


class Reducer:
    ORDERS = (("y", "x", "z"), ("x", "y", "z"))

    @staticmethod
    def scratch(rows, width, size):
        shapes = [pltpu.VMEM((rows // 2, width), BF)]
        sends = 2
        for order in Reducer.ORDERS:
            blk = rows // 2
            for axis in order:
                blk //= size[axis]
                shapes.append(pltpu.VMEM((size[axis] - 1, blk, width // 2), BF))
                sends += 2 * (size[axis] - 1)
            shapes.append(pltpu.VMEM((blk, width // 2), BF))
            sends += 1
        shapes += [pltpu.SemaphoreType.DMA((sends,)), pltpu.SemaphoreType.DMA((sends,)), pltpu.SemaphoreType.DMA((2,))]
        return shapes

    COUNT = 12

    def __init__(self, place, rows, width, src, out, first, bufs):
        self.place, self.rows, self.width, self.src, self.out, self.first = place, rows, width, src, out, first
        self.core = bufs[0]
        self.bufs = (bufs[1:4], bufs[5:8])
        self.fin = (bufs[4], bufs[8])
        self.ssem, self.rsem, self.lsem = bufs[9:12]
        self.next = 0
        self.copies = []
        self.half = [self.plan(0), self.plan(1)]

    def copy(self, src, dst, dev):
        k = self.next
        self.next += 1
        cp = (src, dst, k, dev)
        self.copies.append(cp)
        return cp

    def make(self, cp):
        src, dst, k, dev = cp
        return pltpu.make_async_remote_copy(
            src_ref=src(), dst_ref=dst(), send_sem=self.ssem.at[k], recv_sem=self.rsem.at[k], device_id=dev, device_id_type=MESH
        )

    def start(self, cps):
        for cp in cps:
            self.make(cp).start()

    def arrived(self, cps):
        for cp in cps:
            self.make(cp).wait_recv()

    def finish(self):
        for cp in self.copies:
            self.make(cp).wait_send()

    def plan(self, h):
        pc, hw = self.place, self.width // 2
        order = self.ORDERS[h]
        lanes = pl.ds(h * hw, hw)
        c = pc.at["c"]
        top = self.rows // 2
        core, bufs, fin, src, out, first = self.core, self.bufs[h], self.fin[h], self.src, self.out, self.first
        blk, rel = [top], [0]
        for axis in order:
            blk.append(blk[-1] // pc.size[axis])
            rel.append(rel[-1] + pc.at[axis] * blk[-1])
        stages = []
        (_, cdev, _), = pc.peers("c")
        ccopy = self.copy(
            lambda: src.at[rows_at((1 - c) * top, top), lanes], lambda: core.at[:, lanes], cdev
        )
        stages.append(lambda: self.start([ccopy]))
        out_at = lambda level: out.at[rows_at(first + c * top + rel[level], blk[level]), lanes]
        prev = [ccopy]
        downs = []
        for lv, axis in enumerate(order):
            cps = [
                self.copy(
                    lambda lv=lv, pos=pos: core.at[rows_at(rel[lv] + pos * blk[lv + 1], blk[lv + 1]), lanes],
                    lambda lv=lv, off=off: bufs[lv].at[off - 1],
                    dev,
                )
                for off, dev, pos in pc.peers(axis)
            ]
            downs.append(cps)

        def fold(lv, last):
            if lv == 0:
                terms = [
                    lambda o, n: src[pl.ds(pl.multiple_of(c * top + o, 16), n), lanes],
                    lambda o, n: core[pl.ds(o, n), lanes],
                ]
                add_into(core, 0, lanes, terms, top)
                return
            terms = [lambda o, n: core[pl.ds(pl.multiple_of(rel[lv] + o, 16), n), lanes]]
            for k in range(pc.size[order[lv - 1]] - 1):
                terms.append(lambda o, n, k=k: bufs[lv - 1][k, pl.ds(o, n), :])
            if last:
                add_into(fin, 0, slice(None), terms, blk[lv])
            else:
                add_into(core, rel[lv], lanes, terms, blk[lv])

        def step(lv):
            def run():
                self.arrived([ccopy] if lv == 0 else downs[lv - 1])
                fold(lv, False)
                self.start(downs[lv])

            return run

        for lv in range(3):
            stages.append(step(lv))
        up = [[self.copy(lambda: fin, lambda: out_at(3), dev) for _, dev, _ in pc.peers("z")]]
        up.append([self.copy(lambda: out_at(2), lambda: out_at(2), dev) for _, dev, _ in pc.peers(order[1])])
        up.append([self.copy(lambda: out_at(1), lambda: out_at(1), dev) for _, dev, _ in pc.peers(order[0])])
        up.append([self.copy(lambda: out_at(0), lambda: out_at(0), cdev)])
        mine = lambda: pltpu.make_async_copy(fin, out_at(3), self.lsem.at[h])

        def turn():
            self.arrived(downs[2])
            fold(3, True)
            mine().start()
            self.start(up[0])

        stages.append(turn)

        def climb(i):
            def run():
                if i == 0:
                    mine().wait()
                self.arrived(up[i])
                if i + 1 < len(up):
                    self.start(up[i + 1])

            return run

        for i in range(4):
            stages.append(climb(i))
        return stages

    def stage(self, i):
        for h in range(2):
            self.half[h][i]()

    STAGES = 9


FLAT = {"f1i": 0, "f1o": 2048, "q": 4096, "k": 4608, "v": 5120, "p": 5632, "o": 6144, "ci": 6656, "co": 7680, "f2i": 8192, "f2o": 10240}
FLAT_ROWS = 12288
ORDER = tuple(FLAT)
FOLDS = {"f1i": 4, "ci": 2, "f2i": 4}
FLAT_SIZE = {n: (list(FLAT.values()) + [FLAT_ROWS])[i + 1] - FLAT[n] for i, n in enumerate(FLAT)}


def gather_body(*refs):
    shard, raws, wn = refs[0], refs[1:12], refs[12]
    nb, wf, scr, ssem, rsem, lsem, wsem = refs[13:]
    pc = Place()
    x, c, z, y = (pc.at[a] for a in "xczy")
    loads = []
    for name, raw in zip(ORDER, raws):
        for j in range(FOLDS.get(name, 1)):
            size = FLAT_SIZE[name] // FOLDS.get(name, 1)
            dst = wf.at[pl.ds(FLAT[name] + j * size, size), :]
            loads.append(pltpu.make_async_copy(raw.at[:, pl.ds(j * 512, 512)], dst, wsem.at[len(loads)]))
    own = pltpu.make_async_copy(shard, nb.at[x, c, z, y], lsem.at[0])
    own.start()
    for cp in loads:
        cp.start()
    pc.greet("cxyz")
    own.wait()
    shard_rows = shard.shape[0]
    pieces = 3
    part = shard_rows // pieces
    hw = 256
    count = [0]
    sent = []

    def copy(ref, dev):
        k = count[0]
        count[0] += 1
        cp = pltpu.make_async_remote_copy(
            src_ref=ref, dst_ref=ref, send_sem=ssem.at[k], recv_sem=rsem.at[k], device_id=dev, device_id_type=MESH
        )
        sent.append(cp)
        return cp

    plans = {}
    for q in range(pieces):
        for h in range(2):
            lanes, rows = pl.ds(h * hw, hw), pl.ds(q * part, part)
            second, third = ("x", "y") if h == 0 else ("y", "x")
            blocks = {
                "z": nb.at[x, c, z, y, rows, lanes],
                second: nb.at[x, c, :, y, rows, lanes],
                third: nb.at[:, c, :, y, rows, lanes] if third == "y" else nb.at[x, c, :, :, rows, lanes],
                "c": nb.at[:, c, :, :, rows, lanes],
            }
            plans[q, h] = [[copy(blocks[a], dev) for _, dev, _ in pc.peers(a)] for a in ("z", second, third, "c")]

    unit = 128 if part % 128 == 0 else 64
    sub = math.gcd(unit, part)

    def noise_at(row):
        got = []
        for i in range(unit // sub):
            at = row + i * sub
            d = lax.div(at, shard_rows)
            tm, sl = lax.div(d, pc.size["z"] * pc.size["y"]), lax.rem(d, pc.size["z"] * pc.size["y"])
            off = pl.multiple_of(lax.rem(at, shard_rows), 16)
            got.append(
                nb[lax.div(tm, 2), lax.rem(tm, 2), lax.div(sl, pc.size["y"]), lax.rem(sl, pc.size["y"]), pl.ds(off, sub), :].astype(F32)
            )
        return got[0] if len(got) == 1 else jnp.concatenate(got, axis=0)

    def mix(row, base, size, fold):
        value = noise_at(row)
        if fold == 1:
            at = rows_at(row, unit)
            wf[at, :] = (wf[at, :].astype(F32) + value).astype(BF)
            return
        for b in range(512 // LANE):
            scr[b, pl.ds(0, unit), :] = value[:, b * LANE : (b + 1) * LANE]
        high = unit // fold
        for j in range(fold):
            at = rows_at(base + j * (size // fold) + lax.div(row - base, fold), high)
            for b in range(512 // LANE):
                lanes = pl.ds(b * LANE, LANE)
                wf[at, lanes] = (wf[at, lanes].astype(F32) + scr[b, pl.ds(j, high, stride=fold), :]).astype(BF)

    def mix_range(low, high, q):
        for name in ORDER:
            base, size = FLAT[name], FLAT_SIZE[name]
            if not low <= base < high:
                continue
            if q is None:
                lax.fori_loop(0, size // unit, lambda i, t: (mix(base + i * unit, base, size, FOLDS.get(name, 1)), t)[1], 0)
                continue
            begin, end = base // unit, (base + size) // unit
            start = begin + (q - begin) % pieces
            lax.fori_loop(
                0, (end - start + pieces - 1) // pieces,
                lambda i, t: (mix((start + i * pieces) * unit, base, size, FOLDS.get(name, 1)), t)[1], 0,
            )

    def arrived(cps):
        for cp in cps:
            cp.wait_recv()

    loaded = False
    for t in range(pieces + 4):
        for q in range(pieces):
            s = t - q
            if 0 <= s <= 4:
                for h in range(2):
                    if s > 0:
                        arrived(plans[q, h][s - 1])
                    if s < 4:
                        for cp in plans[q, h][s]:
                            cp.start()
        q = t - 4
        if q >= 0 and part == unit:
            if not loaded:
                for cp in loads:
                    cp.wait()
                loaded = True
            mix_range(0, FLAT_ROWS, q)
    if part != unit:
        for cp in loads:
            cp.wait()
        mix_range(0, FLAT_ROWS, None)
    outs = [pltpu.make_async_copy(wf.at[pl.ds(i * 2048, 2048), :], wn.at[pl.ds(i * 2048, 2048), :], wsem.at[i]) for i in range(6)]
    for cp in outs:
        cp.start()
    for cp in sent:
        cp.wait_send()
    for cp in outs:
        cp.wait()


def chunk(c):
    return pl.ds(pl.multiple_of(c * 512, 512), 512)


def ffn_forward(normed, w_in, w_out, pre_ref):
    def one(c, acc):
        pre = dot(normed, w_in[chunk(c), :])
        pre_ref[:, chunk(c)] = pre
        return acc + dot((pre * sigmoid(pre)).astype(BF), w_out[chunk(c), :])

    return lax.fori_loop(0, w_in.shape[0] // 512, one, jnp.zeros((normed.shape[0], w_out.shape[1]), F32))


def ffn_backward(g_low, normed, w_in, w_out, pre_ref, gin_ref, gout_ref):
    normed_t = normed.T

    def one(c, acc):
        sw, slope = swish_and_slope(pre_ref[:, chunk(c)])
        gout_ref[chunk(c), :] = dot_tn(sw.astype(BF), g_low).astype(gout_ref.dtype)
        dpre = (dot_nt(g_low, w_out[chunk(c), :]) * slope).astype(BF)
        gin_ref[chunk(c), :] = dot(normed_t, dpre).astype(gin_ref.dtype)
        return acc + dot_nt(dpre, w_in[chunk(c), :])

    return lax.fori_loop(0, w_in.shape[0] // 512, one, jnp.zeros(g_low.shape, F32))


class Fetch:
    def __init__(self, sems):
        self.sems, self.n = sems, 0

    def __call__(self, src, dst):
        cp = pltpu.make_async_copy(src, dst, self.sems.at[self.n])
        self.n += 1
        cp.start()
        return cp


def part_of(wn, name):
    return wn.at[pl.ds(FLAT[name], FLAT_SIZE[name]), :]


def fwd1_body(x_ref, w1, wqkv, gain1, gain2, pos_u, pos_v, x1_ref, pre_ref, a2_ref, qu_ref, qv_ref, k_ref, v_ref):
    x = x_ref[...].astype(F32)
    a1 = norm(x, gain1[...]).astype(BF)
    x1 = x + 0.5 * ffn_forward(a1, w1.at[pl.ds(0, 2048), :], w1.at[pl.ds(2048, 2048), :], pre_ref)
    x1_ref[...] = x1
    a2 = norm(x1, gain2[...]).astype(BF)
    a2_ref[...] = a2
    q = dot(a2, wqkv[pl.ds(0, 512), :])
    scale = HD**-0.5
    qu_ref[...] = ((q + pos_u[...]).astype(BF).astype(F32) * scale).astype(BF)
    qv_ref[...] = ((q + pos_v[...]).astype(BF).astype(F32) * scale).astype(BF)
    k_ref[...] = dot(a2, wqkv[pl.ds(512, 512), :]).astype(BF)
    v_ref[...] = dot(a2, wqkv[pl.ds(1024, 512), :]).astype(BF)


def att_fwd_body(lens, qu, qv, k, v, w_pos, trig, sin, cos, att_ref, p_ref, s_scr):
    rows, frames = qu.shape[0], k.shape[0]
    half = sin.shape[1]
    ok = lax.broadcasted_iota(jnp.int32, (1, frames), 1) < lens[0]

    def pair(p, carry):
        at = cols(p)
        mixed = None
        for e in range(2):
            mine = lane_half(e)
            qve = jnp.where(mine, qv[:, at], jnp.zeros((), BF))
            que = jnp.where(mine, qu[:, at], jnp.zeros((), BF))
            a_s = dot_nt(qve, w_pos[pl.ds(0, half), at])
            a_c = dot_nt(qve, w_pos[pl.ds(half, half), at])
            b_c = (a_s * sin[...] + a_c * cos[...]).astype(BF)
            b_s = (a_c * sin[...] - a_s * cos[...]).astype(BF)
            s = dot_nt(b_s, trig[:, pl.ds(0, half)]) + dot_nt(b_c, trig[:, pl.ds(half, half)]) + dot_nt(que, k[:, at])
            s = jnp.where(ok, s, FILL)
            m = jnp.max(s, axis=-1, keepdims=True)
            ex = jnp.exp(s - m)
            tot = jnp.sum(ex, axis=-1, keepdims=True)
            low = (ex * (1.0 / tot)).astype(BF)
            p_ref[2 * p + e] = low
            part = dot(low, v[:, at])
            mixed = part if e == 0 else jnp.where(mine, part, mixed)
        att_ref[:, at] = mixed.astype(BF)
        return carry

    lax.fori_loop(0, H // 2, pair, 0)


def att_bwd_body(qu, qv, k, v, w_pos, trig, sin, cos, p_ref, datt, att, dq_ref, dkt_ref, dvt_ref, gpos_ref, gu_ref, gv_ref, qut, qvt, datt_t, gpost):
    half = sin.shape[1]
    qut[...] = qu[...].T
    qvt[...] = qv[...].T
    datt_t[...] = datt[...].T

    def pair(p, carry):
        at = cols(p)
        dqu = dqv = None
        for e in range(2):
            mine = lane_half(e)
            rows = pl.ds(pl.multiple_of(p * LANE + e * HD, HD), HD)
            dm = jnp.where(mine, datt[:, at], jnp.zeros((), BF))
            inner = jnp.sum(dm.astype(F32) * att[:, at].astype(F32), axis=-1, keepdims=True)
            low = p_ref[2 * p + e]
            dp = dot_nt(dm, v[:, at])
            ds = (low.astype(F32) * (dp - inner)).astype(BF)
            dkt_ref[rows, :] = dot(qut[rows, :], ds).astype(BF)
            dvt_ref[rows, :] = dot(datt_t[rows, :], low).astype(BF)
            db_s = dot(ds, trig[:, pl.ds(0, half)])
            db_c = dot(ds, trig[:, pl.ds(half, half)])
            da_s = (db_c * sin[...] - db_s * cos[...]).astype(BF)
            da_c = (db_c * cos[...] + db_s * sin[...]).astype(BF)
            gpost[rows, pl.ds(0, half)] = dot(qvt[rows, :], da_s)
            gpost[rows, pl.ds(half, half)] = dot(qvt[rows, :], da_c)
            part_v = dot(da_s, w_pos[pl.ds(0, half), at]) + dot(da_c, w_pos[pl.ds(half, half), at])
            part_u = dot(ds, k[:, at])
            dqu = part_u if e == 0 else jnp.where(mine, part_u, dqu)
            dqv = part_v if e == 0 else jnp.where(mine, part_v, dqv)
        scale = HD**-0.5
        dqu = dqu * scale
        dqv = dqv * scale
        dq_ref[:, at] = (dqu + dqv).astype(BF)
        gu_ref[:, at] = jnp.sum(dqu, axis=0, keepdims=True)
        gv_ref[:, at] = jnp.sum(dqv, axis=0, keepdims=True)
        return carry

    lax.fori_loop(0, H // 2, pair, 0)
    gpos_ref[...] = gpost[...].T.astype(gpos_ref.dtype)


def valid_rows(lens, rows):
    first = lax.axis_index("tm") * rows
    return ((first + lax.broadcasted_iota(jnp.int32, (rows, 1), 0)) < lens[0]).astype(F32)


def spread(ext, start, value):
    value = value.astype(F32)
    for b in range(ext.shape[0]):
        ext[b, pl.ds(start, value.shape[0]), :] = value[:, b * LANE : (b + 1) * LANE]


def tap_sum(ext, taps, out_ref, offset):
    count = taps.shape[0]
    rows = out_ref.shape[0]
    block = 64 if rows % 64 == 0 else 16

    def one(i, carry):
        for b in range(ext.shape[0]):
            at = pl.ds(b * LANE, LANE)
            acc = jnp.zeros((block, LANE), F32)
            for k in range(count):
                acc = acc + taps[pl.ds(k, 1), at] * ext[b, pl.ds(i * block + offset(k), block), :]
            out_ref[pl.ds(pl.multiple_of(i * block, block), block), at] = acc
        return carry

    lax.fori_loop(0, rows // block, one, 0)


def bn_stats(sums):
    total = sums[2:3, :]
    mu = sums[0:1, :] / total
    var = sums[1:2, :] / total - mu * mu
    return mu, lax.rsqrt(var + EPS), total


class Totals:
    @staticmethod
    def scratch(tms, slots, width):
        n = tms + slots - 2
        return [
            pltpu.VMEM((tms, 8, width), F32),
            pltpu.VMEM((slots, 8, width), F32),
            pltpu.SemaphoreType.DMA((n,)),
            pltpu.SemaphoreType.DMA((n,)),
        ]

    def __init__(self, pc, bufs):
        self.pc, self.bufs = pc, bufs

    def __call__(self, value):
        pc = self.pc
        tmb, slb, ssem, rsem = self.bufs
        sent = []
        k = 0
        for buf, axis, me in ((tmb, "tm", pc.tm), (slb, "slot", pc.slot)):
            buf[me] = value
            n = buf.shape[0]
            cps = []
            for off in range(1, n):
                to = lax.rem(me + off, n)
                dev = (to, pc.slot) if axis == "tm" else (pc.tm, to)
                cp = pltpu.make_async_remote_copy(
                    src_ref=buf.at[me], dst_ref=buf.at[me], send_sem=ssem.at[k], recv_sem=rsem.at[k], device_id=dev, device_id_type=MESH
                )
                cp.start()
                cps.append(cp)
                k += 1
            for cp in cps:
                cp.wait_recv()
            sent += cps
            value = buf[0]
            for i in range(1, n):
                value = value + buf[i]
        for cp in sent:
            cp.wait_send()
        return value


def greet_rows(pc, tms, slots):
    bar = pltpu.get_barrier_semaphore()
    for off in range(1, tms):
        pl.semaphore_signal(bar, inc=1, device_id=(lax.rem(pc.tm + off, tms), pc.slot), device_id_type=MESH)
    for off in range(1, slots):
        pl.semaphore_signal(bar, inc=1, device_id=(pc.tm, lax.rem(pc.slot + off, slots)), device_id_type=MESH)
    pl.semaphore_wait(bar, tms + slots - 2)


def middle_body(
    lens, att, x1_ref, cot, wn, taps, bn_gain, bn_bias, gain3, gain4, gain5,
    out_ref, dx2_ref, datt_ref, g_ref, smalls_ref, bns_ref,
    w_o, w_ci, w_co, w_f2i, w_f2o, fsem, early, late, hsem, gm_ref, ddwo_ref, z_ref, ext, ext2, dwo_ref, pre_ref, dgm_ref, acc, x2_ref, *bufs,
):
    pc = Place()
    tms, slots = lax.axis_size("tm"), lax.axis_size("slot")
    rows, width = x1_ref.shape
    count = taps.shape[0]
    fetch = Fetch(fsem)
    got = {n: fetch(part_of(wn, n), d) for n, d in (("o", w_o), ("ci", w_ci), ("co", w_co), ("f2i", w_f2i), ("f2o", w_f2o))}
    greet_rows(pc, tms, slots)
    totals = Totals(pc, bufs[:4]), Totals(pc, bufs[4:])

    def halo(src, dst, k, step):
        dev = (lax.rem(pc.tm + step + tms, tms), pc.slot)
        return pltpu.make_async_remote_copy(
            src_ref=src, dst_ref=dst, send_sem=hsem.at[2 * k], recv_sem=hsem.at[2 * k + 1], device_id=dev, device_id_type=MESH
        )

    got["o"].wait()
    x2 = x1_ref[...] + dot(att[...], w_o[...])
    x2_ref[...] = x2
    a3 = norm(x2, gain3[...]).astype(BF)
    got["ci"].wait()
    z1 = dot(a3, w_ci[pl.ds(0, width), :])
    z2 = dot(a3, w_ci[pl.ds(width, width), :])
    z_ref[:, pl.ds(0, width)] = z1
    z_ref[:, pl.ds(width, width)] = z2
    ok = valid_rows(lens, rows)
    gm_ref[...] = (z1 * sigmoid(z2) * ok).astype(BF)
    cp = halo(gm_ref.at[pl.ds(rows - count, count), :], early, 0, 1)
    cp.start()
    spread(ext, count, gm_ref[...])
    cp.wait()
    spread(ext, 0, jnp.where(pc.tm > 0, early[...], jnp.zeros((), BF)))
    tap_sum(ext, taps, dwo_ref, lambda k: k + 1)
    dwo = dwo_ref[...]
    dwv = dwo * ok
    sums = totals[0](
        jnp.concatenate(
            [
                jnp.sum(dwv, axis=0, keepdims=True),
                jnp.sum(dwv * dwv, axis=0, keepdims=True),
                jnp.zeros((1, width), F32) + jnp.sum(ok, axis=0, keepdims=True),
                jnp.zeros((5, width), F32),
            ],
            axis=0,
        )
    )
    mu, inv, total = bn_stats(sums)
    xhat = (dwo_ref[...] - mu) * inv
    sw, slope = swish_and_slope(xhat * bn_gain[...] + bn_bias[...])
    sw = sw.astype(BF)
    got["co"].wait()
    x3 = x2_ref[...] + dot(sw, w_co[...])
    a4 = norm(x3, gain4[...]).astype(BF)
    got["f2i"].wait()
    got["f2o"].wait()
    x4 = x3 + 0.5 * ffn_forward(a4, w_f2i, w_f2o, pre_ref)
    out_ref[...] = norm(x4, gain5[...]).astype(BF)
    dx4, gg5 = norm_back(x4, gain5[...], cot[...].astype(F32))
    g4 = (0.5 * dx4).astype(BF)
    lo = FLAT["o"]
    da4 = ffn_backward(
        g4, a4, w_f2i, w_f2o, pre_ref,
        g_ref.at[pl.ds(FLAT["f2i"] - lo, 2048), :], g_ref.at[pl.ds(FLAT["f2o"] - lo, 2048), :],
    )
    back, gg4 = norm_back(x3, gain4[...], da4)
    dx3 = dx4 + back
    g3 = dx3.astype(BF)
    dbn = dot_nt(g3, w_co[...]) * slope
    sums2 = totals[1](
        jnp.concatenate(
            [jnp.sum(dbn * xhat, axis=0, keepdims=True), jnp.sum(dbn, axis=0, keepdims=True), jnp.zeros((6, width), F32)], axis=0
        )
    )
    bns_ref[...] = sums2
    ddwo_ref[...] = (bn_gain[...] * inv * (dbn - ok * (sums2[1:2, :] + xhat * sums2[0:1, :]) / total)).astype(BF)
    cp = halo(ddwo_ref.at[pl.ds(0, count), :], late, 1, -1)
    cp.start()
    g_ref[pl.ds(FLAT["co"] - lo, width), :] = dot_tn(sw, g3).astype(BF)
    spread(ext2, 0, ddwo_ref[...])
    cp.wait()
    spread(ext2, rows, jnp.where(pc.tm < tms - 1, late[...], jnp.zeros((), BF)))
    tap_sum(ext2, taps, dgm_ref, lambda k: count - 1 - k)
    block = 64 if rows % 64 == 0 else 16
    for b in range(ext.shape[0]):
        acc[...] = jnp.zeros(acc.shape, F32)

        def one(i, carry, b=b):
            mine = ext2[b, pl.ds(pl.multiple_of(i * block, block), block), :]
            for k in range(count):
                prod = mine * ext[b, pl.ds(i * block + k + 1, block), :]
                acc[k] = acc[k] + jnp.sum(prod.reshape(block // 8, 8, LANE), axis=0)
            return carry

        lax.fori_loop(0, rows // block, one, 0)
        smalls_ref[pl.ds(0, count), pl.ds(b * LANE, LANE)] = jnp.sum(acc[...], axis=1)
    z1 = z_ref[:, pl.ds(0, width)]
    sg = sigmoid(z_ref[:, pl.ds(width, width)])
    dg = dgm_ref[...] * ok
    dz1 = (dg * sg).astype(BF)
    dz2 = (dg * z1 * sg * (1.0 - sg)).astype(BF)
    a3t = norm(x2_ref[...], gain3[...]).astype(BF).T
    g_ref[pl.ds(FLAT["ci"] - lo, width), :] = dot(a3t, dz1).astype(BF)
    g_ref[pl.ds(FLAT["ci"] - lo + width, width), :] = dot(a3t, dz2).astype(BF)
    da3 = dot_nt(dz1, w_ci[pl.ds(0, width), :]) + dot_nt(dz2, w_ci[pl.ds(width, width), :])
    back, gg3 = norm_back(x2_ref[...], gain3[...], da3)
    dx2 = dx3 + back
    dx2_ref[...] = dx2
    g2 = dx2.astype(BF)
    g_ref[pl.ds(0, width), :] = dot_tn(att[...], g2).astype(BF)
    datt_ref[...] = dot_nt(g2, w_o[...]).astype(BF)
    smalls_ref[pl.ds(count, 8), :] = jnp.concatenate([gg3, gg4, gg5, jnp.zeros((5, width), F32)], axis=0)


def bwd3_body(
    dq, dkt, dvt, gpos, a2, x1_ref, dx2_ref, x_ref, pre_ref, wqkv, w1, gain2, gain1,
    dx0_ref, g_ref, gg_ref,
):
    a2t = a2[...].T
    lo = FLAT["q"]
    g_ref[pl.ds(FLAT["q"], 512), :] = dot(a2t, dq[...]).astype(BF)
    g_ref[pl.ds(FLAT["k"], 512), :] = dot_nt(a2t, dkt[...]).astype(BF)
    g_ref[pl.ds(FLAT["v"], 512), :] = dot_nt(a2t, dvt[...]).astype(BF)
    g_ref[pl.ds(FLAT["p"], 512), :] = gpos[...]
    da2 = dot_nt(dq[...], wqkv[pl.ds(0, 512), :]) + dot_nt(dkt[...].T, wqkv[pl.ds(512, 512), :]) + dot_nt(dvt[...].T, wqkv[pl.ds(1024, 512), :])
    back, gg2 = norm_back(x1_ref[...], gain2[...], da2)
    dx1 = dx2_ref[...] + back
    g1 = (0.5 * dx1).astype(BF)
    x = x_ref[...].astype(F32)
    a1 = norm(x, gain1[...]).astype(BF)
    da1 = ffn_backward(
        g1, a1, w1.at[pl.ds(0, 2048), :], w1.at[pl.ds(2048, 2048), :], pre_ref, g_ref.at[pl.ds(0, 2048), :], g_ref.at[pl.ds(2048, 2048), :]
    )
    back, gg1 = norm_back(x, gain1[...], da1)
    dx0_ref[...] = (dx1 + back).astype(BF)
    gg_ref[0:1, :] = gg1
    gg_ref[1:2, :] = gg2


class Butterfly:
    @staticmethod
    def scratch(devices, shape):
        n = devices.bit_length() - 1
        return [pltpu.VMEM((n,) + shape, F32), pltpu.SemaphoreType.DMA((n,)), pltpu.SemaphoreType.DMA((n,))]

    def __init__(self, pc, value, bufs):
        self.value, (self.got, self.ssem, self.rsem) = value, bufs
        self.devs = []
        for axis, me in (("tm", pc.tm), ("slot", pc.slot)):
            bit = 1
            while bit < lax.axis_size(axis):
                to = me + bit - 2 * bit * lax.rem(lax.div(me, bit), 2)
                self.devs.append((to, pc.slot) if axis == "tm" else (pc.tm, to))
                bit *= 2

    def copy(self, k):
        return pltpu.make_async_remote_copy(
            src_ref=self.value, dst_ref=self.got.at[k], send_sem=self.ssem.at[k], recv_sem=self.rsem.at[k],
            device_id=self.devs[k], device_id_type=MESH,
        )

    def stage(self, k):
        if k > 0:
            self.copy(k - 1).wait()
            self.value[...] = self.value[...] + self.got[k - 1]
        if k < len(self.devs):
            self.copy(k).start()


GROUP = 2048


def reduce_body(g_low, g_high, smalls, out, total_ref, *bufs):
    pc = Place()
    pc.greet("cxyz")
    groups = []
    per = Reducer.COUNT
    size = g_low.shape[0] // GROUP
    n = 2 * size
    for i in range(n):
        src = (g_high if i < size else g_low).at[pl.ds(GROUP * (i % size), GROUP), :]
        first = GROUP * (i % size) + (g_low.shape[0] if i < size else 0)
        groups.append(Reducer(pc, GROUP, 512, src, out, first, bufs[i * per : (i + 1) * per]))
    fly = Butterfly(pc, total_ref, bufs[n * per :])
    total_ref[...] = smalls[...]
    for t in range(Reducer.STAGES + n - 1):
        for i, grp in enumerate(groups):
            if 0 <= t - i < Reducer.STAGES:
                grp.stage(t - i)
        if t <= len(fly.devs):
            fly.stage(t)
    for t in range(Reducer.STAGES + n - 1, len(fly.devs) + 1):
        fly.stage(t)
    for grp in groups:
        grp.finish()


def widen_body(flat, *refs):
    outs, (ibuf, obuf, isem, osem) = refs[:11], refs[11:]
    step = 512
    n = FLAT_ROWS // step
    loads = [pltpu.make_async_copy(flat.at[pl.ds(i * step, step), :], ibuf.at[i], isem.at[i]) for i in range(n)]
    for cp in loads:
        cp.start()
    stores = []
    slots = obuf.shape[0]
    for i in range(n):
        name = [m for m in ORDER if FLAT[m] <= i * step][-1]
        out = outs[ORDER.index(name)]
        off = i * step - FLAT[name]
        fold = FOLDS.get(name, 1)
        if fold == 1:
            dst = out.at[pl.ds(off, step), :]
        else:
            dst = out.at[:, pl.ds(off, step)]
        loads[i].wait()
        if i >= slots:
            stores[i - slots].wait()
        obuf[i % slots] = ibuf[i].astype(F32)
        stores.append(pltpu.make_async_copy(obuf.at[i % slots], dst, osem.at[i % slots]))
        stores[-1].start()
    for cp in stores[-slots:]:
        cp.wait()


def remote(body, cid, outs, ins, scratch, name):
    def space(x):
        if x is None:
            return pl.BlockSpec(memory_space=pl.ANY)
        return pl.BlockSpec(memory_space=x)

    return pl.pallas_call(
        body,
        out_shape=[jax.ShapeDtypeStruct(s, d) for s, d, _ in outs],
        in_specs=[space(m) for _, m in ins],
        out_specs=[space(m) for _, _, m in outs],
        scratch_shapes=list(scratch),
        compiler_params=pltpu.CompilerParams(collective_id=cid, has_side_effects=True, vmem_limit_bytes=VMEM_LIMIT),
        name=name,
    )(*[x for x, _ in ins])


def local(
    inputs, cotangent, lengths, weight_noise, ffn1_in, ffn1_out, query_w, key_w, value_w, pos_w, out_w,
    conv_in, conv_out, ffn2_in, ffn2_out, conv_kernel, ffn1_gain, attn_gain, conv_gain, ffn2_gain,
    final_gain, bn_gain, bn_bias, pos_u, pos_v,
):
    _, rows, width = inputs.shape
    tms, slots = lax.axis_size("tm"), lax.axis_size("slot")
    frames = rows * tms
    count = conv_kernel.shape[0]
    devices = tms * slots
    size = Place().size
    x = inputs[0]
    cot = cotangent[0]
    gains = [g.reshape(1, -1) for g in (ffn1_gain, attn_gain, conv_gain, ffn2_gain, final_gain)]
    bng, bnb, pu, pv = (g.reshape(1, -1) for g in (bn_gain, bn_bias, pos_u, pos_v))
    raws = (ffn1_in, ffn1_out, query_w, key_w, value_w, pos_w, out_w, conv_in, conv_out, ffn2_in, ffn2_out)
    VM, HB, SM = pltpu.VMEM, None, pltpu.SMEM
    DMA = pltpu.SemaphoreType.DMA
    shard = weight_noise.reshape(-1, width)
    links = sum(n - 1 for n in size.values())
    (wn,) = remote(
        gather_body, 0, [((FLAT_ROWS, width), BF, HB)], [(shard, HB)] + [(r, HB) for r in raws],
        [
            pltpu.VMEM((size["x"], 2, size["z"], size["y"], shard.shape[0], width), BF),
            pltpu.VMEM((FLAT_ROWS, width), BF),
            pltpu.VMEM((width // LANE, 128, LANE), F32),
            DMA((6 * links,)), DMA((6 * links,)), DMA((1,)), DMA((18,)),
        ],
        "gather",
    )
    w1, wqkv, w_p = wn[:4096], wn[4096:5632], wn[5632:6144]

    half = width // 2
    rates = jnp.exp(jnp.arange(half, dtype=F32) * (-2.0 * math.log(10000.0) / width))
    angles = jnp.arange(frames, dtype=F32)[:, None] * rates[None, :]
    sin_all, cos_all = jnp.sin(angles), jnp.cos(angles)
    trig = jnp.concatenate([sin_all, cos_all], axis=1).astype(BF)
    first = lax.axis_index("tm") * rows
    sin = lax.dynamic_slice_in_dim(sin_all, first, rows, 0)
    cos = lax.dynamic_slice_in_dim(cos_all, first, rows, 0)

    act, actb = ((rows, width), F32), ((rows, width), BF)
    hidden = 2048
    x1, pre1, a2, qu, qv, k, v = call(
        fwd1_body, [act, ((rows, hidden), F32), actb, actb, actb, actb, actb],
        (x, w1, wqkv, gains[0], gains[1], pu, pv), name="fwd1",
    )
    k_all = lax.all_gather(k, "tm", axis=0, tiled=True)
    v_all = lax.all_gather(v, "tm", axis=0, tiled=True)
    att, probs = call(
        att_fwd_body, [actb, ((H, rows, frames), BF)], (lengths, qu, qv, k_all, v_all, w_p, trig, sin, cos),
        [pltpu.VMEM((8, LANE), F32)], name="att_fwd",
    )
    ext = pltpu.VMEM((width // LANE, rows + count, LANE), F32)
    output, dx2, datt, g_high, smalls2, bns = remote(
        middle_body, 1,
        [((rows, width), BF, VM), ((rows, width), F32, VM), ((rows, width), BF, VM), ((FLAT_ROWS // 2, width), BF, VM),
         ((count + 8, width), F32, VM), ((8, width), F32, VM)],
        [(lengths, SM), (att, VM), (x1, VM), (cot, VM), (wn, HB), (conv_kernel, VM), (bng, VM), (bnb, VM)] + [(g, VM) for g in gains[2:]],
        [pltpu.VMEM((FLAT_SIZE[n], width), BF) for n in ("o", "ci", "co", "f2i", "f2o")]
        + [DMA((5,)), pltpu.VMEM((count, width), BF), pltpu.VMEM((count, width), BF), DMA((4,)),
           pltpu.VMEM((rows, width), BF), pltpu.VMEM((rows, width), BF), pltpu.VMEM((rows, 2 * width), F32), ext, ext,
           pltpu.VMEM((rows, width), F32), pltpu.VMEM((rows, hidden), F32), pltpu.VMEM((rows, width), F32),
           pltpu.VMEM((count, 8, LANE), F32), pltpu.VMEM((rows, width), F32)]
        + Totals.scratch(tms, slots, width) * 2,
        "middle",
    )
    wide = ((width, frames), BF)
    vec = ((1, width), F32)
    dq, dkt, dvt, g_p, gu, gv = call(
        att_bwd_body, [actb, wide, wide, ((width, width), BF), vec, vec],
        (qu, qv, k_all, v_all, w_p, trig, sin, cos, probs, datt, att),
        [pltpu.VMEM((width, rows), BF)] * 3 + [pltpu.VMEM((width, width), F32)], name="att_bwd",
    )
    dkt = lax.psum_scatter(dkt, "tm", scatter_dimension=1, tiled=True)
    dvt = lax.psum_scatter(dvt, "tm", scatter_dimension=1, tiled=True)
    dx0, g_low, gg12 = call(
        bwd3_body, [actb, ((FLAT_ROWS // 2, width), BF), ((2, width), F32)],
        (dq, dkt, dvt, g_p, a2, x1, dx2, x, pre1, wqkv, w1, gains[1], gains[0]), name="bwd3",
    )
    smalls = jnp.concatenate([smalls2[: count + 3], gg12, gu, gv, jnp.zeros((1, width), F32)], axis=0)
    flat, total = remote(
        reduce_body, 2, [((FLAT_ROWS, width), BF, HB), (smalls.shape, F32, VM)],
        [(g_low, VM), (g_high, VM), (smalls, VM)],
        Reducer.scratch(GROUP, width, size) * (FLAT_ROWS // GROUP) + Butterfly.scratch(devices, smalls.shape), "reduce",
    )
    big = pl.pallas_call(
        widen_body,
        out_shape=[jax.ShapeDtypeStruct(r.shape, F32) for r in raws],
        in_specs=[pl.BlockSpec(memory_space=pl.ANY)],
        out_specs=[pl.BlockSpec(memory_space=pl.ANY)] * 11,
        scratch_shapes=[pltpu.VMEM((24, 512, width), BF), pltpu.VMEM((4, 512, width), F32), DMA((24,)), DMA((4,))],
        compiler_params=pltpu.CompilerParams(vmem_limit_bytes=VMEM_LIMIT),
        name="widen",
    )(flat)
    t = total[count:]
    return (output[None], dx0[None]) + tuple(big) + (
        total[:count], t[3], t[4], t[0], t[1], t[2], bns[0], bns[1], t[5], t[6],
    )


def solution(mesh):
    split = P("slot", "tm", None)
    in_specs = (split, split, P("slot"), P(("tm", "slot"), None)) + (P(),) * 21
    out_specs = (split, split) + (P(),) * 21
    return jax.shard_map(local, mesh=mesh, in_specs=in_specs, out_specs=out_specs, check_vma=False)
```

```python
import math

import jax
import jax.numpy as jnp
from jax import lax
from jax.experimental import pallas as pl
from jax.experimental.pallas import tpu as pltpu
from jax.sharding import PartitionSpec as P

H = 8
HD = 64
LANE = 128
F32 = jnp.float32
BF = jnp.bfloat16
EPS = 1e-05
FILL = -1e30
VMEM_LIMIT = 60 * 2**20


def dot(a, b):
    return lax.dot_general(a, b, (((1,), (0,)), ((), ())), preferred_element_type=F32)


def dot_nt(a, b):
    return lax.dot_general(a, b, (((1,), (1,)), ((), ())), preferred_element_type=F32)


def dot_tn(a, b):
    return lax.dot_general(a, b, (((0,), (0,)), ((), ())), preferred_element_type=F32)


def norm_parts(v):
    mean = jnp.mean(v, axis=-1, keepdims=True)
    cen = v - mean
    r = lax.rsqrt(jnp.mean(cen * cen, axis=-1, keepdims=True) + EPS)
    return cen * r, r


def norm(v, gain):
    u, _ = norm_parts(v)
    return u * gain


def norm_back(v, gain, e):
    u, r = norm_parts(v)
    eg = e * gain
    back = r * (eg - jnp.mean(eg, axis=-1, keepdims=True) - u * jnp.mean(eg * u, axis=-1, keepdims=True))
    return back, jnp.sum(e * u, axis=0, keepdims=True)


def sigmoid(v):
    return 1.0 / (1.0 + jnp.exp(-v))


def swish_and_slope(v):
    s = sigmoid(v)
    sv = s * v
    return sv, s + sv * (1.0 - s)


def cols(p, width=LANE):
    return pl.ds(pl.multiple_of(p * width, width), width)


def lane_half(e):
    lane = lax.broadcasted_iota(jnp.int32, (1, LANE), 1)
    return (lane < HD) if e == 0 else (lane >= HD)


def call(body, outs, ins, scratch=(), name=None):
    return pl.pallas_call(
        body,
        out_shape=[jax.ShapeDtypeStruct(s, d) for s, d in outs],
        in_specs=[
            pl.BlockSpec(memory_space=pltpu.SMEM) if x.dtype == jnp.int32 else pl.BlockSpec(memory_space=pltpu.VMEM)
            for x in ins
        ],
        out_specs=[pl.BlockSpec(memory_space=pltpu.VMEM) for _ in outs],
        scratch_shapes=list(scratch),
        compiler_params=pltpu.CompilerParams(vmem_limit_bytes=VMEM_LIMIT),
        name=name,
    )(*ins)


MESH = pl.DeviceIdType.MESH


class Place:
    def __init__(self):
        tms, slots = lax.axis_size("tm"), lax.axis_size("slot")
        wide = 1 << ((slots.bit_length() - 1) // 2)
        self.size = {"c": 2, "x": tms // 2, "y": wide, "z": slots // wide}
        self.tm, self.slot = lax.axis_index("tm"), lax.axis_index("slot")
        self.at = {
            "c": lax.rem(self.tm, 2),
            "x": lax.div(self.tm, 2),
            "y": lax.rem(self.slot, wide),
            "z": lax.div(self.slot, wide),
        }

    def peer(self, axis, off):
        pos = dict(self.at)
        pos[axis] = lax.rem(pos[axis] + off, self.size[axis])
        return (pos["x"] * 2 + pos["c"], pos["z"] * self.size["y"] + pos["y"]), pos[axis]

    def peers(self, axis):
        return [(off,) + self.peer(axis, off) for off in range(1, self.size[axis])]

    def greet(self, axes):
        bar = pltpu.get_barrier_semaphore()
        count = 0
        for axis in axes:
            for _, dev, _ in self.peers(axis):
                pl.semaphore_signal(bar, inc=1, device_id=dev, device_id_type=MESH)
                count += 1
        pl.semaphore_wait(bar, count)


def rows_at(start, size):
    return pl.ds(pl.multiple_of(start, 16), size)


def add_into(dst, start, lanes, terms, size):
    step = 64 if size % 64 == 0 else 16

    def one(i, carry):
        off = pl.multiple_of(i * step, step)
        total = terms[0](off, step).astype(F32)
        for term in terms[1:]:
            total = total + term(off, step).astype(F32)
        dst[pl.ds(pl.multiple_of(start + off, 16), step), lanes] = total.astype(dst.dtype)
        return carry

    lax.fori_loop(0, size // step, one, 0)


class Reducer:
    ORDERS = (("y", "x", "z"), ("x", "y", "z"))

    @staticmethod
    def scratch(rows, width, size):
        shapes = [pltpu.VMEM((rows // 2, width), BF)]
        sends = 2
        for order in Reducer.ORDERS:
            blk = rows // 2
            for axis in order:
                blk //= size[axis]
                shapes.append(pltpu.VMEM((size[axis] - 1, blk, width // 2), BF))
                sends += 2 * (size[axis] - 1)
            shapes.append(pltpu.VMEM((blk, width // 2), BF))
            sends += 1
        shapes += [pltpu.SemaphoreType.DMA((sends,)), pltpu.SemaphoreType.DMA((sends,)), pltpu.SemaphoreType.DMA((2,))]
        return shapes

    COUNT = 12

    def __init__(self, place, rows, width, src, out, first, bufs, own=None):
        self.place, self.rows, self.width, self.src, self.out, self.first = place, rows, width, src, out, first
        self.own, self.now = own, 0
        self.core = bufs[0]
        self.bufs = (bufs[1:4], bufs[5:8])
        self.fin = (bufs[4], bufs[8])
        self.ssem, self.rsem, self.lsem = bufs[9:12]
        self.next = 0
        self.copies = []
        self.half = [self.plan(0), self.plan(1)]

    def copy(self, src, dst, dev):
        k = self.next
        self.next += 1
        cp = (src, dst, k, dev)
        self.copies.append(cp)
        return cp

    def make(self, cp):
        src, dst, k, dev = cp
        return pltpu.make_async_remote_copy(
            src_ref=src(), dst_ref=dst(), send_sem=self.ssem.at[k], recv_sem=self.rsem.at[k], device_id=dev, device_id_type=MESH
        )

    def start(self, cps):
        for cp in cps:
            self.make(cp).start()

    def arrived(self, cps):
        for cp in cps:
            self.make(cp).wait_recv()

    def finish(self):
        for cp in self.copies:
            self.make(cp).wait_send()

    def plan(self, h):
        pc, hw = self.place, self.width // 2
        order = self.ORDERS[h]
        lanes = pl.ds(h * hw, hw)
        c = pc.at["c"]
        top = self.rows // 2
        core, bufs, fin, src, out, first = self.core, self.bufs[h], self.fin[h], self.src, self.out, self.first
        blk, rel = [top], [0]
        for axis in order:
            blk.append(blk[-1] // pc.size[axis])
            rel.append(rel[-1] + pc.at[axis] * blk[-1])
        stages = []
        (_, cdev, _), = pc.peers("c")
        ccopy = self.copy(
            lambda: src.at[rows_at((1 - c) * top, top), lanes], lambda: core.at[:, lanes], cdev
        )
        stages.append(lambda: self.start([ccopy]))
        out_at = lambda level: out.at[rows_at(first + c * top + rel[level], blk[level]), lanes]
        prev = [ccopy]
        downs = []
        for lv, axis in enumerate(order):
            cps = [
                self.copy(
                    lambda lv=lv, pos=pos: core.at[rows_at(rel[lv] + pos * blk[lv + 1], blk[lv + 1]), lanes],
                    lambda lv=lv, off=off: bufs[lv].at[off - 1],
                    dev,
                )
                for off, dev, pos in pc.peers(axis)
            ]
            downs.append(cps)

        def fold(lv, last):
            if lv == 0:
                if self.own is None:
                    mine = lambda o, n: src[pl.ds(pl.multiple_of(c * top + o, 16), n), lanes]
                else:
                    mine = lambda o, n: self.own[pl.ds(o, n), lanes]
                terms = [mine, lambda o, n: core[pl.ds(o, n), lanes]]
                add_into(core, 0, lanes, terms, top)
                return
            terms = [lambda o, n: core[pl.ds(pl.multiple_of(rel[lv] + o, 16), n), lanes]]
            for k in range(pc.size[order[lv - 1]] - 1):
                terms.append(lambda o, n, k=k: bufs[lv - 1][k, pl.ds(o, n), :])
            if last:
                add_into(fin, 0, slice(None), terms, blk[lv])
            else:
                add_into(core, rel[lv], lanes, terms, blk[lv])

        def step(lv):
            def run():
                self.arrived([ccopy] if lv == 0 else downs[lv - 1])
                fold(lv, False)
                self.start(downs[lv])

            return run

        for lv in range(3):
            stages.append(step(lv))
        up = [[self.copy(lambda: fin, lambda: out_at(3), dev) for _, dev, _ in pc.peers("z")]]
        up.append([self.copy(lambda: out_at(2), lambda: out_at(2), dev) for _, dev, _ in pc.peers(order[1])])
        up.append([self.copy(lambda: out_at(1), lambda: out_at(1), dev) for _, dev, _ in pc.peers(order[0])])
        up.append([self.copy(lambda: out_at(0), lambda: out_at(0), cdev)])
        mine = lambda: pltpu.make_async_copy(fin, out_at(3), self.lsem.at[h])

        def turn():
            self.arrived(downs[2])
            fold(3, True)
            mine().start()
            self.start(up[0])

        stages.append(turn)

        def climb(i):
            def run():
                if i == 0:
                    mine().wait()
                self.arrived(up[i])
                if i + 1 < len(up):
                    self.start(up[i + 1])

            return run

        for i in range(4):
            stages.append(climb(i))
        return stages

    def take(self):
        i, self.now = self.now, self.now + 1
        return lambda: [self.half[h][i]() for h in range(2)]

    def advance(self):
        if self.now < self.STAGES:
            self.take()()

    STAGES = 9


FLAT = {"f1i": 0, "f1o": 2048, "q": 4096, "k": 4608, "v": 5120, "p": 5632, "o": 6144, "ci": 6656, "co": 7680, "f2i": 8192, "f2o": 10240}
FLAT_ROWS = 12288
ORDER = tuple(FLAT)
FOLDS = {"f1i": 4, "ci": 2, "f2i": 4}
FLAT_SIZE = {n: (list(FLAT.values()) + [FLAT_ROWS])[i + 1] - FLAT[n] for i, n in enumerate(FLAT)}


def gather_body(*refs):
    shard, raws, wn = refs[0], refs[1:12], refs[12]
    nb, wf, scr, ssem, rsem, lsem, wsem = refs[13:]
    pc = Place()
    x, c, z, y = (pc.at[a] for a in "xczy")
    loads = []
    for name, raw in zip(ORDER, raws):
        for j in range(FOLDS.get(name, 1)):
            size = FLAT_SIZE[name] // FOLDS.get(name, 1)
            dst = wf.at[pl.ds(FLAT[name] + j * size, size), :]
            loads.append(pltpu.make_async_copy(raw.at[:, pl.ds(j * 512, 512)], dst, wsem.at[len(loads)]))
    own = pltpu.make_async_copy(shard, nb.at[x, c, z, y], lsem.at[0])
    own.start()
    for cp in loads:
        cp.start()
    pc.greet("cxyz")
    own.wait()
    shard_rows = shard.shape[0]
    pieces = 3
    part = shard_rows // pieces
    hw = 256
    count = [0]
    sent = []

    def copy(ref, dev):
        k = count[0]
        count[0] += 1
        cp = pltpu.make_async_remote_copy(
            src_ref=ref, dst_ref=ref, send_sem=ssem.at[k], recv_sem=rsem.at[k], device_id=dev, device_id_type=MESH
        )
        sent.append(cp)
        return cp

    plans = {}
    for q in range(pieces):
        for h in range(2):
            lanes, rows = pl.ds(h * hw, hw), pl.ds(q * part, part)
            second, third = ("x", "y") if h == 0 else ("y", "x")
            blocks = {
                "z": nb.at[x, c, z, y, rows, lanes],
                second: nb.at[x, c, :, y, rows, lanes],
                third: nb.at[:, c, :, y, rows, lanes] if third == "y" else nb.at[x, c, :, :, rows, lanes],
                "c": nb.at[:, c, :, :, rows, lanes],
            }
            plans[q, h] = [[copy(blocks[a], dev) for _, dev, _ in pc.peers(a)] for a in ("z", second, third, "c")]

    unit = 128 if part % 128 == 0 else 64
    sub = math.gcd(unit, part)

    def noise_at(row):
        got = []
        for i in range(unit // sub):
            at = row + i * sub
            d = lax.div(at, shard_rows)
            tm, sl = lax.div(d, pc.size["z"] * pc.size["y"]), lax.rem(d, pc.size["z"] * pc.size["y"])
            off = pl.multiple_of(lax.rem(at, shard_rows), 16)
            got.append(
                nb[lax.div(tm, 2), lax.rem(tm, 2), lax.div(sl, pc.size["y"]), lax.rem(sl, pc.size["y"]), pl.ds(off, sub), :].astype(F32)
            )
        return got[0] if len(got) == 1 else jnp.concatenate(got, axis=0)

    def mix(row, base, size, fold):
        value = noise_at(row)
        if fold == 1:
            at = rows_at(row, unit)
            wf[at, :] = (wf[at, :].astype(F32) + value).astype(BF)
            return
        for b in range(512 // LANE):
            scr[b, pl.ds(0, unit), :] = value[:, b * LANE : (b + 1) * LANE]
        high = unit // fold
        for j in range(fold):
            at = rows_at(base + j * (size // fold) + lax.div(row - base, fold), high)
            for b in range(512 // LANE):
                lanes = pl.ds(b * LANE, LANE)
                wf[at, lanes] = (wf[at, lanes].astype(F32) + scr[b, pl.ds(j, high, stride=fold), :]).astype(BF)

    def mix_range(low, high, q):
        for name in ORDER:
            base, size = FLAT[name], FLAT_SIZE[name]
            if not low <= base < high:
                continue
            if q is None:
                lax.fori_loop(0, size // unit, lambda i, t: (mix(base + i * unit, base, size, FOLDS.get(name, 1)), t)[1], 0)
                continue
            begin, end = base // unit, (base + size) // unit
            start = begin + (q - begin) % pieces
            lax.fori_loop(
                0, (end - start + pieces - 1) // pieces,
                lambda i, t: (mix((start + i * pieces) * unit, base, size, FOLDS.get(name, 1)), t)[1], 0,
            )

    def arrived(cps):
        for cp in cps:
            cp.wait_recv()

    loaded = False
    for t in range(pieces + 4):
        for q in range(pieces):
            s = t - q
            if 0 <= s <= 4:
                for h in range(2):
                    if s > 0:
                        arrived(plans[q, h][s - 1])
                    if s < 4:
                        for cp in plans[q, h][s]:
                            cp.start()
        q = t - 4
        if q >= 0 and part == unit:
            if not loaded:
                for cp in loads:
                    cp.wait()
                loaded = True
            mix_range(0, FLAT_ROWS, q)
    if part != unit:
        for cp in loads:
            cp.wait()
        mix_range(0, FLAT_ROWS, None)
    outs = [pltpu.make_async_copy(wf.at[pl.ds(i * 2048, 2048), :], wn.at[pl.ds(i * 2048, 2048), :], wsem.at[i]) for i in range(6)]
    for cp in outs:
        cp.start()
    for cp in sent:
        cp.wait_send()
    for cp in outs:
        cp.wait()


def chunk(c):
    return pl.ds(pl.multiple_of(c * 512, 512), 512)


def ffn_forward(normed, w_in, w_out, pre_ref):
    def one(c, acc):
        pre = dot(normed, w_in[chunk(c), :])
        pre_ref[:, chunk(c)] = pre
        return acc + dot((pre * sigmoid(pre)).astype(BF), w_out[chunk(c), :])

    return lax.fori_loop(0, w_in.shape[0] // 512, one, jnp.zeros((normed.shape[0], w_out.shape[1]), F32))


def ffn_backward(g_low, normed, w_in, w_out, pre_ref, gin_ref, gout_ref):
    normed_t = normed.T

    def one(c, acc):
        sw, slope = swish_and_slope(pre_ref[:, chunk(c)])
        gout_ref[chunk(c), :] = dot_tn(sw.astype(BF), g_low).astype(gout_ref.dtype)
        dpre = (dot_nt(g_low, w_out[chunk(c), :]) * slope).astype(BF)
        gin_ref[chunk(c), :] = dot(normed_t, dpre).astype(gin_ref.dtype)
        return acc + dot_nt(dpre, w_in[chunk(c), :])

    return lax.fori_loop(0, w_in.shape[0] // 512, one, jnp.zeros(g_low.shape, F32))


class Fetch:
    def __init__(self, sems):
        self.sems, self.n = sems, 0

    def __call__(self, src, dst):
        cp = pltpu.make_async_copy(src, dst, self.sems.at[self.n])
        self.n += 1
        cp.start()
        return cp


def part_of(wn, name):
    return wn.at[pl.ds(FLAT[name], FLAT_SIZE[name]), :]


def fwd1_body(x_ref, w1, wqkv, gain1, gain2, pos_u, pos_v, x1_ref, pre_ref, a2_ref, qu_ref, qv_ref, k_ref, v_ref):
    x = x_ref[...].astype(F32)
    a1 = norm(x, gain1[...]).astype(BF)
    x1 = x + 0.5 * ffn_forward(a1, w1.at[pl.ds(0, 2048), :], w1.at[pl.ds(2048, 2048), :], pre_ref)
    x1_ref[...] = x1
    a2 = norm(x1, gain2[...]).astype(BF)
    a2_ref[...] = a2
    q = dot(a2, wqkv[pl.ds(0, 512), :])
    scale = HD**-0.5
    qu_ref[...] = ((q + pos_u[...]).astype(BF).astype(F32) * scale).astype(BF)
    qv_ref[...] = ((q + pos_v[...]).astype(BF).astype(F32) * scale).astype(BF)
    k_ref[...] = dot(a2, wqkv[pl.ds(512, 512), :]).astype(BF)
    v_ref[...] = dot(a2, wqkv[pl.ds(1024, 512), :]).astype(BF)


def att_fwd_body(lens, qu, qv, k, v, w_pos, trig, sin, cos, att_ref, p_ref, s_scr):
    rows, frames = qu.shape[0], k.shape[0]
    half = sin.shape[1]
    ok = lax.broadcasted_iota(jnp.int32, (1, frames), 1) < lens[0]

    def pair(p, carry):
        at = cols(p)
        mixed = None
        for e in range(2):
            mine = lane_half(e)
            qve = jnp.where(mine, qv[:, at], jnp.zeros((), BF))
            que = jnp.where(mine, qu[:, at], jnp.zeros((), BF))
            a_s = dot_nt(qve, w_pos[pl.ds(0, half), at])
            a_c = dot_nt(qve, w_pos[pl.ds(half, half), at])
            b_c = (a_s * sin[...] + a_c * cos[...]).astype(BF)
            b_s = (a_c * sin[...] - a_s * cos[...]).astype(BF)
            s = dot_nt(b_s, trig[:, pl.ds(0, half)]) + dot_nt(b_c, trig[:, pl.ds(half, half)]) + dot_nt(que, k[:, at])
            s = jnp.where(ok, s, FILL)
            m = jnp.max(s, axis=-1, keepdims=True)
            ex = jnp.exp(s - m)
            tot = jnp.sum(ex, axis=-1, keepdims=True)
            low = (ex * (1.0 / tot)).astype(BF)
            p_ref[2 * p + e] = low
            part = dot(low, v[:, at])
            mixed = part if e == 0 else jnp.where(mine, part, mixed)
        att_ref[:, at] = mixed.astype(BF)
        return carry

    lax.fori_loop(0, H // 2, pair, 0)


def valid_rows(lens, rows):
    first = lax.axis_index("tm") * rows
    return ((first + lax.broadcasted_iota(jnp.int32, (rows, 1), 0)) < lens[0]).astype(F32)


def spread(ext, start, value):
    value = value.astype(F32)
    for b in range(ext.shape[0]):
        ext[b, pl.ds(start, value.shape[0]), :] = value[:, b * LANE : (b + 1) * LANE]


def tap_sum(ext, taps, out_ref, offset):
    count = taps.shape[0]
    rows = out_ref.shape[0]
    block = 64 if rows % 64 == 0 else 16

    def one(i, carry):
        for b in range(ext.shape[0]):
            at = pl.ds(b * LANE, LANE)
            acc = jnp.zeros((block, LANE), F32)
            for k in range(count):
                acc = acc + taps[pl.ds(k, 1), at] * ext[b, pl.ds(i * block + offset(k), block), :]
            out_ref[pl.ds(pl.multiple_of(i * block, block), block), at] = acc
        return carry

    lax.fori_loop(0, rows // block, one, 0)


def bn_stats(sums):
    total = sums[2:3, :]
    mu = sums[0:1, :] / total
    var = sums[1:2, :] / total - mu * mu
    return mu, lax.rsqrt(var + EPS), total


class Totals:
    @staticmethod
    def scratch(tms, slots, width):
        n = tms + slots - 2
        return [
            pltpu.VMEM((tms, 8, width), F32),
            pltpu.VMEM((slots, 8, width), F32),
            pltpu.SemaphoreType.DMA((n,)),
            pltpu.SemaphoreType.DMA((n,)),
        ]

    def __init__(self, pc, bufs):
        self.pc, self.bufs = pc, bufs

    def __call__(self, value):
        pc = self.pc
        tmb, slb, ssem, rsem = self.bufs
        sent = []
        k = 0
        for buf, axis, me in ((tmb, "tm", pc.tm), (slb, "slot", pc.slot)):
            buf[me] = value
            n = buf.shape[0]
            cps = []
            for off in range(1, n):
                to = lax.rem(me + off, n)
                dev = (to, pc.slot) if axis == "tm" else (pc.tm, to)
                cp = pltpu.make_async_remote_copy(
                    src_ref=buf.at[me], dst_ref=buf.at[me], send_sem=ssem.at[k], recv_sem=rsem.at[k], device_id=dev, device_id_type=MESH
                )
                cp.start()
                cps.append(cp)
                k += 1
            for cp in cps:
                cp.wait_recv()
            sent += cps
            value = buf[0]
            for i in range(1, n):
                value = value + buf[i]
        for cp in sent:
            cp.wait_send()
        return value


def greet_rows(pc, tms, slots):
    bar = pltpu.get_barrier_semaphore()
    for off in range(1, tms):
        pl.semaphore_signal(bar, inc=1, device_id=(lax.rem(pc.tm + off, tms), pc.slot), device_id_type=MESH)
    for off in range(1, slots):
        pl.semaphore_signal(bar, inc=1, device_id=(pc.tm, lax.rem(pc.slot + off, slots)), device_id_type=MESH)
    pl.semaphore_wait(bar, tms + slots - 2)


def middle_body(
    lens, att, x1_ref, cot, wn, taps, bn_gain, bn_bias, gain3, gain4, gain5,
    out_ref, dx2_ref, datt_ref, g_ref, smalls_ref, bns_ref,
    w_o, w_ci, w_co, w_f2i, w_f2o, fsem, early, late, hsem, gm_ref, ddwo_ref, z_ref, ext, ext2, dwo_ref, pre_ref, dgm_ref, acc, x2_ref, *bufs,
):
    pc = Place()
    tms, slots = lax.axis_size("tm"), lax.axis_size("slot")
    rows, width = x1_ref.shape
    count = taps.shape[0]
    fetch = Fetch(fsem)
    got = {n: fetch(part_of(wn, n), d) for n, d in (("o", w_o), ("ci", w_ci), ("co", w_co), ("f2i", w_f2i), ("f2o", w_f2o))}
    greet_rows(pc, tms, slots)
    totals = Totals(pc, bufs[:4]), Totals(pc, bufs[4:])

    def halo(src, dst, k, step):
        dev = (lax.rem(pc.tm + step + tms, tms), pc.slot)
        return pltpu.make_async_remote_copy(
            src_ref=src, dst_ref=dst, send_sem=hsem.at[2 * k], recv_sem=hsem.at[2 * k + 1], device_id=dev, device_id_type=MESH
        )

    got["o"].wait()
    x2 = x1_ref[...] + dot(att[...], w_o[...])
    x2_ref[...] = x2
    a3 = norm(x2, gain3[...]).astype(BF)
    got["ci"].wait()
    z1 = dot(a3, w_ci[pl.ds(0, width), :])
    z2 = dot(a3, w_ci[pl.ds(width, width), :])
    z_ref[:, pl.ds(0, width)] = z1
    z_ref[:, pl.ds(width, width)] = z2
    ok = valid_rows(lens, rows)
    gm_ref[...] = (z1 * sigmoid(z2) * ok).astype(BF)
    cp = halo(gm_ref.at[pl.ds(rows - count, count), :], early, 0, 1)
    cp.start()
    spread(ext, count, gm_ref[...])
    cp.wait()
    spread(ext, 0, jnp.where(pc.tm > 0, early[...], jnp.zeros((), BF)))
    tap_sum(ext, taps, dwo_ref, lambda k: k + 1)
    dwo = dwo_ref[...]
    dwv = dwo * ok
    sums = totals[0](
        jnp.concatenate(
            [
                jnp.sum(dwv, axis=0, keepdims=True),
                jnp.sum(dwv * dwv, axis=0, keepdims=True),
                jnp.zeros((1, width), F32) + jnp.sum(ok, axis=0, keepdims=True),
                jnp.zeros((5, width), F32),
            ],
            axis=0,
        )
    )
    mu, inv, total = bn_stats(sums)
    xhat = (dwo_ref[...] - mu) * inv
    sw, slope = swish_and_slope(xhat * bn_gain[...] + bn_bias[...])
    sw = sw.astype(BF)
    got["co"].wait()
    x3 = x2_ref[...] + dot(sw, w_co[...])
    a4 = norm(x3, gain4[...]).astype(BF)
    got["f2i"].wait()
    got["f2o"].wait()
    x4 = x3 + 0.5 * ffn_forward(a4, w_f2i, w_f2o, pre_ref)
    out_ref[...] = norm(x4, gain5[...]).astype(BF)
    dx4, gg5 = norm_back(x4, gain5[...], cot[...].astype(F32))
    g4 = (0.5 * dx4).astype(BF)
    lo = FLAT["o"]
    da4 = ffn_backward(
        g4, a4, w_f2i, w_f2o, pre_ref,
        g_ref.at[pl.ds(FLAT["f2i"] - lo, 2048), :], g_ref.at[pl.ds(FLAT["f2o"] - lo, 2048), :],
    )
    back, gg4 = norm_back(x3, gain4[...], da4)
    dx3 = dx4 + back
    g3 = dx3.astype(BF)
    dbn = dot_nt(g3, w_co[...]) * slope
    sums2 = totals[1](
        jnp.concatenate(
            [jnp.sum(dbn * xhat, axis=0, keepdims=True), jnp.sum(dbn, axis=0, keepdims=True), jnp.zeros((6, width), F32)], axis=0
        )
    )
    bns_ref[...] = sums2
    ddwo_ref[...] = (bn_gain[...] * inv * (dbn - ok * (sums2[1:2, :] + xhat * sums2[0:1, :]) / total)).astype(BF)
    cp = halo(ddwo_ref.at[pl.ds(0, count), :], late, 1, -1)
    cp.start()
    g_ref[pl.ds(FLAT["co"] - lo, width), :] = dot_tn(sw, g3).astype(BF)
    spread(ext2, 0, ddwo_ref[...])
    cp.wait()
    spread(ext2, rows, jnp.where(pc.tm < tms - 1, late[...], jnp.zeros((), BF)))
    tap_sum(ext2, taps, dgm_ref, lambda k: count - 1 - k)
    block = 64 if rows % 64 == 0 else 16
    for b in range(ext.shape[0]):
        acc[...] = jnp.zeros(acc.shape, F32)

        def one(i, carry, b=b):
            mine = ext2[b, pl.ds(pl.multiple_of(i * block, block), block), :]
            for k in range(count):
                prod = mine * ext[b, pl.ds(i * block + k + 1, block), :]
                acc[k] = acc[k] + jnp.sum(prod.reshape(block // 8, 8, LANE), axis=0)
            return carry

        lax.fori_loop(0, rows // block, one, 0)
        smalls_ref[pl.ds(0, count), pl.ds(b * LANE, LANE)] = jnp.sum(acc[...], axis=1)
    z1 = z_ref[:, pl.ds(0, width)]
    sg = sigmoid(z_ref[:, pl.ds(width, width)])
    dg = dgm_ref[...] * ok
    dz1 = (dg * sg).astype(BF)
    dz2 = (dg * z1 * sg * (1.0 - sg)).astype(BF)
    a3t = norm(x2_ref[...], gain3[...]).astype(BF).T
    g_ref[pl.ds(FLAT["ci"] - lo, width), :] = dot(a3t, dz1).astype(BF)
    g_ref[pl.ds(FLAT["ci"] - lo + width, width), :] = dot(a3t, dz2).astype(BF)
    da3 = dot_nt(dz1, w_ci[pl.ds(0, width), :]) + dot_nt(dz2, w_ci[pl.ds(width, width), :])
    back, gg3 = norm_back(x2_ref[...], gain3[...], da3)
    dx2 = dx3 + back
    dx2_ref[...] = dx2
    g2 = dx2.astype(BF)
    g_ref[pl.ds(0, width), :] = dot_tn(att[...], g2).astype(BF)
    datt_ref[...] = dot_nt(g2, w_o[...]).astype(BF)
    smalls_ref[pl.ds(count, 8), :] = jnp.concatenate([gg3, gg4, gg5, jnp.zeros((5, width), F32)], axis=0)


class Butterfly:
    @staticmethod
    def scratch(devices, shape):
        n = devices.bit_length() - 1
        return [pltpu.VMEM((n,) + shape, F32), pltpu.SemaphoreType.DMA((n,)), pltpu.SemaphoreType.DMA((n,))]

    def __init__(self, pc, value, bufs):
        self.value, (self.got, self.ssem, self.rsem) = value, bufs
        self.devs = []
        for axis, me in (("tm", pc.tm), ("slot", pc.slot)):
            bit = 1
            while bit < lax.axis_size(axis):
                to = me + bit - 2 * bit * lax.rem(lax.div(me, bit), 2)
                self.devs.append((to, pc.slot) if axis == "tm" else (pc.tm, to))
                bit *= 2

    def copy(self, k):
        return pltpu.make_async_remote_copy(
            src_ref=self.value, dst_ref=self.got.at[k], send_sem=self.ssem.at[k], recv_sem=self.rsem.at[k],
            device_id=self.devs[k], device_id_type=MESH,
        )

    def stage(self, k):
        if k > 0:
            self.copy(k - 1).wait()
            self.value[...] = self.value[...] + self.got[k - 1]
        if k < len(self.devs):
            self.copy(k).start()


GROUP = 2048


class KeyGrads:
    @staticmethod
    def scratch(tms, rows):
        pairs, xs = H // 2, tms // 2
        sems = pltpu.SemaphoreType.DMA((pairs, xs + 1))
        return [
            pltpu.VMEM((pairs, 2, 2, tms, HD, rows), BF),
            pltpu.VMEM((pairs, 2, tms, HD, rows), BF),
            pltpu.VMEM((xs - 1, pairs, 2, 2, HD, rows), BF),
            pltpu.VMEM((pairs, 2, 2, HD, rows), BF),
            pltpu.VMEM((pairs, 2, HD, rows), BF),
            sems,
            sems,
        ]

    def __init__(self, pc, bufs):
        self.pc = pc
        self.mine, self.core, self.line, self.both, self.got, self.ssem, self.rsem = bufs

    def put(self, p, kind, e, value):
        rows = self.mine.shape[-1]
        for t in range(self.mine.shape[3]):
            self.mine[p, kind, e, t] = value[:, t * rows : (t + 1) * rows].astype(BF)

    def copy(self, p, k, src, dst, dev):
        return pltpu.make_async_remote_copy(
            src_ref=src, dst_ref=dst, send_sem=self.ssem.at[p, k], recv_sem=self.rsem.at[p, k], device_id=dev, device_id_type=MESH
        )

    def first(self, p):
        ((_, dev, _),) = self.pc.peers("c")
        return [self.copy(p, 0, self.mine.at[p, :, 1 - self.pc.at["c"]], self.core.at[p], dev)]

    def second(self, p):
        return [
            self.copy(p, off, self.core.at[p, :, pl.ds(2 * pos, 2)], self.line.at[off - 1, p], dev) for off, dev, pos in self.pc.peers("x")
        ]

    def third(self, p):
        ((_, dev, _),) = self.pc.peers("c")
        return [self.copy(p, self.pc.size["x"], self.both.at[p, :, 1 - self.pc.at["c"]], self.got.at[p], dev)]

    def step(self, p, i):
        c, x = self.pc.at["c"], self.pc.at["x"]
        if i == 1:
            for cp in self.first(p):
                cp.wait_recv()
            for kind in range(2):
                for t in range(self.core.shape[2]):
                    total = self.core[p, kind, t].astype(F32) + self.mine[p, kind, c, t].astype(F32)
                    self.core[p, kind, t] = total.astype(BF)
        if i == 2:
            for cp in self.second(p):
                cp.wait_recv()
            for kind in range(2):
                for t in range(2):
                    total = self.core[p, kind, 2 * x + t].astype(F32)
                    for j in range(self.line.shape[0]):
                        total = total + self.line[j, p, kind, t].astype(F32)
                    self.both[p, kind, t] = total.astype(BF)
        if i == 3:
            for cp in self.third(p):
                cp.wait_recv()
            return
        for cp in (self.first, self.second, self.third)[i](p):
            cp.start()

    def sent(self, p):
        for cp in self.first(p) + self.second(p) + self.third(p):
            cp.wait_send()

    def collect(self, p, kind, dst):
        c = self.pc.at["c"]
        own = self.both[p, kind, c]
        other = self.got[p, kind]
        dst[pl.ds(pl.multiple_of(p * LANE + c * HD, HD), HD), :] = own
        dst[pl.ds(pl.multiple_of(p * LANE + (1 - c) * HD, HD), HD), :] = other


def ticks(point, plan, p):
    for at, run in plan.items():
        if at % 2 == point:
            pl.when(p == at // 2)(lambda run=run: (run(), None)[1])


def late_body(
    qu_h, qv_h, k_h, v_h, wn, trig_h, sin_h, cos_h, probs, datt_h, att_h, g_high, a2_h, x1_h, dx2_h, x_h, pre_h, smalls2, gain2, gain1,
    dx0_ref, flat, total_ref,
    qu, qv, k, v, w_p, trig, sin, cos, datt, att, a2, x1_ref, dx2_ref, x_ref, pre_ref, wqkv, w1, own, pbuf, psem, fsem,
    dq_ref, dkt, dvt, gpost, qut, qvt, datt_t, g_low, *bufs,
):
    pc = Place()
    rows = qu.shape[0]
    half = sin.shape[1]
    fetch = Fetch(fsem)
    size = g_low.shape[0] // GROUP
    c = pc.at["c"]
    owns = [fetch(g_high.at[rows_at(i * GROUP + c * (GROUP // 2), GROUP // 2), :], own.at[i]) for i in range(size)]
    early = [fetch(s, d) for s, d in ((qu_h, qu), (qv_h, qv), (datt_h, datt), (k_h, k), (v_h, v), (att_h, att), (part_of(wn, "p"), w_p), (trig_h, trig), (sin_h, sin), (cos_h, cos))]
    loads = [pltpu.make_async_copy(probs.at[e], pbuf.at[e], psem.at[e]) for e in range(2)]
    for cp in loads:
        cp.start()
    later = [
        fetch(s, d)
        for s, d in (
            (a2_h, a2), (x1_h, x1_ref), (dx2_h, dx2_ref), (x_h, x_ref), (pre_h, pre_ref),
            (wn.at[pl.ds(FLAT["q"], 1536), :], wqkv), (wn.at[pl.ds(0, 4096), :], w1),
        )
    ]
    pc.greet("cxyz")
    per = Reducer.COUNT
    groups = []
    for i in range(2 * size):
        at = GROUP * (i % size)
        scratch = bufs[i * per : (i + 1) * per]
        if i < size:
            src, first, mine = g_high.at[pl.ds(at, GROUP), :], at + g_low.shape[0], own.at[i]
        else:
            at = GROUP * (size - 1) if i == size else at - GROUP
            src, first, mine = g_low.at[pl.ds(at, GROUP), :], at, None
        groups.append(Reducer(pc, GROUP, 512, src, flat, first, scratch, mine))
    rest = bufs[2 * size * per :]
    keys = KeyGrads(pc, rest[:7])
    fly = Butterfly(pc, total_ref, rest[7:])
    high, low = groups[:size], groups[size:]
    for grp in high:
        grp.advance()
    for cp in owns:
        cp.wait()
    for cp in early:
        cp.wait()
    qut[...] = qu[...].T
    qvt[...] = qv[...].T
    datt_t[...] = datt[...].T

    def run(members):
        stages = [high[i].take() for i in members]
        return lambda: [stage() for stage in stages]

    plan = {at: run(members) for at, members in ((1, [0]), (2, [0, 1]), (4, [0, 1, 2]), (5, [0, 1, 2]), (7, [0, 1, 2]))}
    scale = HD**-0.5

    def pair(p, carry):
        at = cols(p)
        dqu = dqv = None
        for e in range(2):
            mine = lane_half(e)
            part = pl.ds(pl.multiple_of(p * LANE + e * HD, HD), HD)
            dm = jnp.where(mine, datt[:, at], jnp.zeros((), BF))
            inner = jnp.sum(dm.astype(F32) * att[:, at].astype(F32), axis=-1, keepdims=True)
            dp = dot_nt(dm, v[:, at])
            loads[e].wait()
            low_p = pbuf[e]
            ds = (low_p.astype(F32) * (dp - inner)).astype(BF)
            keys.put(p, 0, e, dot(qut[part, :], ds))
            keys.put(p, 1, e, dot(datt_t[part, :], low_p))

            @pl.when(p < H // 2 - 1)
            def _():
                pltpu.make_async_copy(probs.at[2 * p + 2 + e], pbuf.at[e], psem.at[e]).start()

            db_s = dot(ds, trig[:, pl.ds(0, half)])
            db_c = dot(ds, trig[:, pl.ds(half, half)])
            da_s = (db_c * sin[...] - db_s * cos[...]).astype(BF)
            da_c = (db_c * cos[...] + db_s * sin[...]).astype(BF)
            gpost[part, pl.ds(0, half)] = dot(qvt[part, :], da_s)
            gpost[part, pl.ds(half, half)] = dot(qvt[part, :], da_c)
            part_v = dot(da_s, w_p[pl.ds(0, half), at]) + dot(da_c, w_p[pl.ds(half, half), at])
            part_u = dot(ds, k[:, at])
            dqu = part_u if e == 0 else jnp.where(mine, part_u, dqu)
            dqv = part_v if e == 0 else jnp.where(mine, part_v, dqv)
            if e == 0:
                pl.when(p > 0)(lambda: keys.step(p - 1, 1))
            else:
                pl.when(p > 1)(lambda: keys.step(p - 2, 2))
                keys.step(p, 0)
            ticks(e, plan, p)
        dqu = dqu * scale
        dqv = dqv * scale
        dq_ref[:, at] = (dqu + dqv).astype(BF)
        total_ref[pl.ds(37, 1), at] = jnp.sum(dqu, axis=0, keepdims=True)
        total_ref[pl.ds(38, 1), at] = jnp.sum(dqv, axis=0, keepdims=True)
        return carry

    lax.fori_loop(0, H // 2, pair, 0)
    last = H // 2 - 1
    g_low[pl.ds(FLAT["p"], 512), :] = gpost[...].T.astype(BF)
    for cp in later:
        cp.wait()
    a2t = a2[...].T
    g_low[pl.ds(FLAT["q"], 512), :] = dot(a2t, dq_ref[...]).astype(BF)
    keys.step(last, 1)
    keys.step(last - 1, 2)
    run([0, 1, 2])()
    da2 = dot_nt(dq_ref[...], wqkv[pl.ds(0, 512), :])
    keys.step(last, 2)
    for p in range(H // 2):
        keys.step(p, 3)
        keys.collect(p, 0, dkt)
        keys.collect(p, 1, dvt)
    g_low[pl.ds(FLAT["k"], 512), :] = dot_nt(a2t, dkt[...]).astype(BF)
    g_low[pl.ds(FLAT["v"], 512), :] = dot_nt(a2t, dvt[...]).astype(BF)
    low[0].advance()
    run([0, 1, 2])()
    da2 = da2 + dot_nt(dkt[...].T, wqkv[pl.ds(512, 512), :]) + dot_nt(dvt[...].T, wqkv[pl.ds(1024, 512), :])
    back, gg2 = norm_back(x1_ref[...], gain2[...], da2)
    dx1 = dx2_ref[...] + back
    g1 = (0.5 * dx1).astype(BF)
    x = x_ref[...].astype(F32)
    a1 = norm(x, gain1[...]).astype(BF)
    low[0].advance()
    run([0, 1, 2])()
    da1 = ffn_backward(
        g1, a1, w1.at[pl.ds(0, 2048), :], w1.at[pl.ds(2048, 2048), :], pre_ref, g_low.at[pl.ds(0, 2048), :], g_low.at[pl.ds(2048, 2048), :]
    )
    for grp in low[1:]:
        grp.advance()
    back, gg1 = norm_back(x, gain1[...], da1)
    dx0_ref[...] = (dx1 + back).astype(BF)
    count = smalls2.shape[0] - 8
    total_ref[pl.ds(0, count), :] = smalls2[pl.ds(0, count), :]
    total_ref[pl.ds(count, 3), :] = smalls2[pl.ds(count, 3), :]
    total_ref[pl.ds(count + 3, 2), :] = jnp.concatenate([gg1, gg2], axis=0)
    total_ref[pl.ds(count + 7, 1), :] = jnp.zeros((1, 512), F32)
    t = 0
    while any(grp.now < grp.STAGES for grp in groups) or t <= len(fly.devs):
        for i, grp in enumerate(groups):
            if i <= size or t >= i - size - 1:
                grp.advance()
        if t <= len(fly.devs):
            fly.stage(t)
        t += 1
    for p in range(H // 2):
        keys.sent(p)
    for grp in groups:
        grp.finish()


def widen_body(flat, *refs):
    outs, (ibuf, obuf, isem, osem) = refs[:11], refs[11:]
    step = 512
    n = FLAT_ROWS // step
    loads = [pltpu.make_async_copy(flat.at[pl.ds(i * step, step), :], ibuf.at[i], isem.at[i]) for i in range(n)]
    for cp in loads:
        cp.start()
    stores = []
    slots = obuf.shape[0]
    for i in range(n):
        name = [m for m in ORDER if FLAT[m] <= i * step][-1]
        out = outs[ORDER.index(name)]
        off = i * step - FLAT[name]
        fold = FOLDS.get(name, 1)
        if fold == 1:
            dst = out.at[pl.ds(off, step), :]
        else:
            dst = out.at[:, pl.ds(off, step)]
        loads[i].wait()
        if i >= slots:
            stores[i - slots].wait()
        obuf[i % slots] = ibuf[i].astype(F32)
        stores.append(pltpu.make_async_copy(obuf.at[i % slots], dst, osem.at[i % slots]))
        stores[-1].start()
    for cp in stores[-slots:]:
        cp.wait()


def remote(body, cid, outs, ins, scratch, name):
    def space(x):
        if x is None:
            return pl.BlockSpec(memory_space=pl.ANY)
        return pl.BlockSpec(memory_space=x)

    return pl.pallas_call(
        body,
        out_shape=[jax.ShapeDtypeStruct(s, d) for s, d, _ in outs],
        in_specs=[space(m) for _, m in ins],
        out_specs=[space(m) for _, _, m in outs],
        scratch_shapes=list(scratch),
        compiler_params=pltpu.CompilerParams(collective_id=cid, has_side_effects=True, vmem_limit_bytes=VMEM_LIMIT),
        name=name,
    )(*[x for x, _ in ins])


def local(
    inputs, cotangent, lengths, weight_noise, ffn1_in, ffn1_out, query_w, key_w, value_w, pos_w, out_w,
    conv_in, conv_out, ffn2_in, ffn2_out, conv_kernel, ffn1_gain, attn_gain, conv_gain, ffn2_gain,
    final_gain, bn_gain, bn_bias, pos_u, pos_v,
):
    _, rows, width = inputs.shape
    tms, slots = lax.axis_size("tm"), lax.axis_size("slot")
    frames = rows * tms
    count = conv_kernel.shape[0]
    devices = tms * slots
    size = Place().size
    x = inputs[0]
    cot = cotangent[0]
    gains = [g.reshape(1, -1) for g in (ffn1_gain, attn_gain, conv_gain, ffn2_gain, final_gain)]
    bng, bnb, pu, pv = (g.reshape(1, -1) for g in (bn_gain, bn_bias, pos_u, pos_v))
    raws = (ffn1_in, ffn1_out, query_w, key_w, value_w, pos_w, out_w, conv_in, conv_out, ffn2_in, ffn2_out)
    VM, HB, SM = pltpu.VMEM, None, pltpu.SMEM
    DMA = pltpu.SemaphoreType.DMA
    shard = weight_noise.reshape(-1, width)
    links = sum(n - 1 for n in size.values())
    (wn,) = remote(
        gather_body, 0, [((FLAT_ROWS, width), BF, HB)], [(shard, HB)] + [(r, HB) for r in raws],
        [
            pltpu.VMEM((size["x"], 2, size["z"], size["y"], shard.shape[0], width), BF),
            pltpu.VMEM((FLAT_ROWS, width), BF),
            pltpu.VMEM((width // LANE, 128, LANE), F32),
            DMA((6 * links,)), DMA((6 * links,)), DMA((1,)), DMA((18,)),
        ],
        "gather",
    )
    w1, wqkv, w_p = wn[:4096], wn[4096:5632], wn[5632:6144]

    half = width // 2
    rates = jnp.exp(jnp.arange(half, dtype=F32) * (-2.0 * math.log(10000.0) / width))
    angles = jnp.arange(frames, dtype=F32)[:, None] * rates[None, :]
    sin_all, cos_all = jnp.sin(angles), jnp.cos(angles)
    trig = jnp.concatenate([sin_all, cos_all], axis=1).astype(BF)
    first = lax.axis_index("tm") * rows
    sin = lax.dynamic_slice_in_dim(sin_all, first, rows, 0)
    cos = lax.dynamic_slice_in_dim(cos_all, first, rows, 0)

    act, actb = ((rows, width), F32), ((rows, width), BF)
    hidden = 2048
    x1, pre1, a2, qu, qv, k, v = call(
        fwd1_body, [act, ((rows, hidden), F32), actb, actb, actb, actb, actb],
        (x, w1, wqkv, gains[0], gains[1], pu, pv), name="fwd1",
    )
    k_all = lax.all_gather(k, "tm", axis=0, tiled=True)
    v_all = lax.all_gather(v, "tm", axis=0, tiled=True)
    att, probs = call(
        att_fwd_body, [actb, ((H, rows, frames), BF)], (lengths, qu, qv, k_all, v_all, w_p, trig, sin, cos),
        [pltpu.VMEM((8, LANE), F32)], name="att_fwd",
    )
    ext = pltpu.VMEM((width // LANE, rows + count, LANE), F32)
    output, dx2, datt, g_high, smalls2, bns = remote(
        middle_body, 1,
        [((rows, width), BF, VM), ((rows, width), F32, VM), ((rows, width), BF, VM), ((FLAT_ROWS // 2, width), BF, VM),
         ((count + 8, width), F32, VM), ((8, width), F32, VM)],
        [(lengths, SM), (att, VM), (x1, VM), (cot, VM), (wn, HB), (conv_kernel, VM), (bng, VM), (bnb, VM)] + [(g, VM) for g in gains[2:]],
        [pltpu.VMEM((FLAT_SIZE[n], width), BF) for n in ("o", "ci", "co", "f2i", "f2o")]
        + [DMA((5,)), pltpu.VMEM((count, width), BF), pltpu.VMEM((count, width), BF), DMA((4,)),
           pltpu.VMEM((rows, width), BF), pltpu.VMEM((rows, width), BF), pltpu.VMEM((rows, 2 * width), F32), ext, ext,
           pltpu.VMEM((rows, width), F32), pltpu.VMEM((rows, hidden), F32), pltpu.VMEM((rows, width), F32),
           pltpu.VMEM((count, 8, LANE), F32), pltpu.VMEM((rows, width), F32)]
        + Totals.scratch(tms, slots, width) * 2,
        "middle",
    )
    V = lambda shape, dtype=BF: pltpu.VMEM(shape, dtype)
    dx0, flat, total = remote(
        late_body, 2, [((rows, width), BF, VM), ((FLAT_ROWS, width), BF, HB), ((count + 8, width), F32, VM)],
        [(t, HB) for t in (qu, qv, k_all, v_all, wn, trig, sin, cos, probs, datt, att, g_high, a2, x1, dx2, x, pre1)]
        + [(smalls2, VM), (gains[1], VM), (gains[0], VM)],
        [V((rows, width)), V((rows, width)), V((frames, width)), V((frames, width)), V((width, width)), V((frames, width)),
         V((rows, half), F32), V((rows, half), F32), V((rows, width)), V((rows, width)), V((rows, width)),
         V((rows, width), F32), V((rows, width), F32), V((rows, width)), V((rows, hidden), F32), V((3 * width, width)), V((4096, width)),
         V((FLAT_ROWS // 2 // GROUP, GROUP // 2, width)), V((2, rows, frames)), DMA((2,)), DMA((20,)),
         V((rows, width)), V((width, rows)), V((width, rows)), V((width, width), F32), V((width, rows)), V((width, rows)), V((width, rows)),
         V((FLAT_ROWS // 2, width))]
        + Reducer.scratch(GROUP, width, size) * (FLAT_ROWS // GROUP) + KeyGrads.scratch(tms, rows)
        + Butterfly.scratch(devices, (count + 8, width)),
        "late",
    )
    big = pl.pallas_call(
        widen_body,
        out_shape=[jax.ShapeDtypeStruct(r.shape, F32) for r in raws],
        in_specs=[pl.BlockSpec(memory_space=pl.ANY)],
        out_specs=[pl.BlockSpec(memory_space=pl.ANY)] * 11,
        scratch_shapes=[pltpu.VMEM((24, 512, width), BF), pltpu.VMEM((4, 512, width), F32), DMA((24,)), DMA((4,))],
        compiler_params=pltpu.CompilerParams(vmem_limit_bytes=VMEM_LIMIT),
        name="widen",
    )(flat)
    t = total[count:]
    return (output[None], dx0[None]) + tuple(big) + (
        total[:count], t[3], t[4], t[0], t[1], t[2], bns[0], bns[1], t[5], t[6],
    )


def solution(mesh):
    split = P("slot", "tm", None)
    in_specs = (split, split, P("slot"), P(("tm", "slot"), None)) + (P(),) * 21
    out_specs = (split, split) + (P(),) * 21
    return jax.shard_map(local, mesh=mesh, in_specs=in_specs, out_specs=out_specs, check_vma=False)
```

```python
import math

import jax
import jax.numpy as jnp
from jax import lax
from jax.experimental import pallas as pl
from jax.experimental.pallas import tpu as pltpu
from jax.sharding import PartitionSpec as P

H = 8
HD = 64
LANE = 128
F32 = jnp.float32
BF = jnp.bfloat16
EPS = 1e-05
FILL = -1e30
VMEM_LIMIT = 60 * 2**20


def dot(a, b):
    return lax.dot_general(a, b, (((1,), (0,)), ((), ())), preferred_element_type=F32)


def dot_nt(a, b):
    return lax.dot_general(a, b, (((1,), (1,)), ((), ())), preferred_element_type=F32)


def dot_tn(a, b):
    return lax.dot_general(a, b, (((0,), (0,)), ((), ())), preferred_element_type=F32)


def norm_parts(v):
    mean = jnp.mean(v, axis=-1, keepdims=True)
    cen = v - mean
    r = lax.rsqrt(jnp.mean(cen * cen, axis=-1, keepdims=True) + EPS)
    return cen * r, r


def norm(v, gain):
    u, _ = norm_parts(v)
    return u * gain


def norm_back(v, gain, e):
    u, r = norm_parts(v)
    eg = e * gain
    back = r * (eg - jnp.mean(eg, axis=-1, keepdims=True) - u * jnp.mean(eg * u, axis=-1, keepdims=True))
    return back, jnp.sum(e * u, axis=0, keepdims=True)


def sigmoid(v):
    return 1.0 / (1.0 + jnp.exp(-v))


def swish_and_slope(v):
    s = sigmoid(v)
    sv = s * v
    return sv, s + sv * (1.0 - s)


def cols(p, width=LANE):
    return pl.ds(pl.multiple_of(p * width, width), width)


def lane_half(e):
    lane = lax.broadcasted_iota(jnp.int32, (1, LANE), 1)
    return (lane < HD) if e == 0 else (lane >= HD)


def call(body, outs, ins, scratch=(), name=None):
    return pl.pallas_call(
        body,
        out_shape=[jax.ShapeDtypeStruct(s, d) for s, d in outs],
        in_specs=[
            pl.BlockSpec(memory_space=pltpu.SMEM) if x.dtype == jnp.int32 else pl.BlockSpec(memory_space=pltpu.VMEM)
            for x in ins
        ],
        out_specs=[pl.BlockSpec(memory_space=pltpu.VMEM) for _ in outs],
        scratch_shapes=list(scratch),
        compiler_params=pltpu.CompilerParams(vmem_limit_bytes=VMEM_LIMIT),
        name=name,
    )(*ins)


MESH = pl.DeviceIdType.MESH


class Place:
    def __init__(self):
        tms, slots = lax.axis_size("tm"), lax.axis_size("slot")
        wide = 1 << ((slots.bit_length() - 1) // 2)
        self.size = {"c": 2, "x": tms // 2, "y": wide, "z": slots // wide}
        self.tm, self.slot = lax.axis_index("tm"), lax.axis_index("slot")
        self.at = {
            "c": lax.rem(self.tm, 2),
            "x": lax.div(self.tm, 2),
            "y": lax.rem(self.slot, wide),
            "z": lax.div(self.slot, wide),
        }

    def peer(self, axis, off):
        pos = dict(self.at)
        pos[axis] = lax.rem(pos[axis] + off, self.size[axis])
        return (pos["x"] * 2 + pos["c"], pos["z"] * self.size["y"] + pos["y"]), pos[axis]

    def peers(self, axis):
        return [(off,) + self.peer(axis, off) for off in range(1, self.size[axis])]

    def greet(self, axes):
        bar = pltpu.get_barrier_semaphore()
        count = 0
        for axis in axes:
            for _, dev, _ in self.peers(axis):
                pl.semaphore_signal(bar, inc=1, device_id=dev, device_id_type=MESH)
                count += 1
        pl.semaphore_wait(bar, count)


def rows_at(start, size):
    return pl.ds(pl.multiple_of(start, 16), size)


def add_into(dst, start, lanes, terms, size):
    step = 64 if size % 64 == 0 else 16

    def one(i, carry):
        off = pl.multiple_of(i * step, step)
        total = terms[0](off, step).astype(F32)
        for term in terms[1:]:
            total = total + term(off, step).astype(F32)
        dst[pl.ds(pl.multiple_of(start + off, 16), step), lanes] = total.astype(dst.dtype)
        return carry

    lax.fori_loop(0, size // step, one, 0)


class Reducer:
    ORDERS = (("y", "x", "z"), ("x", "y", "z"))

    @staticmethod
    def scratch(rows, width, size):
        shapes = [pltpu.VMEM((rows // 2, width), BF)]
        sends = 2
        for order in Reducer.ORDERS:
            blk = rows // 2
            for axis in order:
                blk //= size[axis]
                shapes.append(pltpu.VMEM((size[axis] - 1, blk, width // 2), BF))
                sends += 2 * (size[axis] - 1)
            shapes.append(pltpu.VMEM((blk, width // 2), BF))
            sends += 1
        shapes += [pltpu.SemaphoreType.DMA((sends,)), pltpu.SemaphoreType.DMA((sends,)), pltpu.SemaphoreType.DMA((2,))]
        return shapes

    COUNT = 12

    def __init__(self, place, rows, width, src, out, first, bufs, own=None):
        self.place, self.rows, self.width, self.src, self.out, self.first = place, rows, width, src, out, first
        self.own, self.now = own, 0
        self.core = bufs[0]
        self.bufs = (bufs[1:4], bufs[5:8])
        self.fin = (bufs[4], bufs[8])
        self.ssem, self.rsem, self.lsem = bufs[9:12]
        self.next = 0
        self.copies = []
        self.half = [self.plan(0), self.plan(1)]

    def copy(self, src, dst, dev):
        k = self.next
        self.next += 1
        cp = (src, dst, k, dev)
        self.copies.append(cp)
        return cp

    def make(self, cp):
        src, dst, k, dev = cp
        return pltpu.make_async_remote_copy(
            src_ref=src(), dst_ref=dst(), send_sem=self.ssem.at[k], recv_sem=self.rsem.at[k], device_id=dev, device_id_type=MESH
        )

    def start(self, cps):
        for cp in cps:
            self.make(cp).start()

    def arrived(self, cps):
        for cp in cps:
            self.make(cp).wait_recv()

    def finish(self):
        for cp in self.copies:
            self.make(cp).wait_send()

    def plan(self, h):
        pc, hw = self.place, self.width // 2
        order = self.ORDERS[h]
        lanes = pl.ds(h * hw, hw)
        c = pc.at["c"]
        top = self.rows // 2
        core, bufs, fin, src, out, first = self.core, self.bufs[h], self.fin[h], self.src, self.out, self.first
        blk, rel = [top], [0]
        for axis in order:
            blk.append(blk[-1] // pc.size[axis])
            rel.append(rel[-1] + pc.at[axis] * blk[-1])
        stages = []
        (_, cdev, _), = pc.peers("c")
        ccopy = self.copy(
            lambda: src.at[rows_at((1 - c) * top, top), lanes], lambda: core.at[:, lanes], cdev
        )
        stages.append(lambda: self.start([ccopy]))
        out_at = lambda level: out.at[rows_at(first + c * top + rel[level], blk[level]), lanes]
        prev = [ccopy]
        downs = []
        for lv, axis in enumerate(order):
            cps = [
                self.copy(
                    lambda lv=lv, pos=pos: core.at[rows_at(rel[lv] + pos * blk[lv + 1], blk[lv + 1]), lanes],
                    lambda lv=lv, off=off: bufs[lv].at[off - 1],
                    dev,
                )
                for off, dev, pos in pc.peers(axis)
            ]
            downs.append(cps)

        def fold(lv, last):
            if lv == 0:
                if self.own is None:
                    mine = lambda o, n: src[pl.ds(pl.multiple_of(c * top + o, 16), n), lanes]
                else:
                    mine = lambda o, n: self.own[pl.ds(o, n), lanes]
                terms = [mine, lambda o, n: core[pl.ds(o, n), lanes]]
                add_into(core, 0, lanes, terms, top)
                return
            terms = [lambda o, n: core[pl.ds(pl.multiple_of(rel[lv] + o, 16), n), lanes]]
            for k in range(pc.size[order[lv - 1]] - 1):
                terms.append(lambda o, n, k=k: bufs[lv - 1][k, pl.ds(o, n), :])
            if last:
                add_into(fin, 0, slice(None), terms, blk[lv])
            else:
                add_into(core, rel[lv], lanes, terms, blk[lv])

        def step(lv):
            def run():
                self.arrived([ccopy] if lv == 0 else downs[lv - 1])
                fold(lv, False)
                self.start(downs[lv])

            return run

        for lv in range(3):
            stages.append(step(lv))
        up = [[self.copy(lambda: fin, lambda: out_at(3), dev) for _, dev, _ in pc.peers("z")]]
        up.append([self.copy(lambda: out_at(2), lambda: out_at(2), dev) for _, dev, _ in pc.peers(order[1])])
        up.append([self.copy(lambda: out_at(1), lambda: out_at(1), dev) for _, dev, _ in pc.peers(order[0])])
        up.append([self.copy(lambda: out_at(0), lambda: out_at(0), cdev)])
        mine = lambda: pltpu.make_async_copy(fin, out_at(3), self.lsem.at[h])

        def turn():
            self.arrived(downs[2])
            fold(3, True)
            mine().start()
            self.start(up[0])

        stages.append(turn)

        def climb(i):
            def run():
                if i == 0:
                    mine().wait()
                self.arrived(up[i])
                if i + 1 < len(up):
                    self.start(up[i + 1])

            return run

        for i in range(4):
            stages.append(climb(i))
        return stages

    def take(self):
        i, self.now = self.now, self.now + 1
        return lambda: [self.half[h][i]() for h in range(2)]

    def advance(self):
        if self.now < self.STAGES:
            self.take()()

    STAGES = 9


FLAT = {"f1i": 0, "f1o": 2048, "q": 4096, "k": 4608, "v": 5120, "p": 5632, "o": 6144, "ci": 6656, "co": 7680, "f2i": 8192, "f2o": 10240}
FLAT_ROWS = 12288
ORDER = tuple(FLAT)
FOLDS = {"f1i": 4, "ci": 2, "f2i": 4}
FLAT_SIZE = {n: (list(FLAT.values()) + [FLAT_ROWS])[i + 1] - FLAT[n] for i, n in enumerate(FLAT)}


def ticks(point, plan, p):
    for at, run in plan.items():
        if at % 2 == point:
            pl.when(p == at // 2)(lambda run=run: (run(), None)[1])


class Gather:
    STAGES = 5

    @staticmethod
    def scratch(size, shard_rows, width):
        part, pieces = Gather.cut(shard_rows)
        links = 2 * pieces * sum(n - 1 for n in size.values())
        sems = pltpu.SemaphoreType.DMA((links,))
        return [
            pltpu.VMEM((size["x"], 2, size["z"], size["y"], shard_rows, width), BF),
            pltpu.VMEM((width // LANE, 64, LANE), F32),
            sems,
            sems,
        ]

    @staticmethod
    def cut(shard_rows):
        part = 64 if shard_rows % 64 == 0 else 16
        return part, shard_rows // part

    def __init__(self, pc, wf, bufs):
        self.pc, self.wf = pc, wf
        self.nb, self.scr, self.ssem, self.rsem = bufs
        self.shard_rows = self.nb.shape[4]
        self.part, self.pieces = self.cut(self.shard_rows)
        self.xs = pc.size["x"]
        self.now = 0
        self.used = 0
        self.stages = [self.plan(hx, q) for hx in range(2) for q in range(self.pieces)]

    def copies(self, ref, axis):
        out = []
        for off, dev, _ in self.pc.peers(axis):
            k = self.used
            self.used += 1
            out.append(
                (off, pltpu.make_async_remote_copy(
                    src_ref=ref, dst_ref=ref, send_sem=self.ssem.at[k], recv_sem=self.rsem.at[k], device_id=dev, device_id_type=MESH
                ))
            )
        return out

    def plan(self, hx, q):
        pc, nb = self.pc, self.nb
        x, c, z, y = (pc.at[a] for a in "xczy")
        rows = pl.ds(q * self.part, self.part)
        side = pl.ds(hx * (self.xs // 2), self.xs // 2)
        in_half = lambda pos: lax.div(pos, self.xs // 2) == hx
        along = {
            "x": self.copies(nb.at[x, c, z, y, rows], "x"),
            "z": self.copies(nb.at[side, c, z, y, rows], "z"),
            "y": self.copies(nb.at[side, c, :, y, rows], "y"),
            "c": self.copies(nb.at[side, c, :, :, rows], "c"),
        }

        def each(axis, what, cond=None):
            for off, cp in along[axis]:
                if cond is None:
                    getattr(cp, what)()
                else:
                    pl.when(cond(off))(lambda cp=cp: getattr(cp, what)())

        sends = lambda off: in_half(x)
        gets = lambda off: in_half(lax.rem(x - off + self.xs, self.xs))

        def end():
            each("c", "wait_recv")
            if self.part == 64:
                self.mix_half(hx, q)
            elif q == self.pieces - 1:
                self.mix_half(hx, None)

        def done():
            each("x", "wait_send", sends)
            for axis in "zyc":
                each(axis, "wait_send")

        return [
            lambda: each("x", "start", sends),
            lambda: (each("x", "wait_recv", gets), each("z", "start")),
            lambda: (each("z", "wait_recv"), each("y", "start")),
            lambda: (each("y", "wait_recv"), each("c", "start")),
            end,
            done,
        ]

    def take(self):
        t, self.now = self.now, self.now + 1

        def run():
            for i, stages in enumerate(self.stages):
                if 0 <= t - i < self.STAGES:
                    stages[t - i]()

        return run

    def finish(self):
        for stages in self.stages:
            stages[self.STAGES]()

    def noise_at(self, row):
        pc = self.pc
        got = []
        sub = min(64, self.part)
        for i in range(64 // sub):
            at = row + i * sub
            d = lax.div(at, self.shard_rows)
            slots = pc.size["z"] * pc.size["y"]
            tm, sl = lax.div(d, slots), lax.rem(d, slots)
            off = pl.multiple_of(lax.rem(at, self.shard_rows), 16)
            got.append(
                self.nb[lax.div(tm, 2), lax.rem(tm, 2), lax.div(sl, pc.size["y"]), lax.rem(sl, pc.size["y"]), pl.ds(off, sub), :].astype(F32)
            )
        return got[0] if len(got) == 1 else jnp.concatenate(got, axis=0)

    def mix(self, row, base, size, fold):
        wf, scr = self.wf, self.scr
        value = self.noise_at(row)
        if fold == 1:
            at = rows_at(row, 64)
            wf[at, :] = (wf[at, :].astype(F32) + value).astype(BF)
            return
        for b in range(512 // LANE):
            scr[b] = value[:, b * LANE : (b + 1) * LANE]
        high = 64 // fold
        for j in range(fold):
            at = rows_at(base + j * (size // fold) + lax.div(row - base, fold), high)
            for b in range(512 // LANE):
                lanes = pl.ds(b * LANE, LANE)
                wf[at, lanes] = (wf[at, lanes].astype(F32) + scr[b, pl.ds(j, high, stride=fold), :]).astype(BF)

    def mix_half(self, hx, q):
        for name in ORDER:
            base, size, fold = FLAT[name], FLAT_SIZE[name], FOLDS.get(name, 1)
            if (base < FLAT_ROWS // 2) != (hx == 0):
                continue
            begin, end = base // 64, (base + size) // 64
            start, stride = (begin, 1) if q is None else (begin + (q - begin) % self.pieces, self.pieces)
            lax.fori_loop(
                0, (end - start + stride - 1) // stride,
                lambda i, t: (self.mix((start + i * stride) * 64, base, size, fold), t)[1], 0,
            )


class KeysAll:
    @staticmethod
    def scratch(xs):
        n = 2 * xs - 1
        sems = pltpu.SemaphoreType.DMA((H // 2, n))
        return [sems, sems]

    def __init__(self, pc, kv, bufs):
        self.pc, self.kv = pc, kv
        self.ssem, self.rsem = bufs

    def copy(self, p, k, tm, dev):
        ref = self.kv.at[p, :, tm]
        return pltpu.make_async_remote_copy(
            src_ref=ref, dst_ref=ref, send_sem=self.ssem.at[p, k], recv_sem=self.rsem.at[p, k], device_id=dev, device_id_type=MESH
        )

    def core(self, p):
        ((_, dev, _),) = self.pc.peers("c")
        return [self.copy(p, 0, self.pc.tm, dev)]

    def line(self, p):
        return [self.copy(p, off, self.pc.tm, dev) for off, dev, _ in self.pc.peers("x")]

    def relay(self, p):
        ((_, dev, _),) = self.pc.peers("c")
        xs = self.pc.size["x"]
        out = []
        for off in range(1, xs):
            source = lax.rem(self.pc.at["x"] - off + xs, xs) * 2 + self.pc.at["c"]
            out.append(self.copy(p, xs - 1 + off, source, dev))
        return out

    def send(self, p):
        for cp in self.line(p) + self.core(p):
            cp.start()

    def forward(self, p):
        for come, on in zip(self.line(p), self.relay(p)):
            come.wait_recv()
            on.start()

    def ready(self, p):
        for cp in self.core(p) + self.relay(p):
            cp.wait_recv()

    def sent(self, p):
        for cp in self.line(p) + self.core(p) + self.relay(p):
            cp.wait_send()


def angle_tables(hi, lo, rates):
    for ref, step in ((hi, 64.0), (lo, 1.0)):
        count = ref.shape[1]
        angle = lax.broadcasted_iota(jnp.int32, (count, rates.shape[1]), 0).astype(F32) * step * rates
        ref[0] = jnp.sin(angle)
        ref[1] = jnp.cos(angle)


def angle_block(hi, lo, m):
    hs, hc = hi[0, pl.ds(m, 1), :], hi[1, pl.ds(m, 1), :]
    ls, lc = lo[0], lo[1]
    return hs * lc + hc * ls, hc * lc - hs * ls


def early_body(*refs):
    lens, noise, raws = refs[0], refs[1], refs[2:13]
    x_ref, gain1, gain2, pos_u, pos_v = refs[13:18]
    wn, x1_out, pre_out, a2_out, qu_out, qv_out, kv_out, trig_out, sin_out, cos_out, att_out, probs = refs[18:30]
    wf, flat, x1_ref, pre_ref, a2_ref, qu, qv, kv, trig, sin, cos, hi, lo, att, pbuf, wsem, osem, psem = refs[30:48]
    bufs = refs[48:]
    pc = Place()
    rows, width = x_ref.shape
    half = width // 2
    tms = lax.axis_size("tm")
    frames = rows * tms
    loads = []
    for name, raw in zip(ORDER, raws):
        for j in range(FOLDS.get(name, 1)):
            size = FLAT_SIZE[name] // FOLDS.get(name, 1)
            dst = wf.at[pl.ds(FLAT[name] + j * size, size), :]
            loads.append(pltpu.make_async_copy(raw.at[:, pl.ds(j * 512, 512)], dst, wsem.at[len(loads)]))
            loads[-1].start()
    gather = Gather(pc, wf, bufs[:4])
    keys = KeysAll(pc, kv, bufs[4:6])

    def unfold(i, carry):
        for r in range(8):
            for b in range(width // LANE):
                at = pl.ds(pl.multiple_of((i * 8 + r) * width + b * LANE, LANE), LANE)
                flat[b, pl.ds(i * 8 + r, 1), :] = noise[:, at].astype(F32)
        return carry

    shard_rows = gather.shard_rows
    lax.fori_loop(0, shard_rows // 8, unfold, 0)
    for b in range(width // LANE):
        gather.nb[pc.at["x"], pc.at["c"], pc.at["z"], pc.at["y"], :, pl.ds(b * LANE, LANE)] = flat[b].astype(BF)
    pc.greet("cxyz")
    for _ in range(3):
        gather.take()()
    rates = jnp.exp(lax.broadcasted_iota(jnp.int32, (1, half), 1).astype(F32) * (-2.0 * math.log(10000.0) / width))
    angle_tables(hi, lo, rates)

    def angles(m, carry):
        s, c = angle_block(hi, lo, m)
        at = rows_at(m * 64, 64)
        trig[at, pl.ds(0, half)] = s.astype(BF)
        trig[at, pl.ds(half, half)] = c.astype(BF)
        return carry

    def own_angles(m, carry):
        s, c = angle_block(hi, lo, pc.tm * (rows // 64) + m)
        sin[rows_at(m * 64, 64), :] = s
        cos[rows_at(m * 64, 64), :] = c
        return carry

    lax.fori_loop(0, frames // 64, angles, 0)
    lax.fori_loop(0, rows // 64, own_angles, 0)
    for cp in loads:
        cp.wait()
    outs = []

    def put(src, dst):
        cp = pltpu.make_async_copy(src, dst, osem.at[len(outs)])
        cp.start()
        outs.append(cp)

    x = x_ref[...].astype(F32)
    a1 = norm(x, gain1[...]).astype(BF)
    while gather.now < gather.pieces + gather.STAGES - 1:
        gather.take()()
    part = lambda name: wf.at[pl.ds(FLAT[name], FLAT_SIZE[name]), :]
    x1 = x + 0.5 * ffn_forward(a1, part("f1i"), part("f1o"), pre_ref)
    x1_ref[...] = x1
    a2 = norm(x1, gain2[...]).astype(BF)
    a2_ref[...] = a2
    k = dot(a2, part("k")[...]).astype(BF)
    v = dot(a2, part("v")[...]).astype(BF)
    for p in range(H // 2):
        kv[p, 0, pc.tm] = k[:, p * LANE : (p + 1) * LANE]
        kv[p, 1, pc.tm] = v[:, p * LANE : (p + 1) * LANE]
        keys.send(p)
    gather.take()()
    q = dot(a2, part("q")[...])
    scale = HD**-0.5
    qu[...] = ((q + pos_u[...]).astype(BF).astype(F32) * scale).astype(BF)
    qv[...] = ((q + pos_v[...]).astype(BF).astype(F32) * scale).astype(BF)
    for src, dst in ((x1_ref, x1_out), (pre_ref, pre_out), (a2_ref, a2_out), (qu, qu_out), (qv, qv_out), (trig, trig_out), (sin, sin_out), (cos, cos_out)):
        put(src, dst)
    put(wf.at[pl.ds(0, FLAT_ROWS // 2), :], wn.at[pl.ds(0, FLAT_ROWS // 2), :])
    gather.take()()
    total = 2 * gather.pieces + gather.STAGES - 1
    left = [gather.take() for _ in range(total - gather.now)]
    plan = {}
    for i, run in enumerate(left):
        at = i * H // len(left)
        plan.setdefault(at, []).append(run)
    plan = {at: (lambda runs=runs: [r() for r in runs]) for at, runs in plan.items()}
    ok = lax.broadcasted_iota(jnp.int32, (1, frames), 1) < lens[0]
    w_pos = part("p")
    store = lambda p, e: pltpu.make_async_copy(pbuf.at[e], probs.at[2 * p + e], psem.at[e])

    def pair(p, carry):
        at = cols(p)
        mixed = None
        for e in range(2):
            mine = lane_half(e)
            qve = jnp.where(mine, qv[:, at], jnp.zeros((), BF))
            que = jnp.where(mine, qu[:, at], jnp.zeros((), BF))
            a_s = dot_nt(qve, w_pos[pl.ds(0, half), at])
            a_c = dot_nt(qve, w_pos[pl.ds(half, half), at])
            b_c = (a_s * sin[...] + a_c * cos[...]).astype(BF)
            b_s = (a_c * sin[...] - a_s * cos[...]).astype(BF)
            s = dot_nt(b_s, trig[:, pl.ds(0, half)]) + dot_nt(b_c, trig[:, pl.ds(half, half)])
            if e == 0:
                pl.when(p == 0)(lambda: keys.forward(0))
                keys.ready(p)
            s = s + dot_nt(que, kv[p, 0].reshape(frames, LANE))
            s = jnp.where(ok, s, FILL)
            m = jnp.max(s, axis=-1, keepdims=True)
            ex = jnp.exp(s - m)
            tot = jnp.sum(ex, axis=-1, keepdims=True)
            low = (ex * (1.0 / tot)).astype(BF)
            pl.when(p > 0)(lambda: store(p - 1, e).wait())
            pbuf[e] = low
            store(p, e).start()
            got = dot(low, kv[p, 1].reshape(frames, LANE))
            mixed = got if e == 0 else jnp.where(mine, got, mixed)
            if e == 1:
                pl.when(p < H // 2 - 1)(lambda: keys.forward(p + 1))
            ticks(e, plan, p)
        att[:, at] = mixed.astype(BF)
        return carry

    lax.fori_loop(0, H // 2, pair, 0)
    put(kv, kv_out)
    put(att, att_out)
    put(wf.at[pl.ds(FLAT_ROWS // 2, FLAT_ROWS // 2), :], wn.at[pl.ds(FLAT_ROWS // 2, FLAT_ROWS // 2), :])
    for e in range(2):
        store(H // 2 - 1, e).wait()
    for p in range(H // 2):
        keys.sent(p)
    gather.finish()
    for cp in outs:
        cp.wait()


def chunk(c):
    return pl.ds(pl.multiple_of(c * 512, 512), 512)


def ffn_forward(normed, w_in, w_out, pre_ref):
    def one(c, acc):
        pre = dot(normed, w_in[chunk(c), :])
        pre_ref[:, chunk(c)] = pre
        return acc + dot((pre * sigmoid(pre)).astype(BF), w_out[chunk(c), :])

    return lax.fori_loop(0, w_in.shape[0] // 512, one, jnp.zeros((normed.shape[0], w_out.shape[1]), F32))


def ffn_backward(g_low, normed, w_in, w_out, pre_ref, gin_ref, gout_ref):
    normed_t = normed.T

    def one(c, acc):
        sw, slope = swish_and_slope(pre_ref[:, chunk(c)])
        gout_ref[chunk(c), :] = dot_tn(sw.astype(BF), g_low).astype(gout_ref.dtype)
        dpre = (dot_nt(g_low, w_out[chunk(c), :]) * slope).astype(BF)
        gin_ref[chunk(c), :] = dot(normed_t, dpre).astype(gin_ref.dtype)
        return acc + dot_nt(dpre, w_in[chunk(c), :])

    return lax.fori_loop(0, w_in.shape[0] // 512, one, jnp.zeros(g_low.shape, F32))


class Fetch:
    def __init__(self, sems):
        self.sems, self.n = sems, 0

    def __call__(self, src, dst):
        cp = pltpu.make_async_copy(src, dst, self.sems.at[self.n])
        self.n += 1
        cp.start()
        return cp


def part_of(wn, name):
    return wn.at[pl.ds(FLAT[name], FLAT_SIZE[name]), :]


def valid_rows(lens, rows):
    first = lax.axis_index("tm") * rows
    return ((first + lax.broadcasted_iota(jnp.int32, (rows, 1), 0)) < lens[0]).astype(F32)


def spread(ext, start, value):
    value = value.astype(F32)
    for b in range(ext.shape[0]):
        ext[b, pl.ds(start, value.shape[0]), :] = value[:, b * LANE : (b + 1) * LANE]


def tap_sum(ext, taps, out_ref, offset):
    count = taps.shape[0]
    rows = out_ref.shape[0]
    block = 64 if rows % 64 == 0 else 16

    def one(i, carry):
        for b in range(ext.shape[0]):
            at = pl.ds(b * LANE, LANE)
            acc = jnp.zeros((block, LANE), F32)
            for k in range(count):
                acc = acc + taps[pl.ds(k, 1), at] * ext[b, pl.ds(i * block + offset(k), block), :]
            out_ref[pl.ds(pl.multiple_of(i * block, block), block), at] = acc
        return carry

    lax.fori_loop(0, rows // block, one, 0)


def bn_stats(sums):
    total = sums[2:3, :]
    mu = sums[0:1, :] / total
    var = sums[1:2, :] / total - mu * mu
    return mu, lax.rsqrt(var + EPS), total


class Totals:
    @staticmethod
    def scratch(tms, slots, width):
        n = tms + slots - 2
        return [
            pltpu.VMEM((tms, 8, width), F32),
            pltpu.VMEM((slots, 8, width), F32),
            pltpu.SemaphoreType.DMA((n,)),
            pltpu.SemaphoreType.DMA((n,)),
        ]

    def __init__(self, pc, bufs):
        self.pc, self.bufs = pc, bufs

    def __call__(self, value):
        pc = self.pc
        tmb, slb, ssem, rsem = self.bufs
        sent = []
        k = 0
        for buf, axis, me in ((tmb, "tm", pc.tm), (slb, "slot", pc.slot)):
            buf[me] = value
            n = buf.shape[0]
            cps = []
            for off in range(1, n):
                to = lax.rem(me + off, n)
                dev = (to, pc.slot) if axis == "tm" else (pc.tm, to)
                cp = pltpu.make_async_remote_copy(
                    src_ref=buf.at[me], dst_ref=buf.at[me], send_sem=ssem.at[k], recv_sem=rsem.at[k], device_id=dev, device_id_type=MESH
                )
                cp.start()
                cps.append(cp)
                k += 1
            for cp in cps:
                cp.wait_recv()
            sent += cps
            value = buf[0]
            for i in range(1, n):
                value = value + buf[i]
        for cp in sent:
            cp.wait_send()
        return value


def greet_rows(pc, tms, slots):
    bar = pltpu.get_barrier_semaphore()
    for off in range(1, tms):
        pl.semaphore_signal(bar, inc=1, device_id=(lax.rem(pc.tm + off, tms), pc.slot), device_id_type=MESH)
    for off in range(1, slots):
        pl.semaphore_signal(bar, inc=1, device_id=(pc.tm, lax.rem(pc.slot + off, slots)), device_id_type=MESH)
    pl.semaphore_wait(bar, tms + slots - 2)


def middle_body(
    lens, att, x1_ref, cot, wn, taps, bn_gain, bn_bias, gain3, gain4, gain5,
    out_ref, dx2_ref, datt_ref, g_ref, smalls_ref, bns_ref,
    w_o, w_ci, w_co, w_f2i, w_f2o, fsem, early, late, hsem, gm_ref, ddwo_ref, z_ref, ext, ext2, dwo_ref, pre_ref, dgm_ref, acc, x2_ref, *bufs,
):
    pc = Place()
    tms, slots = lax.axis_size("tm"), lax.axis_size("slot")
    rows, width = x1_ref.shape
    count = taps.shape[0]
    fetch = Fetch(fsem)
    got = {n: fetch(part_of(wn, n), d) for n, d in (("o", w_o), ("ci", w_ci), ("co", w_co), ("f2i", w_f2i), ("f2o", w_f2o))}
    greet_rows(pc, tms, slots)
    totals = Totals(pc, bufs[:4]), Totals(pc, bufs[4:])

    def halo(src, dst, k, step):
        dev = (lax.rem(pc.tm + step + tms, tms), pc.slot)
        return pltpu.make_async_remote_copy(
            src_ref=src, dst_ref=dst, send_sem=hsem.at[2 * k], recv_sem=hsem.at[2 * k + 1], device_id=dev, device_id_type=MESH
        )

    got["o"].wait()
    x2 = x1_ref[...] + dot(att[...], w_o[...])
    x2_ref[...] = x2
    a3 = norm(x2, gain3[...]).astype(BF)
    got["ci"].wait()
    z1 = dot(a3, w_ci[pl.ds(0, width), :])
    z2 = dot(a3, w_ci[pl.ds(width, width), :])
    z_ref[:, pl.ds(0, width)] = z1
    z_ref[:, pl.ds(width, width)] = z2
    ok = valid_rows(lens, rows)
    gm_ref[...] = (z1 * sigmoid(z2) * ok).astype(BF)
    cp = halo(gm_ref.at[pl.ds(rows - count, count), :], early, 0, 1)
    cp.start()
    spread(ext, count, gm_ref[...])
    cp.wait()
    spread(ext, 0, jnp.where(pc.tm > 0, early[...], jnp.zeros((), BF)))
    tap_sum(ext, taps, dwo_ref, lambda k: k + 1)
    dwo = dwo_ref[...]
    dwv = dwo * ok
    sums = totals[0](
        jnp.concatenate(
            [
                jnp.sum(dwv, axis=0, keepdims=True),
                jnp.sum(dwv * dwv, axis=0, keepdims=True),
                jnp.zeros((1, width), F32) + jnp.sum(ok, axis=0, keepdims=True),
                jnp.zeros((5, width), F32),
            ],
            axis=0,
        )
    )
    mu, inv, total = bn_stats(sums)
    xhat = (dwo_ref[...] - mu) * inv
    sw, slope = swish_and_slope(xhat * bn_gain[...] + bn_bias[...])
    sw = sw.astype(BF)
    got["co"].wait()
    x3 = x2_ref[...] + dot(sw, w_co[...])
    a4 = norm(x3, gain4[...]).astype(BF)
    got["f2i"].wait()
    got["f2o"].wait()
    x4 = x3 + 0.5 * ffn_forward(a4, w_f2i, w_f2o, pre_ref)
    out_ref[...] = norm(x4, gain5[...]).astype(BF)
    dx4, gg5 = norm_back(x4, gain5[...], cot[...].astype(F32))
    g4 = (0.5 * dx4).astype(BF)
    lo = FLAT["o"]
    da4 = ffn_backward(
        g4, a4, w_f2i, w_f2o, pre_ref,
        g_ref.at[pl.ds(FLAT["f2i"] - lo, 2048), :], g_ref.at[pl.ds(FLAT["f2o"] - lo, 2048), :],
    )
    back, gg4 = norm_back(x3, gain4[...], da4)
    dx3 = dx4 + back
    g3 = dx3.astype(BF)
    dbn = dot_nt(g3, w_co[...]) * slope
    sums2 = totals[1](
        jnp.concatenate(
            [jnp.sum(dbn * xhat, axis=0, keepdims=True), jnp.sum(dbn, axis=0, keepdims=True), jnp.zeros((6, width), F32)], axis=0
        )
    )
    bns_ref[...] = sums2
    ddwo_ref[...] = (bn_gain[...] * inv * (dbn - ok * (sums2[1:2, :] + xhat * sums2[0:1, :]) / total)).astype(BF)
    cp = halo(ddwo_ref.at[pl.ds(0, count), :], late, 1, -1)
    cp.start()
    g_ref[pl.ds(FLAT["co"] - lo, width), :] = dot_tn(sw, g3).astype(BF)
    spread(ext2, 0, ddwo_ref[...])
    cp.wait()
    spread(ext2, rows, jnp.where(pc.tm < tms - 1, late[...], jnp.zeros((), BF)))
    tap_sum(ext2, taps, dgm_ref, lambda k: count - 1 - k)
    block = 64 if rows % 64 == 0 else 16
    for b in range(ext.shape[0]):
        acc[...] = jnp.zeros(acc.shape, F32)

        def one(i, carry, b=b):
            mine = ext2[b, pl.ds(pl.multiple_of(i * block, block), block), :]
            for k in range(count):
                prod = mine * ext[b, pl.ds(i * block + k + 1, block), :]
                acc[k] = acc[k] + jnp.sum(prod.reshape(block // 8, 8, LANE), axis=0)
            return carry

        lax.fori_loop(0, rows // block, one, 0)
        smalls_ref[pl.ds(0, count), pl.ds(b * LANE, LANE)] = jnp.sum(acc[...], axis=1)
    z1 = z_ref[:, pl.ds(0, width)]
    sg = sigmoid(z_ref[:, pl.ds(width, width)])
    dg = dgm_ref[...] * ok
    dz1 = (dg * sg).astype(BF)
    dz2 = (dg * z1 * sg * (1.0 - sg)).astype(BF)
    a3t = norm(x2_ref[...], gain3[...]).astype(BF).T
    g_ref[pl.ds(FLAT["ci"] - lo, width), :] = dot(a3t, dz1).astype(BF)
    g_ref[pl.ds(FLAT["ci"] - lo + width, width), :] = dot(a3t, dz2).astype(BF)
    da3 = dot_nt(dz1, w_ci[pl.ds(0, width), :]) + dot_nt(dz2, w_ci[pl.ds(width, width), :])
    back, gg3 = norm_back(x2_ref[...], gain3[...], da3)
    dx2 = dx3 + back
    dx2_ref[...] = dx2
    g2 = dx2.astype(BF)
    g_ref[pl.ds(0, width), :] = dot_tn(att[...], g2).astype(BF)
    datt_ref[...] = dot_nt(g2, w_o[...]).astype(BF)
    smalls_ref[pl.ds(count, 8), :] = jnp.concatenate([gg3, gg4, gg5, jnp.zeros((5, width), F32)], axis=0)


class Butterfly:
    @staticmethod
    def scratch(devices, shape):
        n = devices.bit_length() - 1
        return [pltpu.VMEM((n,) + shape, F32), pltpu.SemaphoreType.DMA((n,)), pltpu.SemaphoreType.DMA((n,))]

    def __init__(self, pc, value, bufs):
        self.value, (self.got, self.ssem, self.rsem) = value, bufs
        self.devs = []
        for axis, me in (("tm", pc.tm), ("slot", pc.slot)):
            bit = 1
            while bit < lax.axis_size(axis):
                to = me + bit - 2 * bit * lax.rem(lax.div(me, bit), 2)
                self.devs.append((to, pc.slot) if axis == "tm" else (pc.tm, to))
                bit *= 2

    def copy(self, k):
        return pltpu.make_async_remote_copy(
            src_ref=self.value, dst_ref=self.got.at[k], send_sem=self.ssem.at[k], recv_sem=self.rsem.at[k],
            device_id=self.devs[k], device_id_type=MESH,
        )

    def stage(self, k):
        if k > 0:
            self.copy(k - 1).wait()
            self.value[...] = self.value[...] + self.got[k - 1]
        if k < len(self.devs):
            self.copy(k).start()


GROUP = 2048


class KeyGrads:
    @staticmethod
    def scratch(tms, rows):
        pairs, xs = H // 2, tms // 2
        sems = pltpu.SemaphoreType.DMA((pairs, xs + 1))
        return [
            pltpu.VMEM((pairs, 2, 2, tms, HD, rows), BF),
            pltpu.VMEM((pairs, 2, tms, HD, rows), BF),
            pltpu.VMEM((xs - 1, pairs, 2, 2, HD, rows), BF),
            pltpu.VMEM((pairs, 2, 2, HD, rows), BF),
            pltpu.VMEM((pairs, 2, HD, rows), BF),
            sems,
            sems,
        ]

    def __init__(self, pc, bufs):
        self.pc = pc
        self.mine, self.core, self.line, self.both, self.got, self.ssem, self.rsem = bufs

    def put(self, p, kind, e, value):
        rows = self.mine.shape[-1]
        for t in range(self.mine.shape[3]):
            self.mine[p, kind, e, t] = value[:, t * rows : (t + 1) * rows].astype(BF)

    def copy(self, p, k, src, dst, dev):
        return pltpu.make_async_remote_copy(
            src_ref=src, dst_ref=dst, send_sem=self.ssem.at[p, k], recv_sem=self.rsem.at[p, k], device_id=dev, device_id_type=MESH
        )

    def first(self, p):
        ((_, dev, _),) = self.pc.peers("c")
        return [self.copy(p, 0, self.mine.at[p, :, 1 - self.pc.at["c"]], self.core.at[p], dev)]

    def second(self, p):
        return [
            self.copy(p, off, self.core.at[p, :, pl.ds(2 * pos, 2)], self.line.at[off - 1, p], dev) for off, dev, pos in self.pc.peers("x")
        ]

    def third(self, p):
        ((_, dev, _),) = self.pc.peers("c")
        return [self.copy(p, self.pc.size["x"], self.both.at[p, :, 1 - self.pc.at["c"]], self.got.at[p], dev)]

    def step(self, p, i):
        c, x = self.pc.at["c"], self.pc.at["x"]
        if i == 1:
            for cp in self.first(p):
                cp.wait_recv()
            for kind in range(2):
                for t in range(self.core.shape[2]):
                    total = self.core[p, kind, t].astype(F32) + self.mine[p, kind, c, t].astype(F32)
                    self.core[p, kind, t] = total.astype(BF)
        if i == 2:
            for cp in self.second(p):
                cp.wait_recv()
            for kind in range(2):
                for t in range(2):
                    total = self.core[p, kind, 2 * x + t].astype(F32)
                    for j in range(self.line.shape[0]):
                        total = total + self.line[j, p, kind, t].astype(F32)
                    self.both[p, kind, t] = total.astype(BF)
        if i == 3:
            for cp in self.third(p):
                cp.wait_recv()
            return
        for cp in (self.first, self.second, self.third)[i](p):
            cp.start()

    def sent(self, p):
        for cp in self.first(p) + self.second(p) + self.third(p):
            cp.wait_send()

    def collect(self, p, kind, dst):
        c = self.pc.at["c"]
        own = self.both[p, kind, c]
        other = self.got[p, kind]
        dst[pl.ds(pl.multiple_of(p * LANE + c * HD, HD), HD), :] = own
        dst[pl.ds(pl.multiple_of(p * LANE + (1 - c) * HD, HD), HD), :] = other


def late_body(
    qu_h, qv_h, kv_h, wn, trig_h, sin_h, cos_h, probs, datt_h, att_h, g_high, a2_h, x1_h, dx2_h, x_h, pre_h, smalls2, gain2, gain1,
    dx0_ref, flat, total_ref,
    qu, qv, kv, w_p, trig, sin, cos, datt, att, a2, x1_ref, dx2_ref, x_ref, pre_ref, wqkv, w1, own, pbuf, psem, fsem,
    dq_ref, dkt, dvt, gpost, qut, qvt, datt_t, g_low, *bufs,
):
    pc = Place()
    rows = qu.shape[0]
    half = sin.shape[1]
    fetch = Fetch(fsem)
    size = g_low.shape[0] // GROUP
    c = pc.at["c"]
    owns = [fetch(g_high.at[rows_at(i * GROUP + c * (GROUP // 2), GROUP // 2), :], own.at[i]) for i in range(size)]
    early = [fetch(s, d) for s, d in ((qu_h, qu), (qv_h, qv), (datt_h, datt), (kv_h, kv), (att_h, att), (part_of(wn, "p"), w_p), (trig_h, trig), (sin_h, sin), (cos_h, cos))]
    loads = [pltpu.make_async_copy(probs.at[e], pbuf.at[e], psem.at[e]) for e in range(2)]
    for cp in loads:
        cp.start()
    later = [
        fetch(s, d)
        for s, d in (
            (a2_h, a2), (x1_h, x1_ref), (dx2_h, dx2_ref), (x_h, x_ref), (pre_h, pre_ref),
            (wn.at[pl.ds(FLAT["q"], 1536), :], wqkv), (wn.at[pl.ds(0, 4096), :], w1),
        )
    ]
    pc.greet("cxyz")
    per = Reducer.COUNT
    groups = []
    for i in range(2 * size):
        at = GROUP * (i % size)
        scratch = bufs[i * per : (i + 1) * per]
        if i < size:
            src, first, mine = g_high.at[pl.ds(at, GROUP), :], at + g_low.shape[0], own.at[i]
        else:
            at = GROUP * (size - 1) if i == size else at - GROUP
            src, first, mine = g_low.at[pl.ds(at, GROUP), :], at, None
        groups.append(Reducer(pc, GROUP, 512, src, flat, first, scratch, mine))
    rest = bufs[2 * size * per :]
    keys = KeyGrads(pc, rest[:7])
    fly = Butterfly(pc, total_ref, rest[7:])
    high, low = groups[:size], groups[size:]
    for grp in high:
        grp.advance()
    for cp in owns:
        cp.wait()
    for cp in early:
        cp.wait()
    qut[...] = qu[...].T
    qvt[...] = qv[...].T
    datt_t[...] = datt[...].T

    def run(members):
        stages = [high[i].take() for i in members]
        return lambda: [stage() for stage in stages]

    plan = {at: run(members) for at, members in ((1, [0]), (2, [0, 1]), (4, [0, 1, 2]), (5, [0, 1, 2]), (7, [0, 1, 2]))}
    scale = HD**-0.5

    def pair(p, carry):
        at = cols(p)
        dqu = dqv = None
        for e in range(2):
            mine = lane_half(e)
            part = pl.ds(pl.multiple_of(p * LANE + e * HD, HD), HD)
            dm = jnp.where(mine, datt[:, at], jnp.zeros((), BF))
            inner = jnp.sum(dm.astype(F32) * att[:, at].astype(F32), axis=-1, keepdims=True)
            dp = dot_nt(dm, kv[p, 1].reshape(-1, LANE))
            loads[e].wait()
            low_p = pbuf[e]
            ds = (low_p.astype(F32) * (dp - inner)).astype(BF)
            keys.put(p, 0, e, dot(qut[part, :], ds))
            keys.put(p, 1, e, dot(datt_t[part, :], low_p))

            @pl.when(p < H // 2 - 1)
            def _():
                pltpu.make_async_copy(probs.at[2 * p + 2 + e], pbuf.at[e], psem.at[e]).start()

            db_s = dot(ds, trig[:, pl.ds(0, half)])
            db_c = dot(ds, trig[:, pl.ds(half, half)])
            da_s = (db_c * sin[...] - db_s * cos[...]).astype(BF)
            da_c = (db_c * cos[...] + db_s * sin[...]).astype(BF)
            gpost[part, pl.ds(0, half)] = dot(qvt[part, :], da_s)
            gpost[part, pl.ds(half, half)] = dot(qvt[part, :], da_c)
            part_v = dot(da_s, w_p[pl.ds(0, half), at]) + dot(da_c, w_p[pl.ds(half, half), at])
            part_u = dot(ds, kv[p, 0].reshape(-1, LANE))
            dqu = part_u if e == 0 else jnp.where(mine, part_u, dqu)
            dqv = part_v if e == 0 else jnp.where(mine, part_v, dqv)
            if e == 0:
                pl.when(p > 0)(lambda: keys.step(p - 1, 1))
            else:
                pl.when(p > 1)(lambda: keys.step(p - 2, 2))
                keys.step(p, 0)
            ticks(e, plan, p)
        dqu = dqu * scale
        dqv = dqv * scale
        dq_ref[:, at] = (dqu + dqv).astype(BF)
        total_ref[pl.ds(37, 1), at] = jnp.sum(dqu, axis=0, keepdims=True)
        total_ref[pl.ds(38, 1), at] = jnp.sum(dqv, axis=0, keepdims=True)
        return carry

    lax.fori_loop(0, H // 2, pair, 0)
    last = H // 2 - 1
    g_low[pl.ds(FLAT["p"], 512), :] = gpost[...].T.astype(BF)
    for cp in later:
        cp.wait()
    a2t = a2[...].T
    g_low[pl.ds(FLAT["q"], 512), :] = dot(a2t, dq_ref[...]).astype(BF)
    keys.step(last, 1)
    keys.step(last - 1, 2)
    run([0, 1, 2])()
    da2 = dot_nt(dq_ref[...], wqkv[pl.ds(0, 512), :])
    keys.step(last, 2)
    for p in range(H // 2):
        keys.step(p, 3)
        keys.collect(p, 0, dkt)
        keys.collect(p, 1, dvt)
    g_low[pl.ds(FLAT["k"], 512), :] = dot_nt(a2t, dkt[...]).astype(BF)
    g_low[pl.ds(FLAT["v"], 512), :] = dot_nt(a2t, dvt[...]).astype(BF)
    low[0].advance()
    run([0, 1, 2])()
    da2 = da2 + dot_nt(dkt[...].T, wqkv[pl.ds(512, 512), :]) + dot_nt(dvt[...].T, wqkv[pl.ds(1024, 512), :])
    back, gg2 = norm_back(x1_ref[...], gain2[...], da2)
    dx1 = dx2_ref[...] + back
    g1 = (0.5 * dx1).astype(BF)
    x = x_ref[...].astype(F32)
    a1 = norm(x, gain1[...]).astype(BF)
    low[0].advance()
    run([0, 1, 2])()
    da1 = ffn_backward(
        g1, a1, w1.at[pl.ds(0, 2048), :], w1.at[pl.ds(2048, 2048), :], pre_ref, g_low.at[pl.ds(0, 2048), :], g_low.at[pl.ds(2048, 2048), :]
    )
    for grp in low[1:]:
        grp.advance()
    back, gg1 = norm_back(x, gain1[...], da1)
    dx0_ref[...] = (dx1 + back).astype(BF)
    count = smalls2.shape[0] - 8
    total_ref[pl.ds(0, count), :] = smalls2[pl.ds(0, count), :]
    total_ref[pl.ds(count, 3), :] = smalls2[pl.ds(count, 3), :]
    total_ref[pl.ds(count + 3, 2), :] = jnp.concatenate([gg1, gg2], axis=0)
    total_ref[pl.ds(count + 7, 1), :] = jnp.zeros((1, 512), F32)
    t = 0
    while any(grp.now < grp.STAGES for grp in groups) or t <= len(fly.devs):
        for i, grp in enumerate(groups):
            if i <= size or t >= i - size - 1:
                grp.advance()
        if t <= len(fly.devs):
            fly.stage(t)
        t += 1
    for p in range(H // 2):
        keys.sent(p)
    for grp in groups:
        grp.finish()


def widen_body(flat, *refs):
    outs, (ibuf, obuf, isem, osem) = refs[:11], refs[11:]
    step = 512
    n = FLAT_ROWS // step
    loads = [pltpu.make_async_copy(flat.at[pl.ds(i * step, step), :], ibuf.at[i], isem.at[i]) for i in range(n)]
    for cp in loads:
        cp.start()
    stores = []
    slots = obuf.shape[0]
    for i in range(n):
        name = [m for m in ORDER if FLAT[m] <= i * step][-1]
        out = outs[ORDER.index(name)]
        off = i * step - FLAT[name]
        fold = FOLDS.get(name, 1)
        if fold == 1:
            dst = out.at[pl.ds(off, step), :]
        else:
            dst = out.at[:, pl.ds(off, step)]
        loads[i].wait()
        if i >= slots:
            stores[i - slots].wait()
        obuf[i % slots] = ibuf[i].astype(F32)
        stores.append(pltpu.make_async_copy(obuf.at[i % slots], dst, osem.at[i % slots]))
        stores[-1].start()
    for cp in stores[-slots:]:
        cp.wait()


def remote(body, cid, outs, ins, scratch, name):
    def space(x):
        if x is None:
            return pl.BlockSpec(memory_space=pl.ANY)
        return pl.BlockSpec(memory_space=x)

    return pl.pallas_call(
        body,
        out_shape=[jax.ShapeDtypeStruct(s, d) for s, d, _ in outs],
        in_specs=[space(m) for _, m in ins],
        out_specs=[space(m) for _, _, m in outs],
        scratch_shapes=list(scratch),
        compiler_params=pltpu.CompilerParams(collective_id=cid, has_side_effects=True, vmem_limit_bytes=VMEM_LIMIT),
        name=name,
    )(*[x for x, _ in ins])


def local(
    inputs, cotangent, lengths, weight_noise, ffn1_in, ffn1_out, query_w, key_w, value_w, pos_w, out_w,
    conv_in, conv_out, ffn2_in, ffn2_out, conv_kernel, ffn1_gain, attn_gain, conv_gain, ffn2_gain,
    final_gain, bn_gain, bn_bias, pos_u, pos_v,
):
    _, rows, width = inputs.shape
    tms, slots = lax.axis_size("tm"), lax.axis_size("slot")
    frames = rows * tms
    count = conv_kernel.shape[0]
    devices = tms * slots
    size = Place().size
    x = inputs[0]
    cot = cotangent[0]
    gains = [g.reshape(1, -1) for g in (ffn1_gain, attn_gain, conv_gain, ffn2_gain, final_gain)]
    bng, bnb, pu, pv = (g.reshape(1, -1) for g in (bn_gain, bn_bias, pos_u, pos_v))
    raws = (ffn1_in, ffn1_out, query_w, key_w, value_w, pos_w, out_w, conv_in, conv_out, ffn2_in, ffn2_out)
    VM, HB, SM = pltpu.VMEM, None, pltpu.SMEM
    DMA = pltpu.SemaphoreType.DMA
    V = lambda shape, dtype=BF: pltpu.VMEM(shape, dtype)
    shard_rows = weight_noise.shape[1] // width
    half, hidden = width // 2, 2048
    keys = (H // 2, 2, tms, rows, LANE)
    specs = [
        ((FLAT_ROWS, width), BF), ((rows, width), F32), ((rows, hidden), F32), ((rows, width), BF), ((rows, width), BF), ((rows, width), BF),
        (keys, BF), ((frames, width), BF), ((rows, half), F32), ((rows, half), F32), ((rows, width), BF), ((H, rows, frames), BF),
    ]
    wn, x1, pre1, a2, qu, qv, kv, trig, sin, cos, att, probs = remote(
        early_body, 0, [spec + (HB,) for spec in specs],
        [(lengths, SM), (weight_noise, VM)] + [(r, HB) for r in raws] + [(x, VM), (gains[0], VM), (gains[1], VM), (pu, VM), (pv, VM)],
        [V((FLAT_ROWS, width)), V((width // LANE, shard_rows, LANE), F32)]
        + [V(*spec) for spec in specs[1:10]]
        + [V((2, frames // 64, half), F32), V((2, 64, half), F32), V((rows, width)), V((2, rows, frames)), DMA((18,)), DMA((16,)), DMA((2,))]
        + Gather.scratch(size, shard_rows, width) + KeysAll.scratch(size["x"]),
        "early",
    )
    ext = pltpu.VMEM((width // LANE, rows + count, LANE), F32)
    output, dx2, datt, g_high, smalls2, bns = remote(
        middle_body, 1,
        [((rows, width), BF, VM), ((rows, width), F32, VM), ((rows, width), BF, VM), ((FLAT_ROWS // 2, width), BF, VM),
         ((count + 8, width), F32, VM), ((8, width), F32, VM)],
        [(lengths, SM), (att, VM), (x1, VM), (cot, VM), (wn, HB), (conv_kernel, VM), (bng, VM), (bnb, VM)] + [(g, VM) for g in gains[2:]],
        [pltpu.VMEM((FLAT_SIZE[n], width), BF) for n in ("o", "ci", "co", "f2i", "f2o")]
        + [DMA((5,)), pltpu.VMEM((count, width), BF), pltpu.VMEM((count, width), BF), DMA((4,)),
           pltpu.VMEM((rows, width), BF), pltpu.VMEM((rows, width), BF), pltpu.VMEM((rows, 2 * width), F32), ext, ext,
           pltpu.VMEM((rows, width), F32), pltpu.VMEM((rows, hidden), F32), pltpu.VMEM((rows, width), F32),
           pltpu.VMEM((count, 8, LANE), F32), pltpu.VMEM((rows, width), F32)]
        + Totals.scratch(tms, slots, width) * 2,
        "middle",
    )
    dx0, flat, total = remote(
        late_body, 2, [((rows, width), BF, VM), ((FLAT_ROWS, width), BF, HB), ((count + 8, width), F32, VM)],
        [(t, HB) for t in (qu, qv, kv, wn, trig, sin, cos, probs, datt, att, g_high, a2, x1, dx2, x, pre1)]
        + [(smalls2, VM), (gains[1], VM), (gains[0], VM)],
        [V((rows, width)), V((rows, width)), V(keys), V((width, width)), V((frames, width)),
         V((rows, half), F32), V((rows, half), F32), V((rows, width)), V((rows, width)), V((rows, width)),
         V((rows, width), F32), V((rows, width), F32), V((rows, width)), V((rows, hidden), F32), V((3 * width, width)), V((4096, width)),
         V((FLAT_ROWS // 2 // GROUP, GROUP // 2, width)), V((2, rows, frames)), DMA((2,)), DMA((20,)),
         V((rows, width)), V((width, rows)), V((width, rows)), V((width, width), F32), V((width, rows)), V((width, rows)), V((width, rows)),
         V((FLAT_ROWS // 2, width))]
        + Reducer.scratch(GROUP, width, size) * (FLAT_ROWS // GROUP) + KeyGrads.scratch(tms, rows)
        + Butterfly.scratch(devices, (count + 8, width)),
        "late",
    )
    big = pl.pallas_call(
        widen_body,
        out_shape=[jax.ShapeDtypeStruct(r.shape, F32) for r in raws],
        in_specs=[pl.BlockSpec(memory_space=pl.ANY)],
        out_specs=[pl.BlockSpec(memory_space=pl.ANY)] * 11,
        scratch_shapes=[pltpu.VMEM((24, 512, width), BF), pltpu.VMEM((4, 512, width), F32), DMA((24,)), DMA((4,))],
        compiler_params=pltpu.CompilerParams(vmem_limit_bytes=VMEM_LIMIT),
        name="widen",
    )(flat)
    t = total[count:]
    return (output[None], dx0[None]) + tuple(big) + (
        total[:count], t[3], t[4], t[0], t[1], t[2], bns[0], bns[1], t[5], t[6],
    )


def solution(mesh):
    split = P("slot", "tm", None)
    in_specs = (split, split, P("slot"), P(("tm", "slot"), None)) + (P(),) * 21
    out_specs = (split, split) + (P(),) * 21
    return jax.shard_map(local, mesh=mesh, in_specs=in_specs, out_specs=out_specs, check_vma=False)
```

```python
import math

import jax
import jax.numpy as jnp
from jax import lax
from jax.experimental import pallas as pl
from jax.experimental.pallas import tpu as pltpu
from jax.sharding import PartitionSpec as P

H = 8
HD = 64
LANE = 128
F32 = jnp.float32
BF = jnp.bfloat16
EPS = 1e-05
FILL = -1e30
VMEM_LIMIT = 60 * 2**20


def dot(a, b):
    return lax.dot_general(a, b, (((1,), (0,)), ((), ())), preferred_element_type=F32)


def dot_nt(a, b):
    return lax.dot_general(a, b, (((1,), (1,)), ((), ())), preferred_element_type=F32)


def dot_tn(a, b):
    return lax.dot_general(a, b, (((0,), (0,)), ((), ())), preferred_element_type=F32)


def norm_parts(v):
    mean = jnp.mean(v, axis=-1, keepdims=True)
    cen = v - mean
    r = lax.rsqrt(jnp.mean(cen * cen, axis=-1, keepdims=True) + EPS)
    return cen * r, r


def norm(v, gain):
    u, _ = norm_parts(v)
    return u * gain


def norm_back(v, gain, e):
    u, r = norm_parts(v)
    eg = e * gain
    back = r * (eg - jnp.mean(eg, axis=-1, keepdims=True) - u * jnp.mean(eg * u, axis=-1, keepdims=True))
    return back, jnp.sum(e * u, axis=0, keepdims=True)


def sigmoid(v):
    return 1.0 / (1.0 + jnp.exp(-v))


def swish_and_slope(v):
    s = sigmoid(v)
    sv = s * v
    return sv, s + sv * (1.0 - s)


def cols(p, width=LANE):
    return pl.ds(pl.multiple_of(p * width, width), width)


def lane_half(e):
    lane = lax.broadcasted_iota(jnp.int32, (1, LANE), 1)
    return (lane < HD) if e == 0 else (lane >= HD)


def call(body, outs, ins, scratch=(), name=None):
    return pl.pallas_call(
        body,
        out_shape=[jax.ShapeDtypeStruct(s, d) for s, d in outs],
        in_specs=[
            pl.BlockSpec(memory_space=pltpu.SMEM) if x.dtype == jnp.int32 else pl.BlockSpec(memory_space=pltpu.VMEM)
            for x in ins
        ],
        out_specs=[pl.BlockSpec(memory_space=pltpu.VMEM) for _ in outs],
        scratch_shapes=list(scratch),
        compiler_params=pltpu.CompilerParams(vmem_limit_bytes=VMEM_LIMIT),
        name=name,
    )(*ins)


MESH = pl.DeviceIdType.MESH


class Place:
    def __init__(self):
        tms, slots = lax.axis_size("tm"), lax.axis_size("slot")
        wide = 1 << ((slots.bit_length() - 1) // 2)
        self.size = {"c": 2, "x": tms // 2, "y": wide, "z": slots // wide}
        self.tm, self.slot = lax.axis_index("tm"), lax.axis_index("slot")
        self.at = {
            "c": lax.rem(self.tm, 2),
            "x": lax.div(self.tm, 2),
            "y": lax.rem(self.slot, wide),
            "z": lax.div(self.slot, wide),
        }

    def peer(self, axis, off):
        pos = dict(self.at)
        pos[axis] = lax.rem(pos[axis] + off, self.size[axis])
        return (pos["x"] * 2 + pos["c"], pos["z"] * self.size["y"] + pos["y"]), pos[axis]

    def peers(self, axis):
        return [(off,) + self.peer(axis, off) for off in range(1, self.size[axis])]

    def greet(self, axes):
        bar = pltpu.get_barrier_semaphore()
        count = 0
        for axis in axes:
            for _, dev, _ in self.peers(axis):
                pl.semaphore_signal(bar, inc=1, device_id=dev, device_id_type=MESH)
                count += 1
        pl.semaphore_wait(bar, count)


def rows_at(start, size):
    return pl.ds(pl.multiple_of(start, 16), size)


def add_into(dst, start, lanes, terms, size):
    step = 64 if size % 64 == 0 else 16

    def one(i, carry):
        off = pl.multiple_of(i * step, step)
        total = terms[0](off, step).astype(F32)
        for term in terms[1:]:
            total = total + term(off, step).astype(F32)
        dst[pl.ds(pl.multiple_of(start + off, 16), step), lanes] = total.astype(dst.dtype)
        return carry

    lax.fori_loop(0, size // step, one, 0)


GROUP = 2048


class Flow:
    STAGES = 9

    @staticmethod
    def lane_parts(order, size):
        rows = GROUP // 2
        for axis in order[:2]:
            rows //= size[axis]
        return max(1, 16 * size[order[2]] // rows)

    @staticmethod
    def scratch(order, width, size, kind):
        shapes, sends = [], 2
        blk = GROUP // 2
        parts = Flow.lane_parts(order, size)
        for lv, axis in enumerate(order):
            n = size[axis]
            blk = blk * parts // n if lv == 2 else blk // n
            w = width // parts if lv == 2 else width
            if (kind != "front" or lv == 0) and (kind != "back" or lv > 0):
                shapes.append(pltpu.VMEM((n - 1, blk, w), BF))
            sends += 2 * (n - 1)
        if kind != "front":
            shapes.append(pltpu.VMEM((blk, width // parts), BF))
        sems = pltpu.SemaphoreType.DMA((sends,))
        return shapes + [sems, sems, pltpu.SemaphoreType.DMA((1,))]

    def __init__(self, pc, order, lane, width, kind, src, own, core, out, first, bufs):
        self.ssem, self.rsem, self.lsem = bufs[-3:]
        bufs = list(bufs[:-3])
        self.used, self.now = 0, 2 if kind == "back" else 0
        self.made, self.local = [], []
        size = pc.size
        lanes = pl.ds(lane, width)
        c = pc.at["c"]
        top = GROUP // 2
        parts = self.lane_parts(order, size)
        blk, rel = [top], [0]
        for lv, axis in enumerate(order):
            if lv < 2:
                blk.append(blk[-1] // size[axis])
                rel.append(rel[-1] + pc.at[axis] * blk[-1])
        low = blk[2] * parts // size[order[2]]

        def share(pos):
            if parts == 1:
                return rel[2] + pos * low, lanes
            at = pl.multiple_of(lane + lax.rem(pos, parts) * (width // parts), LANE)
            return rel[2] + lax.div(pos, parts) * low, pl.ds(at, width // parts)

        ((_, cdev, _),) = pc.peers("c")
        into = [None] * 3
        if kind != "back":
            into[0] = bufs.pop(0)
        if kind != "front":
            into[1], into[2], fin = bufs
        core_copy = [self.copy(lambda: src.at[rows_at((1 - c) * top, top), lanes], lambda: core.at[:, lanes], cdev)]
        down = []
        for lv, axis in enumerate(order):
            cps = []
            for off, dev, pos in pc.peers(axis):
                if lv < 2:
                    s = lambda lv=lv, pos=pos: core.at[rows_at(rel[lv] + pos * blk[lv + 1], blk[lv + 1]), lanes]
                else:
                    s = lambda pos=pos: core.at[rows_at(share(pos)[0], low), share(pos)[1]]
                cps.append(self.copy(s, lambda lv=lv, off=off: into[lv].at[off - 1], dev))
            down.append(cps)
        mine = share(pc.at[order[2]])
        out_share = lambda: out.at[rows_at(first + c * top + mine[0], low), mine[1]]
        out_at = lambda lv: out.at[rows_at(first + c * top + rel[lv], blk[lv]), lanes]
        up = [[self.copy(lambda: fin, out_share, dev) for _, dev, _ in pc.peers(order[2])]]
        for lv in (2, 1):
            up.append([self.copy(lambda lv=lv: out_at(lv), lambda lv=lv: out_at(lv), dev) for _, dev, _ in pc.peers(order[lv - 1])])
        up.append([self.copy(lambda: out_at(0), lambda: out_at(0), cdev)])

        def fold(lv):
            if lv == 0:
                add_into(core, 0, lanes, [lambda o, n: own(o, n, lanes), lambda o, n: core[pl.ds(o, n), lanes]], top)
                return
            row, ln, size_ = (mine + (low,)) if lv == 3 else (rel[lv], lanes, blk[lv])
            terms = [lambda o, n: core[pl.ds(pl.multiple_of(row + o, 16), n), ln]]
            for k in range(size[order[lv - 1]] - 1):
                terms.append(lambda o, n, k=k: into[lv - 1][k, pl.ds(o, n), :])
            if lv == 3:
                add_into(fin, 0, slice(None), terms, size_)
            else:
                add_into(core, row, lanes, terms, size_)

        keep = lambda: pltpu.make_async_copy(fin, out_share(), self.lsem.at[0])

        def s1():
            self.arrived(core_copy)
            fold(0)
            self.start(down[0])

        def s2():
            if kind != "back":
                self.arrived(down[0])
                fold(1)
            if kind != "front":
                self.start(down[1])

        def s3():
            self.arrived(down[1])
            fold(2)
            self.start(down[2])

        def s4():
            self.arrived(down[2])
            fold(3)
            keep().start()
            self.start(up[0])

        def climb(i):
            def run():
                if i == 0:
                    keep().wait()
                self.arrived(up[i])
                if i < 3:
                    self.start(up[i + 1])

            return run

        self.stages = [lambda: self.start(core_copy), s1, s2, s3, s4] + [climb(i) for i in range(4)]
        self.last = 3 if kind == "front" else self.STAGES
        self.sent = {"front": core_copy + down[0], "back": down[1] + down[2] + sum(up, []), "whole": core_copy + sum(down + up, [])}[kind]

    def copy(self, src, dst, dev):
        k = self.used
        self.used += 1
        return src, dst, k, dev

    def make(self, cp):
        src, dst, k, dev = cp
        return pltpu.make_async_remote_copy(
            src_ref=src(), dst_ref=dst(), send_sem=self.ssem.at[k], recv_sem=self.rsem.at[k], device_id=dev, device_id_type=MESH
        )

    def start(self, cps):
        for cp in cps:
            self.make(cp).start()

    def arrived(self, cps):
        for cp in cps:
            self.make(cp).wait_recv()

    def finish(self):
        for cp in self.sent:
            self.make(cp).wait_send()

    def take(self):
        if self.now >= self.last:
            return lambda: None
        self.now += 1
        return self.stages[self.now - 1]


def advance(flows):
    for flow in flows:
        flow.take()()


EARLY = ((("y", "x", "z"), 0, 384), (("x", "y", "z"), 384, 128))
EVEN = ((("y", "x", "z"), 0, 256), (("x", "y", "z"), 256, 256))


ZFIRST = ((("z", "x", "y"), 0, 256), (("z", "y", "x"), 256, 256))
LASTA = ((("y", "x", "z"), 0, 256), (("x", "y", "z"), 256, 128), (("z", "x", "y"), 384, 128))
LASTB = ((("y", "x", "z"), 0, 128), (("x", "y", "z"), 128, 256), (("z", "y", "x"), 384, 128))
MID = {"f2i": 2048, "f2o": 4096, "o": 0}
FRONT = ("f2i",)
LAYOUT = {"f2i": EVEN, "f2o": EVEN, "o": EVEN, "q": LASTA, "f1i": LASTB, "f1o": EVEN}
TICKS = {0: "f2o o", 4: "f2i", 9: "f2o o", 10: "f2i", 16: "f2o o", 17: "f2i", 19: "f2o o f2i q"}
REST = ("f2i", "f2o", "o", "q", "f1o", "f1i")


def lanes_of(size, wanted):
    return wanted if max(Flow.lane_parts(order, size) for order, _, _ in wanted) == 1 else EVEN


def flow_scratch(size, layout, kind):
    return [Flow.scratch(order, width, size, kind) for order, _, width in lanes_of(size, layout)]


def flat_list(lists):
    return [x for part in lists for x in part]


class Taker:
    def __init__(self, refs):
        self.refs = list(refs)

    def __call__(self, n):
        got, self.refs = self.refs[:n], self.refs[n:]
        return got


def make_flows(pc, layout, kind, src, own, core, out, first, taker):
    flows = []
    for (order, lane, width), shapes in zip(lanes_of(pc.size, layout), flow_scratch(pc.size, layout, kind)):
        flows.append(Flow(pc, order, lane, width, kind, src, own, core, out, first, taker(len(shapes))))
    return flows


FLAT = {"f1i": 0, "f1o": 2048, "q": 4096, "k": 4608, "v": 5120, "p": 5632, "o": 6144, "ci": 6656, "co": 7680, "f2i": 8192, "f2o": 10240}
FLAT_ROWS = 12288
ORDER = tuple(FLAT)
FOLDS = {"f1i": 4, "ci": 2, "f2i": 4}
FLAT_SIZE = {n: (list(FLAT.values()) + [FLAT_ROWS])[i + 1] - FLAT[n] for i, n in enumerate(FLAT)}


def ticks(point, plan, p):
    for at, run in plan.items():
        if at % 2 == point:
            pl.when(p == at // 2)(lambda run=run: (run(), None)[1])


class Gather:
    @staticmethod
    def scratch(size, shard_rows, width):
        part, pieces = Gather.cut(shard_rows)
        links = 2 * pieces * sum(n - 1 for n in size.values())
        sems = pltpu.SemaphoreType.DMA((links,))
        return [
            pltpu.VMEM((size["x"], 2, size["z"], size["y"], shard_rows, width), BF),
            pltpu.VMEM((width // LANE, 64, LANE), F32),
            sems,
            sems,
        ]

    @staticmethod
    def cut(shard_rows):
        part = 64 if shard_rows % 64 == 0 else 16
        return part, shard_rows // part

    def __init__(self, pc, wf, bufs):
        self.pc, self.wf = pc, wf
        self.nb, self.scr, self.ssem, self.rsem = bufs
        self.shard_rows = self.nb.shape[4]
        self.part, self.pieces = self.cut(self.shard_rows)
        self.xs = pc.size["x"]
        self.used = 0
        self.stages = [self.plan(hx, q) for hx in range(2) for q in range(self.pieces)]

    def copies(self, ref, axis):
        out = []
        for off, dev, _ in self.pc.peers(axis):
            k = self.used
            self.used += 1
            out.append(
                (off, pltpu.make_async_remote_copy(
                    src_ref=ref, dst_ref=ref, send_sem=self.ssem.at[k], recv_sem=self.rsem.at[k], device_id=dev, device_id_type=MESH
                ))
            )
        return out

    def plan(self, hx, q):
        pc, nb = self.pc, self.nb
        x, c, z, y = (pc.at[a] for a in "xczy")
        rows = pl.ds(q * self.part, self.part)
        side = pl.ds(hx * (self.xs // 2), self.xs // 2)
        in_half = lambda pos: lax.div(pos, self.xs // 2) == hx
        along = {
            "x": self.copies(nb.at[x, c, z, y, rows], "x"),
            "z": self.copies(nb.at[side, c, z, y, rows], "z"),
            "y": self.copies(nb.at[side, c, :, y, rows], "y"),
            "c": self.copies(nb.at[side, c, :, :, rows], "c"),
        }

        def each(axis, what, cond=None):
            for off, cp in along[axis]:
                if cond is None:
                    getattr(cp, what)()
                else:
                    pl.when(cond(off))(lambda cp=cp: getattr(cp, what)())

        sends = lambda off: in_half(x)
        gets = lambda off: in_half(lax.rem(x - off + self.xs, self.xs))

        def end():
            each("c", "wait_recv")
            if self.part == 64:
                self.mix_half(hx, q)
            elif q == self.pieces - 1:
                self.mix_half(hx, None)

        def done():
            each("x", "wait_send", sends)
            for axis in "zyc":
                each(axis, "wait_send")

        return {
            "X": lambda: each("x", "start", sends),
            "Z": lambda: (each("x", "wait_recv", gets), each("z", "start")),
            "Y": lambda: (each("z", "wait_recv"), each("y", "start")),
            "C": lambda: (each("y", "wait_recv"), each("c", "start")),
            "E": end,
            "D": done,
        }

    def run(self, ops):
        for op in ops:
            if 0 <= op[1] < len(self.stages):
                self.stages[op[1]][op[0]]()

    def finish(self):
        for stages in self.stages:
            stages["D"]()

    def noise_at(self, row):
        pc = self.pc
        got = []
        sub = min(64, self.part)
        for i in range(64 // sub):
            at = row + i * sub
            d = lax.div(at, self.shard_rows)
            slots = pc.size["z"] * pc.size["y"]
            tm, sl = lax.div(d, slots), lax.rem(d, slots)
            off = pl.multiple_of(lax.rem(at, self.shard_rows), 16)
            got.append(
                self.nb[lax.div(tm, 2), lax.rem(tm, 2), lax.div(sl, pc.size["y"]), lax.rem(sl, pc.size["y"]), pl.ds(off, sub), :].astype(F32)
            )
        return got[0] if len(got) == 1 else jnp.concatenate(got, axis=0)

    def mix(self, row, base, size, fold):
        wf, scr = self.wf, self.scr
        value = self.noise_at(row)
        if fold == 1:
            at = rows_at(row, 64)
            wf[at, :] = (wf[at, :].astype(F32) + value).astype(BF)
            return
        for b in range(512 // LANE):
            scr[b] = value[:, b * LANE : (b + 1) * LANE]
        high = 64 // fold
        for j in range(fold):
            at = rows_at(base + j * (size // fold) + lax.div(row - base, fold), high)
            for b in range(512 // LANE):
                lanes = pl.ds(b * LANE, LANE)
                wf[at, lanes] = (wf[at, lanes].astype(F32) + scr[b, pl.ds(j, high, stride=fold), :]).astype(BF)

    def mix_half(self, hx, q):
        for name in ORDER:
            base, size, fold = FLAT[name], FLAT_SIZE[name], FOLDS.get(name, 1)
            if (base < FLAT_ROWS // 2) != (hx == 0):
                continue
            begin, end = base // 64, (base + size) // 64
            start, stride = (begin, 1) if q is None else (begin + (q - begin) % self.pieces, self.pieces)
            lax.fori_loop(
                0, (end - start + stride - 1) // stride,
                lambda i, t: (self.mix((start + i * stride) * 64, base, size, fold), t)[1], 0,
            )


class KeysAll:
    @staticmethod
    def scratch(xs):
        n = 2 * xs - 1
        sems = pltpu.SemaphoreType.DMA((H // 2, n))
        return [sems, sems]

    def __init__(self, pc, kv, bufs):
        self.pc, self.kv = pc, kv
        self.ssem, self.rsem = bufs

    def copy(self, p, k, tm, dev):
        ref = self.kv.at[p, :, tm]
        return pltpu.make_async_remote_copy(
            src_ref=ref, dst_ref=ref, send_sem=self.ssem.at[p, k], recv_sem=self.rsem.at[p, k], device_id=dev, device_id_type=MESH
        )

    def core(self, p):
        ((_, dev, _),) = self.pc.peers("c")
        return [self.copy(p, 0, self.pc.tm, dev)]

    def line(self, p):
        return [self.copy(p, off, self.pc.tm, dev) for off, dev, _ in self.pc.peers("x")]

    def relay(self, p):
        ((_, dev, _),) = self.pc.peers("c")
        xs = self.pc.size["x"]
        out = []
        for off in range(1, xs):
            source = lax.rem(self.pc.at["x"] - off + xs, xs) * 2 + self.pc.at["c"]
            out.append(self.copy(p, xs - 1 + off, source, dev))
        return out

    def send(self, p):
        for cp in self.core(p):
            cp.start()

    def send_line(self, p):
        for cp in self.line(p):
            cp.start()

    def forward(self, p):
        for come, on in zip(self.line(p), self.relay(p)):
            come.wait_recv()
            on.start()

    def ready(self, p):
        for cp in self.core(p) + self.relay(p):
            cp.wait_recv()

    def sent(self, p):
        for cp in self.line(p) + self.core(p) + self.relay(p):
            cp.wait_send()


def angle_tables(hi, lo, rates):
    for ref, step in ((hi, 64.0), (lo, 1.0)):
        count = ref.shape[1]
        angle = lax.broadcasted_iota(jnp.int32, (count, rates.shape[1]), 0).astype(F32) * step * rates
        ref[0] = jnp.sin(angle)
        ref[1] = jnp.cos(angle)


def angle_block(hi, lo, m):
    hs, hc = hi[0, pl.ds(m, 1), :], hi[1, pl.ds(m, 1), :]
    ls, lc = lo[0], lo[1]
    return hs * lc + hc * ls, hc * lc - hs * ls


def early_body(*refs):
    lens, noise, raws = refs[0], refs[1], refs[2:13]
    x_ref, gain1, gain2, pos_u, pos_v = refs[13:18]
    wn, x1_out, pre_out, a2_out, qu_out, qv_out, kv_out, trig_out, sin_out, cos_out, att_out, probs = refs[18:30]
    wf, flat, x1_ref, pre_ref, a2_ref, qu, qv, kv, trig, sin, cos, hi, lo, att, pbuf, wsem, osem, psem = refs[30:48]
    bufs = refs[48:]
    pc = Place()
    rows, width = x_ref.shape
    half = width // 2
    tms = lax.axis_size("tm")
    frames = rows * tms
    loads = []
    for name, raw in zip(ORDER, raws):
        for j in range(FOLDS.get(name, 1)):
            size = FLAT_SIZE[name] // FOLDS.get(name, 1)
            dst = wf.at[pl.ds(FLAT[name] + j * size, size), :]
            loads.append(pltpu.make_async_copy(raw.at[:, pl.ds(j * 512, 512)], dst, wsem.at[len(loads)]))
            loads[-1].start()
    gather = Gather(pc, wf, bufs[:4])
    keys = KeysAll(pc, kv, bufs[4:6])

    def unfold(i, carry):
        for r in range(8):
            for b in range(width // LANE):
                at = pl.ds(pl.multiple_of((i * 8 + r) * width + b * LANE, LANE), LANE)
                flat[b, pl.ds(i * 8 + r, 1), :] = noise[:, at].astype(F32)
        return carry

    shard_rows = gather.shard_rows
    lax.fori_loop(0, shard_rows // 8, unfold, 0)
    for b in range(width // LANE):
        gather.nb[pc.at["x"], pc.at["c"], pc.at["z"], pc.at["y"], :, pl.ds(b * LANE, LANE)] = flat[b].astype(BF)
    pc.greet("cxyz")
    n = gather.pieces
    gather.run([("X", i) for i in range(2 * n)])
    gather.run([("Z", 0), ("Z", 1)])
    rates = jnp.exp(lax.broadcasted_iota(jnp.int32, (1, half), 1).astype(F32) * (-2.0 * math.log(10000.0) / width))
    angle_tables(hi, lo, rates)

    def angles(m, carry):
        s, c = angle_block(hi, lo, m)
        at = rows_at(m * 64, 64)
        trig[at, pl.ds(0, half)] = s.astype(BF)
        trig[at, pl.ds(half, half)] = c.astype(BF)
        return carry

    def own_angles(m, carry):
        s, c = angle_block(hi, lo, pc.tm * (rows // 64) + m)
        sin[rows_at(m * 64, 64), :] = s
        cos[rows_at(m * 64, 64), :] = c
        return carry

    lax.fori_loop(0, frames // 64, angles, 0)
    lax.fori_loop(0, rows // 64, own_angles, 0)
    for cp in loads:
        cp.wait()
    outs = []

    def put(src, dst):
        cp = pltpu.make_async_copy(src, dst, osem.at[len(outs)])
        cp.start()
        outs.append(cp)

    x = x_ref[...].astype(F32)
    a1 = norm(x, gain1[...]).astype(BF)
    for t in range(2, n + 1):
        gather.run([("Z", t), ("Y", t - 2), ("C", t - 3), ("E", t - 4)])
    gather.run([("Y", n - 1), ("C", n - 2), ("E", n - 3), ("C", n - 1), ("E", n - 2), ("Z", n + 1), ("E", n - 1)])
    part = lambda name: wf.at[pl.ds(FLAT[name], FLAT_SIZE[name]), :]
    x1 = x + 0.5 * ffn_forward(a1, part("f1i"), part("f1o"), pre_ref)
    x1_ref[...] = x1
    a2 = norm(x1, gain2[...]).astype(BF)
    a2_ref[...] = a2
    k = dot(a2, part("k")[...]).astype(BF)
    v = dot(a2, part("v")[...]).astype(BF)
    for p in range(H // 2):
        kv[p, 0, pc.tm] = k[:, p * LANE : (p + 1) * LANE]
        kv[p, 1, pc.tm] = v[:, p * LANE : (p + 1) * LANE]
        if p == 0:
            keys.send_line(0)
        keys.send(p)
    gather.run([("Z", n + 2), ("Y", n)])
    q = dot(a2, part("q")[...])
    scale = HD**-0.5
    qu[...] = ((q + pos_u[...]).astype(BF).astype(F32) * scale).astype(BF)
    qv[...] = ((q + pos_v[...]).astype(BF).astype(F32) * scale).astype(BF)
    for src, dst in ((x1_ref, x1_out), (pre_ref, pre_out), (a2_ref, a2_out), (qu, qu_out), (qv, qv_out), (trig, trig_out), (sin, sin_out), (cos, cos_out)):
        put(src, dst)
    put(wf.at[pl.ds(0, FLAT_ROWS // 2), :], wn.at[pl.ds(0, FLAT_ROWS // 2), :])
    steps = {
        0: "Y1 Z3", 1: "Y2 Z4 C0", 2: "C1 E0", 3: "Y3 Z5 E1", 4: "Y4 C2", 5: "C3 E2", 6: "Y5 E3", 7: "C4", 8: "C5 E4 E5",
    }
    if n != 6:
        steps = {8: " ".join("%s%d" % (op, i) for op, low in (("Z", 3), ("Y", 1), ("C", 0), ("E", 0)) for i in range(low, n))}
    steps = {at: [(op[0], n + int(op[1:])) for op in text.split()] for at, text in steps.items()}
    plan = {at: (lambda ops=ops: gather.run(ops)) for at, ops in steps.items() if at < H}
    ok = lax.broadcasted_iota(jnp.int32, (1, frames), 1) < lens[0]
    w_pos = part("p")
    store = lambda p, e: pltpu.make_async_copy(pbuf.at[e], probs.at[2 * p + e], psem.at[e])

    def pair(p, carry):
        at = cols(p)
        mixed = None
        for e in range(2):
            mine = lane_half(e)
            qve = jnp.where(mine, qv[:, at], jnp.zeros((), BF))
            que = jnp.where(mine, qu[:, at], jnp.zeros((), BF))
            a_s = dot_nt(qve, w_pos[pl.ds(0, half), at])
            a_c = dot_nt(qve, w_pos[pl.ds(half, half), at])
            b_c = (a_s * sin[...] + a_c * cos[...]).astype(BF)
            b_s = (a_c * sin[...] - a_s * cos[...]).astype(BF)
            if e == 0:
                pl.when(p == 1)(lambda: keys.send_line(3))
            else:
                pl.when(p == 0)(lambda: keys.send_line(2))
            s = dot_nt(b_s, trig[:, pl.ds(0, half)]) + dot_nt(b_c, trig[:, pl.ds(half, half)])
            if e == 0:
                pl.when(p == 0)(lambda: (keys.forward(0), keys.send_line(1))[1])
                keys.ready(p)
            s = s + dot_nt(que, kv[p, 0].reshape(frames, LANE))
            s = jnp.where(ok, s, FILL)
            m = jnp.max(s, axis=-1, keepdims=True)
            ex = jnp.exp(s - m)
            tot = jnp.sum(ex, axis=-1, keepdims=True)
            low = (ex * (1.0 / tot)).astype(BF)
            pl.when(p > 0)(lambda: store(p - 1, e).wait())
            pbuf[e] = low
            store(p, e).start()
            got = dot(low, kv[p, 1].reshape(frames, LANE))
            mixed = got if e == 0 else jnp.where(mine, got, mixed)
            if e == 1:
                pl.when(p < H // 2 - 1)(lambda: keys.forward(p + 1))
            ticks(e, plan, p)
        att[:, at] = mixed.astype(BF)
        return carry

    lax.fori_loop(0, H // 2, pair, 0)
    put(kv, kv_out)
    put(att, att_out)
    gather.run(steps[8])
    put(wf.at[pl.ds(FLAT_ROWS // 2, FLAT_ROWS // 2), :], wn.at[pl.ds(FLAT_ROWS // 2, FLAT_ROWS // 2), :])
    for e in range(2):
        store(H // 2 - 1, e).wait()
    for p in range(H // 2):
        keys.sent(p)
    gather.finish()
    for cp in outs:
        cp.wait()


def chunk(c):
    return pl.ds(pl.multiple_of(c * 512, 512), 512)


def ffn_forward(normed, w_in, w_out, pre_ref):
    def one(c, acc):
        pre = dot(normed, w_in[chunk(c), :])
        pre_ref[:, chunk(c)] = pre
        return acc + dot((pre * sigmoid(pre)).astype(BF), w_out[chunk(c), :])

    return lax.fori_loop(0, w_in.shape[0] // 512, one, jnp.zeros((normed.shape[0], w_out.shape[1]), F32))


def ffn_through(g_low, w_in, w_out, pre_ref, hid_ref, dpre_ref):
    def one(c, acc):
        sw, slope = swish_and_slope(pre_ref[:, chunk(c)])
        hid_ref[:, chunk(c)] = sw.astype(BF)
        dpre = (dot_nt(g_low, w_out[chunk(c), :]) * slope).astype(BF)
        dpre_ref[:, chunk(c)] = dpre
        return acc + dot_nt(dpre, w_in[chunk(c), :])

    return lax.fori_loop(0, w_in.shape[0] // 512, one, jnp.zeros(g_low.shape, F32))


def ffn_in_grad(normed, dpre_ref, gin_ref):
    normed_t = normed.T

    def one(c, carry):
        gin_ref[chunk(c), :] = dot(normed_t, dpre_ref[:, chunk(c)]).astype(gin_ref.dtype)
        return carry

    lax.fori_loop(0, gin_ref.shape[0] // 512, one, 0)


def ffn_out_grad(g_low, hid_ref, gout_ref):
    def one(c, carry):
        gout_ref[chunk(c), :] = dot_tn(hid_ref[:, chunk(c)], g_low).astype(gout_ref.dtype)
        return carry

    lax.fori_loop(0, gout_ref.shape[0] // 512, one, 0)


def ffn_hidden(pre_ref, hid_ref):
    def one(c, carry):
        pre = pre_ref[:, chunk(c)]
        hid_ref[:, chunk(c)] = (pre * sigmoid(pre)).astype(BF)
        return carry

    lax.fori_loop(0, pre_ref.shape[1] // 512, one, 0)


class Fetch:
    def __init__(self, sems):
        self.sems, self.n = sems, 0

    def __call__(self, src, dst):
        cp = pltpu.make_async_copy(src, dst, self.sems.at[self.n])
        self.n += 1
        cp.start()
        return cp


def part_of(wn, name):
    return wn.at[pl.ds(FLAT[name], FLAT_SIZE[name]), :]


def valid_rows(lens, rows):
    first = lax.axis_index("tm") * rows
    return ((first + lax.broadcasted_iota(jnp.int32, (rows, 1), 0)) < lens[0]).astype(F32)


def spread(ext, start, value):
    value = value.astype(F32)
    for b in range(ext.shape[0]):
        ext[b, pl.ds(start, value.shape[0]), :] = value[:, b * LANE : (b + 1) * LANE]


def tap_sum(ext, taps, out_ref, offset):
    count = taps.shape[0]
    rows = out_ref.shape[0]
    block = 64 if rows % 64 == 0 else 16

    def one(i, carry):
        for b in range(ext.shape[0]):
            at = pl.ds(b * LANE, LANE)
            acc = jnp.zeros((block, LANE), F32)
            for k in range(count):
                acc = acc + taps[pl.ds(k, 1), at] * ext[b, pl.ds(i * block + offset(k), block), :]
            out_ref[pl.ds(pl.multiple_of(i * block, block), block), at] = acc
        return carry

    lax.fori_loop(0, rows // block, one, 0)


def bn_stats(sums):
    total = sums[2:3, :]
    mu = sums[0:1, :] / total
    var = sums[1:2, :] / total - mu * mu
    return mu, lax.rsqrt(var + EPS), total


class Totals:
    @staticmethod
    def scratch(tms, slots, width):
        n = tms + slots - 2
        return [
            pltpu.VMEM((tms, 8, width), F32),
            pltpu.VMEM((slots, 8, width), F32),
            pltpu.SemaphoreType.DMA((n,)),
            pltpu.SemaphoreType.DMA((n,)),
        ]

    def __init__(self, pc, bufs):
        self.pc, self.bufs = pc, bufs

    def begin(self, value):
        self.sent = []
        self.cps = self.send(0, value)

    def turn(self):
        self.cps = self.send(1, self.end(0))

    def done(self):
        value = self.end(1)
        for cp in self.sent:
            cp.wait_send()
        return value

    def send(self, i, value):
        pc, buf = self.pc, self.bufs[i]
        ssem, rsem = self.bufs[2:]
        me = (pc.tm, pc.slot)[i]
        buf[me] = value
        n = buf.shape[0]
        for off in range(1, n):
            to = lax.rem(me + off, n)
            k = off - 1 + i * (self.bufs[0].shape[0] - 1)
            cp = pltpu.make_async_remote_copy(
                src_ref=buf.at[me], dst_ref=buf.at[me], send_sem=ssem.at[k], recv_sem=rsem.at[k],
                device_id=(to, pc.slot) if i == 0 else (pc.tm, to), device_id_type=MESH,
            )
            cp.start()
            self.sent.append(cp)
        return self.sent[-(n - 1) :]

    def end(self, i):
        for cp in self.cps:
            cp.wait_recv()
        buf = self.bufs[i]
        value = buf[0]
        for j in range(1, buf.shape[0]):
            value = value + buf[j]
        return value


def greet_rows(pc, tms, slots):
    bar = pltpu.get_barrier_semaphore()
    for off in range(1, tms):
        pl.semaphore_signal(bar, inc=1, device_id=(lax.rem(pc.tm + off, tms), pc.slot), device_id_type=MESH)
    for off in range(1, slots):
        pl.semaphore_signal(bar, inc=1, device_id=(pc.tm, lax.rem(pc.slot + off, slots)), device_id_type=MESH)
    pl.semaphore_wait(bar, tms + slots - 2)


def middle_body(
    lens, att, x1_ref, cot, wn, taps, bn_gain, bn_bias, gain3, gain4, gain5,
    out_h, dx2_h, datt_h, g_h, smalls_ref, bns_ref, cores,
    w_o, w_ci, w_co, w_f2i, w_f2o, fsem, early, late, hsem, gm_ref, ddwo_ref, z_ref, ext, ext2, dwo_ref, pre_ref, dgm_ref, acc, x2_ref, core, out_ref, dx2_ref, datt_ref, g_ref, hid_ref, dpre_ref, csem, *bufs,
):
    pc = Place()
    tms, slots = lax.axis_size("tm"), lax.axis_size("slot")
    rows, width = x1_ref.shape
    count = taps.shape[0]
    fetch, put = Fetch(fsem), Fetch(csem)
    outs = []
    got = {n: fetch(part_of(wn, n), d) for n, d in (("o", w_o), ("ci", w_ci), ("co", w_co), ("f2i", w_f2i), ("f2o", w_f2o))}
    greet_rows(pc, tms, slots)
    taker = Taker(bufs)
    totals = Totals(pc, taker(4)), Totals(pc, taker(4))
    flows = []
    for i, name in enumerate(FRONT):
        src = g_ref.at[pl.ds(MID[name], GROUP), :]
        half_rows = lambda o, n, lanes, src=src: src[pl.ds(pl.multiple_of(pc.at["c"] * (GROUP // 2) + o, 16), n), lanes]
        flows += make_flows(pc, LAYOUT[name], "front", src, half_rows, core.at[i], None, 0, taker)

    def halo(src, dst, k, step):
        dev = (lax.rem(pc.tm + step + tms, tms), pc.slot)
        return pltpu.make_async_remote_copy(
            src_ref=src, dst_ref=dst, send_sem=hsem.at[2 * k], recv_sem=hsem.at[2 * k + 1], device_id=dev, device_id_type=MESH
        )

    got["o"].wait()
    x2 = x1_ref[...] + dot(att[...], w_o[...])
    x2_ref[...] = x2
    a3 = norm(x2, gain3[...]).astype(BF)
    got["ci"].wait()
    z1 = dot(a3, w_ci[pl.ds(0, width), :])
    z2 = dot(a3, w_ci[pl.ds(width, width), :])
    z_ref[:, pl.ds(0, width)] = z1
    z_ref[:, pl.ds(width, width)] = z2
    ok = valid_rows(lens, rows)
    gm_ref[...] = (z1 * sigmoid(z2) * ok).astype(BF)
    cp = halo(gm_ref.at[pl.ds(rows - count, count), :], early, 0, 1)
    cp.start()
    spread(ext, count, gm_ref[...])
    cp.wait()
    spread(ext, 0, jnp.where(pc.tm > 0, early[...], jnp.zeros((), BF)))
    tap_sum(ext, taps, dwo_ref, lambda k: k + 1)
    dwo = dwo_ref[...]
    dwv = dwo * ok
    totals[0].begin(
        jnp.concatenate(
            [
                jnp.sum(dwv, axis=0, keepdims=True),
                jnp.sum(dwv * dwv, axis=0, keepdims=True),
                jnp.zeros((1, width), F32) + jnp.sum(ok, axis=0, keepdims=True),
                jnp.zeros((5, width), F32),
            ],
            axis=0,
        )
    )
    totals[0].turn()
    sums = totals[0].done()
    mu, inv, total = bn_stats(sums)
    xhat = (dwo_ref[...] - mu) * inv
    sw, slope = swish_and_slope(xhat * bn_gain[...] + bn_bias[...])
    sw = sw.astype(BF)
    got["co"].wait()
    x3 = x2_ref[...] + dot(sw, w_co[...])
    a4 = norm(x3, gain4[...]).astype(BF)
    got["f2i"].wait()
    got["f2o"].wait()
    x4 = x3 + 0.5 * ffn_forward(a4, w_f2i, w_f2o, pre_ref)
    out_ref[...] = norm(x4, gain5[...]).astype(BF)
    outs.append(put(out_ref, out_h))
    dx4, gg5 = norm_back(x4, gain5[...], cot[...].astype(F32))
    g4 = (0.5 * dx4).astype(BF)
    lo = FLAT["o"]
    da4 = ffn_through(g4, w_f2i, w_f2o, pre_ref, hid_ref, dpre_ref)
    back, gg4 = norm_back(x3, gain4[...], da4)
    dx3 = dx4 + back
    g3 = dx3.astype(BF)
    dbn = dot_nt(g3, w_co[...]) * slope
    totals[1].begin(
        jnp.concatenate(
            [jnp.sum(dbn * xhat, axis=0, keepdims=True), jnp.sum(dbn, axis=0, keepdims=True), jnp.zeros((6, width), F32)], axis=0
        )
    )
    part = lambda name: g_ref.at[pl.ds(MID[name], GROUP), :]
    ffn_in_grad(a4, dpre_ref, part("f2i"))
    totals[1].turn()
    advance(flows)
    ffn_out_grad(g4, hid_ref, part("f2o"))
    g_ref[pl.ds(FLAT["co"] - lo, width), :] = dot_tn(sw, g3).astype(BF)
    for name in ("f2i", "f2o"):
        if name not in FRONT:
            outs.append(put(part(name), g_h.at[pl.ds(MID[name], GROUP), :]))
    sums2 = totals[1].done()
    bns_ref[...] = sums2
    ddwo_ref[...] = (bn_gain[...] * inv * (dbn - ok * (sums2[1:2, :] + xhat * sums2[0:1, :]) / total)).astype(BF)
    cp = halo(ddwo_ref.at[pl.ds(0, count), :], late, 1, -1)
    cp.start()
    advance(flows)
    spread(ext2, 0, ddwo_ref[...])
    cp.wait()
    spread(ext2, rows, jnp.where(pc.tm < tms - 1, late[...], jnp.zeros((), BF)))
    tap_sum(ext2, taps, dgm_ref, lambda k: count - 1 - k)
    block = 64 if rows % 64 == 0 else 16
    for b in range(ext.shape[0]):
        acc[...] = jnp.zeros(acc.shape, F32)

        def one(i, carry, b=b):
            mine = ext2[b, pl.ds(pl.multiple_of(i * block, block), block), :]
            for k in range(count):
                prod = mine * ext[b, pl.ds(i * block + k + 1, block), :]
                acc[k] = acc[k] + jnp.sum(prod.reshape(block // 8, 8, LANE), axis=0)
            return carry

        lax.fori_loop(0, rows // block, one, 0)
        smalls_ref[pl.ds(0, count), pl.ds(b * LANE, LANE)] = jnp.sum(acc[...], axis=1)
    z1 = z_ref[:, pl.ds(0, width)]
    sg = sigmoid(z_ref[:, pl.ds(width, width)])
    dg = dgm_ref[...] * ok
    dz1 = (dg * sg).astype(BF)
    dz2 = (dg * z1 * sg * (1.0 - sg)).astype(BF)
    a3t = norm(x2_ref[...], gain3[...]).astype(BF).T
    g_ref[pl.ds(FLAT["ci"] - lo, width), :] = dot(a3t, dz1).astype(BF)
    g_ref[pl.ds(FLAT["ci"] - lo + width, width), :] = dot(a3t, dz2).astype(BF)
    da3 = dot_nt(dz1, w_ci[pl.ds(0, width), :]) + dot_nt(dz2, w_ci[pl.ds(width, width), :])
    back, gg3 = norm_back(x2_ref[...], gain3[...], da3)
    dx2 = dx3 + back
    dx2_ref[...] = dx2
    outs.append(put(dx2_ref, dx2_h))
    g2 = dx2.astype(BF)
    g_ref[pl.ds(0, width), :] = dot_tn(att[...], g2).astype(BF)
    outs.append(put(g_ref.at[pl.ds(0, GROUP), :], g_h.at[pl.ds(0, GROUP), :]))
    datt_ref[...] = dot_nt(g2, w_o[...]).astype(BF)
    outs.append(put(datt_ref, datt_h))
    advance(flows)
    outs.append(put(core, cores))
    smalls_ref[pl.ds(count, 8), :] = jnp.concatenate([gg3, gg4, gg5, jnp.zeros((5, width), F32)], axis=0)
    for flow in flows:
        flow.finish()
    for cp in outs:
        cp.wait()


class Butterfly:
    @staticmethod
    def scratch(devices, shape):
        n = devices.bit_length() - 1
        return [pltpu.VMEM((n,) + shape, F32), pltpu.SemaphoreType.DMA((n,)), pltpu.SemaphoreType.DMA((n,))]

    def __init__(self, pc, value, bufs):
        self.value, (self.got, self.ssem, self.rsem) = value, bufs
        self.devs = []
        for axis, me in (("tm", pc.tm), ("slot", pc.slot)):
            bit = 1
            while bit < lax.axis_size(axis):
                to = me + bit - 2 * bit * lax.rem(lax.div(me, bit), 2)
                self.devs.append((to, pc.slot) if axis == "tm" else (pc.tm, to))
                bit *= 2

    def copy(self, k):
        return pltpu.make_async_remote_copy(
            src_ref=self.value, dst_ref=self.got.at[k], send_sem=self.ssem.at[k], recv_sem=self.rsem.at[k],
            device_id=self.devs[k], device_id_type=MESH,
        )

    def stage(self, k):
        if k > 0:
            self.copy(k - 1).wait()
            self.value[...] = self.value[...] + self.got[k - 1]
        if k < len(self.devs):
            self.copy(k).start()


GROUP = 2048


class KeyGrads:
    @staticmethod
    def scratch(tms, rows):
        pairs, xs = H // 2, tms // 2
        sems = pltpu.SemaphoreType.DMA((pairs, xs + 1))
        return [
            pltpu.VMEM((pairs, 2, 2, tms, HD, rows), BF),
            pltpu.VMEM((pairs, 2, tms, HD, rows), BF),
            pltpu.VMEM((xs - 1, pairs, 2, 2, HD, rows), BF),
            pltpu.VMEM((pairs, 2, 2, HD, rows), BF),
            pltpu.VMEM((pairs, 2, HD, rows), BF),
            sems,
            sems,
        ]

    def __init__(self, pc, bufs):
        self.pc = pc
        self.mine, self.core, self.line, self.both, self.got, self.ssem, self.rsem = bufs

    def put(self, p, kind, e, value):
        rows = self.mine.shape[-1]
        for t in range(self.mine.shape[3]):
            self.mine[p, kind, e, t] = value[:, t * rows : (t + 1) * rows].astype(BF)

    def copy(self, p, k, src, dst, dev):
        return pltpu.make_async_remote_copy(
            src_ref=src, dst_ref=dst, send_sem=self.ssem.at[p, k], recv_sem=self.rsem.at[p, k], device_id=dev, device_id_type=MESH
        )

    def first(self, p):
        ((_, dev, _),) = self.pc.peers("c")
        return [self.copy(p, 0, self.mine.at[p, :, 1 - self.pc.at["c"]], self.core.at[p], dev)]

    def second(self, p):
        return [
            self.copy(p, off, self.core.at[p, :, pl.ds(2 * pos, 2)], self.line.at[off - 1, p], dev) for off, dev, pos in self.pc.peers("x")
        ]

    def third(self, p):
        ((_, dev, _),) = self.pc.peers("c")
        return [self.copy(p, self.pc.size["x"], self.both.at[p, :, 1 - self.pc.at["c"]], self.got.at[p], dev)]

    def step(self, p, i):
        c, x = self.pc.at["c"], self.pc.at["x"]
        if i == 1:
            for cp in self.first(p):
                cp.wait_recv()
            for kind in range(2):
                for t in range(self.core.shape[2]):
                    total = self.core[p, kind, t].astype(F32) + self.mine[p, kind, c, t].astype(F32)
                    self.core[p, kind, t] = total.astype(BF)
        if i == 2:
            for cp in self.second(p):
                cp.wait_recv()
            for kind in range(2):
                for t in range(2):
                    total = self.core[p, kind, 2 * x + t].astype(F32)
                    for j in range(self.line.shape[0]):
                        total = total + self.line[j, p, kind, t].astype(F32)
                    self.both[p, kind, t] = total.astype(BF)
        if i == 3:
            for cp in self.third(p):
                cp.wait_recv()
            return
        for cp in (self.first, self.second, self.third)[i](p):
            cp.start()

    def sent(self, p):
        for cp in self.first(p) + self.second(p) + self.third(p):
            cp.wait_send()

    def collect(self, p, kind, dst):
        c = self.pc.at["c"]
        own = self.both[p, kind, c]
        other = self.got[p, kind]
        dst[pl.ds(pl.multiple_of(p * LANE + c * HD, HD), HD), :] = own
        dst[pl.ds(pl.multiple_of(p * LANE + (1 - c) * HD, HD), HD), :] = other


def late_body(
    qu_h, qv_h, kv_h, wn, trig_h, sin_h, cos_h, probs, datt_h, att_h, g_mid, cores_h, a2_h, x1_h, dx2_h, x_h, pre_h, smalls2, gain2, gain1,
    dx0_ref, flat, total_ref,
    qu, qv, kv, w_p, trig, sin, cos, datt, att, a2, x1_ref, dx2_ref, x_ref, wqkv, own, core, psem, fsem,
    dq_ref, dkt, dvt, gpost, qut, qvt, datt_t, g_low, *bufs,
):
    pc = Place()
    rows = qu.shape[0]
    half = sin.shape[1]
    fetch = Fetch(fsem)
    c = pc.at["c"]
    whole = [name for name in MID if name not in FRONT]
    owns = [fetch(g_mid.at[rows_at(MID[name] + c * (GROUP // 2), GROUP // 2), :], own.at[i]) for i, name in enumerate(whole)]
    owns += [fetch(cores_h.at[i], core.at[i]) for i in range(len(FRONT))]
    early = [fetch(s, d) for s, d in ((qu_h, qu), (qv_h, qv), (datt_h, datt), (kv_h, kv), (att_h, att), (part_of(wn, "p"), w_p), (trig_h, trig), (sin_h, sin), (cos_h, cos))]
    later = [
        fetch(s, d)
        for s, d in (
            (a2_h, a2), (x1_h, x1_ref), (dx2_h, dx2_ref), (x_h, x_ref), (wn.at[pl.ds(FLAT["q"], 1536), :], wqkv),
        )
    ]
    pc.greet("cxyz")
    taker = Taker(bufs)
    keys = KeyGrads(pc, taker(7))
    fly = Butterfly(pc, total_ref, taker(3))
    groups = {}
    for i, name in enumerate(FRONT):
        groups[name] = make_flows(pc, LAYOUT[name], "back", None, None, core.at[i], flat, FLAT[name], taker)
    for i, name in enumerate(whole):
        mine = lambda o, n, lanes, i=i: own[i, pl.ds(o, n), lanes]
        src = g_mid.at[pl.ds(MID[name], GROUP), :]
        groups[name] = make_flows(pc, LAYOUT[name], "whole", src, mine, core.at[len(FRONT) + i], flat, FLAT[name], taker)
    for i, name in enumerate(("q", "f1i", "f1o")):
        at = FLAT[name]
        mine = lambda o, n, lanes, at=at: g_low[pl.ds(pl.multiple_of(at + c * (GROUP // 2) + o, 16), n), lanes]
        groups[name] = make_flows(pc, LAYOUT[name], "whole", g_low.at[pl.ds(at, GROUP), :], mine, core.at[3 + i], flat, at, taker)
    for cp in owns:
        cp.wait()
    for name in MID:
        advance(groups[name])
    for cp in early:
        cp.wait()
    qut[...] = qu[...].T
    qvt[...] = qv[...].T
    datt_t[...] = datt[...].T

    def run(members):
        stages = [flow.take() for name in members.split() for flow in groups[name]]
        return lambda: [stage() for stage in stages]

    plan = {at: run(members) for at, members in sorted(TICKS.items()) if at < 2 * H}
    after = lambda point: run(TICKS.get(point, ""))()
    scale = HD**-0.5

    def scores(p, pbuf, load):
        at = cols(p)
        for e in range(2):
            mine = lane_half(e)
            part = pl.ds(pl.multiple_of(p * LANE + e * HD, HD), HD)
            dm = jnp.where(mine, datt[:, at], jnp.zeros((), BF))
            inner = jnp.sum(dm.astype(F32) * att[:, at].astype(F32), axis=-1, keepdims=True)
            dp = dot_nt(dm, kv[p, 1].reshape(-1, LANE))
            load(2 * p + e).wait()
            low_p = pbuf[2 * p + e]
            ds = (low_p.astype(F32) * (dp - inner)).astype(BF)
            pbuf[2 * p + e] = ds
            keys.put(p, 0, e, dot(qut[part, :], ds))
            keys.put(p, 1, e, dot(datt_t[part, :], low_p))
            if e == 0:
                pl.when(p > 0)(lambda: keys.step(p - 1, 1))
            else:
                keys.step(p, 0)
            ticks(e, plan, p)

    def queries(p, pbuf):
        at = cols(p)
        dqu = dqv = None
        for e in range(2):
            mine = lane_half(e)
            part = pl.ds(pl.multiple_of(p * LANE + e * HD, HD), HD)
            ds = pbuf[2 * p + e]
            db_s = dot(ds, trig[:, pl.ds(0, half)])
            db_c = dot(ds, trig[:, pl.ds(half, half)])
            da_s = (db_c * sin[...] - db_s * cos[...]).astype(BF)
            da_c = (db_c * cos[...] + db_s * sin[...]).astype(BF)
            gpost[part, pl.ds(0, half)] = dot(qvt[part, :], da_s)
            gpost[part, pl.ds(half, half)] = dot(qvt[part, :], da_c)
            part_v = dot(da_s, w_p[pl.ds(0, half), at]) + dot(da_c, w_p[pl.ds(half, half), at])
            part_u = dot(ds, kv[p, 0].reshape(-1, LANE))
            dqu = part_u if e == 0 else jnp.where(mine, part_u, dqu)
            dqv = part_v if e == 0 else jnp.where(mine, part_v, dqv)
            if e == 0:
                pl.when(p == 0)(lambda: keys.step(last, 1))
            else:
                keys.step(p, 2)
            ticks(e, plan, p + H // 2)
        dqu = dqu * scale
        dqv = dqv * scale
        dq_ref[:, at] = (dqu + dqv).astype(BF)
        total_ref[pl.ds(37, 1), at] = jnp.sum(dqu, axis=0, keepdims=True)
        total_ref[pl.ds(38, 1), at] = jnp.sum(dqv, axis=0, keepdims=True)

    def attention(pbuf):
        load = lambda h: pltpu.make_async_copy(probs.at[h], pbuf.at[h], psem.at[h])
        for h in range(H):
            load(h).start()
        lax.fori_loop(0, H // 2, lambda p, t: (scores(p, pbuf, load), t)[1], 0)
        lax.fori_loop(0, H // 2, lambda p, t: (queries(p, pbuf), t)[1], 0)

    last = H // 2 - 1
    pl.run_scoped(attention, pltpu.VMEM((H, rows, kv.shape[2] * rows), BF))
    def tail(pre_ref, w1, hid_ref, dpre_ref):
        last_in = [fetch(pre_h, pre_ref), fetch(wn.at[pl.ds(0, 4096), :], w1)]
        g_low[pl.ds(FLAT["p"], 512), :] = gpost[...].T.astype(BF)
        for cp in later:
            cp.wait()
        a2t = a2[...].T
        g_low[pl.ds(FLAT["q"], 512), :] = dot(a2t, dq_ref[...]).astype(BF)
        da2 = dot_nt(dq_ref[...], wqkv[pl.ds(0, 512), :])
        after(16)
        for p in range(H // 2):
            keys.step(p, 3)
            keys.collect(p, 0, dkt)
            keys.collect(p, 1, dvt)
        g_low[pl.ds(FLAT["k"], 512), :] = dot_nt(a2t, dkt[...]).astype(BF)
        g_low[pl.ds(FLAT["v"], 512), :] = dot_nt(a2t, dvt[...]).astype(BF)
        advance(groups["q"])
        after(17)
        for cp in last_in:
            cp.wait()
        ffn_hidden(pre_ref, hid_ref)
        da2 = da2 + dot_nt(dkt[...].T, wqkv[pl.ds(512, 512), :]) + dot_nt(dvt[...].T, wqkv[pl.ds(1024, 512), :])
        back, gg2 = norm_back(x1_ref[...], gain2[...], da2)
        dx1 = dx2_ref[...] + back
        g1 = (0.5 * dx1).astype(BF)
        x = x_ref[...].astype(F32)
        a1 = norm(x, gain1[...]).astype(BF)
        after(18)
        ffn_out_grad(g1, hid_ref, g_low.at[pl.ds(2048, 2048), :])
        advance(groups["f1o"])
        da1 = ffn_through(g1, w1.at[pl.ds(0, 2048), :], w1.at[pl.ds(2048, 2048), :], pre_ref, hid_ref, dpre_ref)
        ffn_in_grad(a1, dpre_ref, g_low.at[pl.ds(0, 2048), :])
        advance(groups["f1i"])
        after(19)
        back, gg1 = norm_back(x, gain1[...], da1)
        dx0_ref[...] = (dx1 + back).astype(BF)
        total_ref[pl.ds(smalls2.shape[0] - 5, 2), :] = jnp.concatenate([gg1, gg2], axis=0)

    pl.run_scoped(tail, pltpu.VMEM(pre_h.shape, F32), pltpu.VMEM((4096, 512), BF), pltpu.VMEM(pre_h.shape, BF), pltpu.VMEM(pre_h.shape, BF))
    count = smalls2.shape[0] - 8
    total_ref[pl.ds(0, count), :] = smalls2[pl.ds(0, count), :]
    total_ref[pl.ds(count, 3), :] = smalls2[pl.ds(count, 3), :]
    total_ref[pl.ds(count + 7, 1), :] = jnp.zeros((1, 512), F32)
    flows = flat_list(list(groups.values()))
    t = 0
    while any(flow.now < flow.last for flow in flows) or t <= len(fly.devs):
        advance([flow for i in range(4) for name in REST if i < len(groups[name]) for flow in groups[name][i : i + 1]])
        if t <= len(fly.devs):
            fly.stage(t)
        t += 1
    for p in range(H // 2):
        keys.sent(p)
    for flow in flows:
        flow.finish()


def widen_body(flat, total, bns, *refs):
    outs, smalls, (ibuf, obuf, isem, osem) = refs[:11], refs[11:21], refs[21:]
    count = smalls[0].shape[0]
    smalls[0][...] = total[pl.ds(0, count), :]
    for i, ref in enumerate(smalls[1:8]):
        ref[...] = total[pl.ds(count + i, 1), :]
    for i, ref in enumerate(smalls[8:]):
        ref[...] = bns[pl.ds(i, 1), :]
    step = 512
    n = FLAT_ROWS // step
    loads = [pltpu.make_async_copy(flat.at[pl.ds(i * step, step), :], ibuf.at[i], isem.at[i]) for i in range(n)]
    for cp in loads:
        cp.start()
    stores = []
    slots = obuf.shape[0]
    for i in range(n):
        name = [m for m in ORDER if FLAT[m] <= i * step][-1]
        out = outs[ORDER.index(name)]
        off = i * step - FLAT[name]
        fold = FOLDS.get(name, 1)
        if fold == 1:
            dst = out.at[pl.ds(off, step), :]
        else:
            dst = out.at[:, pl.ds(off, step)]
        loads[i].wait()
        if i >= slots:
            stores[i - slots].wait()
        obuf[i % slots] = ibuf[i].astype(F32)
        stores.append(pltpu.make_async_copy(obuf.at[i % slots], dst, osem.at[i % slots]))
        stores[-1].start()
    for cp in stores[-slots:]:
        cp.wait()


def remote(body, cid, outs, ins, scratch, name):
    def space(x):
        if x is None:
            return pl.BlockSpec(memory_space=pl.ANY)
        return pl.BlockSpec(memory_space=x)

    return pl.pallas_call(
        body,
        out_shape=[jax.ShapeDtypeStruct(s, d) for s, d, _ in outs],
        in_specs=[space(m) for _, m in ins],
        out_specs=[space(m) for _, _, m in outs],
        scratch_shapes=list(scratch),
        compiler_params=pltpu.CompilerParams(collective_id=cid, has_side_effects=True, vmem_limit_bytes=VMEM_LIMIT),
        name=name,
    )(*[x for x, _ in ins])


def local(
    inputs, cotangent, lengths, weight_noise, ffn1_in, ffn1_out, query_w, key_w, value_w, pos_w, out_w,
    conv_in, conv_out, ffn2_in, ffn2_out, conv_kernel, ffn1_gain, attn_gain, conv_gain, ffn2_gain,
    final_gain, bn_gain, bn_bias, pos_u, pos_v,
):
    _, rows, width = inputs.shape
    tms, slots = lax.axis_size("tm"), lax.axis_size("slot")
    frames = rows * tms
    count = conv_kernel.shape[0]
    devices = tms * slots
    size = Place().size
    x = inputs[0]
    cot = cotangent[0]
    gains = [g.reshape(1, -1) for g in (ffn1_gain, attn_gain, conv_gain, ffn2_gain, final_gain)]
    bng, bnb, pu, pv = (g.reshape(1, -1) for g in (bn_gain, bn_bias, pos_u, pos_v))
    raws = (ffn1_in, ffn1_out, query_w, key_w, value_w, pos_w, out_w, conv_in, conv_out, ffn2_in, ffn2_out)
    VM, HB, SM = pltpu.VMEM, None, pltpu.SMEM
    DMA = pltpu.SemaphoreType.DMA
    V = lambda shape, dtype=BF: pltpu.VMEM(shape, dtype)
    shard_rows = weight_noise.shape[1] // width
    half, hidden = width // 2, 2048
    keys = (H // 2, 2, tms, rows, LANE)
    specs = [
        ((FLAT_ROWS, width), BF), ((rows, width), F32), ((rows, hidden), F32), ((rows, width), BF), ((rows, width), BF), ((rows, width), BF),
        (keys, BF), ((frames, width), BF), ((rows, half), F32), ((rows, half), F32), ((rows, width), BF), ((H, rows, frames), BF),
    ]
    wn, x1, pre1, a2, qu, qv, kv, trig, sin, cos, att, probs = remote(
        early_body, 0, [spec + (HB,) for spec in specs],
        [(lengths, SM), (weight_noise, VM)] + [(r, HB) for r in raws] + [(x, VM), (gains[0], VM), (gains[1], VM), (pu, VM), (pv, VM)],
        [V((FLAT_ROWS, width)), V((width // LANE, shard_rows, LANE), F32)]
        + [V(*spec) for spec in specs[1:10]]
        + [V((2, frames // 64, half), F32), V((2, 64, half), F32), V((rows, width)), V((2, rows, frames)), DMA((18,)), DMA((16,)), DMA((2,))]
        + Gather.scratch(size, shard_rows, width) + KeysAll.scratch(size["x"]),
        "early",
    )
    ext = pltpu.VMEM((width // LANE, rows + count, LANE), F32)
    output, dx2, datt, g_mid, smalls2, bns, cores = remote(
        middle_body, 1,
        [((rows, width), BF, HB), ((rows, width), F32, HB), ((rows, width), BF, HB), ((3 * GROUP, width), BF, HB),
         ((count + 8, width), F32, VM), ((8, width), F32, VM), ((max(1, len(FRONT)), GROUP // 2, width), BF, HB)],
        [(lengths, SM), (att, VM), (x1, VM), (cot, VM), (wn, HB), (conv_kernel, VM), (bng, VM), (bnb, VM)] + [(g, VM) for g in gains[2:]],
        [pltpu.VMEM((FLAT_SIZE[n], width), BF) for n in ("o", "ci", "co", "f2i", "f2o")]
        + [DMA((5,)), pltpu.VMEM((count, width), BF), pltpu.VMEM((count, width), BF), DMA((4,)),
           pltpu.VMEM((rows, width), BF), pltpu.VMEM((rows, width), BF), pltpu.VMEM((rows, 2 * width), F32), ext, ext,
           pltpu.VMEM((rows, width), F32), pltpu.VMEM((rows, hidden), F32), pltpu.VMEM((rows, width), F32),
           pltpu.VMEM((count, 8, LANE), F32), pltpu.VMEM((rows, width), F32), V((max(1, len(FRONT)), GROUP // 2, width)),
           V((rows, width)), V((rows, width), F32), V((rows, width)), V((3 * GROUP, width)),
           V((rows, hidden)), V((rows, hidden)), DMA((7,))]
        + Totals.scratch(tms, slots, width) * 2 + flat_list([flat_list(flow_scratch(size, LAYOUT[n], "front")) for n in FRONT]),
        "middle",
    )
    dx0, flat, total = remote(
        late_body, 2, [((rows, width), BF, VM), ((FLAT_ROWS, width), BF, HB), ((count + 8, width), F32, VM)],
        [(t, HB) for t in (qu, qv, kv, wn, trig, sin, cos, probs, datt, att, g_mid, cores, a2, x1, dx2, x, pre1)]
        + [(smalls2, VM), (gains[1], VM), (gains[0], VM)],
        [V((rows, width)), V((rows, width)), V(keys), V((width, width)), V((frames, width)),
         V((rows, half), F32), V((rows, half), F32), V((rows, width)), V((rows, width)), V((rows, width)),
         V((rows, width), F32), V((rows, width), F32), V((rows, width)), V((3 * width, width)),
         V((3 - len(FRONT), GROUP // 2, width)), V((6, GROUP // 2, width)), DMA((H,)), DMA((20,)),
         V((rows, width)), V((width, rows)), V((width, rows)), V((width, width), F32), V((width, rows)), V((width, rows)), V((width, rows)),
         V((FLAT_ROWS // 2, width))]
        + KeyGrads.scratch(tms, rows) + Butterfly.scratch(devices, (count + 8, width))
        + flat_list([flat_list(flow_scratch(size, LAYOUT[n], "back")) for n in FRONT])
        + flat_list([flat_list(flow_scratch(size, LAYOUT[n], "whole")) for n in MID if n not in FRONT])
        + flat_list([flat_list(flow_scratch(size, LAYOUT[n], "whole")) for n in ("q", "f1i", "f1o")]),
        "late",
    )
    big = pl.pallas_call(
        widen_body,
        out_shape=[jax.ShapeDtypeStruct(r.shape, F32) for r in raws]
        + [jax.ShapeDtypeStruct((count, width), F32)] + [jax.ShapeDtypeStruct((1, width), F32)] * 9,
        in_specs=[pl.BlockSpec(memory_space=pl.ANY)] + [pl.BlockSpec(memory_space=pltpu.VMEM)] * 2,
        out_specs=[pl.BlockSpec(memory_space=pl.ANY)] * 11 + [pl.BlockSpec(memory_space=pltpu.VMEM)] * 10,
        scratch_shapes=[pltpu.VMEM((24, 512, width), BF), pltpu.VMEM((4, 512, width), F32), DMA((24,)), DMA((4,))],
        compiler_params=pltpu.CompilerParams(vmem_limit_bytes=VMEM_LIMIT),
        name="widen",
    )(flat, total, bns)
    t = [r[0] for r in big[12:]]
    return (output[None], dx0[None]) + tuple(big[:11]) + (
        big[11], t[3], t[4], t[0], t[1], t[2], t[7], t[8], t[5], t[6],
    )


def solution(mesh):
    split = P("slot", "tm", None)
    in_specs = (split, split, P("slot"), P(("tm", "slot"), None)) + (P(),) * 21
    out_specs = (split, split) + (P(),) * 21
    return jax.shard_map(local, mesh=mesh, in_specs=in_specs, out_specs=out_specs, check_vma=False)
```

```python
import math

import jax
import jax.numpy as jnp
from jax import lax
from jax.experimental import pallas as pl
from jax.experimental.pallas import tpu as pltpu
from jax.sharding import PartitionSpec as P

H = 8
HD = 64
LANE = 128
F32 = jnp.float32
BF = jnp.bfloat16
EPS = 1e-05
FILL = -1e30
VMEM_LIMIT = 60 * 2**20


def dot(a, b):
    return lax.dot_general(a, b, (((1,), (0,)), ((), ())), preferred_element_type=F32)


def dot_nt(a, b):
    return lax.dot_general(a, b, (((1,), (1,)), ((), ())), preferred_element_type=F32)


def dot_tn(a, b):
    return lax.dot_general(a, b, (((0,), (0,)), ((), ())), preferred_element_type=F32)


def norm_parts(v):
    mean = jnp.mean(v, axis=-1, keepdims=True)
    cen = v - mean
    r = lax.rsqrt(jnp.mean(cen * cen, axis=-1, keepdims=True) + EPS)
    return cen * r, r


def norm(v, gain):
    u, _ = norm_parts(v)
    return u * gain


def norm_back(v, gain, e):
    u, r = norm_parts(v)
    eg = e * gain
    back = r * (eg - jnp.mean(eg, axis=-1, keepdims=True) - u * jnp.mean(eg * u, axis=-1, keepdims=True))
    return back, jnp.sum(e * u, axis=0, keepdims=True)


def sigmoid(v):
    return 1.0 / (1.0 + jnp.exp(-v))


def swish_and_slope(v):
    s = sigmoid(v)
    sv = s * v
    return sv, s + sv * (1.0 - s)


def cols(p, width=LANE):
    return pl.ds(pl.multiple_of(p * width, width), width)


def lane_half(e):
    lane = lax.broadcasted_iota(jnp.int32, (1, LANE), 1)
    return (lane < HD) if e == 0 else (lane >= HD)


def call(body, outs, ins, scratch=(), name=None):
    return pl.pallas_call(
        body,
        out_shape=[jax.ShapeDtypeStruct(s, d) for s, d in outs],
        in_specs=[
            pl.BlockSpec(memory_space=pltpu.SMEM) if x.dtype == jnp.int32 else pl.BlockSpec(memory_space=pltpu.VMEM)
            for x in ins
        ],
        out_specs=[pl.BlockSpec(memory_space=pltpu.VMEM) for _ in outs],
        scratch_shapes=list(scratch),
        compiler_params=pltpu.CompilerParams(vmem_limit_bytes=VMEM_LIMIT),
        name=name,
    )(*ins)


MESH = pl.DeviceIdType.MESH


class Place:
    def __init__(self):
        tms, slots = lax.axis_size("tm"), lax.axis_size("slot")
        wide = 1 << ((slots.bit_length() - 1) // 2)
        self.size = {"c": 2, "x": tms // 2, "y": wide, "z": slots // wide}
        self.tm, self.slot = lax.axis_index("tm"), lax.axis_index("slot")
        self.at = {
            "c": lax.rem(self.tm, 2),
            "x": lax.div(self.tm, 2),
            "y": lax.rem(self.slot, wide),
            "z": lax.div(self.slot, wide),
        }

    def peer(self, axis, off):
        pos = dict(self.at)
        pos[axis] = lax.rem(pos[axis] + off, self.size[axis])
        return (pos["x"] * 2 + pos["c"], pos["z"] * self.size["y"] + pos["y"]), pos[axis]

    def peers(self, axis):
        return [(off,) + self.peer(axis, off) for off in range(1, self.size[axis])]

    def greet(self, axes):
        bar = pltpu.get_barrier_semaphore()
        count = 0
        for axis in axes:
            for _, dev, _ in self.peers(axis):
                pl.semaphore_signal(bar, inc=1, device_id=dev, device_id_type=MESH)
                count += 1
        pl.semaphore_wait(bar, count)


def rows_at(start, size):
    return pl.ds(pl.multiple_of(start, 16), size)


def add_into(dst, start, lanes, terms, size):
    step = 64 if size % 64 == 0 else 16

    def one(i, carry):
        off = pl.multiple_of(i * step, step)
        total = terms[0](off, step).astype(F32)
        for term in terms[1:]:
            total = total + term(off, step).astype(F32)
        dst[pl.ds(pl.multiple_of(start + off, 16), step), lanes] = total.astype(dst.dtype)
        return carry

    lax.fori_loop(0, size // step, one, 0)


GROUP = 2048


class Flow:
    STAGES = 9

    @staticmethod
    def lane_parts(order, size):
        rows = GROUP // 2
        for axis in order[:2]:
            rows //= size[axis]
        return max(1, 16 * size[order[2]] // rows)

    @staticmethod
    def scratch(order, width, size, kind):
        shapes, sends = [], 2
        blk = GROUP // 2
        parts = Flow.lane_parts(order, size)
        for lv, axis in enumerate(order):
            n = size[axis]
            blk = blk * parts // n if lv == 2 else blk // n
            w = width // parts if lv == 2 else width
            if (kind != "front" or lv == 0) and (kind != "back" or lv > 0):
                shapes.append(pltpu.VMEM((n - 1, blk, w), BF))
            sends += 2 * (n - 1)
        if kind != "front":
            shapes.append(pltpu.VMEM((blk, width // parts), BF))
        sems = pltpu.SemaphoreType.DMA((sends,))
        return shapes + [sems, sems, pltpu.SemaphoreType.DMA((1,))]

    def __init__(self, pc, order, lane, width, kind, src, own, core, out, first, bufs):
        self.ssem, self.rsem, self.lsem = bufs[-3:]
        bufs = list(bufs[:-3])
        self.used, self.now = 0, 2 if kind == "back" else 0
        self.made, self.local = [], []
        size = pc.size
        lanes = pl.ds(lane, width)
        c = pc.at["c"]
        top = GROUP // 2
        parts = self.lane_parts(order, size)
        blk, rel = [top], [0]
        for lv, axis in enumerate(order):
            if lv < 2:
                blk.append(blk[-1] // size[axis])
                rel.append(rel[-1] + pc.at[axis] * blk[-1])
        low = blk[2] * parts // size[order[2]]

        def share(pos):
            if parts == 1:
                return rel[2] + pos * low, lanes
            at = pl.multiple_of(lane + lax.rem(pos, parts) * (width // parts), LANE)
            return rel[2] + lax.div(pos, parts) * low, pl.ds(at, width // parts)

        ((_, cdev, _),) = pc.peers("c")
        into = [None] * 3
        if kind != "back":
            into[0] = bufs.pop(0)
        if kind != "front":
            into[1], into[2], fin = bufs
        core_copy = [self.copy(lambda: src.at[rows_at((1 - c) * top, top), lanes], lambda: core.at[:, lanes], cdev)]
        down = []
        for lv, axis in enumerate(order):
            cps = []
            for off, dev, pos in pc.peers(axis):
                if lv < 2:
                    s = lambda lv=lv, pos=pos: core.at[rows_at(rel[lv] + pos * blk[lv + 1], blk[lv + 1]), lanes]
                else:
                    s = lambda pos=pos: core.at[rows_at(share(pos)[0], low), share(pos)[1]]
                cps.append(self.copy(s, lambda lv=lv, off=off: into[lv].at[off - 1], dev))
            down.append(cps)
        mine = share(pc.at[order[2]])
        out_share = lambda: out.at[rows_at(first + c * top + mine[0], low), mine[1]]
        out_at = lambda lv: out.at[rows_at(first + c * top + rel[lv], blk[lv]), lanes]
        up = [[self.copy(lambda: fin, out_share, dev) for _, dev, _ in pc.peers(order[2])]]
        for lv in (2, 1):
            up.append([self.copy(lambda lv=lv: out_at(lv), lambda lv=lv: out_at(lv), dev) for _, dev, _ in pc.peers(order[lv - 1])])
        up.append([self.copy(lambda: out_at(0), lambda: out_at(0), cdev)])

        def fold(lv):
            if lv == 0:
                add_into(core, 0, lanes, [lambda o, n: own(o, n, lanes), lambda o, n: core[pl.ds(o, n), lanes]], top)
                return
            row, ln, size_ = (mine + (low,)) if lv == 3 else (rel[lv], lanes, blk[lv])
            terms = [lambda o, n: core[pl.ds(pl.multiple_of(row + o, 16), n), ln]]
            for k in range(size[order[lv - 1]] - 1):
                terms.append(lambda o, n, k=k: into[lv - 1][k, pl.ds(o, n), :])
            if lv == 3:
                add_into(fin, 0, slice(None), terms, size_)
            else:
                add_into(core, row, lanes, terms, size_)

        keep = lambda: pltpu.make_async_copy(fin, out_share(), self.lsem.at[0])

        def s1():
            self.arrived(core_copy)
            fold(0)
            self.start(down[0])

        def s2():
            if kind != "back":
                self.arrived(down[0])
                fold(1)
            if kind != "front":
                self.start(down[1])

        def s3():
            self.arrived(down[1])
            fold(2)
            self.start(down[2])

        def s4():
            self.arrived(down[2])
            fold(3)
            keep().start()
            self.start(up[0])

        def climb(i):
            def run():
                if i == 0:
                    keep().wait()
                self.arrived(up[i])
                if i < 3:
                    self.start(up[i + 1])

            return run

        self.stages = [lambda: self.start(core_copy), s1, s2, s3, s4] + [climb(i) for i in range(4)]
        self.last = 3 if kind == "front" else self.STAGES
        self.sent = {"front": core_copy + down[0], "back": down[1] + down[2] + sum(up, []), "whole": core_copy + sum(down + up, [])}[kind]

    def copy(self, src, dst, dev):
        k = self.used
        self.used += 1
        return src, dst, k, dev

    def make(self, cp):
        src, dst, k, dev = cp
        return pltpu.make_async_remote_copy(
            src_ref=src(), dst_ref=dst(), send_sem=self.ssem.at[k], recv_sem=self.rsem.at[k], device_id=dev, device_id_type=MESH
        )

    def start(self, cps):
        for cp in cps:
            self.make(cp).start()

    def arrived(self, cps):
        for cp in cps:
            self.make(cp).wait_recv()

    def finish(self):
        for cp in self.sent:
            self.make(cp).wait_send()

    def take(self):
        if self.now >= self.last:
            return lambda: None
        self.now += 1
        return self.stages[self.now - 1]


def advance(flows):
    for flow in flows:
        flow.take()()


MID = {"f2i": 2048, "f2o": 4096, "o": 0}
NAMES = ("f2i", "f2o", "o", "q", "f1o", "f1i")
AXES = {"A": ("y", "x", "z"), "B": ("x", "y", "z"), "X": ("z", "x", "y"), "Y": ("z", "y", "x")}
FRONT = ("f2i",)
LANES = {"f2i": "A1 B3", "f2o": "A2 B1 B1", "o": "A2 B2", "q": "A2 B1 X1", "f1o": "A1 B1 A1 X1", "f1i": "B1 A1 B1 A1"}
TURNS = {
    -1: (4, 5, 6, 8, 9, 0, 1,),
    0: (5, 6, 4,),
    1: (0, 1,),
    3: (8, 9, 0,),
    5: (1,),
    6: (5,),
    7: (6,),
    9: (5, 1, 6,),
    12: (9, 4, 5,),
    13: (8, 6,),
    15: (9, 0, 5,),
    16: (4, 1, 6,),
    17: (8, 0, 5,),
    18: (9,),
    19: (12, 14, 13,),
    20: (17, 4, 0,),
    21: (16, 12, 13, 18, 19, 20, 8, 1, 0, 5, 14, 21, 5, 22, 17, 1, 4, 12, 20, 23, 13, 16, 18, 14, 9, 17, 22, 19, 21, 20, 8, 12, 16, 6, 4, 14, 13, 19, 23, 18, 16, 9, 8, 19, 14, 21, 6, 12, 17, 13, 22, 6, 20, 18, 4, 16, 23, 17, 21, 12, 13, 4, 19, 22, 20, 14, 18, 8, 9, 16, 23, 21, 17, 8, 9, 22, 19, 13, 20, 13, 18, 21, 23, 16, 17, 22, 16, 14, 17, 20, 23, 12, 14, 20, 19, 22, 12, 19, 18, 21, 22, 23, 18, 21, 23,),
}


def layout(name, size):
    words = LANES[name].split()
    if max(Flow.lane_parts(AXES[word[0]], size) for word in words) > 1:
        words = ["A2", "B2"]
    got, lane = [], 0
    for word in words:
        got.append((AXES[word[0]], lane, int(word[1]) * LANE))
        lane += got[-1][2]
    return got


def flow_scratch(size, name, kind):
    return [Flow.scratch(order, width, size, kind) for order, _, width in layout(name, size)]


def flat_list(lists):
    return [x for part in lists for x in part]


class Taker:
    def __init__(self, refs):
        self.refs = list(refs)

    def __call__(self, n):
        got, self.refs = self.refs[:n], self.refs[n:]
        return got


def make_flows(pc, name, kind, src, own, core, out, first, taker):
    flows = []
    for (order, lane, width), shapes in zip(layout(name, pc.size), flow_scratch(pc.size, name, kind)):
        flows.append(Flow(pc, order, lane, width, kind, src, own, core, out, first, taker(len(shapes))))
    return flows


FLAT = {"f1i": 0, "f1o": 2048, "q": 4096, "k": 4608, "v": 5120, "p": 5632, "o": 6144, "ci": 6656, "co": 7680, "f2i": 8192, "f2o": 10240}
FLAT_ROWS = 12288
ORDER = tuple(FLAT)
FOLDS = {"f1i": 4, "ci": 2, "f2i": 4}
FLAT_SIZE = {n: (list(FLAT.values()) + [FLAT_ROWS])[i + 1] - FLAT[n] for i, n in enumerate(FLAT)}


def ticks(point, plan, p):
    for at, run in plan.items():
        if at % 2 == point:
            pl.when(p == at // 2)(lambda run=run: (run(), None)[1])


class Gather:
    @staticmethod
    def scratch(size, shard_rows, width):
        part, pieces = Gather.cut(shard_rows)
        links = 2 * pieces * (2 * (size["x"] + size["y"] + size["z"] - 3) + 2)
        sems = pltpu.SemaphoreType.DMA((links,))
        return [
            pltpu.VMEM((size["x"], 2, size["z"], size["y"], shard_rows, width), BF),
            pltpu.VMEM((width // LANE, 64, LANE), F32),
            sems,
            sems,
            pltpu.SemaphoreType.REGULAR,
        ]

    @staticmethod
    def cut(shard_rows):
        part = 64 if shard_rows % 64 == 0 else 16
        return part, shard_rows // part

    def __init__(self, pc, wf, bufs):
        self.pc, self.wf = pc, wf
        self.nb, self.scr, self.ssem, self.rsem, self.free = bufs
        self.shard_rows = self.nb.shape[4]
        self.part, self.pieces = self.cut(self.shard_rows)
        self.xs = pc.size["x"]
        self.used = 0
        self.stages = [self.plan(hx, q) for hx in range(2) for q in range(self.pieces)]

    def copies(self, ref, axis, only=None):
        out = []
        for off, dev, _ in self.pc.peers(axis):
            if only is not None and off != only:
                continue
            k = self.used
            self.used += 1
            out.append(
                (off, pltpu.make_async_remote_copy(
                    src_ref=ref, dst_ref=ref, send_sem=self.ssem.at[k], recv_sem=self.rsem.at[k], device_id=dev, device_id_type=MESH
                ))
            )
        return out

    def plan(self, hx, q):
        pc, nb = self.pc, self.nb
        x, c, z, y = (pc.at[a] for a in "xczy")
        rows = pl.ds(q * self.part, self.part)
        across = self.xs // 2
        side = pl.ds(hx * across, across)
        in_half = lambda pos: lax.div(pos, across) == hx
        width = nb.shape[5]
        wide, quarter = pl.ds(0, width // 2), width // 4
        away = pl.ds(3 * quarter, quarter)
        source = jnp.where(in_half(x), x, lax.rem(x + across, self.xs))
        lanes = pl.ds(pl.multiple_of(jnp.where(in_half(x), 2 * quarter, 3 * quarter), LANE), quarter)
        along = {
            "xa": self.copies(nb.at[x, c, z, y, rows, wide], "x"),
            "xd": self.copies(nb.at[x, c, z, y, rows, away], "x", across),
            "za": self.copies(nb.at[side, c, z, y, rows, wide], "z"),
            "zb": self.copies(nb.at[source, c, z, y, rows, lanes], "z"),
            "ya": self.copies(nb.at[side, c, :, y, rows, wide], "y"),
            "yb": self.copies(nb.at[source, c, :, y, rows, lanes], "y"),
            "xb": self.copies(nb.at[source, c, :, :, rows, lanes], "x"),
            "c": self.copies(nb.at[side, c, :, :, rows], "c"),
        }

        def each(axis, what, cond=None):
            for off, cp in along[axis]:
                if cond is None:
                    getattr(cp, what)()
                else:
                    pl.when(cond(off))(lambda cp=cp: getattr(cp, what)())

        sends = lambda off: in_half(x)
        gets = lambda off: in_half(lax.rem(x - off + self.xs, self.xs))

        def end():
            each("c", "wait_recv")
            if self.part == 64:
                self.mix_half(hx, q)
            elif q == self.pieces - 1:
                self.mix_half(hx, None)

        def done():
            each("xa", "wait_send", sends)
            for axis in ("za", "zb", "ya", "yb", "xb", "c"):
                each(axis, "wait_send")

        def then(*acts):
            return lambda: [each(*act) for act in acts]

        def let():
            @pl.when(in_half(x))
            def _():
                ((_, cp),) = along["xd"]
                cp.wait_send()
                ((_, dev, _),) = [peer for peer in pc.peers("x") if peer[0] == across]
                pl.semaphore_signal(self.free, inc=1, device_id=dev, device_id_type=MESH)

        def allowed():
            pl.when(jnp.logical_not(in_half(x)))(lambda: pl.semaphore_wait(self.free, 1))

        return {
            "X": then(("xa", "start", sends), ("xd", "start", sends)),
            "Z": then(("xa", "wait_recv", gets), ("xd", "wait_recv", gets), ("za", "start"), ("zb", "start")),
            "Y": lambda: (then(("za", "wait_recv"), ("zb", "wait_recv"), ("ya", "start"), ("yb", "start"))(), let()),
            "W": lambda: (each("yb", "wait_recv"), allowed(), each("xb", "start")),
            "C": then(("ya", "wait_recv"), ("xb", "wait_recv"), ("c", "start")),
            "E": end,
            "D": done,
        }

    def run(self, ops):
        for op in ops:
            if 0 <= op[1] < len(self.stages):
                self.stages[op[1]][op[0]]()

    def finish(self):
        for stages in self.stages:
            stages["D"]()

    def noise_at(self, row):
        pc = self.pc
        got = []
        sub = min(64, self.part)
        for i in range(64 // sub):
            at = row + i * sub
            d = lax.div(at, self.shard_rows)
            slots = pc.size["z"] * pc.size["y"]
            tm, sl = lax.div(d, slots), lax.rem(d, slots)
            off = pl.multiple_of(lax.rem(at, self.shard_rows), 16)
            got.append(
                self.nb[lax.div(tm, 2), lax.rem(tm, 2), lax.div(sl, pc.size["y"]), lax.rem(sl, pc.size["y"]), pl.ds(off, sub), :].astype(F32)
            )
        return got[0] if len(got) == 1 else jnp.concatenate(got, axis=0)

    def mix(self, row, base, size, fold):
        wf, scr = self.wf, self.scr
        value = self.noise_at(row)
        if fold == 1:
            at = rows_at(row, 64)
            wf[at, :] = (wf[at, :].astype(F32) + value).astype(BF)
            return
        for b in range(512 // LANE):
            scr[b] = value[:, b * LANE : (b + 1) * LANE]
        high = 64 // fold
        for j in range(fold):
            at = rows_at(base + j * (size // fold) + lax.div(row - base, fold), high)
            for b in range(512 // LANE):
                lanes = pl.ds(b * LANE, LANE)
                wf[at, lanes] = (wf[at, lanes].astype(F32) + scr[b, pl.ds(j, high, stride=fold), :]).astype(BF)

    def mix_half(self, hx, q):
        for name in ORDER:
            base, size, fold = FLAT[name], FLAT_SIZE[name], FOLDS.get(name, 1)
            if (base < FLAT_ROWS // 2) != (hx == 0):
                continue
            begin, end = base // 64, (base + size) // 64
            start, stride = (begin, 1) if q is None else (begin + (q - begin) % self.pieces, self.pieces)
            lax.fori_loop(
                0, (end - start + stride - 1) // stride,
                lambda i, t: (self.mix((start + i * stride) * 64, base, size, fold), t)[1], 0,
            )


class KeysAll:
    @staticmethod
    def scratch(xs):
        n = 2 * xs - 1
        sems = pltpu.SemaphoreType.DMA((H // 2, n))
        return [sems, sems]

    def __init__(self, pc, kv, bufs):
        self.pc, self.kv = pc, kv
        self.ssem, self.rsem = bufs

    def copy(self, p, k, tm, dev):
        ref = self.kv.at[p, :, tm]
        return pltpu.make_async_remote_copy(
            src_ref=ref, dst_ref=ref, send_sem=self.ssem.at[p, k], recv_sem=self.rsem.at[p, k], device_id=dev, device_id_type=MESH
        )

    def core(self, p):
        ((_, dev, _),) = self.pc.peers("c")
        return [self.copy(p, 0, self.pc.tm, dev)]

    def line(self, p):
        return [self.copy(p, off, self.pc.tm, dev) for off, dev, _ in self.pc.peers("x")]

    def relay(self, p):
        ((_, dev, _),) = self.pc.peers("c")
        xs = self.pc.size["x"]
        out = []
        for off in range(1, xs):
            source = lax.rem(self.pc.at["x"] - off + xs, xs) * 2 + self.pc.at["c"]
            out.append(self.copy(p, xs - 1 + off, source, dev))
        return out

    def send(self, p):
        for cp in self.core(p):
            cp.start()

    def send_line(self, p):
        for cp in self.line(p):
            cp.start()

    def forward(self, p):
        for come, on in zip(self.line(p), self.relay(p)):
            come.wait_recv()
            on.start()

    def ready(self, p):
        for cp in self.core(p) + self.relay(p):
            cp.wait_recv()

    def sent(self, p):
        for cp in self.line(p) + self.core(p) + self.relay(p):
            cp.wait_send()


def angle_tables(hi, lo, rates):
    for ref, step in ((hi, 64.0), (lo, 1.0)):
        count = ref.shape[1]
        angle = lax.broadcasted_iota(jnp.int32, (count, rates.shape[1]), 0).astype(F32) * step * rates
        ref[0] = jnp.sin(angle)
        ref[1] = jnp.cos(angle)


def angle_block(hi, lo, m):
    hs, hc = hi[0, pl.ds(m, 1), :], hi[1, pl.ds(m, 1), :]
    ls, lc = lo[0], lo[1]
    return hs * lc + hc * ls, hc * lc - hs * ls


def early_body(*refs):
    lens, noise, raws = refs[0], refs[1], refs[2:13]
    x_ref, gain1, gain2, pos_u, pos_v = refs[13:18]
    wn, x1_out, pre_out, a2_out, qu_out, qv_out, kv_out, trig_out, sin_out, cos_out, att_out, probs = refs[18:30]
    wf, flat, x1_ref, pre_ref, a2_ref, qu, qv, kv, trig, sin, cos, hi, lo, att, pbuf, wsem, osem, psem = refs[30:48]
    bufs = refs[48:]
    pc = Place()
    rows, width = x_ref.shape
    half = width // 2
    tms = lax.axis_size("tm")
    frames = rows * tms
    loads = []
    for name, raw in zip(ORDER, raws):
        for j in range(FOLDS.get(name, 1)):
            size = FLAT_SIZE[name] // FOLDS.get(name, 1)
            dst = wf.at[pl.ds(FLAT[name] + j * size, size), :]
            loads.append(pltpu.make_async_copy(raw.at[:, pl.ds(j * 512, 512)], dst, wsem.at[len(loads)]))
            loads[-1].start()
    gather = Gather(pc, wf, bufs[:5])
    keys = KeysAll(pc, kv, bufs[5:7])

    def unfold(i, carry):
        for r in range(8):
            for b in range(width // LANE):
                at = pl.ds(pl.multiple_of((i * 8 + r) * width + b * LANE, LANE), LANE)
                flat[b, pl.ds(i * 8 + r, 1), :] = noise[:, at].astype(F32)
        return carry

    shard_rows = gather.shard_rows
    lax.fori_loop(0, shard_rows // 8, unfold, 0)
    for b in range(width // LANE):
        gather.nb[pc.at["x"], pc.at["c"], pc.at["z"], pc.at["y"], :, pl.ds(b * LANE, LANE)] = flat[b].astype(BF)
    pc.greet("cxyz")
    n = gather.pieces
    gather.run([("X", i) for i in range(2 * n)])
    gather.run([("Z", 0), ("Z", 1)])
    rates = jnp.exp(lax.broadcasted_iota(jnp.int32, (1, half), 1).astype(F32) * (-2.0 * math.log(10000.0) / width))
    angle_tables(hi, lo, rates)

    def angles(m, carry):
        s, c = angle_block(hi, lo, m)
        at = rows_at(m * 64, 64)
        trig[at, pl.ds(0, half)] = s.astype(BF)
        trig[at, pl.ds(half, half)] = c.astype(BF)
        return carry

    def own_angles(m, carry):
        s, c = angle_block(hi, lo, pc.tm * (rows // 64) + m)
        sin[rows_at(m * 64, 64), :] = s
        cos[rows_at(m * 64, 64), :] = c
        return carry

    lax.fori_loop(0, frames // 64, angles, 0)
    lax.fori_loop(0, rows // 64, own_angles, 0)
    for cp in loads:
        cp.wait()
    outs = []

    def put(src, dst):
        cp = pltpu.make_async_copy(src, dst, osem.at[len(outs)])
        cp.start()
        outs.append(cp)

    x = x_ref[...].astype(F32)
    a1 = norm(x, gain1[...]).astype(BF)
    for t in range(2, n + 2):
        gather.run([("Z", t), ("Y", t - 2), ("W", t - 3), ("C", t - 4), ("E", t - 5)])
    gather.run([("W", n - 1), ("C", n - 2), ("E", n - 3), ("C", n - 1), ("E", n - 2), ("Z", n + 2), ("E", n - 1)])
    part = lambda name: wf.at[pl.ds(FLAT[name], FLAT_SIZE[name]), :]
    x1 = x + 0.5 * ffn_forward(a1, part("f1i"), part("f1o"), pre_ref)
    x1_ref[...] = x1
    a2 = norm(x1, gain2[...]).astype(BF)
    a2_ref[...] = a2
    k = dot(a2, part("k")[...]).astype(BF)
    v = dot(a2, part("v")[...]).astype(BF)
    for p in range(H // 2):
        kv[p, 0, pc.tm] = k[:, p * LANE : (p + 1) * LANE]
        kv[p, 1, pc.tm] = v[:, p * LANE : (p + 1) * LANE]
        if p == 0:
            keys.send_line(0)
        keys.send(p)
    gather.run([("Z", n + 3), ("Y", n), ("Y", n + 1)])
    q = dot(a2, part("q")[...])
    scale = HD**-0.5
    qu[...] = ((q + pos_u[...]).astype(BF).astype(F32) * scale).astype(BF)
    qv[...] = ((q + pos_v[...]).astype(BF).astype(F32) * scale).astype(BF)
    for src, dst in ((x1_ref, x1_out), (pre_ref, pre_out), (a2_ref, a2_out), (qu, qu_out), (qv, qv_out), (trig, trig_out), (sin, sin_out), (cos, cos_out)):
        put(src, dst)
    put(wf.at[pl.ds(0, FLAT_ROWS // 2), :], wn.at[pl.ds(0, FLAT_ROWS // 2), :])
    steps = {
        0: "W0 Y2 Z4", 1: "W1 Y3 Z5", 2: "C0 W2 Y4", 3: "E0 W3 Y5", 4: "C1 W4", 5: "E1 C2 W5", 6: "E2 C3", 7: "E3 C4 C5", 8: "E4 E5",
    }
    if n != 6:
        order = (("Z", 4), ("Y", 2), ("W", 0), ("C", 0), ("E", 0))
        steps = {8: " ".join("%s%d" % (op, i) for op, low in order for i in range(low, n))}
    steps = {at: [(op[0], n + int(op[1:])) for op in text.split()] for at, text in steps.items()}
    plan = {at: (lambda ops=ops: gather.run(ops)) for at, ops in steps.items() if at < H}
    ok = lax.broadcasted_iota(jnp.int32, (1, frames), 1) < lens[0]
    w_pos = part("p")
    store = lambda p, e: pltpu.make_async_copy(pbuf.at[e], probs.at[2 * p + e], psem.at[e])

    def pair(p, carry):
        at = cols(p)
        mixed = None
        for e in range(2):
            mine = lane_half(e)
            qve = jnp.where(mine, qv[:, at], jnp.zeros((), BF))
            que = jnp.where(mine, qu[:, at], jnp.zeros((), BF))
            turned = dot_nt(qve, w_pos[:, at])
            a_s, a_c = turned[:, :half], turned[:, half:]
            b_c = (a_s * sin[...] + a_c * cos[...]).astype(BF)
            b_s = (a_c * sin[...] - a_s * cos[...]).astype(BF)
            if e == 0:
                pl.when(p == 1)(lambda: keys.send_line(3))
                pl.when(p == 0)(lambda: (keys.forward(0), keys.send_line(1))[1])
                keys.ready(p)
            else:
                pl.when(p == 0)(lambda: keys.send_line(2))
            s = dot_nt(jnp.concatenate([b_s, b_c, que], axis=1), jnp.concatenate([trig[...], kv[p, 0].reshape(frames, LANE)], axis=1))
            s = jnp.where(ok, s, FILL)
            m = jnp.max(s, axis=-1, keepdims=True)
            ex = jnp.exp(s - m)
            tot = jnp.sum(ex, axis=-1, keepdims=True)
            low = (ex * (1.0 / tot)).astype(BF)
            pl.when(p > 0)(lambda: store(p - 1, e).wait())
            pbuf[e] = low
            store(p, e).start()
            got = dot(low, kv[p, 1].reshape(frames, LANE))
            mixed = got if e == 0 else jnp.where(mine, got, mixed)
            if e == 1:
                pl.when(p < H // 2 - 1)(lambda: keys.forward(p + 1))
            ticks(e, plan, p)
        att[:, at] = mixed.astype(BF)
        return carry

    lax.fori_loop(0, H // 2, pair, 0)
    put(kv, kv_out)
    put(att, att_out)
    gather.run(steps[8])
    put(wf.at[pl.ds(FLAT_ROWS // 2, FLAT_ROWS // 2), :], wn.at[pl.ds(FLAT_ROWS // 2, FLAT_ROWS // 2), :])
    for e in range(2):
        store(H // 2 - 1, e).wait()
    for p in range(H // 2):
        keys.sent(p)
    gather.finish()
    for cp in outs:
        cp.wait()


def chunk(c):
    return pl.ds(pl.multiple_of(c * 512, 512), 512)


def ffn_forward(normed, w_in, w_out, pre_ref):
    def one(c, acc):
        pre = dot(normed, w_in[chunk(c), :])
        pre_ref[:, chunk(c)] = pre
        return acc + dot((pre * sigmoid(pre)).astype(BF), w_out[chunk(c), :])

    return lax.fori_loop(0, w_in.shape[0] // 512, one, jnp.zeros((normed.shape[0], w_out.shape[1]), F32))


def ffn_through(g_low, w_in, w_out, pre_ref, hid_ref, dpre_ref):
    def one(c, acc):
        sw, slope = swish_and_slope(pre_ref[:, chunk(c)])
        hid_ref[:, chunk(c)] = sw.astype(BF)
        dpre = (dot_nt(g_low, w_out[chunk(c), :]) * slope).astype(BF)
        dpre_ref[:, chunk(c)] = dpre
        return acc + dot_nt(dpre, w_in[chunk(c), :])

    return lax.fori_loop(0, w_in.shape[0] // 512, one, jnp.zeros(g_low.shape, F32))


def ffn_in_grad(normed, dpre_ref, gin_ref):
    normed_t = normed.T

    def one(c, carry):
        gin_ref[chunk(c), :] = dot(normed_t, dpre_ref[:, chunk(c)]).astype(gin_ref.dtype)
        return carry

    lax.fori_loop(0, gin_ref.shape[0] // 512, one, 0)


def ffn_out_grad(g_low, hid_ref, gout_ref):
    def one(c, carry):
        gout_ref[chunk(c), :] = dot_tn(hid_ref[:, chunk(c)], g_low).astype(gout_ref.dtype)
        return carry

    lax.fori_loop(0, gout_ref.shape[0] // 512, one, 0)


def ffn_hidden(pre_ref, hid_ref):
    def one(c, carry):
        pre = pre_ref[:, chunk(c)]
        hid_ref[:, chunk(c)] = (pre * sigmoid(pre)).astype(BF)
        return carry

    lax.fori_loop(0, pre_ref.shape[1] // 512, one, 0)


class Fetch:
    def __init__(self, sems):
        self.sems, self.n = sems, 0

    def __call__(self, src, dst):
        cp = pltpu.make_async_copy(src, dst, self.sems.at[self.n])
        self.n += 1
        cp.start()
        return cp


def part_of(wn, name):
    return wn.at[pl.ds(FLAT[name], FLAT_SIZE[name]), :]


def valid_rows(lens, rows):
    first = lax.axis_index("tm") * rows
    return ((first + lax.broadcasted_iota(jnp.int32, (rows, 1), 0)) < lens[0]).astype(F32)


def spread(ext, start, value):
    value = value.astype(F32)
    for b in range(ext.shape[0]):
        ext[b, pl.ds(start, value.shape[0]), :] = value[:, b * LANE : (b + 1) * LANE]


def tap_sum(ext, taps, out_ref, offset):
    count = taps.shape[0]
    rows = out_ref.shape[0]
    block = 64 if rows % 64 == 0 else 16

    def one(i, carry):
        for b in range(ext.shape[0]):
            at = pl.ds(b * LANE, LANE)
            acc = jnp.zeros((block, LANE), F32)
            for k in range(count):
                acc = acc + taps[pl.ds(k, 1), at] * ext[b, pl.ds(i * block + offset(k), block), :]
            out_ref[pl.ds(pl.multiple_of(i * block, block), block), at] = acc
        return carry

    lax.fori_loop(0, rows // block, one, 0)


def bn_stats(sums):
    total = sums[2:3, :]
    mu = sums[0:1, :] / total
    var = sums[1:2, :] / total - mu * mu
    return mu, lax.rsqrt(var + EPS), total


class Totals:
    @staticmethod
    def scratch(tms, slots, width):
        n = tms + slots - 2
        return [
            pltpu.VMEM((tms, 8, width), F32),
            pltpu.VMEM((slots, 8, width), F32),
            pltpu.SemaphoreType.DMA((n,)),
            pltpu.SemaphoreType.DMA((n,)),
        ]

    def __init__(self, pc, bufs):
        self.pc, self.bufs = pc, bufs

    def begin(self, value):
        self.sent = []
        self.cps = self.send(0, value)

    def turn(self):
        self.cps = self.send(1, self.end(0))

    def done(self):
        value = self.end(1)
        for cp in self.sent:
            cp.wait_send()
        return value

    def send(self, i, value):
        pc, buf = self.pc, self.bufs[i]
        ssem, rsem = self.bufs[2:]
        me = (pc.tm, pc.slot)[i]
        buf[me] = value
        n = buf.shape[0]
        for off in range(1, n):
            to = lax.rem(me + off, n)
            k = off - 1 + i * (self.bufs[0].shape[0] - 1)
            cp = pltpu.make_async_remote_copy(
                src_ref=buf.at[me], dst_ref=buf.at[me], send_sem=ssem.at[k], recv_sem=rsem.at[k],
                device_id=(to, pc.slot) if i == 0 else (pc.tm, to), device_id_type=MESH,
            )
            cp.start()
            self.sent.append(cp)
        return self.sent[-(n - 1) :]

    def end(self, i):
        for cp in self.cps:
            cp.wait_recv()
        buf = self.bufs[i]
        value = buf[0]
        for j in range(1, buf.shape[0]):
            value = value + buf[j]
        return value


def greet_rows(pc, tms, slots):
    bar = pltpu.get_barrier_semaphore()
    for off in range(1, tms):
        pl.semaphore_signal(bar, inc=1, device_id=(lax.rem(pc.tm + off, tms), pc.slot), device_id_type=MESH)
    for off in range(1, slots):
        pl.semaphore_signal(bar, inc=1, device_id=(pc.tm, lax.rem(pc.slot + off, slots)), device_id_type=MESH)
    pl.semaphore_wait(bar, tms + slots - 2)


def middle_body(
    lens, att, x1_ref, cot, wn, taps, bn_gain, bn_bias, gain3, gain4, gain5,
    out_h, dx2_h, datt_h, g_h, smalls_ref, bns_ref, cores,
    w_o, w_ci, w_co, w_f2i, w_f2o, fsem, early, late, hsem, gm_ref, ddwo_ref, z_ref, ext, ext2, dwo_ref, pre_ref, dgm_ref, acc, x2_ref, core, out_ref, dx2_ref, datt_ref, g_ref, hid_ref, dpre_ref, csem, *bufs,
):
    pc = Place()
    tms, slots = lax.axis_size("tm"), lax.axis_size("slot")
    rows, width = x1_ref.shape
    count = taps.shape[0]
    fetch, put = Fetch(fsem), Fetch(csem)
    outs = []
    got = {n: fetch(part_of(wn, n), d) for n, d in (("o", w_o), ("ci", w_ci), ("co", w_co), ("f2i", w_f2i), ("f2o", w_f2o))}
    greet_rows(pc, tms, slots)
    taker = Taker(bufs)
    totals = Totals(pc, taker(4)), Totals(pc, taker(4))
    flows = []
    for i, name in enumerate(FRONT):
        src = g_ref.at[pl.ds(MID[name], GROUP), :]
        half_rows = lambda o, n, lanes, src=src: src[pl.ds(pl.multiple_of(pc.at["c"] * (GROUP // 2) + o, 16), n), lanes]
        flows += make_flows(pc, name, "front", src, half_rows, core.at[i], None, 0, taker)

    def halo(src, dst, k, step):
        dev = (lax.rem(pc.tm + step + tms, tms), pc.slot)
        return pltpu.make_async_remote_copy(
            src_ref=src, dst_ref=dst, send_sem=hsem.at[2 * k], recv_sem=hsem.at[2 * k + 1], device_id=dev, device_id_type=MESH
        )

    got["o"].wait()
    x2 = x1_ref[...] + dot(att[...], w_o[...])
    x2_ref[...] = x2
    a3 = norm(x2, gain3[...]).astype(BF)
    got["ci"].wait()
    z1 = dot(a3, w_ci[pl.ds(0, width), :])
    z2 = dot(a3, w_ci[pl.ds(width, width), :])
    z_ref[:, pl.ds(0, width)] = z1
    z_ref[:, pl.ds(width, width)] = z2
    ok = valid_rows(lens, rows)
    gm_ref[...] = (z1 * sigmoid(z2) * ok).astype(BF)
    cp = halo(gm_ref.at[pl.ds(rows - count, count), :], early, 0, 1)
    cp.start()
    spread(ext, count, gm_ref[...])
    cp.wait()
    spread(ext, 0, jnp.where(pc.tm > 0, early[...], jnp.zeros((), BF)))
    tap_sum(ext, taps, dwo_ref, lambda k: k + 1)
    dwo = dwo_ref[...]
    dwv = dwo * ok
    totals[0].begin(
        jnp.concatenate(
            [
                jnp.sum(dwv, axis=0, keepdims=True),
                jnp.sum(dwv * dwv, axis=0, keepdims=True),
                jnp.zeros((1, width), F32) + jnp.sum(ok, axis=0, keepdims=True),
                jnp.zeros((5, width), F32),
            ],
            axis=0,
        )
    )
    totals[0].turn()
    sums = totals[0].done()
    mu, inv, total = bn_stats(sums)
    xhat = (dwo_ref[...] - mu) * inv
    sw, slope = swish_and_slope(xhat * bn_gain[...] + bn_bias[...])
    sw = sw.astype(BF)
    got["co"].wait()
    x3 = x2_ref[...] + dot(sw, w_co[...])
    a4 = norm(x3, gain4[...]).astype(BF)
    got["f2i"].wait()
    got["f2o"].wait()
    x4 = x3 + 0.5 * ffn_forward(a4, w_f2i, w_f2o, pre_ref)
    out_ref[...] = norm(x4, gain5[...]).astype(BF)
    outs.append(put(out_ref, out_h))
    dx4, gg5 = norm_back(x4, gain5[...], cot[...].astype(F32))
    g4 = (0.5 * dx4).astype(BF)
    lo = FLAT["o"]
    da4 = ffn_through(g4, w_f2i, w_f2o, pre_ref, hid_ref, dpre_ref)
    back, gg4 = norm_back(x3, gain4[...], da4)
    dx3 = dx4 + back
    g3 = dx3.astype(BF)
    dbn = dot_nt(g3, w_co[...]) * slope
    totals[1].begin(
        jnp.concatenate(
            [jnp.sum(dbn * xhat, axis=0, keepdims=True), jnp.sum(dbn, axis=0, keepdims=True), jnp.zeros((6, width), F32)], axis=0
        )
    )
    part = lambda name: g_ref.at[pl.ds(MID[name], GROUP), :]
    ffn_in_grad(a4, dpre_ref, part("f2i"))
    totals[1].turn()
    advance(flows)
    ffn_out_grad(g4, hid_ref, part("f2o"))
    g_ref[pl.ds(FLAT["co"] - lo, width), :] = dot_tn(sw, g3).astype(BF)
    for name in ("f2i", "f2o"):
        if name not in FRONT:
            outs.append(put(part(name), g_h.at[pl.ds(MID[name], GROUP), :]))
    sums2 = totals[1].done()
    bns_ref[...] = sums2
    ddwo_ref[...] = (bn_gain[...] * inv * (dbn - ok * (sums2[1:2, :] + xhat * sums2[0:1, :]) / total)).astype(BF)
    cp = halo(ddwo_ref.at[pl.ds(0, count), :], late, 1, -1)
    cp.start()
    advance(flows)
    spread(ext2, 0, ddwo_ref[...])
    cp.wait()
    spread(ext2, rows, jnp.where(pc.tm < tms - 1, late[...], jnp.zeros((), BF)))
    tap_sum(ext2, taps, dgm_ref, lambda k: count - 1 - k)
    block = 64 if rows % 64 == 0 else 16
    for b in range(ext.shape[0]):
        acc[...] = jnp.zeros(acc.shape, F32)

        def one(i, carry, b=b):
            mine = ext2[b, pl.ds(pl.multiple_of(i * block, block), block), :]
            for k in range(count):
                prod = mine * ext[b, pl.ds(i * block + k + 1, block), :]
                acc[k] = acc[k] + jnp.sum(prod.reshape(block // 8, 8, LANE), axis=0)
            return carry

        lax.fori_loop(0, rows // block, one, 0)
        smalls_ref[pl.ds(0, count), pl.ds(b * LANE, LANE)] = jnp.sum(acc[...], axis=1)
    z1 = z_ref[:, pl.ds(0, width)]
    sg = sigmoid(z_ref[:, pl.ds(width, width)])
    dg = dgm_ref[...] * ok
    dz1 = (dg * sg).astype(BF)
    dz2 = (dg * z1 * sg * (1.0 - sg)).astype(BF)
    a3t = norm(x2_ref[...], gain3[...]).astype(BF).T
    g_ref[pl.ds(FLAT["ci"] - lo, width), :] = dot(a3t, dz1).astype(BF)
    g_ref[pl.ds(FLAT["ci"] - lo + width, width), :] = dot(a3t, dz2).astype(BF)
    da3 = dot_nt(dz1, w_ci[pl.ds(0, width), :]) + dot_nt(dz2, w_ci[pl.ds(width, width), :])
    back, gg3 = norm_back(x2_ref[...], gain3[...], da3)
    dx2 = dx3 + back
    dx2_ref[...] = dx2
    outs.append(put(dx2_ref, dx2_h))
    g2 = dx2.astype(BF)
    g_ref[pl.ds(0, width), :] = dot_tn(att[...], g2).astype(BF)
    outs.append(put(g_ref.at[pl.ds(0, GROUP), :], g_h.at[pl.ds(0, GROUP), :]))
    datt_ref[...] = dot_nt(g2, w_o[...]).astype(BF)
    outs.append(put(datt_ref, datt_h))
    advance(flows)
    outs.append(put(core, cores))
    smalls_ref[pl.ds(count, 8), :] = jnp.concatenate([gg3, gg4, gg5, jnp.zeros((5, width), F32)], axis=0)
    for flow in flows:
        flow.finish()
    for cp in outs:
        cp.wait()


class Butterfly:
    @staticmethod
    def scratch(devices, shape):
        n = devices.bit_length() - 1
        return [pltpu.VMEM((n,) + shape, F32), pltpu.SemaphoreType.DMA((n,)), pltpu.SemaphoreType.DMA((n,))]

    def __init__(self, pc, value, bufs):
        self.value, (self.got, self.ssem, self.rsem) = value, bufs
        self.devs = []
        for axis, me in (("tm", pc.tm), ("slot", pc.slot)):
            bit = 1
            while bit < lax.axis_size(axis):
                to = me + bit - 2 * bit * lax.rem(lax.div(me, bit), 2)
                self.devs.append((to, pc.slot) if axis == "tm" else (pc.tm, to))
                bit *= 2

    def copy(self, k):
        return pltpu.make_async_remote_copy(
            src_ref=self.value, dst_ref=self.got.at[k], send_sem=self.ssem.at[k], recv_sem=self.rsem.at[k],
            device_id=self.devs[k], device_id_type=MESH,
        )

    def stage(self, k):
        if k > 0:
            self.copy(k - 1).wait()
            self.value[...] = self.value[...] + self.got[k - 1]
        if k < len(self.devs):
            self.copy(k).start()


GROUP = 2048


class KeyGrads:
    @staticmethod
    def scratch(tms, rows):
        pairs, xs = H // 2, tms // 2
        sems = pltpu.SemaphoreType.DMA((pairs, xs + 1))
        return [
            pltpu.VMEM((pairs, 2, 2, tms, HD, rows), BF),
            pltpu.VMEM((pairs, 2, tms, HD, rows), BF),
            pltpu.VMEM((xs - 1, pairs, 2, 2, HD, rows), BF),
            pltpu.VMEM((pairs, 2, 2, HD, rows), BF),
            pltpu.VMEM((pairs, 2, HD, rows), BF),
            sems,
            sems,
        ]

    def __init__(self, pc, bufs):
        self.pc = pc
        self.mine, self.core, self.line, self.both, self.got, self.ssem, self.rsem = bufs

    def put(self, p, kind, e, value):
        rows = self.mine.shape[-1]
        for t in range(self.mine.shape[3]):
            self.mine[p, kind, e, t] = value[:, t * rows : (t + 1) * rows].astype(BF)

    def copy(self, p, k, src, dst, dev):
        return pltpu.make_async_remote_copy(
            src_ref=src, dst_ref=dst, send_sem=self.ssem.at[p, k], recv_sem=self.rsem.at[p, k], device_id=dev, device_id_type=MESH
        )

    def first(self, p):
        ((_, dev, _),) = self.pc.peers("c")
        return [self.copy(p, 0, self.mine.at[p, :, 1 - self.pc.at["c"]], self.core.at[p], dev)]

    def second(self, p):
        return [
            self.copy(p, off, self.core.at[p, :, pl.ds(2 * pos, 2)], self.line.at[off - 1, p], dev) for off, dev, pos in self.pc.peers("x")
        ]

    def third(self, p):
        ((_, dev, _),) = self.pc.peers("c")
        return [self.copy(p, self.pc.size["x"], self.both.at[p, :, 1 - self.pc.at["c"]], self.got.at[p], dev)]

    def step(self, p, i):
        c, x = self.pc.at["c"], self.pc.at["x"]
        if i == 1:
            for cp in self.first(p):
                cp.wait_recv()
            for kind in range(2):
                for t in range(self.core.shape[2]):
                    total = self.core[p, kind, t].astype(F32) + self.mine[p, kind, c, t].astype(F32)
                    self.core[p, kind, t] = total.astype(BF)
        if i == 2:
            for cp in self.second(p):
                cp.wait_recv()
            for kind in range(2):
                for t in range(2):
                    total = self.core[p, kind, 2 * x + t].astype(F32)
                    for j in range(self.line.shape[0]):
                        total = total + self.line[j, p, kind, t].astype(F32)
                    self.both[p, kind, t] = total.astype(BF)
        if i == 3:
            for cp in self.third(p):
                cp.wait_recv()
            return
        for cp in (self.first, self.second, self.third)[i](p):
            cp.start()

    def sent(self, p):
        for cp in self.first(p) + self.second(p) + self.third(p):
            cp.wait_send()

    def collect(self, p, kind, dst):
        c = self.pc.at["c"]
        own = self.both[p, kind, c]
        other = self.got[p, kind]
        dst[pl.ds(pl.multiple_of(p * LANE + c * HD, HD), HD), :] = own
        dst[pl.ds(pl.multiple_of(p * LANE + (1 - c) * HD, HD), HD), :] = other


def late_body(
    qu_h, qv_h, kv_h, wn, trig_h, sin_h, cos_h, probs, datt_h, att_h, g_mid, cores_h, a2_h, x1_h, dx2_h, x_h, pre_h, smalls2, gain2, gain1,
    dx0_ref, flat, total_ref,
    qu, qv, kv, w_p, trig, sin, cos, datt, att, a2, x1_ref, dx2_ref, x_ref, wqkv, own, core, psem, fsem,
    dq_ref, dkt, dvt, gpost, qut, qvt, datt_t, g_low, *bufs,
):
    pc = Place()
    rows = qu.shape[0]
    half = sin.shape[1]
    fetch = Fetch(fsem)
    c = pc.at["c"]
    whole = [name for name in MID if name not in FRONT]
    owns = [fetch(g_mid.at[rows_at(MID[name] + c * (GROUP // 2), GROUP // 2), :], own.at[i]) for i, name in enumerate(whole)]
    owns += [fetch(cores_h.at[i], core.at[i]) for i in range(len(FRONT))]
    early = [fetch(s, d) for s, d in ((qu_h, qu), (qv_h, qv), (datt_h, datt), (kv_h, kv), (att_h, att), (part_of(wn, "p"), w_p), (trig_h, trig), (sin_h, sin), (cos_h, cos))]
    later = [
        fetch(s, d)
        for s, d in (
            (a2_h, a2), (x1_h, x1_ref), (dx2_h, dx2_ref), (x_h, x_ref), (wn.at[pl.ds(FLAT["q"], 1536), :], wqkv),
        )
    ]
    pc.greet("cxyz")
    taker = Taker(bufs)
    keys = KeyGrads(pc, taker(7))
    fly = Butterfly(pc, total_ref, taker(3))
    groups = {}
    for i, name in enumerate(FRONT):
        groups[name] = make_flows(pc, name, "back", None, None, core.at[i], flat, FLAT[name], taker)
    for i, name in enumerate(whole):
        mine = lambda o, n, lanes, i=i: own[i, pl.ds(o, n), lanes]
        src = g_mid.at[pl.ds(MID[name], GROUP), :]
        groups[name] = make_flows(pc, name, "whole", src, mine, core.at[len(FRONT) + i], flat, FLAT[name], taker)
    for i, name in enumerate(("q", "f1i", "f1o")):
        at = FLAT[name]
        mine = lambda o, n, lanes, at=at: g_low[pl.ds(pl.multiple_of(at + c * (GROUP // 2) + o, 16), n), lanes]
        groups[name] = make_flows(pc, name, "whole", g_low.at[pl.ds(at, GROUP), :], mine, core.at[3 + i], flat, at, taker)
    for cp in owns:
        cp.wait()
    def run(point):
        picked = [(NAMES[token // 4], token % 4) for token in TURNS.get(point, ())]
        stages = [groups[name][i].take() for name, i in picked if i < len(groups[name])]
        return lambda: [stage() for stage in stages]

    run(-1)()
    for cp in early:
        cp.wait()
    qut[...] = qu[...].T
    qvt[...] = qv[...].T
    datt_t[...] = datt[...].T

    plan = {at: run(at) for at in range(2 * H)}
    after = lambda point: run(point)()
    scale = HD**-0.5

    def scores(p, pbuf, load):
        at = cols(p)
        for e in range(2):
            mine = lane_half(e)
            part = pl.ds(pl.multiple_of(p * LANE + e * HD, HD), HD)
            dm = jnp.where(mine, datt[:, at], jnp.zeros((), BF))
            inner = jnp.sum(dm.astype(F32) * att[:, at].astype(F32), axis=-1, keepdims=True)
            dp = dot_nt(dm, kv[p, 1].reshape(-1, LANE))
            load(2 * p + e).wait()
            low_p = pbuf[2 * p + e]
            ds = (low_p.astype(F32) * (dp - inner)).astype(BF)
            pbuf[2 * p + e] = ds
            keys.put(p, 0, e, dot(qut[part, :], ds))
            keys.put(p, 1, e, dot(datt_t[part, :], low_p))
            if e == 0:
                pl.when(p > 0)(lambda: keys.step(p - 1, 1))
            else:
                keys.step(p, 0)
            ticks(e, plan, p)

    def queries(p, pbuf):
        at = cols(p)
        dqu = dqv = None
        for e in range(2):
            mine = lane_half(e)
            part = pl.ds(pl.multiple_of(p * LANE + e * HD, HD), HD)
            ds = pbuf[2 * p + e]
            back = dot(ds, jnp.concatenate([trig[...], kv[p, 0].reshape(-1, LANE)], axis=1))
            db_s, db_c, part_u = back[:, :half], back[:, half : 2 * half], back[:, 2 * half :]
            da_s = (db_c * sin[...] - db_s * cos[...]).astype(BF)
            da_c = (db_c * cos[...] + db_s * sin[...]).astype(BF)
            turned = jnp.concatenate([da_s, da_c], axis=1)
            gpost[part, :] = dot(qvt[part, :], turned)
            part_v = dot(turned, w_p[:, at])
            dqu = part_u if e == 0 else jnp.where(mine, part_u, dqu)
            dqv = part_v if e == 0 else jnp.where(mine, part_v, dqv)
            if e == 0:
                pl.when(p == 0)(lambda: keys.step(last, 1))
            else:
                keys.step(p, 2)
            ticks(e, plan, p + H // 2)
        dqu = dqu * scale
        dqv = dqv * scale
        dq_ref[:, at] = (dqu + dqv).astype(BF)
        total_ref[pl.ds(37, 1), at] = jnp.sum(dqu, axis=0, keepdims=True)
        total_ref[pl.ds(38, 1), at] = jnp.sum(dqv, axis=0, keepdims=True)

    def attention(pbuf):
        load = lambda h: pltpu.make_async_copy(probs.at[h], pbuf.at[h], psem.at[h])
        for h in range(H):
            load(h).start()
        lax.fori_loop(0, H // 2, lambda p, t: (scores(p, pbuf, load), t)[1], 0)
        lax.fori_loop(0, H // 2, lambda p, t: (queries(p, pbuf), t)[1], 0)

    last = H // 2 - 1
    pl.run_scoped(attention, pltpu.VMEM((H, rows, kv.shape[2] * rows), BF))
    def tail(pre_ref, w1, hid_ref, dpre_ref):
        last_in = [fetch(pre_h, pre_ref), fetch(wn.at[pl.ds(0, 4096), :], w1)]
        g_low[pl.ds(FLAT["p"], 512), :] = gpost[...].T.astype(BF)
        for cp in later:
            cp.wait()
        a2t = a2[...].T
        g_low[pl.ds(FLAT["q"], 512), :] = dot(a2t, dq_ref[...]).astype(BF)
        da2 = dot_nt(dq_ref[...], wqkv[pl.ds(0, 512), :])
        after(16)
        for p in range(H // 2):
            keys.step(p, 3)
            keys.collect(p, 0, dkt)
            keys.collect(p, 1, dvt)
        g_low[pl.ds(FLAT["k"], 512), :] = dot_nt(a2t, dkt[...]).astype(BF)
        g_low[pl.ds(FLAT["v"], 512), :] = dot_nt(a2t, dvt[...]).astype(BF)
        advance(groups["q"])
        for cp in last_in:
            cp.wait()
        ffn_hidden(pre_ref, hid_ref)
        after(17)
        da2 = da2 + dot_nt(dkt[...].T, wqkv[pl.ds(512, 512), :]) + dot_nt(dvt[...].T, wqkv[pl.ds(1024, 512), :])
        back, gg2 = norm_back(x1_ref[...], gain2[...], da2)
        dx1 = dx2_ref[...] + back
        g1 = (0.5 * dx1).astype(BF)
        x = x_ref[...].astype(F32)
        a1 = norm(x, gain1[...]).astype(BF)
        after(18)
        ffn_out_grad(g1, hid_ref, g_low.at[pl.ds(2048, 2048), :])
        advance(groups["f1o"])
        after(19)
        da1 = ffn_through(g1, w1.at[pl.ds(0, 2048), :], w1.at[pl.ds(2048, 2048), :], pre_ref, hid_ref, dpre_ref)
        after(20)
        ffn_in_grad(a1, dpre_ref, g_low.at[pl.ds(0, 2048), :])
        advance(groups["f1i"])
        back, gg1 = norm_back(x, gain1[...], da1)
        dx0_ref[...] = (dx1 + back).astype(BF)
        total_ref[pl.ds(smalls2.shape[0] - 5, 2), :] = jnp.concatenate([gg1, gg2], axis=0)

    pl.run_scoped(tail, pltpu.VMEM(pre_h.shape, F32), pltpu.VMEM((4096, 512), BF), pltpu.VMEM(pre_h.shape, BF), pltpu.VMEM(pre_h.shape, BF))
    count = smalls2.shape[0] - 8
    total_ref[pl.ds(0, count), :] = smalls2[pl.ds(0, count), :]
    total_ref[pl.ds(count, 3), :] = smalls2[pl.ds(count, 3), :]
    total_ref[pl.ds(count + 7, 1), :] = jnp.zeros((1, 512), F32)
    flows = flat_list(list(groups.values()))
    turns, steps = TURNS[21], len(fly.devs) + 1
    for i, token in enumerate(turns):
        if i * steps // len(turns) != (i - 1) * steps // len(turns):
            fly.stage(i * steps // len(turns))
        name, k = NAMES[token // 4], token % 4
        advance(groups[name][k : k + 1])
    while any(flow.now < flow.last for flow in flows):
        advance(flows)
    for p in range(H // 2):
        keys.sent(p)
    for flow in flows:
        flow.finish()


def widen_body(flat, total, bns, *refs):
    outs, smalls, (ibuf, obuf, isem, osem) = refs[:11], refs[11:21], refs[21:]
    count = smalls[0].shape[0]
    smalls[0][...] = total[pl.ds(0, count), :]
    for i, ref in enumerate(smalls[1:8]):
        ref[...] = total[pl.ds(count + i, 1), :]
    for i, ref in enumerate(smalls[8:]):
        ref[...] = bns[pl.ds(i, 1), :]
    step = 512
    n = FLAT_ROWS // step
    loads = [pltpu.make_async_copy(flat.at[pl.ds(i * step, step), :], ibuf.at[i], isem.at[i]) for i in range(n)]
    for cp in loads:
        cp.start()
    stores = []
    slots = obuf.shape[0]
    for i in range(n):
        name = [m for m in ORDER if FLAT[m] <= i * step][-1]
        out = outs[ORDER.index(name)]
        off = i * step - FLAT[name]
        fold = FOLDS.get(name, 1)
        if fold == 1:
            dst = out.at[pl.ds(off, step), :]
        else:
            dst = out.at[:, pl.ds(off, step)]
        loads[i].wait()
        if i >= slots:
            stores[i - slots].wait()
        obuf[i % slots] = ibuf[i].astype(F32)
        stores.append(pltpu.make_async_copy(obuf.at[i % slots], dst, osem.at[i % slots]))
        stores[-1].start()
    for cp in stores[-slots:]:
        cp.wait()


def remote(body, cid, outs, ins, scratch, name):
    def space(x):
        if x is None:
            return pl.BlockSpec(memory_space=pl.ANY)
        return pl.BlockSpec(memory_space=x)

    return pl.pallas_call(
        body,
        out_shape=[jax.ShapeDtypeStruct(s, d) for s, d, _ in outs],
        in_specs=[space(m) for _, m in ins],
        out_specs=[space(m) for _, _, m in outs],
        scratch_shapes=list(scratch),
        compiler_params=pltpu.CompilerParams(collective_id=cid, has_side_effects=True, vmem_limit_bytes=VMEM_LIMIT),
        name=name,
    )(*[x for x, _ in ins])


def local(
    inputs, cotangent, lengths, weight_noise, ffn1_in, ffn1_out, query_w, key_w, value_w, pos_w, out_w,
    conv_in, conv_out, ffn2_in, ffn2_out, conv_kernel, ffn1_gain, attn_gain, conv_gain, ffn2_gain,
    final_gain, bn_gain, bn_bias, pos_u, pos_v,
):
    _, rows, width = inputs.shape
    tms, slots = lax.axis_size("tm"), lax.axis_size("slot")
    frames = rows * tms
    count = conv_kernel.shape[0]
    devices = tms * slots
    size = Place().size
    x = inputs[0]
    cot = cotangent[0]
    gains = [g.reshape(1, -1) for g in (ffn1_gain, attn_gain, conv_gain, ffn2_gain, final_gain)]
    bng, bnb, pu, pv = (g.reshape(1, -1) for g in (bn_gain, bn_bias, pos_u, pos_v))
    raws = (ffn1_in, ffn1_out, query_w, key_w, value_w, pos_w, out_w, conv_in, conv_out, ffn2_in, ffn2_out)
    VM, HB, SM = pltpu.VMEM, None, pltpu.SMEM
    DMA = pltpu.SemaphoreType.DMA
    V = lambda shape, dtype=BF: pltpu.VMEM(shape, dtype)
    shard_rows = weight_noise.shape[1] // width
    half, hidden = width // 2, 2048
    keys = (H // 2, 2, tms, rows, LANE)
    specs = [
        ((FLAT_ROWS, width), BF), ((rows, width), F32), ((rows, hidden), F32), ((rows, width), BF), ((rows, width), BF), ((rows, width), BF),
        (keys, BF), ((frames, width), BF), ((rows, half), F32), ((rows, half), F32), ((rows, width), BF), ((H, rows, frames), BF),
    ]
    wn, x1, pre1, a2, qu, qv, kv, trig, sin, cos, att, probs = remote(
        early_body, 0, [spec + (HB,) for spec in specs],
        [(lengths, SM), (weight_noise, VM)] + [(r, HB) for r in raws] + [(x, VM), (gains[0], VM), (gains[1], VM), (pu, VM), (pv, VM)],
        [V((FLAT_ROWS, width)), V((width // LANE, shard_rows, LANE), F32)]
        + [V(*spec) for spec in specs[1:10]]
        + [V((2, frames // 64, half), F32), V((2, 64, half), F32), V((rows, width)), V((2, rows, frames)), DMA((18,)), DMA((16,)), DMA((2,))]
        + Gather.scratch(size, shard_rows, width) + KeysAll.scratch(size["x"]),
        "early",
    )
    ext = pltpu.VMEM((width // LANE, rows + count, LANE), F32)
    output, dx2, datt, g_mid, smalls2, bns, cores = remote(
        middle_body, 1,
        [((rows, width), BF, HB), ((rows, width), F32, HB), ((rows, width), BF, HB), ((3 * GROUP, width), BF, HB),
         ((count + 8, width), F32, VM), ((8, width), F32, VM), ((max(1, len(FRONT)), GROUP // 2, width), BF, HB)],
        [(lengths, SM), (att, VM), (x1, VM), (cot, VM), (wn, HB), (conv_kernel, VM), (bng, VM), (bnb, VM)] + [(g, VM) for g in gains[2:]],
        [pltpu.VMEM((FLAT_SIZE[n], width), BF) for n in ("o", "ci", "co", "f2i", "f2o")]
        + [DMA((5,)), pltpu.VMEM((count, width), BF), pltpu.VMEM((count, width), BF), DMA((4,)),
           pltpu.VMEM((rows, width), BF), pltpu.VMEM((rows, width), BF), pltpu.VMEM((rows, 2 * width), F32), ext, ext,
           pltpu.VMEM((rows, width), F32), pltpu.VMEM((rows, hidden), F32), pltpu.VMEM((rows, width), F32),
           pltpu.VMEM((count, 8, LANE), F32), pltpu.VMEM((rows, width), F32), V((max(1, len(FRONT)), GROUP // 2, width)),
           V((rows, width)), V((rows, width), F32), V((rows, width)), V((3 * GROUP, width)),
           V((rows, hidden)), V((rows, hidden)), DMA((7,))]
        + Totals.scratch(tms, slots, width) * 2 + flat_list([flat_list(flow_scratch(size, n, "front")) for n in FRONT]),
        "middle",
    )
    dx0, flat, total = remote(
        late_body, 2, [((rows, width), BF, VM), ((FLAT_ROWS, width), BF, HB), ((count + 8, width), F32, VM)],
        [(t, HB) for t in (qu, qv, kv, wn, trig, sin, cos, probs, datt, att, g_mid, cores, a2, x1, dx2, x, pre1)]
        + [(smalls2, VM), (gains[1], VM), (gains[0], VM)],
        [V((rows, width)), V((rows, width)), V(keys), V((width, width)), V((frames, width)),
         V((rows, half), F32), V((rows, half), F32), V((rows, width)), V((rows, width)), V((rows, width)),
         V((rows, width), F32), V((rows, width), F32), V((rows, width)), V((3 * width, width)),
         V((3 - len(FRONT), GROUP // 2, width)), V((6, GROUP // 2, width)), DMA((H,)), DMA((20,)),
         V((rows, width)), V((width, rows)), V((width, rows)), V((width, width), F32), V((width, rows)), V((width, rows)), V((width, rows)),
         V((FLAT_ROWS // 2, width))]
        + KeyGrads.scratch(tms, rows) + Butterfly.scratch(devices, (count + 8, width))
        + flat_list([flat_list(flow_scratch(size, n, "back")) for n in FRONT])
        + flat_list([flat_list(flow_scratch(size, n, "whole")) for n in MID if n not in FRONT])
        + flat_list([flat_list(flow_scratch(size, n, "whole")) for n in ("q", "f1i", "f1o")]),
        "late",
    )
    big = pl.pallas_call(
        widen_body,
        out_shape=[jax.ShapeDtypeStruct(r.shape, F32) for r in raws]
        + [jax.ShapeDtypeStruct((count, width), F32)] + [jax.ShapeDtypeStruct((1, width), F32)] * 9,
        in_specs=[pl.BlockSpec(memory_space=pl.ANY)] + [pl.BlockSpec(memory_space=pltpu.VMEM)] * 2,
        out_specs=[pl.BlockSpec(memory_space=pl.ANY)] * 11 + [pl.BlockSpec(memory_space=pltpu.VMEM)] * 10,
        scratch_shapes=[pltpu.VMEM((24, 512, width), BF), pltpu.VMEM((4, 512, width), F32), DMA((24,)), DMA((4,))],
        compiler_params=pltpu.CompilerParams(vmem_limit_bytes=VMEM_LIMIT),
        name="widen",
    )(flat, total, bns)
    t = [r[0] for r in big[12:]]
    return (output[None], dx0[None]) + tuple(big[:11]) + (
        big[11], t[3], t[4], t[0], t[1], t[2], t[7], t[8], t[5], t[6],
    )


def solution(mesh):
    split = P("slot", "tm", None)
    in_specs = (split, split, P("slot"), P(("tm", "slot"), None)) + (P(),) * 21
    out_specs = (split, split) + (P(),) * 21
    return jax.shard_map(local, mesh=mesh, in_specs=in_specs, out_specs=out_specs, check_vma=False)
```

```python
import math

import jax
import jax.numpy as jnp
from jax import lax
from jax.experimental import pallas as pl
from jax.experimental.pallas import tpu as pltpu
from jax.sharding import PartitionSpec as P

H = 8
HD = 64
LANE = 128
F32 = jnp.float32
BF = jnp.bfloat16
EPS = 1e-05
FILL = -1e30
VMEM_LIMIT = 60 * 2**20


def dot(a, b):
    return lax.dot_general(a, b, (((1,), (0,)), ((), ())), preferred_element_type=F32)


def dot_nt(a, b):
    return lax.dot_general(a, b, (((1,), (1,)), ((), ())), preferred_element_type=F32)


def dot_tn(a, b):
    return lax.dot_general(a, b, (((0,), (0,)), ((), ())), preferred_element_type=F32)


def norm_parts(v):
    mean = jnp.mean(v, axis=-1, keepdims=True)
    cen = v - mean
    r = lax.rsqrt(jnp.mean(cen * cen, axis=-1, keepdims=True) + EPS)
    return cen * r, r


def norm(v, gain):
    u, _ = norm_parts(v)
    return u * gain


def norm_back(v, gain, e):
    u, r = norm_parts(v)
    eg = e * gain
    back = r * (eg - jnp.mean(eg, axis=-1, keepdims=True) - u * jnp.mean(eg * u, axis=-1, keepdims=True))
    return back, jnp.sum(e * u, axis=0, keepdims=True)


def sigmoid(v):
    return 1.0 / (1.0 + jnp.exp(-v))


def swish_and_slope(v):
    s = sigmoid(v)
    sv = s * v
    return sv, s + sv * (1.0 - s)


def cols(p, width=LANE):
    return pl.ds(pl.multiple_of(p * width, width), width)


def lane_half(e):
    lane = lax.broadcasted_iota(jnp.int32, (1, LANE), 1)
    return (lane < HD) if e == 0 else (lane >= HD)


def call(body, outs, ins, scratch=(), name=None):
    return pl.pallas_call(
        body,
        out_shape=[jax.ShapeDtypeStruct(s, d) for s, d in outs],
        in_specs=[
            pl.BlockSpec(memory_space=pltpu.SMEM) if x.dtype == jnp.int32 else pl.BlockSpec(memory_space=pltpu.VMEM)
            for x in ins
        ],
        out_specs=[pl.BlockSpec(memory_space=pltpu.VMEM) for _ in outs],
        scratch_shapes=list(scratch),
        compiler_params=pltpu.CompilerParams(vmem_limit_bytes=VMEM_LIMIT),
        name=name,
    )(*ins)


MESH = pl.DeviceIdType.MESH


class Place:
    def __init__(self):
        tms, slots = lax.axis_size("tm"), lax.axis_size("slot")
        wide = 1 << ((slots.bit_length() - 1) // 2)
        self.size = {"c": 2, "x": tms // 2, "y": wide, "z": slots // wide}
        self.tm, self.slot = lax.axis_index("tm"), lax.axis_index("slot")
        self.at = {
            "c": lax.rem(self.tm, 2),
            "x": lax.div(self.tm, 2),
            "y": lax.rem(self.slot, wide),
            "z": lax.div(self.slot, wide),
        }

    def peer(self, axis, off):
        pos = dict(self.at)
        pos[axis] = lax.rem(pos[axis] + off, self.size[axis])
        return (pos["x"] * 2 + pos["c"], pos["z"] * self.size["y"] + pos["y"]), pos[axis]

    def peers(self, axis):
        return [(off,) + self.peer(axis, off) for off in range(1, self.size[axis])]

    def greet(self, axes):
        bar = pltpu.get_barrier_semaphore()
        count = 0
        for axis in axes:
            for _, dev, _ in self.peers(axis):
                pl.semaphore_signal(bar, inc=1, device_id=dev, device_id_type=MESH)
                count += 1
        return lambda: pl.semaphore_wait(bar, count)


def rows_at(start, size):
    return pl.ds(pl.multiple_of(start, 16), size)


def add_into(dst, start, lanes, terms, size):
    step = 64 if size % 64 == 0 else 16

    def one(i, carry):
        off = pl.multiple_of(i * step, step)
        total = terms[0](off, step).astype(F32)
        for term in terms[1:]:
            total = total + term(off, step).astype(F32)
        dst[pl.ds(pl.multiple_of(start + off, 16), step), lanes] = total.astype(dst.dtype)
        return carry

    lax.fori_loop(0, size // step, one, 0)


GROUP = 2048


class Flow:
    STAGES = 9

    @staticmethod
    def lane_parts(order, size):
        rows = GROUP // 2
        for axis in order[:2]:
            rows //= size[axis]
        return max(1, 16 * size[order[2]] // rows)

    @staticmethod
    def scratch(order, width, size, kind):
        shapes = []
        blk = GROUP // 2
        parts = Flow.lane_parts(order, size)
        for lv, axis in enumerate(order):
            n = size[axis]
            blk = blk * parts // n if lv == 2 else blk // n
            w = width // parts if lv == 2 else width
            if (kind != "front" or lv == 0) and (kind != "back" or lv > 0):
                shapes.append(pltpu.VMEM((n - 1, blk, w), BF))
        if kind != "front":
            shapes.append(pltpu.VMEM((blk, width // parts), BF))
        sems = pltpu.SemaphoreType.DMA
        return shapes + [sems((3,)), sems((2,)) if kind == "front" else sems((8,)), sems((1,))]

    def __init__(self, pc, order, lane, width, kind, src, own, core, out, first, bufs):
        self.ssem, self.rsem, self.lsem = bufs[-3:]
        bufs = list(bufs[:-3])
        self.now = 2 if kind == "back" else 0
        size = pc.size
        lanes = pl.ds(lane, width)
        c = pc.at["c"]
        top = GROUP // 2
        parts = self.lane_parts(order, size)
        blk, rel = [top], [0]
        for lv, axis in enumerate(order):
            if lv < 2:
                blk.append(blk[-1] // size[axis])
                rel.append(rel[-1] + pc.at[axis] * blk[-1])
        low = blk[2] * parts // size[order[2]]

        def share(pos):
            if parts == 1:
                return rel[2] + pos * low, lanes
            at = pl.multiple_of(lane + lax.rem(pos, parts) * (width // parts), LANE)
            return rel[2] + lax.div(pos, parts) * low, pl.ds(at, width // parts)

        ((_, cdev, _),) = pc.peers("c")
        into = [None] * 3
        if kind != "back":
            into[0] = bufs.pop(0)
        if kind != "front":
            into[1], into[2], fin = bufs
        copies = [[(lambda: src.at[rows_at((1 - c) * top, top), lanes], lambda: core.at[:, lanes], cdev)]]
        bytes_of = [lambda: core.at[:, lanes]]
        for lv, axis in enumerate(order):
            cps = []
            for off, dev, pos in pc.peers(axis):
                if lv < 2:
                    s = lambda lv=lv, pos=pos: core.at[rows_at(rel[lv] + pos * blk[lv + 1], blk[lv + 1]), lanes]
                else:
                    s = lambda pos=pos: core.at[rows_at(share(pos)[0], low), share(pos)[1]]
                cps.append((s, lambda lv=lv, off=off: into[lv].at[off - 1], dev))
            copies.append(cps)
            bytes_of.append(lambda lv=lv: into[lv])
        mine = share(pc.at[order[2]])
        out_share = lambda: out.at[rows_at(first + c * top + mine[0], low), mine[1]]
        out_at = lambda lv: out.at[rows_at(first + c * top + rel[lv], blk[lv]), lanes]
        copies.append([(lambda: fin, out_share, dev) for _, dev, _ in pc.peers(order[2])])
        bytes_of.append(
            lambda: out.at[rows_at(first + c * top + rel[2], (size[order[2]] - 1) * low), pl.ds(lane, width // parts)]
        )
        for lv in (2, 1):
            copies.append([(lambda lv=lv: out_at(lv), lambda lv=lv: out_at(lv), dev) for _, dev, _ in pc.peers(order[lv - 1])])
            bytes_of.append(
                lambda lv=lv: out.at[rows_at(first + c * top + rel[lv - 1], (size[order[lv - 1]] - 1) * blk[lv]), lanes]
            )
        copies.append([(lambda: out_at(0), lambda: out_at(0), cdev)])
        bytes_of.append(lambda: out_at(0))
        self.copies, self.bytes_of = copies, bytes_of

        def fold(lv):
            if lv == 0:
                add_into(core, 0, lanes, [lambda o, n: own(o, n, lanes), lambda o, n: core[pl.ds(o, n), lanes]], top)
                return
            row, ln, size_ = (mine + (low,)) if lv == 3 else (rel[lv], lanes, blk[lv])
            terms = [lambda o, n: core[pl.ds(pl.multiple_of(row + o, 16), n), ln]]
            for k in range(size[order[lv - 1]] - 1):
                terms.append(lambda o, n, k=k: into[lv - 1][k, pl.ds(o, n), :])
            if lv == 3:
                add_into(fin, 0, slice(None), terms, size_)
            else:
                add_into(core, row, lanes, terms, size_)

        keep = lambda: pltpu.make_async_copy(fin, out_share(), self.lsem.at[0])

        def s1():
            self.arrived(0)
            fold(0)
            self.start(1)

        def s2():
            if kind != "back":
                self.arrived(1)
                fold(1)
            if kind != "front":
                self.start(2)

        def s3():
            self.arrived(2)
            fold(2)
            self.start(3)

        def s4():
            self.arrived(3)
            fold(3)
            keep().start()
            self.start(4)

        def climb(i):
            def run():
                if i == 0:
                    keep().wait()
                self.arrived(4 + i)
                if i < 3:
                    self.start(5 + i)

            return run

        self.stages = [lambda: self.start(0), s1, s2, s3, s4] + [climb(i) for i in range(4)]
        self.last = 3 if kind == "front" else self.STAGES
        self.first = 2 if kind == "back" else 0

    def make(self, i, src, dst, dev):
        return pltpu.make_async_remote_copy(
            src_ref=src(), dst_ref=dst(), send_sem=self.ssem.at[i % 3], recv_sem=self.rsem.at[i], device_id=dev, device_id_type=MESH
        )

    def start(self, i):
        for src, dst, dev in self.copies[i]:
            self.make(i, src, dst, dev).start()

    def all_of(self, i):
        if len(self.copies[i]) == 1:
            return self.make(i, *self.copies[i][0])
        return self.make(i, self.bytes_of[i], self.bytes_of[i], self.copies[i][0][2])

    def arrived(self, i):
        self.all_of(i).wait_recv()

    def left(self, i):
        if i >= self.first:
            self.all_of(i).wait_send()

    def finish(self):
        self.left(self.last - 2)

    def take(self):
        if self.now >= self.last:
            return lambda: None
        i, self.now = self.now, self.now + 1

        def run():
            self.stages[i]()
            if i > 1:
                self.left(i - 2)

        return run


def advance(flows):
    for flow in flows:
        flow.take()()


MID = {"f2i": 2048, "f2o": 4096, "o": 0}
NAMES = ("f2i", "f2o", "o", "q", "f1o", "f1i")
AXES = {"A": ("y", "x", "z"), "B": ("x", "y", "z"), "X": ("z", "x", "y"), "Y": ("z", "y", "x")}
FRONT = ("f2i",)
LANES = {"f2i": "A2 B2", "f2o": "B1 A1 B1 A1", "o": "A1 B1 A1 B1", "q": "A1 B1 A1 X1", "f1o": "A2 B1 X1", "f1i": "A1 B2 Y1"}
TURNS = {
    -1: (4, 5, 6, 7, 8, 9, 10, 11, 0, 1,),
    0: (4, 5, 6,),
    1: (8, 0, 10,),
    2: (1, 7,),
    3: (9,),
    4: (0, 4,),
    5: (6, 1,),
    8: (4, 9, 6,),
    9: (1,),
    11: (9, 4, 8,),
    12: (6,),
    13: (5, 0,),
    15: (8, 4, 10,),
    16: (5, 11, 9,),
    17: (8, 0, 4,),
    18: (12, 5, 13,),
    19: (14, 8, 15,),
    20: (16, 17, 18,),
    21: (12, 13, 10, 7, 0, 4, 14, 22, 20, 5, 4, 12, 21, 13, 17, 10, 18, 7, 0, 14, 16, 8, 11, 17, 12, 18, 9, 20, 5, 11, 13, 18, 16, 15, 1, 8, 14, 6, 7, 10, 8, 21, 20, 15, 17, 12, 5, 22, 15, 5, 11, 10, 13, 9, 21, 22, 12, 14, 20, 1, 17, 13, 16, 22, 10, 9, 18, 1, 11, 21, 14, 20, 10, 9, 22, 12, 17, 18, 16, 12, 13, 20, 22, 21, 13, 14, 6, 14, 7, 17, 16, 17, 15, 18, 20, 11, 21, 7, 18, 20, 6, 22, 15, 6, 22, 11, 16, 7, 11, 15, 21, 7, 16, 15, 21,),
}


def layout(name, size):
    words = LANES[name].split()
    if max(Flow.lane_parts(AXES[word[0]], size) for word in words) > 1:
        words = ["A2", "B2"]
    got, lane = [], 0
    for word in words:
        got.append((AXES[word[0]], lane, int(word[1]) * LANE))
        lane += got[-1][2]
    return got


def flow_scratch(size, name, kind):
    return [Flow.scratch(order, width, size, kind) for order, _, width in layout(name, size)]


def flat_list(lists):
    return [x for part in lists for x in part]


class Taker:
    def __init__(self, refs):
        self.refs = list(refs)

    def __call__(self, n):
        got, self.refs = self.refs[:n], self.refs[n:]
        return got


def make_flows(pc, name, kind, src, own, core, out, first, taker):
    flows = []
    for (order, lane, width), shapes in zip(layout(name, pc.size), flow_scratch(pc.size, name, kind)):
        flows.append(Flow(pc, order, lane, width, kind, src, own, core, out, first, taker(len(shapes))))
    return flows


FLAT = {"f1i": 0, "f1o": 2048, "q": 4096, "k": 4608, "v": 5120, "p": 5632, "o": 6144, "ci": 6656, "co": 7680, "f2i": 8192, "f2o": 10240}
FLAT_ROWS = 12288
ORDER = tuple(FLAT)
FOLDS = {"f1i": 4, "ci": 2, "f2i": 4}
FLAT_SIZE = {n: (list(FLAT.values()) + [FLAT_ROWS])[i + 1] - FLAT[n] for i, n in enumerate(FLAT)}


def ticks(point, plan, p):
    for at, run in plan.items():
        if at % 2 == point:
            pl.when(p == at // 2)(lambda run=run: (run(), None)[1])


class Gather:
    @staticmethod
    def scratch(size, shard_rows, width):
        part, pieces = Gather.cut(shard_rows)
        sems = pltpu.SemaphoreType.DMA((2 * pieces * (size["x"] + 6),))
        return [
            pltpu.VMEM((size["x"], 2, size["z"], size["y"], shard_rows, width), BF),
            pltpu.VMEM((width // LANE, 64, LANE), F32),
            sems,
            sems,
            pltpu.SemaphoreType.REGULAR,
        ]

    @staticmethod
    def cut(shard_rows):
        part = 64 if shard_rows % 64 == 0 else 16
        return part, shard_rows // part

    def __init__(self, pc, wf, bufs):
        self.pc, self.wf = pc, wf
        self.nb, self.scr, self.ssem, self.rsem, self.free = bufs
        self.shard_rows = self.nb.shape[4]
        self.part, self.pieces = self.cut(self.shard_rows)
        self.xs = pc.size["x"]
        self.used = 0
        self.stages = [self.plan(hx, q) for hx in range(2) for q in range(self.pieces)]

    def copies(self, ref, axis, only=None, total=None):
        out = []

        def make(ref, dev, k):
            return pltpu.make_async_remote_copy(
                src_ref=ref, dst_ref=ref, send_sem=self.ssem.at[k], recv_sem=self.rsem.at[k], device_id=dev, device_id_type=MESH
            )

        for off, dev, _ in self.pc.peers(axis):
            if only is not None and off != only:
                continue
            out.append((off, make(ref, dev, self.used)))
            if total is None:
                self.used += 1
        if total is None:
            return out, out
        self.used += 1
        return out, [(0, make(total, dev, self.used - 1))]

    def plan(self, hx, q):
        pc, nb = self.pc, self.nb
        x, c, z, y = (pc.at[a] for a in "xczy")
        rows = pl.ds(q * self.part, self.part)
        across = self.xs // 2
        side = pl.ds(hx * across, across)
        in_half = lambda pos: lax.div(pos, across) == hx
        width = nb.shape[5]
        wide, quarter = pl.ds(0, width // 2), width // 4
        away = pl.ds(3 * quarter, quarter)
        source = jnp.where(in_half(x), x, lax.rem(x + across, self.xs))
        lanes = pl.ds(pl.multiple_of(jnp.where(in_half(x), 2 * quarter, 3 * quarter), LANE), quarter)
        others = {axis: pl.ds(0, pc.size[axis] - 1) for axis in "xyz"}
        along = {
            "xa": self.copies(nb.at[x, c, z, y, rows, wide], "x"),
            "xd": self.copies(nb.at[x, c, z, y, rows, away], "x", across),
            "za": self.copies(nb.at[side, c, z, y, rows, wide], "z", None, nb.at[side, c, others["z"], y, rows, wide]),
            "zb": self.copies(nb.at[source, c, z, y, rows, lanes], "z", None, nb.at[source, c, others["z"], y, rows, lanes]),
            "ya": self.copies(nb.at[side, c, :, y, rows, wide], "y", None, nb.at[side, c, :, others["y"], rows, wide]),
            "yb": self.copies(nb.at[source, c, :, y, rows, lanes], "y", None, nb.at[source, c, :, others["y"], rows, lanes]),
            "xb": self.copies(nb.at[source, c, :, :, rows, lanes], "x", None, nb.at[others["x"], c, :, :, rows, lanes]),
            "c": self.copies(nb.at[side, c, :, :, rows], "c"),
        }

        def each(axis, what, cond=None):
            for off, cp in along[axis][0 if what == "start" else 1]:
                if cond is None:
                    getattr(cp, what)()
                else:
                    pl.when(cond(off))(lambda cp=cp: getattr(cp, what)())

        sends = lambda off: in_half(x)
        gets = lambda off: in_half(lax.rem(x - off + self.xs, self.xs))

        def end():
            each("c", "wait_recv")
            each("xa", "wait_send", sends)
            for axis in ("za", "zb", "ya", "yb", "xb"):
                each(axis, "wait_send")
            if self.part == 64:
                self.mix_half(hx, q)
            elif q == self.pieces - 1:
                self.mix_half(hx, None)

        def done():
            each("c", "wait_send")

        def then(*acts):
            return lambda: [each(*act) for act in acts]

        def let():
            @pl.when(in_half(x))
            def _():
                ((_, cp),) = along["xd"][0]
                cp.wait_send()
                ((_, dev, _),) = [peer for peer in pc.peers("x") if peer[0] == across]
                pl.semaphore_signal(self.free, inc=1, device_id=dev, device_id_type=MESH)

        def allowed():
            pl.when(jnp.logical_not(in_half(x)))(lambda: pl.semaphore_wait(self.free, 1))

        return {
            "X": then(("xa", "start", sends), ("xd", "start", sends)),
            "Z": then(("xa", "wait_recv", gets), ("xd", "wait_recv", gets), ("za", "start"), ("zb", "start")),
            "Y": lambda: (then(("za", "wait_recv"), ("zb", "wait_recv"), ("ya", "start"), ("yb", "start"))(), let()),
            "W": lambda: (each("yb", "wait_recv"), allowed(), each("xb", "start")),
            "C": then(("ya", "wait_recv"), ("xb", "wait_recv"), ("c", "start")),
            "E": end,
            "D": done,
        }

    def run(self, ops):
        for op in ops:
            if 0 <= op[1] < len(self.stages):
                self.stages[op[1]][op[0]]()

    def finish(self):
        for stages in self.stages:
            stages["D"]()

    def noise_at(self, row):
        pc = self.pc
        got = []
        sub = min(64, self.part)
        for i in range(64 // sub):
            at = row + i * sub
            d = lax.div(at, self.shard_rows)
            slots = pc.size["z"] * pc.size["y"]
            tm, sl = lax.div(d, slots), lax.rem(d, slots)
            off = pl.multiple_of(lax.rem(at, self.shard_rows), 16)
            got.append(
                self.nb[lax.div(tm, 2), lax.rem(tm, 2), lax.div(sl, pc.size["y"]), lax.rem(sl, pc.size["y"]), pl.ds(off, sub), :].astype(F32)
            )
        return got[0] if len(got) == 1 else jnp.concatenate(got, axis=0)

    def mix(self, row, base, size, fold):
        wf, scr = self.wf, self.scr
        value = self.noise_at(row)
        if fold == 1:
            at = rows_at(row, 64)
            wf[at, :] = (wf[at, :].astype(F32) + value).astype(BF)
            return
        for b in range(512 // LANE):
            scr[b] = value[:, b * LANE : (b + 1) * LANE]
        high = 64 // fold
        for j in range(fold):
            at = rows_at(base + j * (size // fold) + lax.div(row - base, fold), high)
            for b in range(512 // LANE):
                lanes = pl.ds(b * LANE, LANE)
                wf[at, lanes] = (wf[at, lanes].astype(F32) + scr[b, pl.ds(j, high, stride=fold), :]).astype(BF)

    def mix_half(self, hx, q):
        for name in ORDER:
            base, size, fold = FLAT[name], FLAT_SIZE[name], FOLDS.get(name, 1)
            if (base < FLAT_ROWS // 2) != (hx == 0):
                continue
            begin, end = base // 64, (base + size) // 64
            start, stride = (begin, 1) if q is None else (begin + (q - begin) % self.pieces, self.pieces)
            lax.fori_loop(
                0, (end - start + stride - 1) // stride,
                lambda i, t: (self.mix((start + i * stride) * 64, base, size, fold), t)[1], 0,
            )


class KeysAll:
    @staticmethod
    def scratch(xs):
        n = 2 * xs - 1
        sems = pltpu.SemaphoreType.DMA((H // 2, n))
        return [sems, sems]

    def __init__(self, pc, kv, bufs):
        self.pc, self.kv = pc, kv
        self.ssem, self.rsem = bufs

    def copy(self, p, k, tm, dev):
        ref = self.kv.at[p, :, tm]
        return pltpu.make_async_remote_copy(
            src_ref=ref, dst_ref=ref, send_sem=self.ssem.at[p, k], recv_sem=self.rsem.at[p, k], device_id=dev, device_id_type=MESH
        )

    def core(self, p):
        ((_, dev, _),) = self.pc.peers("c")
        return [self.copy(p, 0, self.pc.tm, dev)]

    def line(self, p):
        return [self.copy(p, off, self.pc.tm, dev) for off, dev, _ in self.pc.peers("x")]

    def relay(self, p):
        ((_, dev, _),) = self.pc.peers("c")
        xs = self.pc.size["x"]
        out = []
        for off in range(1, xs):
            source = lax.rem(self.pc.at["x"] - off + xs, xs) * 2 + self.pc.at["c"]
            out.append(self.copy(p, xs - 1 + off, source, dev))
        return out

    def send(self, p):
        for cp in self.core(p):
            cp.start()

    def send_line(self, p):
        for cp in self.line(p):
            cp.start()

    def forward(self, p):
        for come, on in zip(self.line(p), self.relay(p)):
            come.wait_recv()
            on.start()

    def ready(self, p):
        for cp in self.core(p) + self.relay(p):
            cp.wait_recv()

    def sent(self, p):
        for cp in self.line(p) + self.core(p) + self.relay(p):
            cp.wait_send()


def angle_tables(hi, lo, rates):
    for ref, step in ((hi, 64.0), (lo, 1.0)):
        count = ref.shape[1]
        angle = lax.broadcasted_iota(jnp.int32, (count, rates.shape[1]), 0).astype(F32) * step * rates
        ref[0] = jnp.sin(angle)
        ref[1] = jnp.cos(angle)


def angle_block(hi, lo, m):
    hs, hc = hi[0, pl.ds(m, 1), :], hi[1, pl.ds(m, 1), :]
    ls, lc = lo[0], lo[1]
    return hs * lc + hc * ls, hc * lc - hs * ls


def early_body(*refs):
    lens, noise, raws = refs[0], refs[1], refs[2:13]
    x_ref, gain1, gain2, pos_u, pos_v = refs[13:18]
    wn, x1_out, pre_out, a2_out, qu_out, qv_out, kv_out, trig_out, sin_out, cos_out, att_out, probs = refs[18:30]
    wf, flat, x1_ref, pre_ref, a2_ref, qu, qv, kv, trig, sin, cos, hi, lo, att, pbuf, wsem, osem, psem = refs[30:48]
    bufs = refs[48:]
    pc = Place()
    rows, width = x_ref.shape
    half = width // 2
    tms = lax.axis_size("tm")
    frames = rows * tms
    met = pc.greet("cxyz")
    loads = []
    for name, raw in zip(ORDER, raws):
        for j in range(FOLDS.get(name, 1)):
            size = FLAT_SIZE[name] // FOLDS.get(name, 1)
            dst = wf.at[pl.ds(FLAT[name] + j * size, size), :]
            loads.append(pltpu.make_async_copy(raw.at[:, pl.ds(j * 512, 512)], dst, wsem.at[len(loads)]))
            loads[-1].start()
    gather = Gather(pc, wf, bufs[:5])
    keys = KeysAll(pc, kv, bufs[5:7])

    def unfold(i, carry):
        for r in range(8):
            for b in range(width // LANE):
                at = pl.ds(pl.multiple_of((i * 8 + r) * width + b * LANE, LANE), LANE)
                flat[b, pl.ds(i * 8 + r, 1), :] = noise[:, at].astype(F32)
        return carry

    shard_rows = gather.shard_rows
    lax.fori_loop(0, shard_rows // 8, unfold, 0)
    for b in range(width // LANE):
        gather.nb[pc.at["x"], pc.at["c"], pc.at["z"], pc.at["y"], :, pl.ds(b * LANE, LANE)] = flat[b].astype(BF)
    rates = jnp.exp(lax.broadcasted_iota(jnp.int32, (1, half), 1).astype(F32) * (-2.0 * math.log(10000.0) / width))
    angle_tables(hi, lo, rates)

    def angles(m, carry):
        s, c = angle_block(hi, lo, m)
        at = rows_at(m * 64, 64)
        trig[at, pl.ds(0, half)] = s.astype(BF)
        trig[at, pl.ds(half, half)] = c.astype(BF)
        return carry

    def own_angles(m, carry):
        s, c = angle_block(hi, lo, pc.tm * (rows // 64) + m)
        sin[rows_at(m * 64, 64), :] = s
        cos[rows_at(m * 64, 64), :] = c
        return carry

    lax.fori_loop(0, frames // 64, angles, 0)
    lax.fori_loop(0, rows // 64, own_angles, 0)
    met()
    n = gather.pieces
    gather.run([("X", i) for i in range(2 * n)])
    gather.run([("Z", 0), ("Z", 1)])
    for cp in loads:
        cp.wait()
    outs = []

    def put(src, dst):
        cp = pltpu.make_async_copy(src, dst, osem.at[len(outs)])
        cp.start()
        outs.append(cp)

    x = x_ref[...].astype(F32)
    a1 = norm(x, gain1[...]).astype(BF)
    for t in range(2, n + 2):
        gather.run([("Z", t), ("Y", t - 2), ("W", t - 3), ("C", t - 4), ("E", t - 5)])
    gather.run([("W", n - 1), ("C", n - 2), ("E", n - 3), ("C", n - 1), ("E", n - 2), ("Z", n + 2), ("E", n - 1)])
    part = lambda name: wf.at[pl.ds(FLAT[name], FLAT_SIZE[name]), :]
    x1 = x + 0.5 * ffn_forward(a1, part("f1i"), part("f1o"), pre_ref)
    x1_ref[...] = x1
    a2 = norm(x1, gain2[...]).astype(BF)
    a2_ref[...] = a2
    k = dot(a2, part("k")[...]).astype(BF)
    v = dot(a2, part("v")[...]).astype(BF)
    for p in range(H // 2):
        kv[p, 0, pc.tm] = k[:, p * LANE : (p + 1) * LANE]
        kv[p, 1, pc.tm] = v[:, p * LANE : (p + 1) * LANE]
        if p == 0:
            keys.send_line(0)
        keys.send(p)
    gather.run([("Z", n + 3), ("Y", n), ("Y", n + 1)])
    q = dot(a2, part("q")[...])
    scale = HD**-0.5
    qu[...] = ((q + pos_u[...]).astype(BF).astype(F32) * scale).astype(BF)
    qv[...] = ((q + pos_v[...]).astype(BF).astype(F32) * scale).astype(BF)
    for src, dst in ((x1_ref, x1_out), (pre_ref, pre_out), (a2_ref, a2_out), (qu, qu_out), (qv, qv_out), (trig, trig_out), (sin, sin_out), (cos, cos_out)):
        put(src, dst)
    put(wf.at[pl.ds(0, FLAT_ROWS // 2), :], wn.at[pl.ds(0, FLAT_ROWS // 2), :])
    steps = {
        0: "W0 Y2 Z4", 1: "W1 Y3 Z5", 2: "C0 W2 Y4", 3: "E0 W3 Y5", 4: "C1 W4", 5: "E1 C2 W5", 6: "E2 C3", 7: "E3 C4 C5", 8: "E4 E5",
    }
    if n != 6:
        order = (("Z", 4), ("Y", 2), ("W", 0), ("C", 0), ("E", 0))
        steps = {8: " ".join("%s%d" % (op, i) for op, low in order for i in range(low, n))}
    steps = {at: [(op[0], n + int(op[1:])) for op in text.split()] for at, text in steps.items()}
    plan = {at: (lambda ops=ops: gather.run(ops)) for at, ops in steps.items() if at < H}
    ok = lax.broadcasted_iota(jnp.int32, (1, frames), 1) < lens[0]
    w_pos = part("p")
    store = lambda p, e: pltpu.make_async_copy(pbuf.at[e], probs.at[2 * p + e], psem.at[e])

    def pair(p, carry):
        at = cols(p)
        mixed = None
        for e in range(2):
            mine = lane_half(e)
            qve = jnp.where(mine, qv[:, at], jnp.zeros((), BF))
            que = jnp.where(mine, qu[:, at], jnp.zeros((), BF))
            turned = dot_nt(qve, w_pos[:, at])
            a_s, a_c = turned[:, :half], turned[:, half:]
            b_c = (a_s * sin[...] + a_c * cos[...]).astype(BF)
            b_s = (a_c * sin[...] - a_s * cos[...]).astype(BF)
            if e == 0:
                pl.when(p == 1)(lambda: keys.send_line(3))
                pl.when(p == 0)(lambda: (keys.forward(0), keys.send_line(1))[1])
                keys.ready(p)
            else:
                pl.when(p == 0)(lambda: keys.send_line(2))
            s = dot_nt(jnp.concatenate([b_s, b_c, que], axis=1), jnp.concatenate([trig[...], kv[p, 0].reshape(frames, LANE)], axis=1))
            s = jnp.where(ok, s, FILL)
            m = jnp.max(s, axis=-1, keepdims=True)
            ex = jnp.exp(s - m)
            tot = jnp.sum(ex, axis=-1, keepdims=True)
            low = (ex * (1.0 / tot)).astype(BF)
            pl.when(p > 0)(lambda: store(p - 1, e).wait())
            pbuf[e] = low
            store(p, e).start()
            got = dot(low, kv[p, 1].reshape(frames, LANE))
            mixed = got if e == 0 else jnp.where(mine, got, mixed)
            if e == 1:
                pl.when(p < H // 2 - 1)(lambda: keys.forward(p + 1))
            ticks(e, plan, p)
        att[:, at] = mixed.astype(BF)
        return carry

    lax.fori_loop(0, H // 2, pair, 0)
    put(kv, kv_out)
    put(att, att_out)
    gather.run(steps[8])
    put(wf.at[pl.ds(FLAT_ROWS // 2, FLAT_ROWS // 2), :], wn.at[pl.ds(FLAT_ROWS // 2, FLAT_ROWS // 2), :])
    for e in range(2):
        store(H // 2 - 1, e).wait()
    for p in range(H // 2):
        keys.sent(p)
    gather.finish()
    for cp in outs:
        cp.wait()


def chunk(c):
    return pl.ds(pl.multiple_of(c * 512, 512), 512)


def ffn_forward(normed, w_in, w_out, pre_ref):
    def one(c, acc):
        pre = dot(normed, w_in[chunk(c), :])
        pre_ref[:, chunk(c)] = pre
        return acc + dot((pre * sigmoid(pre)).astype(BF), w_out[chunk(c), :])

    return lax.fori_loop(0, w_in.shape[0] // 512, one, jnp.zeros((normed.shape[0], w_out.shape[1]), F32))


def ffn_through(g_low, w_in, w_out, pre_ref, hid_ref, dpre_ref):
    def one(c, acc):
        sw, slope = swish_and_slope(pre_ref[:, chunk(c)])
        hid_ref[:, chunk(c)] = sw.astype(BF)
        dpre = (dot_nt(g_low, w_out[chunk(c), :]) * slope).astype(BF)
        dpre_ref[:, chunk(c)] = dpre
        return acc + dot_nt(dpre, w_in[chunk(c), :])

    return lax.fori_loop(0, w_in.shape[0] // 512, one, jnp.zeros(g_low.shape, F32))


def ffn_in_grad(normed, dpre_ref, gin_ref):
    normed_t = normed.T

    def one(c, carry):
        gin_ref[chunk(c), :] = dot(normed_t, dpre_ref[:, chunk(c)]).astype(gin_ref.dtype)
        return carry

    lax.fori_loop(0, gin_ref.shape[0] // 512, one, 0)


def ffn_out_grad(g_low, hid_ref, gout_ref):
    def one(c, carry):
        gout_ref[chunk(c), :] = dot_tn(hid_ref[:, chunk(c)], g_low).astype(gout_ref.dtype)
        return carry

    lax.fori_loop(0, gout_ref.shape[0] // 512, one, 0)


def ffn_hidden(pre_ref, hid_ref):
    def one(c, carry):
        pre = pre_ref[:, chunk(c)]
        hid_ref[:, chunk(c)] = (pre * sigmoid(pre)).astype(BF)
        return carry

    lax.fori_loop(0, pre_ref.shape[1] // 512, one, 0)


class Fetch:
    def __init__(self, sems):
        self.sems, self.n = sems, 0

    def __call__(self, src, dst):
        cp = pltpu.make_async_copy(src, dst, self.sems.at[self.n])
        self.n += 1
        cp.start()
        return cp


def part_of(wn, name):
    return wn.at[pl.ds(FLAT[name], FLAT_SIZE[name]), :]


def valid_rows(lens, rows):
    first = lax.axis_index("tm") * rows
    return ((first + lax.broadcasted_iota(jnp.int32, (rows, 1), 0)) < lens[0]).astype(F32)


def spread(ext, start, value):
    value = value.astype(F32)
    for b in range(ext.shape[0]):
        ext[b, pl.ds(start, value.shape[0]), :] = value[:, b * LANE : (b + 1) * LANE]


def tap_sum(ext, taps, out_ref, offset):
    count = taps.shape[0]
    rows = out_ref.shape[0]
    block = 64 if rows % 64 == 0 else 16

    def one(i, carry):
        for b in range(ext.shape[0]):
            at = pl.ds(b * LANE, LANE)
            acc = jnp.zeros((block, LANE), F32)
            for k in range(count):
                acc = acc + taps[pl.ds(k, 1), at] * ext[b, pl.ds(i * block + offset(k), block), :]
            out_ref[pl.ds(pl.multiple_of(i * block, block), block), at] = acc
        return carry

    lax.fori_loop(0, rows // block, one, 0)


def bn_stats(sums):
    total = sums[2:3, :]
    mu = sums[0:1, :] / total
    var = sums[1:2, :] / total - mu * mu
    return mu, lax.rsqrt(var + EPS), total


class Totals:
    @staticmethod
    def scratch(tms, slots, width):
        n = tms + slots - 2
        return [
            pltpu.VMEM((tms, 8, width), F32),
            pltpu.VMEM((slots, 8, width), F32),
            pltpu.SemaphoreType.DMA((n,)),
            pltpu.SemaphoreType.DMA((n,)),
        ]

    def __init__(self, pc, bufs):
        self.pc, self.bufs = pc, bufs

    def begin(self, value):
        self.sent = []
        self.cps = self.send(0, value)

    def turn(self):
        self.cps = self.send(1, self.end(0))

    def done(self):
        value = self.end(1)
        for cp in self.sent:
            cp.wait_send()
        return value

    def send(self, i, value):
        pc, buf = self.pc, self.bufs[i]
        ssem, rsem = self.bufs[2:]
        me = (pc.tm, pc.slot)[i]
        buf[me] = value
        n = buf.shape[0]
        for off in range(1, n):
            to = lax.rem(me + off, n)
            k = off - 1 + i * (self.bufs[0].shape[0] - 1)
            cp = pltpu.make_async_remote_copy(
                src_ref=buf.at[me], dst_ref=buf.at[me], send_sem=ssem.at[k], recv_sem=rsem.at[k],
                device_id=(to, pc.slot) if i == 0 else (pc.tm, to), device_id_type=MESH,
            )
            cp.start()
            self.sent.append(cp)
        return self.sent[-(n - 1) :]

    def end(self, i):
        for cp in self.cps:
            cp.wait_recv()
        buf = self.bufs[i]
        value = buf[0]
        for j in range(1, buf.shape[0]):
            value = value + buf[j]
        return value


def greet_rows(pc, tms, slots):
    bar = pltpu.get_barrier_semaphore()
    for off in range(1, tms):
        pl.semaphore_signal(bar, inc=1, device_id=(lax.rem(pc.tm + off, tms), pc.slot), device_id_type=MESH)
    for off in range(1, slots):
        pl.semaphore_signal(bar, inc=1, device_id=(pc.tm, lax.rem(pc.slot + off, slots)), device_id_type=MESH)
    pl.semaphore_wait(bar, tms + slots - 2)


def middle_body(
    lens, att, x1_ref, cot, wn, taps, bn_gain, bn_bias, gain3, gain4, gain5,
    out_h, dx2_h, datt_h, g_h, smalls_ref, bns_ref, cores,
    w_o, w_ci, w_co, w_f2i, w_f2o, fsem, early, late, hsem, gm_ref, ddwo_ref, z_ref, ext, ext2, dwo_ref, pre_ref, dgm_ref, acc, x2_ref, core, out_ref, dx2_ref, datt_ref, g_ref, hid_ref, dpre_ref, csem, *bufs,
):
    pc = Place()
    tms, slots = lax.axis_size("tm"), lax.axis_size("slot")
    rows, width = x1_ref.shape
    count = taps.shape[0]
    fetch, put = Fetch(fsem), Fetch(csem)
    outs = []
    got = {n: fetch(part_of(wn, n), d) for n, d in (("o", w_o), ("ci", w_ci), ("co", w_co), ("f2i", w_f2i), ("f2o", w_f2o))}
    greet_rows(pc, tms, slots)
    taker = Taker(bufs)
    totals = Totals(pc, taker(4)), Totals(pc, taker(4))
    flows = []
    for i, name in enumerate(FRONT):
        src = g_ref.at[pl.ds(MID[name], GROUP), :]
        half_rows = lambda o, n, lanes, src=src: src[pl.ds(pl.multiple_of(pc.at["c"] * (GROUP // 2) + o, 16), n), lanes]
        flows += make_flows(pc, name, "front", src, half_rows, core.at[i], None, 0, taker)

    def halo(src, dst, k, step):
        dev = (lax.rem(pc.tm + step + tms, tms), pc.slot)
        return pltpu.make_async_remote_copy(
            src_ref=src, dst_ref=dst, send_sem=hsem.at[2 * k], recv_sem=hsem.at[2 * k + 1], device_id=dev, device_id_type=MESH
        )

    got["o"].wait()
    x2 = x1_ref[...] + dot(att[...], w_o[...])
    x2_ref[...] = x2
    a3 = norm(x2, gain3[...]).astype(BF)
    got["ci"].wait()
    z1 = dot(a3, w_ci[pl.ds(0, width), :])
    z2 = dot(a3, w_ci[pl.ds(width, width), :])
    z_ref[:, pl.ds(0, width)] = z1
    z_ref[:, pl.ds(width, width)] = z2
    ok = valid_rows(lens, rows)
    gm_ref[...] = (z1 * sigmoid(z2) * ok).astype(BF)
    cp = halo(gm_ref.at[pl.ds(rows - count, count), :], early, 0, 1)
    cp.start()
    spread(ext, count, gm_ref[...])
    cp.wait()
    spread(ext, 0, jnp.where(pc.tm > 0, early[...], jnp.zeros((), BF)))
    tap_sum(ext, taps, dwo_ref, lambda k: k + 1)
    dwo = dwo_ref[...]
    dwv = dwo * ok
    totals[0].begin(
        jnp.concatenate(
            [
                jnp.sum(dwv, axis=0, keepdims=True),
                jnp.sum(dwv * dwv, axis=0, keepdims=True),
                jnp.zeros((1, width), F32) + jnp.sum(ok, axis=0, keepdims=True),
                jnp.zeros((5, width), F32),
            ],
            axis=0,
        )
    )
    totals[0].turn()
    sums = totals[0].done()
    mu, inv, total = bn_stats(sums)
    xhat = (dwo_ref[...] - mu) * inv
    sw, slope = swish_and_slope(xhat * bn_gain[...] + bn_bias[...])
    sw = sw.astype(BF)
    got["co"].wait()
    x3 = x2_ref[...] + dot(sw, w_co[...])
    a4 = norm(x3, gain4[...]).astype(BF)
    got["f2i"].wait()
    got["f2o"].wait()
    x4 = x3 + 0.5 * ffn_forward(a4, w_f2i, w_f2o, pre_ref)
    out_ref[...] = norm(x4, gain5[...]).astype(BF)
    outs.append(put(out_ref, out_h))
    dx4, gg5 = norm_back(x4, gain5[...], cot[...].astype(F32))
    g4 = (0.5 * dx4).astype(BF)
    lo = FLAT["o"]
    da4 = ffn_through(g4, w_f2i, w_f2o, pre_ref, hid_ref, dpre_ref)
    back, gg4 = norm_back(x3, gain4[...], da4)
    dx3 = dx4 + back
    g3 = dx3.astype(BF)
    dbn = dot_nt(g3, w_co[...]) * slope
    totals[1].begin(
        jnp.concatenate(
            [jnp.sum(dbn * xhat, axis=0, keepdims=True), jnp.sum(dbn, axis=0, keepdims=True), jnp.zeros((6, width), F32)], axis=0
        )
    )
    part = lambda name: g_ref.at[pl.ds(MID[name], GROUP), :]
    ffn_in_grad(a4, dpre_ref, part("f2i"))
    totals[1].turn()
    advance(flows)
    ffn_out_grad(g4, hid_ref, part("f2o"))
    g_ref[pl.ds(FLAT["co"] - lo, width), :] = dot_tn(sw, g3).astype(BF)
    for name in ("f2i", "f2o"):
        if name not in FRONT:
            outs.append(put(part(name), g_h.at[pl.ds(MID[name], GROUP), :]))
    sums2 = totals[1].done()
    bns_ref[...] = sums2
    ddwo_ref[...] = (bn_gain[...] * inv * (dbn - ok * (sums2[1:2, :] + xhat * sums2[0:1, :]) / total)).astype(BF)
    cp = halo(ddwo_ref.at[pl.ds(0, count), :], late, 1, -1)
    cp.start()
    advance(flows)
    spread(ext2, 0, ddwo_ref[...])
    cp.wait()
    spread(ext2, rows, jnp.where(pc.tm < tms - 1, late[...], jnp.zeros((), BF)))
    tap_sum(ext2, taps, dgm_ref, lambda k: count - 1 - k)
    block = 64 if rows % 64 == 0 else 16
    for b in range(ext.shape[0]):
        acc[...] = jnp.zeros(acc.shape, F32)

        def one(i, carry, b=b):
            mine = ext2[b, pl.ds(pl.multiple_of(i * block, block), block), :]
            for k in range(count):
                prod = mine * ext[b, pl.ds(i * block + k + 1, block), :]
                acc[k] = acc[k] + jnp.sum(prod.reshape(block // 8, 8, LANE), axis=0)
            return carry

        lax.fori_loop(0, rows // block, one, 0)
        smalls_ref[pl.ds(0, count), pl.ds(b * LANE, LANE)] = jnp.sum(acc[...], axis=1)
    z1 = z_ref[:, pl.ds(0, width)]
    sg = sigmoid(z_ref[:, pl.ds(width, width)])
    dg = dgm_ref[...] * ok
    dz1 = (dg * sg).astype(BF)
    dz2 = (dg * z1 * sg * (1.0 - sg)).astype(BF)
    a3t = norm(x2_ref[...], gain3[...]).astype(BF).T
    g_ref[pl.ds(FLAT["ci"] - lo, width), :] = dot(a3t, dz1).astype(BF)
    g_ref[pl.ds(FLAT["ci"] - lo + width, width), :] = dot(a3t, dz2).astype(BF)
    da3 = dot_nt(dz1, w_ci[pl.ds(0, width), :]) + dot_nt(dz2, w_ci[pl.ds(width, width), :])
    back, gg3 = norm_back(x2_ref[...], gain3[...], da3)
    dx2 = dx3 + back
    dx2_ref[...] = dx2
    outs.append(put(dx2_ref, dx2_h))
    g2 = dx2.astype(BF)
    g_ref[pl.ds(0, width), :] = dot_tn(att[...], g2).astype(BF)
    outs.append(put(g_ref.at[pl.ds(0, GROUP), :], g_h.at[pl.ds(0, GROUP), :]))
    datt_ref[...] = dot_nt(g2, w_o[...]).astype(BF)
    outs.append(put(datt_ref, datt_h))
    advance(flows)
    outs.append(put(core, cores))
    smalls_ref[pl.ds(count, 8), :] = jnp.concatenate([gg3, gg4, gg5, jnp.zeros((5, width), F32)], axis=0)
    for flow in flows:
        flow.finish()
    for cp in outs:
        cp.wait()


class Butterfly:
    @staticmethod
    def scratch(devices, shape):
        n = devices.bit_length() - 1
        return [pltpu.VMEM((n,) + shape, F32), pltpu.SemaphoreType.DMA((n,)), pltpu.SemaphoreType.DMA((n,))]

    def __init__(self, pc, value, bufs):
        self.value, (self.got, self.ssem, self.rsem) = value, bufs
        self.devs = []
        for axis, me in (("tm", pc.tm), ("slot", pc.slot)):
            bit = 1
            while bit < lax.axis_size(axis):
                to = me + bit - 2 * bit * lax.rem(lax.div(me, bit), 2)
                self.devs.append((to, pc.slot) if axis == "tm" else (pc.tm, to))
                bit *= 2

    def copy(self, k):
        return pltpu.make_async_remote_copy(
            src_ref=self.value, dst_ref=self.got.at[k], send_sem=self.ssem.at[k], recv_sem=self.rsem.at[k],
            device_id=self.devs[k], device_id_type=MESH,
        )

    def stage(self, k):
        if k > 0:
            self.copy(k - 1).wait()
            self.value[...] = self.value[...] + self.got[k - 1]
        if k < len(self.devs):
            self.copy(k).start()


GROUP = 2048


class KeyGrads:
    @staticmethod
    def scratch(tms, rows):
        pairs, xs = H // 2, tms // 2
        sems = pltpu.SemaphoreType.DMA((pairs, xs + 1))
        return [
            pltpu.VMEM((pairs, 2, 2, tms, HD, rows), BF),
            pltpu.VMEM((pairs, 2, tms, HD, rows), BF),
            pltpu.VMEM((xs - 1, pairs, 2, 2, HD, rows), BF),
            pltpu.VMEM((pairs, 2, 2, HD, rows), BF),
            pltpu.VMEM((pairs, 2, HD, rows), BF),
            sems,
            sems,
        ]

    def __init__(self, pc, bufs):
        self.pc = pc
        self.mine, self.core, self.line, self.both, self.got, self.ssem, self.rsem = bufs

    def put(self, p, kind, e, value):
        rows = self.mine.shape[-1]
        for t in range(self.mine.shape[3]):
            self.mine[p, kind, e, t] = value[:, t * rows : (t + 1) * rows].astype(BF)

    def copy(self, p, k, src, dst, dev):
        return pltpu.make_async_remote_copy(
            src_ref=src, dst_ref=dst, send_sem=self.ssem.at[p, k], recv_sem=self.rsem.at[p, k], device_id=dev, device_id_type=MESH
        )

    def first(self, p):
        ((_, dev, _),) = self.pc.peers("c")
        return [self.copy(p, 0, self.mine.at[p, :, 1 - self.pc.at["c"]], self.core.at[p], dev)]

    def second(self, p):
        return [
            self.copy(p, off, self.core.at[p, :, pl.ds(2 * pos, 2)], self.line.at[off - 1, p], dev) for off, dev, pos in self.pc.peers("x")
        ]

    def third(self, p):
        ((_, dev, _),) = self.pc.peers("c")
        return [self.copy(p, self.pc.size["x"], self.both.at[p, :, 1 - self.pc.at["c"]], self.got.at[p], dev)]

    def step(self, p, i):
        c, x = self.pc.at["c"], self.pc.at["x"]
        if i == 1:
            for cp in self.first(p):
                cp.wait_recv()
            for kind in range(2):
                for t in range(self.core.shape[2]):
                    total = self.core[p, kind, t].astype(F32) + self.mine[p, kind, c, t].astype(F32)
                    self.core[p, kind, t] = total.astype(BF)
        if i == 2:
            for cp in self.second(p):
                cp.wait_recv()
            for kind in range(2):
                for t in range(2):
                    total = self.core[p, kind, 2 * x + t].astype(F32)
                    for j in range(self.line.shape[0]):
                        total = total + self.line[j, p, kind, t].astype(F32)
                    self.both[p, kind, t] = total.astype(BF)
        if i == 3:
            for cp in self.third(p):
                cp.wait_recv()
            for cp in self.first(p) + self.second(p):
                cp.wait_send()
            return
        for cp in (self.first, self.second, self.third)[i](p):
            cp.start()

    def sent(self, p):
        for cp in self.third(p):
            cp.wait_send()

    def collect(self, p, kind, dst):
        c = self.pc.at["c"]
        own = self.both[p, kind, c]
        other = self.got[p, kind]
        dst[pl.ds(pl.multiple_of(p * LANE + c * HD, HD), HD), :] = own
        dst[pl.ds(pl.multiple_of(p * LANE + (1 - c) * HD, HD), HD), :] = other


def late_body(
    qu_h, qv_h, kv_h, wn, trig_h, sin_h, cos_h, probs, datt_h, att_h, g_mid, cores_h, a2_h, x1_h, dx2_h, x_h, pre_h, smalls2, gain2, gain1,
    dx0_ref, flat, total_ref,
    qu, qv, kv, w_p, trig, sin, cos, datt, att, a2, x1_ref, dx2_ref, x_ref, wqkv, own, core, psem, fsem,
    dq_ref, dkt, dvt, gpost, qut, qvt, datt_t, g_low, *bufs,
):
    pc = Place()
    rows = qu.shape[0]
    half = sin.shape[1]
    fetch = Fetch(fsem)
    c = pc.at["c"]
    whole = [name for name in MID if name not in FRONT]
    met = pc.greet("cxyz")
    owns = [fetch(g_mid.at[rows_at(MID[name] + c * (GROUP // 2), GROUP // 2), :], own.at[i]) for i, name in enumerate(whole)]
    owns += [fetch(cores_h.at[i], core.at[i]) for i in range(len(FRONT))]
    needed = [fetch(s, d) for s, d in ((qu_h, qu), (datt_h, datt), (att_h, att), (kv_h, kv))]

    def copies(first, pairs):
        return lambda: [pltpu.make_async_copy(s, d, fsem.at[first + i]) for i, (s, d) in enumerate(pairs)]

    second = copies(fetch.n, ((qv_h, qv), (part_of(wn, "p"), w_p), (trig_h, trig), (sin_h, sin), (cos_h, cos)))
    later = copies(
        fetch.n + 5, ((a2_h, a2), (x1_h, x1_ref), (dx2_h, dx2_ref), (x_h, x_ref), (wn.at[pl.ds(FLAT["q"], 1536), :], wqkv))
    )
    last_in = lambda pre_ref, w1: copies(fetch.n + 10, ((pre_h, pre_ref), (wn.at[pl.ds(0, 4096), :], w1)))()
    taker = Taker(bufs)
    keys = KeyGrads(pc, taker(7))
    fly = Butterfly(pc, total_ref, taker(3))
    groups = {}
    for i, name in enumerate(FRONT):
        groups[name] = make_flows(pc, name, "back", None, None, core.at[i], flat, FLAT[name], taker)
    for i, name in enumerate(whole):
        mine = lambda o, n, lanes, i=i: own[i, pl.ds(o, n), lanes]
        src = g_mid.at[pl.ds(MID[name], GROUP), :]
        groups[name] = make_flows(pc, name, "whole", src, mine, core.at[len(FRONT) + i], flat, FLAT[name], taker)
    for i, name in enumerate(("q", "f1i", "f1o")):
        at = FLAT[name]
        mine = lambda o, n, lanes, at=at: g_low[pl.ds(pl.multiple_of(at + c * (GROUP // 2) + o, 16), n), lanes]
        groups[name] = make_flows(pc, name, "whole", g_low.at[pl.ds(at, GROUP), :], mine, core.at[3 + i], flat, at, taker)
    def run(point):
        picked = [(NAMES[token // 4], token % 4) for token in TURNS.get(point, ())]
        stages = [groups[name][i].take() for name, i in picked if i < len(groups[name])]
        return lambda: [stage() for stage in stages]

    first = run(-1)
    plan = {at: run(at) for at in range(2 * H)}
    after = lambda point: run(point)()
    scale = HD**-0.5

    def scores(p, pbuf, load):
        at = cols(p)
        for e in range(2):
            mine = lane_half(e)
            part = pl.ds(pl.multiple_of(p * LANE + e * HD, HD), HD)
            dm = jnp.where(mine, datt[:, at], jnp.zeros((), BF))
            inner = jnp.sum(dm.astype(F32) * att[:, at].astype(F32), axis=-1, keepdims=True)
            dp = dot_nt(dm, kv[p, 1].reshape(-1, LANE))
            load(2 * p + e).wait()
            low_p = pbuf[2 * p + e]
            ds = (low_p.astype(F32) * (dp - inner)).astype(BF)
            pbuf[2 * p + e] = ds
            keys.put(p, 0, e, dot(qut[part, :], ds))
            keys.put(p, 1, e, dot(datt_t[part, :], low_p))
            if e == 0:
                pl.when(p > 0)(lambda: keys.step(p - 1, 1))
            else:
                keys.step(p, 0)
            ticks(e, plan, p)

    def queries(p, pbuf):
        at = cols(p)
        dqu = dqv = None
        for e in range(2):
            mine = lane_half(e)
            part = pl.ds(pl.multiple_of(p * LANE + e * HD, HD), HD)
            ds = pbuf[2 * p + e]
            back = dot(ds, jnp.concatenate([trig[...], kv[p, 0].reshape(-1, LANE)], axis=1))
            db_s, db_c, part_u = back[:, :half], back[:, half : 2 * half], back[:, 2 * half :]
            da_s = (db_c * sin[...] - db_s * cos[...]).astype(BF)
            da_c = (db_c * cos[...] + db_s * sin[...]).astype(BF)
            turned = jnp.concatenate([da_s, da_c], axis=1)
            gpost[part, :] = dot(qvt[part, :], turned)
            part_v = dot(turned, w_p[:, at])
            dqu = part_u if e == 0 else jnp.where(mine, part_u, dqu)
            dqv = part_v if e == 0 else jnp.where(mine, part_v, dqv)
            if e == 0:
                pl.when(p == 0)(lambda: keys.step(last, 1))
            else:
                keys.step(p, 2)
            ticks(e, plan, p + H // 2)
        dqu = dqu * scale
        dqv = dqv * scale
        dq_ref[:, at] = (dqu + dqv).astype(BF)
        total_ref[pl.ds(37, 1), at] = jnp.sum(dqu, axis=0, keepdims=True)
        total_ref[pl.ds(38, 1), at] = jnp.sum(dqv, axis=0, keepdims=True)

    last = H // 2 - 1

    def attention(pbuf):
        load = lambda h: pltpu.make_async_copy(probs.at[h], pbuf.at[h], psem.at[h])
        for h in range(H):
            load(h).start()
        for cp in second() + later():
            cp.start()
        met()
        for cp in owns:
            cp.wait()
        first()
        for cp in needed:
            cp.wait()
        qut[...] = qu[...].T
        datt_t[...] = datt[...].T

        lax.fori_loop(0, H // 2, lambda p, t: (scores(p, pbuf, load), t)[1], 0)
        for cp in second():
            cp.wait()
        qvt[...] = qv[...].T
        lax.fori_loop(0, H // 2, lambda p, t: (queries(p, pbuf), t)[1], 0)

    pl.run_scoped(attention, pltpu.VMEM((H, rows, kv.shape[2] * rows), BF))

    def tail(pre_ref, w1, hid_ref, dpre_ref):
        for cp in last_in(pre_ref, w1):
            cp.start()
        g_low[pl.ds(FLAT["p"], 512), :] = gpost[...].T.astype(BF)
        for cp in later():
            cp.wait()
        a2t = a2[...].T
        g_low[pl.ds(FLAT["q"], 512), :] = dot(a2t, dq_ref[...]).astype(BF)
        da2 = dot_nt(dq_ref[...], wqkv[pl.ds(0, 512), :])
        after(16)
        for p in range(H // 2):
            keys.step(p, 3)
            keys.collect(p, 0, dkt)
            keys.collect(p, 1, dvt)
        g_low[pl.ds(FLAT["k"], 512), :] = dot_nt(a2t, dkt[...]).astype(BF)
        g_low[pl.ds(FLAT["v"], 512), :] = dot_nt(a2t, dvt[...]).astype(BF)
        advance(groups["q"])
        for cp in last_in(pre_ref, w1):
            cp.wait()
        ffn_hidden(pre_ref, hid_ref)
        after(17)
        da2 = da2 + dot_nt(dkt[...].T, wqkv[pl.ds(512, 512), :]) + dot_nt(dvt[...].T, wqkv[pl.ds(1024, 512), :])
        back, gg2 = norm_back(x1_ref[...], gain2[...], da2)
        dx1 = dx2_ref[...] + back
        g1 = (0.5 * dx1).astype(BF)
        x = x_ref[...].astype(F32)
        a1 = norm(x, gain1[...]).astype(BF)
        after(18)
        ffn_out_grad(g1, hid_ref, g_low.at[pl.ds(2048, 2048), :])
        advance(groups["f1o"])
        after(19)
        da1 = ffn_through(g1, w1.at[pl.ds(0, 2048), :], w1.at[pl.ds(2048, 2048), :], pre_ref, hid_ref, dpre_ref)
        after(20)
        ffn_in_grad(a1, dpre_ref, g_low.at[pl.ds(0, 2048), :])
        advance(groups["f1i"])
        back, gg1 = norm_back(x, gain1[...], da1)
        dx0_ref[...] = (dx1 + back).astype(BF)
        total_ref[pl.ds(smalls2.shape[0] - 5, 2), :] = jnp.concatenate([gg1, gg2], axis=0)

    pl.run_scoped(tail, pltpu.VMEM(pre_h.shape, F32), pltpu.VMEM((4096, 512), BF), pltpu.VMEM(pre_h.shape, BF), pltpu.VMEM(pre_h.shape, BF))
    count = smalls2.shape[0] - 8
    total_ref[pl.ds(0, count), :] = smalls2[pl.ds(0, count), :]
    total_ref[pl.ds(count, 3), :] = smalls2[pl.ds(count, 3), :]
    total_ref[pl.ds(count + 7, 1), :] = jnp.zeros((1, 512), F32)
    flows = flat_list(list(groups.values()))
    turns, steps = TURNS[21], len(fly.devs) + 1
    for i, token in enumerate(turns):
        if i * steps // len(turns) != (i - 1) * steps // len(turns):
            fly.stage(i * steps // len(turns))
        name, k = NAMES[token // 4], token % 4
        advance(groups[name][k : k + 1])
    while any(flow.now < flow.last for flow in flows):
        advance(flows)
    for p in range(H // 2):
        keys.sent(p)
    for flow in flows:
        flow.finish()


def widen_body(flat, total, bns, *refs):
    outs, smalls, (ibuf, obuf, rbuf, isem, osem, rsem) = refs[:11], refs[11:21], refs[21:]
    count = smalls[0].shape[0]
    lines = [pltpu.make_async_copy(total.at[pl.ds(0, count), :], smalls[0], rsem.at[0])]
    for i, ref in enumerate(smalls[1:]):
        rbuf[i] = total[pl.ds(count + i, 1), :] if i < 7 else bns[pl.ds(i - 7, 1), :]
        lines.append(pltpu.make_async_copy(rbuf.at[i], ref, rsem.at[1 + i]))
    for cp in lines:
        cp.start()
    step = 512
    n = FLAT_ROWS // step
    loads = [pltpu.make_async_copy(flat.at[pl.ds(i * step, step), :], ibuf.at[i], isem.at[i]) for i in range(n)]
    for cp in loads:
        cp.start()
    stores = []
    slots = obuf.shape[0]
    for i in range(n):
        name = [m for m in ORDER if FLAT[m] <= i * step][-1]
        out = outs[ORDER.index(name)]
        off = i * step - FLAT[name]
        fold = FOLDS.get(name, 1)
        if fold == 1:
            dst = out.at[pl.ds(off, step), :]
        else:
            dst = out.at[:, pl.ds(off, step)]
        loads[i].wait()
        if i >= slots:
            stores[i - slots].wait()
        obuf[i % slots] = ibuf[i].astype(F32)
        stores.append(pltpu.make_async_copy(obuf.at[i % slots], dst, osem.at[i % slots]))
        stores[-1].start()
    for cp in stores[-slots:] + lines:
        cp.wait()


def remote(body, cid, outs, ins, scratch, name):
    def space(x):
        if x is None:
            return pl.BlockSpec(memory_space=pl.ANY)
        return pl.BlockSpec(memory_space=x)

    return pl.pallas_call(
        body,
        out_shape=[jax.ShapeDtypeStruct(s, d) for s, d, _ in outs],
        in_specs=[space(m) for _, m in ins],
        out_specs=[space(m) for _, _, m in outs],
        scratch_shapes=list(scratch),
        compiler_params=pltpu.CompilerParams(collective_id=cid, has_side_effects=True, vmem_limit_bytes=VMEM_LIMIT),
        name=name,
    )(*[x for x, _ in ins])


def local(
    inputs, cotangent, lengths, weight_noise, ffn1_in, ffn1_out, query_w, key_w, value_w, pos_w, out_w,
    conv_in, conv_out, ffn2_in, ffn2_out, conv_kernel, ffn1_gain, attn_gain, conv_gain, ffn2_gain,
    final_gain, bn_gain, bn_bias, pos_u, pos_v,
):
    _, rows, width = inputs.shape
    tms, slots = lax.axis_size("tm"), lax.axis_size("slot")
    frames = rows * tms
    count = conv_kernel.shape[0]
    devices = tms * slots
    size = Place().size
    x = inputs[0]
    cot = cotangent[0]
    gains = [g.reshape(1, -1) for g in (ffn1_gain, attn_gain, conv_gain, ffn2_gain, final_gain)]
    bng, bnb, pu, pv = (g.reshape(1, -1) for g in (bn_gain, bn_bias, pos_u, pos_v))
    raws = (ffn1_in, ffn1_out, query_w, key_w, value_w, pos_w, out_w, conv_in, conv_out, ffn2_in, ffn2_out)
    VM, HB, SM = pltpu.VMEM, None, pltpu.SMEM
    DMA = pltpu.SemaphoreType.DMA
    V = lambda shape, dtype=BF: pltpu.VMEM(shape, dtype)
    shard_rows = weight_noise.shape[1] // width
    half, hidden = width // 2, 2048
    keys = (H // 2, 2, tms, rows, LANE)
    specs = [
        ((FLAT_ROWS, width), BF), ((rows, width), F32), ((rows, hidden), F32), ((rows, width), BF), ((rows, width), BF), ((rows, width), BF),
        (keys, BF), ((frames, width), BF), ((rows, half), F32), ((rows, half), F32), ((rows, width), BF), ((H, rows, frames), BF),
    ]
    wn, x1, pre1, a2, qu, qv, kv, trig, sin, cos, att, probs = remote(
        early_body, 0, [spec + (HB,) for spec in specs],
        [(lengths, SM), (weight_noise, VM)] + [(r, HB) for r in raws] + [(x, VM), (gains[0], VM), (gains[1], VM), (pu, VM), (pv, VM)],
        [V((FLAT_ROWS, width)), V((width // LANE, shard_rows, LANE), F32)]
        + [V(*spec) for spec in specs[1:10]]
        + [V((2, frames // 64, half), F32), V((2, 64, half), F32), V((rows, width)), V((2, rows, frames)), DMA((18,)), DMA((16,)), DMA((2,))]
        + Gather.scratch(size, shard_rows, width) + KeysAll.scratch(size["x"]),
        "early",
    )
    ext = pltpu.VMEM((width // LANE, rows + count, LANE), F32)
    output, dx2, datt, g_mid, smalls2, bns, cores = remote(
        middle_body, 1,
        [((rows, width), BF, HB), ((rows, width), F32, HB), ((rows, width), BF, HB), ((3 * GROUP, width), BF, HB),
         ((count + 8, width), F32, VM), ((8, width), F32, VM), ((max(1, len(FRONT)), GROUP // 2, width), BF, HB)],
        [(lengths, SM), (att, VM), (x1, VM), (cot, VM), (wn, HB), (conv_kernel, VM), (bng, VM), (bnb, VM)] + [(g, VM) for g in gains[2:]],
        [pltpu.VMEM((FLAT_SIZE[n], width), BF) for n in ("o", "ci", "co", "f2i", "f2o")]
        + [DMA((5,)), pltpu.VMEM((count, width), BF), pltpu.VMEM((count, width), BF), DMA((4,)),
           pltpu.VMEM((rows, width), BF), pltpu.VMEM((rows, width), BF), pltpu.VMEM((rows, 2 * width), F32), ext, ext,
           pltpu.VMEM((rows, width), F32), pltpu.VMEM((rows, hidden), F32), pltpu.VMEM((rows, width), F32),
           pltpu.VMEM((count, 8, LANE), F32), pltpu.VMEM((rows, width), F32), V((max(1, len(FRONT)), GROUP // 2, width)),
           V((rows, width)), V((rows, width), F32), V((rows, width)), V((3 * GROUP, width)),
           V((rows, hidden)), V((rows, hidden)), DMA((7,))]
        + Totals.scratch(tms, slots, width) * 2 + flat_list([flat_list(flow_scratch(size, n, "front")) for n in FRONT]),
        "middle",
    )
    dx0, flat, total = remote(
        late_body, 2, [((rows, width), BF, VM), ((FLAT_ROWS, width), BF, HB), ((count + 8, width), F32, VM)],
        [(t, HB) for t in (qu, qv, kv, wn, trig, sin, cos, probs, datt, att, g_mid, cores, a2, x1, dx2, x, pre1)]
        + [(smalls2, VM), (gains[1], VM), (gains[0], VM)],
        [V((rows, width)), V((rows, width)), V(keys), V((width, width)), V((frames, width)),
         V((rows, half), F32), V((rows, half), F32), V((rows, width)), V((rows, width)), V((rows, width)),
         V((rows, width), F32), V((rows, width), F32), V((rows, width)), V((3 * width, width)),
         V((3 - len(FRONT), GROUP // 2, width)), V((6, GROUP // 2, width)), DMA((H,)), DMA((20,)),
         V((rows, width)), V((width, rows)), V((width, rows)), V((width, width), F32), V((width, rows)), V((width, rows)), V((width, rows)),
         V((FLAT_ROWS // 2, width))]
        + KeyGrads.scratch(tms, rows) + Butterfly.scratch(devices, (count + 8, width))
        + flat_list([flat_list(flow_scratch(size, n, "back")) for n in FRONT])
        + flat_list([flat_list(flow_scratch(size, n, "whole")) for n in MID if n not in FRONT])
        + flat_list([flat_list(flow_scratch(size, n, "whole")) for n in ("q", "f1i", "f1o")]),
        "late",
    )
    big = pl.pallas_call(
        widen_body,
        out_shape=[jax.ShapeDtypeStruct(r.shape, F32) for r in raws]
        + [jax.ShapeDtypeStruct((count, width), F32)] + [jax.ShapeDtypeStruct((1, width), F32)] * 9,
        in_specs=[pl.BlockSpec(memory_space=pl.ANY)] + [pl.BlockSpec(memory_space=pltpu.VMEM)] * 2,
        out_specs=[pl.BlockSpec(memory_space=pl.ANY)] * 21,
        scratch_shapes=[pltpu.VMEM((24, 512, width), BF), pltpu.VMEM((4, 512, width), F32), pltpu.VMEM((9, 1, width), F32), DMA((24,)), DMA((4,)), DMA((10,))],
        compiler_params=pltpu.CompilerParams(vmem_limit_bytes=VMEM_LIMIT),
        name="widen",
    )(flat, total, bns)
    t = [r[0] for r in big[12:]]
    return (output[None], dx0[None]) + tuple(big[:11]) + (
        big[11], t[3], t[4], t[0], t[1], t[2], t[7], t[8], t[5], t[6],
    )


def solution(mesh):
    split = P("slot", "tm", None)
    in_specs = (split, split, P("slot"), P(("tm", "slot"), None)) + (P(),) * 21
    out_specs = (split, split) + (P(),) * 21
    return jax.shard_map(local, mesh=mesh, in_specs=in_specs, out_specs=out_specs, check_vma=False)
```

```python
import math

import jax
import jax.numpy as jnp
from jax import lax
from jax.experimental import pallas as pl
from jax.experimental.pallas import tpu as pltpu
from jax.sharding import PartitionSpec as P

H = 8
HD = 64
LANE = 128
F32 = jnp.float32
BF = jnp.bfloat16
EPS = 1e-05
FILL = -1e30
VMEM_LIMIT = 60 * 2**20


def dot(a, b):
    return lax.dot_general(a, b, (((1,), (0,)), ((), ())), preferred_element_type=F32)


def dot_nt(a, b):
    return lax.dot_general(a, b, (((1,), (1,)), ((), ())), preferred_element_type=F32)


def dot_tn(a, b):
    return lax.dot_general(a, b, (((0,), (0,)), ((), ())), preferred_element_type=F32)


def norm_parts(v):
    mean = jnp.mean(v, axis=-1, keepdims=True)
    cen = v - mean
    r = lax.rsqrt(jnp.mean(cen * cen, axis=-1, keepdims=True) + EPS)
    return cen * r, r


def norm(v, gain):
    u, _ = norm_parts(v)
    return u * gain


def norm_back(v, gain, e):
    u, r = norm_parts(v)
    eg = e * gain
    back = r * (eg - jnp.mean(eg, axis=-1, keepdims=True) - u * jnp.mean(eg * u, axis=-1, keepdims=True))
    return back, jnp.sum(e * u, axis=0, keepdims=True)


def sigmoid(v):
    return 1.0 / (1.0 + jnp.exp(-v))


def swish_and_slope(v):
    s = sigmoid(v)
    sv = s * v
    return sv, s + sv * (1.0 - s)


def cols(p, width=LANE):
    return pl.ds(pl.multiple_of(p * width, width), width)


def lane_half(e):
    lane = lax.broadcasted_iota(jnp.int32, (1, LANE), 1)
    return (lane < HD) if e == 0 else (lane >= HD)


def call(body, outs, ins, scratch=(), name=None):
    return pl.pallas_call(
        body,
        out_shape=[jax.ShapeDtypeStruct(s, d) for s, d in outs],
        in_specs=[
            pl.BlockSpec(memory_space=pltpu.SMEM) if x.dtype == jnp.int32 else pl.BlockSpec(memory_space=pltpu.VMEM)
            for x in ins
        ],
        out_specs=[pl.BlockSpec(memory_space=pltpu.VMEM) for _ in outs],
        scratch_shapes=list(scratch),
        compiler_params=pltpu.CompilerParams(vmem_limit_bytes=VMEM_LIMIT),
        name=name,
    )(*ins)


MESH = pl.DeviceIdType.MESH


class Place:
    def __init__(self):
        tms, slots = lax.axis_size("tm"), lax.axis_size("slot")
        wide = 1 << ((slots.bit_length() - 1) // 2)
        self.size = {"c": 2, "x": tms // 2, "y": wide, "z": slots // wide}
        self.tm, self.slot = lax.axis_index("tm"), lax.axis_index("slot")
        self.at = {
            "c": lax.rem(self.tm, 2),
            "x": lax.div(self.tm, 2),
            "y": lax.rem(self.slot, wide),
            "z": lax.div(self.slot, wide),
        }

    def peer(self, axis, off):
        pos = dict(self.at)
        pos[axis] = lax.rem(pos[axis] + off, self.size[axis])
        return (pos["x"] * 2 + pos["c"], pos["z"] * self.size["y"] + pos["y"]), pos[axis]

    def peers(self, axis):
        return [(off,) + self.peer(axis, off) for off in range(1, self.size[axis])]

    def greet(self, axes):
        bar = pltpu.get_barrier_semaphore()
        count = 0
        for axis in axes:
            for _, dev, _ in self.peers(axis):
                pl.semaphore_signal(bar, inc=1, device_id=dev, device_id_type=MESH)
                count += 1
        return lambda: pl.semaphore_wait(bar, count)


def rows_at(start, size):
    return pl.ds(pl.multiple_of(start, 16), size)


def add_into(dst, start, lanes, terms, size):
    step = 64 if size % 64 == 0 else 16

    def one(i, carry):
        off = pl.multiple_of(i * step, step)
        total = terms[0](off, step).astype(F32)
        for term in terms[1:]:
            total = total + term(off, step).astype(F32)
        dst[pl.ds(pl.multiple_of(start + off, 16), step), lanes] = total.astype(dst.dtype)
        return carry

    lax.fori_loop(0, size // step, one, 0)


GROUP = 2048


class Flow:
    STAGES = 9

    @staticmethod
    def lane_parts(order, size):
        rows = GROUP // 2
        for axis in order[:2]:
            rows //= size[axis]
        return max(1, 16 * size[order[2]] // rows)

    @staticmethod
    def scratch(order, width, size, kind):
        shapes = []
        blk = GROUP // 2
        parts = Flow.lane_parts(order, size)
        for lv, axis in enumerate(order):
            n = size[axis]
            blk = blk * parts // n if lv == 2 else blk // n
            w = width // parts if lv == 2 else width
            if (kind != "front" or lv == 0) and (kind != "back" or lv > 0):
                shapes.append(pltpu.VMEM((n - 1, blk, w), BF))
        if kind != "front":
            shapes.append(pltpu.VMEM((blk, width // parts), BF))
        sems = pltpu.SemaphoreType.DMA
        return shapes + [sems((3,)), sems((2,)) if kind == "front" else sems((8,)), sems((1,))]

    def __init__(self, pc, order, lane, width, kind, src, own, core, out, first, bufs):
        self.ssem, self.rsem, self.lsem = bufs[-3:]
        bufs = list(bufs[:-3])
        self.now = 2 if kind == "back" else 0
        size = pc.size
        lanes = pl.ds(lane, width)
        c = pc.at["c"]
        top = GROUP // 2
        parts = self.lane_parts(order, size)
        blk, rel = [top], [0]
        for lv, axis in enumerate(order):
            if lv < 2:
                blk.append(blk[-1] // size[axis])
                rel.append(rel[-1] + pc.at[axis] * blk[-1])
        low = blk[2] * parts // size[order[2]]

        def share(pos):
            if parts == 1:
                return rel[2] + pos * low, lanes
            at = pl.multiple_of(lane + lax.rem(pos, parts) * (width // parts), LANE)
            return rel[2] + lax.div(pos, parts) * low, pl.ds(at, width // parts)

        ((_, cdev, _),) = pc.peers("c")
        into = [None] * 3
        if kind != "back":
            into[0] = bufs.pop(0)
        if kind != "front":
            into[1], into[2], fin = bufs
        copies = [[(lambda: src.at[rows_at((1 - c) * top, top), lanes], lambda: core.at[:, lanes], cdev)]]
        bytes_of = [lambda: core.at[:, lanes]]
        for lv, axis in enumerate(order):
            cps = []
            for off, dev, pos in pc.peers(axis):
                if lv < 2:
                    s = lambda lv=lv, pos=pos: core.at[rows_at(rel[lv] + pos * blk[lv + 1], blk[lv + 1]), lanes]
                else:
                    s = lambda pos=pos: core.at[rows_at(share(pos)[0], low), share(pos)[1]]
                cps.append((s, lambda lv=lv, off=off: into[lv].at[off - 1], dev))
            copies.append(cps)
            bytes_of.append(lambda lv=lv: into[lv])
        mine = share(pc.at[order[2]])
        out_share = lambda: out.at[rows_at(first + c * top + mine[0], low), mine[1]]
        out_at = lambda lv: out.at[rows_at(first + c * top + rel[lv], blk[lv]), lanes]
        copies.append([(lambda: fin, out_share, dev) for _, dev, _ in pc.peers(order[2])])
        bytes_of.append(
            lambda: out.at[rows_at(first + c * top + rel[2], (size[order[2]] - 1) * low), pl.ds(lane, width // parts)]
        )
        for lv in (2, 1):
            copies.append([(lambda lv=lv: out_at(lv), lambda lv=lv: out_at(lv), dev) for _, dev, _ in pc.peers(order[lv - 1])])
            bytes_of.append(
                lambda lv=lv: out.at[rows_at(first + c * top + rel[lv - 1], (size[order[lv - 1]] - 1) * blk[lv]), lanes]
            )
        copies.append([(lambda: out_at(0), lambda: out_at(0), cdev)])
        bytes_of.append(lambda: out_at(0))
        self.copies, self.bytes_of = copies, bytes_of

        def fold(lv):
            if lv == 0:
                add_into(core, 0, lanes, [lambda o, n: own(o, n, lanes), lambda o, n: core[pl.ds(o, n), lanes]], top)
                return
            row, ln, size_ = (mine + (low,)) if lv == 3 else (rel[lv], lanes, blk[lv])
            terms = [lambda o, n: core[pl.ds(pl.multiple_of(row + o, 16), n), ln]]
            for k in range(size[order[lv - 1]] - 1):
                terms.append(lambda o, n, k=k: into[lv - 1][k, pl.ds(o, n), :])
            if lv == 3:
                add_into(fin, 0, slice(None), terms, size_)
            else:
                add_into(core, row, lanes, terms, size_)

        keep = lambda: pltpu.make_async_copy(fin, out_share(), self.lsem.at[0])

        def s1():
            self.arrived(0)
            fold(0)
            self.start(1)

        def s2():
            if kind != "back":
                self.arrived(1)
                fold(1)
            if kind != "front":
                self.start(2)

        def s3():
            self.arrived(2)
            fold(2)
            self.start(3)

        def s4():
            self.arrived(3)
            fold(3)
            keep().start()
            self.start(4)

        def climb(i):
            def run():
                if i == 0:
                    keep().wait()
                self.arrived(4 + i)
                if i < 3:
                    self.start(5 + i)

            return run

        self.stages = [lambda: self.start(0), s1, s2, s3, s4] + [climb(i) for i in range(4)]
        self.last = 3 if kind == "front" else self.STAGES
        self.first = 2 if kind == "back" else 0

    def make(self, i, src, dst, dev):
        return pltpu.make_async_remote_copy(
            src_ref=src(), dst_ref=dst(), send_sem=self.ssem.at[i % 3], recv_sem=self.rsem.at[i], device_id=dev, device_id_type=MESH
        )

    def start(self, i):
        for src, dst, dev in self.copies[i]:
            self.make(i, src, dst, dev).start()

    def all_of(self, i):
        if len(self.copies[i]) == 1:
            return self.make(i, *self.copies[i][0])
        return self.make(i, self.bytes_of[i], self.bytes_of[i], self.copies[i][0][2])

    def arrived(self, i):
        self.all_of(i).wait_recv()

    def left(self, i):
        if i >= self.first:
            self.all_of(i).wait_send()

    def finish(self):
        self.left(self.last - 2)

    def take(self):
        if self.now >= self.last:
            return lambda: None
        i, self.now = self.now, self.now + 1

        def run():
            self.stages[i]()
            if i > 1:
                self.left(i - 2)

        return run


def advance(flows):
    for flow in flows:
        flow.take()()


MID = {"f2i": 2048, "f2o": 4096, "o": 0}
NAMES = ("f2i", "f2o", "o", "q", "f1o", "f1i")
AXES = {"A": ("y", "x", "z"), "B": ("x", "y", "z"), "X": ("z", "x", "y"), "Y": ("z", "y", "x")}
FRONT = ("f2i",)
LANES = {"f2i": "A2 B1 B1", "f2o": "A2 B1 X1", "o": "A2 B1 X1", "q": "A1 B1 B1 Y1", "f1o": "A1 B1 B1 Y1", "f1i": "A1 B1 A1 B1"}
TURNS = {
    -1: (4, 5, 6, 8, 9, 10, 0, 1, 2,),
    0: (5, 6, 9,),
    1: (4, 8, 10,),
    3: (5, 0,),
    4: (9,),
    5: (6, 1,),
    6: (2,),
    7: (5,),
    8: (6, 9, 0,),
    10: (4, 1, 2,),
    11: (6,),
    12: (5, 9, 8,),
    13: (10, 1, 2,),
    14: (4, 0, 6,),
    15: (10, 5, 9,),
    16: (8, 1, 2,),
    17: (4, 10, 0,),
    18: (12, 8, 13,),
    19: (14, 15, 4,),
    20: (16, 19, 17,),
    21: (18, 12, 13, 14, 15, 6, 0, 1, 2, 20, 21, 22, 17, 23, 0, 12, 1, 2, 13, 14, 18, 16, 6, 15, 17, 12, 8, 21, 10, 13, 19, 6, 23, 20, 16, 14, 4, 18, 22, 19, 17, 15, 21, 13, 12, 5, 20, 8, 23, 22, 19, 14, 16, 9, 18, 13, 21, 5, 20, 17, 15, 22, 5, 23, 4, 16, 14, 19, 10, 9, 18, 13, 15, 21, 4, 9, 20, 13, 19, 22, 12, 23, 16, 17, 14, 18, 8, 14, 20, 8, 21, 17, 23, 22, 17, 18, 12, 10, 16, 15, 18, 19, 12, 21, 10, 20, 16, 15, 23, 19, 22, 21, 20, 23, 22,),
}


def layout(name, size):
    words = LANES[name].split()
    if max(Flow.lane_parts(AXES[word[0]], size) for word in words) > 1:
        words = ["A2", "B2"]
    got, lane = [], 0
    for word in words:
        got.append((AXES[word[0]], lane, int(word[1]) * LANE))
        lane += got[-1][2]
    return got


def flow_scratch(size, name, kind):
    return [Flow.scratch(order, width, size, kind) for order, _, width in layout(name, size)]


def flat_list(lists):
    return [x for part in lists for x in part]


class Taker:
    def __init__(self, refs):
        self.refs = list(refs)

    def __call__(self, n):
        got, self.refs = self.refs[:n], self.refs[n:]
        return got


def make_flows(pc, name, kind, src, own, core, out, first, taker):
    flows = []
    for (order, lane, width), shapes in zip(layout(name, pc.size), flow_scratch(pc.size, name, kind)):
        flows.append(Flow(pc, order, lane, width, kind, src, own, core, out, first, taker(len(shapes))))
    return flows


FLAT = {"f1i": 0, "f1o": 2048, "q": 4096, "k": 4608, "v": 5120, "p": 5632, "o": 6144, "ci": 6656, "co": 7680, "f2i": 8192, "f2o": 10240}
FLAT_ROWS = 12288
ORDER = tuple(FLAT)
FOLDS = {"f1i": 4, "ci": 2, "f2i": 4}
FLAT_SIZE = {n: (list(FLAT.values()) + [FLAT_ROWS])[i + 1] - FLAT[n] for i, n in enumerate(FLAT)}


def ticks(point, plan, p):
    for at, run in plan.items():
        if at % 2 == point:
            pl.when(p == at // 2)(lambda run=run: (run(), None)[1])


class Gather:
    @staticmethod
    def scratch(size, shard_rows, width):
        part, pieces = Gather.cut(shard_rows)
        sems = pltpu.SemaphoreType.DMA((2 * pieces * (size["x"] + 6),))
        return [
            pltpu.VMEM((size["x"], 2, size["z"], size["y"], shard_rows, width), BF),
            pltpu.VMEM((width // LANE, 64, LANE), F32),
            sems,
            sems,
            pltpu.SemaphoreType.REGULAR,
        ]

    @staticmethod
    def cut(shard_rows):
        part = 64 if shard_rows % 64 == 0 else 16
        return part, shard_rows // part

    def __init__(self, pc, wf, bufs):
        self.pc, self.wf = pc, wf
        self.nb, self.scr, self.ssem, self.rsem, self.free = bufs
        self.shard_rows = self.nb.shape[4]
        self.part, self.pieces = self.cut(self.shard_rows)
        self.xs = pc.size["x"]
        self.used = 0
        self.stages = [self.plan(hx, q) for hx in range(2) for q in range(self.pieces)]

    def copies(self, ref, axis, only=None, total=None):
        out = []

        def make(ref, dev, k):
            return pltpu.make_async_remote_copy(
                src_ref=ref, dst_ref=ref, send_sem=self.ssem.at[k], recv_sem=self.rsem.at[k], device_id=dev, device_id_type=MESH
            )

        for off, dev, _ in self.pc.peers(axis):
            if only is not None and off != only:
                continue
            out.append((off, make(ref, dev, self.used)))
            if total is None:
                self.used += 1
        if total is None:
            return out, out
        self.used += 1
        return out, [(0, make(total, dev, self.used - 1))]

    def plan(self, hx, q):
        pc, nb = self.pc, self.nb
        x, c, z, y = (pc.at[a] for a in "xczy")
        rows = pl.ds(q * self.part, self.part)
        across = self.xs // 2
        side = pl.ds(hx * across, across)
        in_half = lambda pos: lax.div(pos, across) == hx
        width = nb.shape[5]
        wide, quarter = pl.ds(0, width // 2), width // 4
        away = pl.ds(3 * quarter, quarter)
        source = jnp.where(in_half(x), x, lax.rem(x + across, self.xs))
        lanes = pl.ds(pl.multiple_of(jnp.where(in_half(x), 2 * quarter, 3 * quarter), LANE), quarter)
        others = {axis: pl.ds(0, pc.size[axis] - 1) for axis in "xyz"}
        along = {
            "xa": self.copies(nb.at[x, c, z, y, rows, wide], "x"),
            "xd": self.copies(nb.at[x, c, z, y, rows, away], "x", across),
            "za": self.copies(nb.at[side, c, z, y, rows, wide], "z", None, nb.at[side, c, others["z"], y, rows, wide]),
            "zb": self.copies(nb.at[source, c, z, y, rows, lanes], "z", None, nb.at[source, c, others["z"], y, rows, lanes]),
            "ya": self.copies(nb.at[side, c, :, y, rows, wide], "y", None, nb.at[side, c, :, others["y"], rows, wide]),
            "yb": self.copies(nb.at[source, c, :, y, rows, lanes], "y", None, nb.at[source, c, :, others["y"], rows, lanes]),
            "xb": self.copies(nb.at[source, c, :, :, rows, lanes], "x", None, nb.at[others["x"], c, :, :, rows, lanes]),
            "c": self.copies(nb.at[side, c, :, :, rows], "c"),
        }

        def each(axis, what, cond=None):
            for off, cp in along[axis][0 if what == "start" else 1]:
                if cond is None:
                    getattr(cp, what)()
                else:
                    pl.when(cond(off))(lambda cp=cp: getattr(cp, what)())

        sends = lambda off: in_half(x)
        gets = lambda off: in_half(lax.rem(x - off + self.xs, self.xs))

        def end():
            each("c", "wait_recv")
            each("xa", "wait_send", sends)
            for axis in ("za", "zb", "ya", "yb", "xb"):
                each(axis, "wait_send")
            if self.part == 64:
                self.mix_half(hx, q)
            elif q == self.pieces - 1:
                self.mix_half(hx, None)

        def done():
            each("c", "wait_send")

        def then(*acts):
            return lambda: [each(*act) for act in acts]

        def let():
            @pl.when(in_half(x))
            def _():
                ((_, cp),) = along["xd"][0]
                cp.wait_send()
                ((_, dev, _),) = [peer for peer in pc.peers("x") if peer[0] == across]
                pl.semaphore_signal(self.free, inc=1, device_id=dev, device_id_type=MESH)

        def allowed():
            pl.when(jnp.logical_not(in_half(x)))(lambda: pl.semaphore_wait(self.free, 1))

        return {
            "X": then(("xa", "start", sends), ("xd", "start", sends)),
            "Z": then(("xa", "wait_recv", gets), ("xd", "wait_recv", gets), ("za", "start"), ("zb", "start")),
            "Y": lambda: (then(("za", "wait_recv"), ("zb", "wait_recv"), ("ya", "start"), ("yb", "start"))(), let()),
            "W": lambda: (each("yb", "wait_recv"), allowed(), each("xb", "start")),
            "C": then(("ya", "wait_recv"), ("xb", "wait_recv"), ("c", "start")),
            "E": end,
            "D": done,
        }

    def run(self, ops):
        for op in ops:
            if 0 <= op[1] < len(self.stages):
                self.stages[op[1]][op[0]]()

    def finish(self):
        for stages in self.stages:
            stages["D"]()

    def noise_at(self, row):
        pc = self.pc
        got = []
        sub = min(64, self.part)
        for i in range(64 // sub):
            at = row + i * sub
            d = lax.div(at, self.shard_rows)
            slots = pc.size["z"] * pc.size["y"]
            tm, sl = lax.div(d, slots), lax.rem(d, slots)
            off = pl.multiple_of(lax.rem(at, self.shard_rows), 16)
            got.append(
                self.nb[lax.div(tm, 2), lax.rem(tm, 2), lax.div(sl, pc.size["y"]), lax.rem(sl, pc.size["y"]), pl.ds(off, sub), :].astype(F32)
            )
        return got[0] if len(got) == 1 else jnp.concatenate(got, axis=0)

    def mix(self, row, base, size, fold):
        wf, scr = self.wf, self.scr
        value = self.noise_at(row)
        if fold == 1:
            at = rows_at(row, 64)
            wf[at, :] = (wf[at, :].astype(F32) + value).astype(BF)
            return
        for b in range(512 // LANE):
            scr[b] = value[:, b * LANE : (b + 1) * LANE]
        high = 64 // fold
        for j in range(fold):
            at = rows_at(base + j * (size // fold) + lax.div(row - base, fold), high)
            for b in range(512 // LANE):
                lanes = pl.ds(b * LANE, LANE)
                wf[at, lanes] = (wf[at, lanes].astype(F32) + scr[b, pl.ds(j, high, stride=fold), :]).astype(BF)

    def mix_half(self, hx, q):
        for name in ORDER:
            base, size, fold = FLAT[name], FLAT_SIZE[name], FOLDS.get(name, 1)
            if (base < FLAT_ROWS // 2) != (hx == 0):
                continue
            begin, end = base // 64, (base + size) // 64
            start, stride = (begin, 1) if q is None else (begin + (q - begin) % self.pieces, self.pieces)
            lax.fori_loop(
                0, (end - start + stride - 1) // stride,
                lambda i, t: (self.mix((start + i * stride) * 64, base, size, fold), t)[1], 0,
            )


class KeysAll:
    @staticmethod
    def scratch(xs):
        n = 2 * xs - 1
        sems = pltpu.SemaphoreType.DMA((H // 2, n))
        return [sems, sems]

    def __init__(self, pc, kv, bufs):
        self.pc, self.kv = pc, kv
        self.ssem, self.rsem = bufs

    def copy(self, p, k, tm, dev):
        ref = self.kv.at[p, :, tm]
        return pltpu.make_async_remote_copy(
            src_ref=ref, dst_ref=ref, send_sem=self.ssem.at[p, k], recv_sem=self.rsem.at[p, k], device_id=dev, device_id_type=MESH
        )

    def core(self, p):
        ((_, dev, _),) = self.pc.peers("c")
        return [self.copy(p, 0, self.pc.tm, dev)]

    def line(self, p):
        return [self.copy(p, off, self.pc.tm, dev) for off, dev, _ in self.pc.peers("x")]

    def relay(self, p):
        ((_, dev, _),) = self.pc.peers("c")
        xs = self.pc.size["x"]
        out = []
        for off in range(1, xs):
            source = lax.rem(self.pc.at["x"] - off + xs, xs) * 2 + self.pc.at["c"]
            out.append(self.copy(p, xs - 1 + off, source, dev))
        return out

    def send(self, p):
        for cp in self.core(p):
            cp.start()

    def send_line(self, p):
        for cp in self.line(p):
            cp.start()

    def forward(self, p):
        for come, on in zip(self.line(p), self.relay(p)):
            come.wait_recv()
            on.start()

    def ready(self, p):
        for cp in self.core(p) + self.relay(p):
            cp.wait_recv()

    def sent(self, p):
        for cp in self.line(p) + self.core(p) + self.relay(p):
            cp.wait_send()


def angle_tables(hi, lo, rates):
    for ref, step in ((hi, 64.0), (lo, 1.0)):
        count = ref.shape[1]
        angle = lax.broadcasted_iota(jnp.int32, (count, rates.shape[1]), 0).astype(F32) * step * rates
        ref[0] = jnp.sin(angle)
        ref[1] = jnp.cos(angle)


def angle_block(hi, lo, m):
    hs, hc = hi[0, pl.ds(m, 1), :], hi[1, pl.ds(m, 1), :]
    ls, lc = lo[0], lo[1]
    return hs * lc + hc * ls, hc * lc - hs * ls


def early_body(*refs):
    lens, noise, raws = refs[0], refs[1], refs[2:13]
    x_ref, gain1, gain2, pos_u, pos_v = refs[13:18]
    wn, x1_out, pre_out, a2_out, qu_out, qv_out, kv_out, trig_out, sin_out, cos_out, att_out, probs = refs[18:30]
    wf, flat, x1_ref, pre_ref, a2_ref, qu, qv, kv, trig, sin, cos, hi, lo, att, pbuf, wsem, osem, psem = refs[30:48]
    bufs = refs[48:]
    pc = Place()
    rows, width = x_ref.shape
    half = width // 2
    tms = lax.axis_size("tm")
    frames = rows * tms
    met = pc.greet("cxyz")
    loads = []
    for name, raw in zip(ORDER, raws):
        for j in range(FOLDS.get(name, 1)):
            size = FLAT_SIZE[name] // FOLDS.get(name, 1)
            dst = wf.at[pl.ds(FLAT[name] + j * size, size), :]
            loads.append(pltpu.make_async_copy(raw.at[:, pl.ds(j * 512, 512)], dst, wsem.at[len(loads)]))
            loads[-1].start()
    gather = Gather(pc, wf, bufs[:5])
    keys = KeysAll(pc, kv, bufs[5:7])

    def unfold(i, carry):
        for r in range(8):
            for b in range(width // LANE):
                at = pl.ds(pl.multiple_of((i * 8 + r) * width + b * LANE, LANE), LANE)
                flat[b, pl.ds(i * 8 + r, 1), :] = noise[:, at].astype(F32)
        return carry

    shard_rows = gather.shard_rows
    lax.fori_loop(0, shard_rows // 8, unfold, 0)
    for b in range(width // LANE):
        gather.nb[pc.at["x"], pc.at["c"], pc.at["z"], pc.at["y"], :, pl.ds(b * LANE, LANE)] = flat[b].astype(BF)
    rates = jnp.exp(lax.broadcasted_iota(jnp.int32, (1, half), 1).astype(F32) * (-2.0 * math.log(10000.0) / width))
    angle_tables(hi, lo, rates)

    def angles(m, carry):
        s, c = angle_block(hi, lo, m)
        at = rows_at(m * 64, 64)
        trig[at, pl.ds(0, half)] = s.astype(BF)
        trig[at, pl.ds(half, half)] = c.astype(BF)
        return carry

    def own_angles(m, carry):
        s, c = angle_block(hi, lo, pc.tm * (rows // 64) + m)
        sin[rows_at(m * 64, 64), :] = s
        cos[rows_at(m * 64, 64), :] = c
        return carry

    lax.fori_loop(0, frames // 64, angles, 0)
    lax.fori_loop(0, rows // 64, own_angles, 0)
    met()
    n = gather.pieces
    gather.run([("X", i) for i in range(2 * n)])
    gather.run([("Z", 0), ("Z", 1)])
    for cp in loads:
        cp.wait()
    outs = []

    def put(src, dst):
        cp = pltpu.make_async_copy(src, dst, osem.at[len(outs)])
        cp.start()
        outs.append(cp)

    x = x_ref[...].astype(F32)
    a1 = norm(x, gain1[...]).astype(BF)
    for t in range(2, n + 2):
        gather.run([("Z", t), ("Y", t - 2), ("W", t - 3), ("C", t - 4), ("E", t - 5)])
    gather.run([("W", n - 1), ("C", n - 2), ("E", n - 3), ("C", n - 1), ("E", n - 2), ("Z", n + 2), ("E", n - 1)])
    part = lambda name: wf.at[pl.ds(FLAT[name], FLAT_SIZE[name]), :]
    x1 = x + 0.5 * ffn_forward(a1, part("f1i"), part("f1o"), pre_ref)
    x1_ref[...] = x1
    a2 = norm(x1, gain2[...]).astype(BF)
    a2_ref[...] = a2
    k = dot(a2, part("k")[...]).astype(BF)
    v = dot(a2, part("v")[...]).astype(BF)
    for p in range(H // 2):
        kv[p, 0, pc.tm] = k[:, p * LANE : (p + 1) * LANE]
        kv[p, 1, pc.tm] = v[:, p * LANE : (p + 1) * LANE]
        if p == 0:
            keys.send_line(0)
        keys.send(p)
    gather.run([("Z", n + 3), ("Y", n), ("Y", n + 1)])
    q = dot(a2, part("q")[...])
    scale = HD**-0.5
    qu[...] = ((q + pos_u[...]).astype(BF).astype(F32) * scale).astype(BF)
    qv[...] = ((q + pos_v[...]).astype(BF).astype(F32) * scale).astype(BF)
    for src, dst in ((x1_ref, x1_out), (pre_ref, pre_out), (a2_ref, a2_out), (qu, qu_out), (qv, qv_out), (trig, trig_out), (sin, sin_out), (cos, cos_out)):
        put(src, dst)
    put(wf.at[pl.ds(0, FLAT_ROWS // 2), :], wn.at[pl.ds(0, FLAT_ROWS // 2), :])
    steps = {
        0: "W0 Y2 Z4", 1: "W1 Y3 Z5", 2: "C0 W2 Y4", 3: "E0 W3 Y5", 4: "C1 W4", 5: "E1 C2 W5", 6: "E2 C3", 7: "E3 C4 C5", 8: "E4 E5",
    }
    if n != 6:
        order = (("Z", 4), ("Y", 2), ("W", 0), ("C", 0), ("E", 0))
        steps = {8: " ".join("%s%d" % (op, i) for op, low in order for i in range(low, n))}
    steps = {at: [(op[0], n + int(op[1:])) for op in text.split()] for at, text in steps.items()}
    plan = {at: (lambda ops=ops: gather.run(ops)) for at, ops in steps.items() if at < H}
    ok = lax.broadcasted_iota(jnp.int32, (1, frames), 1) < lens[0]
    w_pos = part("p")
    store = lambda p, e: pltpu.make_async_copy(pbuf.at[e], probs.at[2 * p + e], psem.at[e])

    def pair(p, carry):
        at = cols(p)
        mixed = None
        for e in range(2):
            mine = lane_half(e)
            qve = jnp.where(mine, qv[:, at], jnp.zeros((), BF))
            que = jnp.where(mine, qu[:, at], jnp.zeros((), BF))
            turned = dot_nt(qve, w_pos[:, at])
            a_s, a_c = turned[:, :half], turned[:, half:]
            b_c = (a_s * sin[...] + a_c * cos[...]).astype(BF)
            b_s = (a_c * sin[...] - a_s * cos[...]).astype(BF)
            if e == 0:
                pl.when(p == 1)(lambda: keys.send_line(3))
                pl.when(p == 0)(lambda: (keys.forward(0), keys.send_line(1))[1])
                keys.ready(p)
            else:
                pl.when(p == 0)(lambda: keys.send_line(2))
            s = dot_nt(jnp.concatenate([b_s, b_c, que], axis=1), jnp.concatenate([trig[...], kv[p, 0].reshape(frames, LANE)], axis=1))
            s = jnp.where(ok, s, FILL)
            m = jnp.max(s, axis=-1, keepdims=True)
            ex = jnp.exp(s - m)
            tot = jnp.sum(ex, axis=-1, keepdims=True)
            low = (ex * (1.0 / tot)).astype(BF)
            pl.when(p > 0)(lambda: store(p - 1, e).wait())
            pbuf[e] = low
            store(p, e).start()
            got = dot(low, kv[p, 1].reshape(frames, LANE))
            mixed = got if e == 0 else jnp.where(mine, got, mixed)
            if e == 1:
                pl.when(p < H // 2 - 1)(lambda: keys.forward(p + 1))
            ticks(e, plan, p)
        att[:, at] = mixed.astype(BF)
        return carry

    lax.fori_loop(0, H // 2, pair, 0)
    put(kv, kv_out)
    put(att, att_out)
    gather.run(steps[8])
    put(wf.at[pl.ds(FLAT_ROWS // 2, FLAT_ROWS // 2), :], wn.at[pl.ds(FLAT_ROWS // 2, FLAT_ROWS // 2), :])
    for e in range(2):
        store(H // 2 - 1, e).wait()
    for p in range(H // 2):
        keys.sent(p)
    gather.finish()
    for cp in outs:
        cp.wait()


def chunk(c):
    return pl.ds(pl.multiple_of(c * 512, 512), 512)


def ffn_forward(normed, w_in, w_out, pre_ref):
    def one(c, acc):
        pre = dot(normed, w_in[chunk(c), :])
        pre_ref[:, chunk(c)] = pre
        return acc + dot((pre * sigmoid(pre)).astype(BF), w_out[chunk(c), :])

    return lax.fori_loop(0, w_in.shape[0] // 512, one, jnp.zeros((normed.shape[0], w_out.shape[1]), F32))


def ffn_through(g_low, w_in, w_out, pre_ref, hid_ref, dpre_ref):
    def one(c, acc):
        sw, slope = swish_and_slope(pre_ref[:, chunk(c)])
        hid_ref[:, chunk(c)] = sw.astype(BF)
        dpre = (dot_nt(g_low, w_out[chunk(c), :]) * slope).astype(BF)
        dpre_ref[:, chunk(c)] = dpre
        return acc + dot_nt(dpre, w_in[chunk(c), :])

    return lax.fori_loop(0, w_in.shape[0] // 512, one, jnp.zeros(g_low.shape, F32))


def ffn_in_grad(normed, dpre_ref, gin_ref):
    normed_t = normed.T

    def one(c, carry):
        gin_ref[chunk(c), :] = dot(normed_t, dpre_ref[:, chunk(c)]).astype(gin_ref.dtype)
        return carry

    lax.fori_loop(0, gin_ref.shape[0] // 512, one, 0)


def ffn_out_grad(g_low, hid_ref, gout_ref):
    def one(c, carry):
        gout_ref[chunk(c), :] = dot_tn(hid_ref[:, chunk(c)], g_low).astype(gout_ref.dtype)
        return carry

    lax.fori_loop(0, gout_ref.shape[0] // 512, one, 0)


def ffn_hidden(pre_ref, hid_ref):
    def one(c, carry):
        pre = pre_ref[:, chunk(c)]
        hid_ref[:, chunk(c)] = (pre * sigmoid(pre)).astype(BF)
        return carry

    lax.fori_loop(0, pre_ref.shape[1] // 512, one, 0)


class Fetch:
    def __init__(self, sems):
        self.sems, self.n = sems, 0

    def __call__(self, src, dst):
        cp = pltpu.make_async_copy(src, dst, self.sems.at[self.n])
        self.n += 1
        cp.start()
        return cp


def part_of(wn, name):
    return wn.at[pl.ds(FLAT[name], FLAT_SIZE[name]), :]


def valid_rows(lens, rows):
    first = lax.axis_index("tm") * rows
    return ((first + lax.broadcasted_iota(jnp.int32, (rows, 1), 0)) < lens[0]).astype(F32)


def spread(ext, start, value):
    value = value.astype(F32)
    for b in range(ext.shape[0]):
        ext[b, pl.ds(start, value.shape[0]), :] = value[:, b * LANE : (b + 1) * LANE]


def tap_sum(ext, taps, out_ref, offset):
    count = taps.shape[0]
    rows = out_ref.shape[0]
    block = 64 if rows % 64 == 0 else 16

    def one(i, carry):
        for b in range(ext.shape[0]):
            at = pl.ds(b * LANE, LANE)
            acc = jnp.zeros((block, LANE), F32)
            for k in range(count):
                acc = acc + taps[pl.ds(k, 1), at] * ext[b, pl.ds(i * block + offset(k), block), :]
            out_ref[pl.ds(pl.multiple_of(i * block, block), block), at] = acc
        return carry

    lax.fori_loop(0, rows // block, one, 0)


class Totals:
    @staticmethod
    def scratch(tms, slots, packed):
        n = tms + slots - 2
        return [
            pltpu.VMEM((tms, packed, LANE), F32),
            pltpu.VMEM((slots, packed, LANE), F32),
            pltpu.SemaphoreType.DMA((n,)),
            pltpu.SemaphoreType.DMA((n,)),
        ]

    def __init__(self, pc, bufs):
        self.pc, self.bufs = pc, bufs

    def begin(self, value):
        self.sent = []
        self.cps = self.send(0, value)

    def turn(self):
        self.cps = self.send(1, self.end(0))

    def done(self):
        value = self.end(1)
        for cp in self.sent:
            cp.wait_send()
        return value

    def send(self, i, value):
        pc, buf = self.pc, self.bufs[i]
        ssem, rsem = self.bufs[2:]
        me = (pc.tm, pc.slot)[i]
        buf[me] = value
        n = buf.shape[0]
        for off in range(1, n):
            to = lax.rem(me + off, n)
            k = off - 1 + i * (self.bufs[0].shape[0] - 1)
            cp = pltpu.make_async_remote_copy(
                src_ref=buf.at[me], dst_ref=buf.at[me], send_sem=ssem.at[k], recv_sem=rsem.at[k],
                device_id=(to, pc.slot) if i == 0 else (pc.tm, to), device_id_type=MESH,
            )
            cp.start()
            self.sent.append(cp)
        return self.sent[-(n - 1) :]

    def end(self, i):
        for cp in self.cps:
            cp.wait_recv()
        buf = self.bufs[i]
        value = buf[0]
        for j in range(1, buf.shape[0]):
            value = value + buf[j]
        return value


def packed(rows):
    return jnp.concatenate([row[:, at : at + LANE] for row in rows for at in range(0, row.shape[1], LANE)], axis=0)


def unpacked(value, row, width):
    n = width // LANE
    return jnp.concatenate([value[row * n + j : row * n + j + 1, :] for j in range(n)], axis=1)


def greet_rows(pc, tms, slots):
    bar = pltpu.get_barrier_semaphore()
    for off in range(1, tms):
        pl.semaphore_signal(bar, inc=1, device_id=(lax.rem(pc.tm + off, tms), pc.slot), device_id_type=MESH)
    for off in range(1, slots):
        pl.semaphore_signal(bar, inc=1, device_id=(pc.tm, lax.rem(pc.slot + off, slots)), device_id_type=MESH)
    pl.semaphore_wait(bar, tms + slots - 2)


def middle_body(
    lens, att, x1_ref, cot, wn, taps, bn_gain, bn_bias, gain3, gain4, gain5,
    out_h, dx2_h, datt_h, g_h, smalls_ref, bns_ref, cores,
    w_o, w_ci, w_co, w_f2i, w_f2o, fsem, early, late, hsem, gm_ref, ddwo_ref, z_ref, ext, ext2, dwo_ref, pre_ref, dgm_ref, acc, x2_ref, core, out_ref, dx2_ref, datt_ref, g_ref, hid_ref, dpre_ref, csem, *bufs,
):
    pc = Place()
    tms, slots = lax.axis_size("tm"), lax.axis_size("slot")
    rows, width = x1_ref.shape
    count = taps.shape[0]
    fetch, put = Fetch(fsem), Fetch(csem)
    outs = []
    got = {n: fetch(part_of(wn, n), d) for n, d in (("o", w_o), ("ci", w_ci), ("co", w_co), ("f2i", w_f2i), ("f2o", w_f2o))}
    greet_rows(pc, tms, slots)
    taker = Taker(bufs)
    totals = Totals(pc, taker(4)), Totals(pc, taker(4))
    flows = []
    for i, name in enumerate(FRONT):
        src = g_ref.at[pl.ds(MID[name], GROUP), :]
        half_rows = lambda o, n, lanes, src=src: src[pl.ds(pl.multiple_of(pc.at["c"] * (GROUP // 2) + o, 16), n), lanes]
        flows += make_flows(pc, name, "front", src, half_rows, core.at[i], None, 0, taker)

    def halo(src, dst, k, step):
        dev = (lax.rem(pc.tm + step + tms, tms), pc.slot)
        return pltpu.make_async_remote_copy(
            src_ref=src, dst_ref=dst, send_sem=hsem.at[2 * k], recv_sem=hsem.at[2 * k + 1], device_id=dev, device_id_type=MESH
        )

    got["o"].wait()
    x2 = x1_ref[...] + dot(att[...], w_o[...])
    x2_ref[...] = x2
    a3 = norm(x2, gain3[...]).astype(BF)
    got["ci"].wait()
    z1 = dot(a3, w_ci[pl.ds(0, width), :])
    z2 = dot(a3, w_ci[pl.ds(width, width), :])
    z_ref[:, pl.ds(0, width)] = z1
    z_ref[:, pl.ds(width, width)] = z2
    ok = valid_rows(lens, rows)
    gm_ref[...] = (z1 * sigmoid(z2) * ok).astype(BF)
    cp = halo(gm_ref.at[pl.ds(rows - count, count), :], early, 0, 1)
    cp.start()
    spread(ext, count, gm_ref[...])
    cp.wait()
    spread(ext, 0, jnp.where(pc.tm > 0, early[...], jnp.zeros((), BF)))
    tap_sum(ext, taps, dwo_ref, lambda k: k + 1)
    dwo = dwo_ref[...]
    dwv = dwo * ok
    totals[0].begin(
        packed(
            [
                jnp.sum(dwv, axis=0, keepdims=True),
                jnp.sum(dwv * dwv, axis=0, keepdims=True),
                jnp.zeros((1, 2 * width), F32) + jnp.sum(ok, axis=0, keepdims=True),
            ]
        )
    )
    totals[0].turn()
    sums = totals[0].done()
    total = sums[2 * width // LANE : 2 * width // LANE + 1, 0:1]
    mu = unpacked(sums, 0, width) / total
    inv = lax.rsqrt(unpacked(sums, 1, width) / total - mu * mu + EPS)
    xhat = (dwo_ref[...] - mu) * inv
    sw, slope = swish_and_slope(xhat * bn_gain[...] + bn_bias[...])
    sw = sw.astype(BF)
    got["co"].wait()
    x3 = x2_ref[...] + dot(sw, w_co[...])
    a4 = norm(x3, gain4[...]).astype(BF)
    got["f2i"].wait()
    got["f2o"].wait()
    x4 = x3 + 0.5 * ffn_forward(a4, w_f2i, w_f2o, pre_ref)
    out_ref[...] = norm(x4, gain5[...]).astype(BF)
    outs.append(put(out_ref, out_h))
    dx4, gg5 = norm_back(x4, gain5[...], cot[...].astype(F32))
    g4 = (0.5 * dx4).astype(BF)
    lo = FLAT["o"]
    da4 = ffn_through(g4, w_f2i, w_f2o, pre_ref, hid_ref, dpre_ref)
    back, gg4 = norm_back(x3, gain4[...], da4)
    dx3 = dx4 + back
    g3 = dx3.astype(BF)
    dbn = dot_nt(g3, w_co[...]) * slope
    totals[1].begin(packed([jnp.sum(dbn * xhat, axis=0, keepdims=True), jnp.sum(dbn, axis=0, keepdims=True)]))
    part = lambda name: g_ref.at[pl.ds(MID[name], GROUP), :]
    ffn_in_grad(a4, dpre_ref, part("f2i"))
    totals[1].turn()
    advance(flows)
    ffn_out_grad(g4, hid_ref, part("f2o"))
    g_ref[pl.ds(FLAT["co"] - lo, width), :] = dot_tn(sw, g3).astype(BF)
    for name in ("f2i", "f2o"):
        if name not in FRONT:
            outs.append(put(part(name), g_h.at[pl.ds(MID[name], GROUP), :]))
    sums2 = totals[1].done()
    gain_sum, bias_sum = unpacked(sums2, 0, width), unpacked(sums2, 1, width)
    bns_ref[0:1, :] = gain_sum
    bns_ref[1:2, :] = bias_sum
    bns_ref[2:8, :] = jnp.zeros((6, width), F32)
    ddwo_ref[...] = (bn_gain[...] * inv * (dbn - ok * (bias_sum + xhat * gain_sum) / total)).astype(BF)
    cp = halo(ddwo_ref.at[pl.ds(0, count), :], late, 1, -1)
    cp.start()
    advance(flows)
    spread(ext2, 0, ddwo_ref[...])
    cp.wait()
    spread(ext2, rows, jnp.where(pc.tm < tms - 1, late[...], jnp.zeros((), BF)))
    tap_sum(ext2, taps, dgm_ref, lambda k: count - 1 - k)
    block = 64 if rows % 64 == 0 else 16
    for b in range(ext.shape[0]):
        acc[...] = jnp.zeros(acc.shape, F32)

        def one(i, carry, b=b):
            mine = ext2[b, pl.ds(pl.multiple_of(i * block, block), block), :]
            for k in range(count):
                prod = mine * ext[b, pl.ds(i * block + k + 1, block), :]
                acc[k] = acc[k] + jnp.sum(prod.reshape(block // 8, 8, LANE), axis=0)
            return carry

        lax.fori_loop(0, rows // block, one, 0)
        smalls_ref[pl.ds(0, count), pl.ds(b * LANE, LANE)] = jnp.sum(acc[...], axis=1)
    z1 = z_ref[:, pl.ds(0, width)]
    sg = sigmoid(z_ref[:, pl.ds(width, width)])
    dg = dgm_ref[...] * ok
    dz1 = (dg * sg).astype(BF)
    dz2 = (dg * z1 * sg * (1.0 - sg)).astype(BF)
    a3t = norm(x2_ref[...], gain3[...]).astype(BF).T
    g_ref[pl.ds(FLAT["ci"] - lo, width), :] = dot(a3t, dz1).astype(BF)
    g_ref[pl.ds(FLAT["ci"] - lo + width, width), :] = dot(a3t, dz2).astype(BF)
    da3 = dot_nt(dz1, w_ci[pl.ds(0, width), :]) + dot_nt(dz2, w_ci[pl.ds(width, width), :])
    back, gg3 = norm_back(x2_ref[...], gain3[...], da3)
    dx2 = dx3 + back
    dx2_ref[...] = dx2
    outs.append(put(dx2_ref, dx2_h))
    g2 = dx2.astype(BF)
    g_ref[pl.ds(0, width), :] = dot_tn(att[...], g2).astype(BF)
    outs.append(put(g_ref.at[pl.ds(0, GROUP), :], g_h.at[pl.ds(0, GROUP), :]))
    datt_ref[...] = dot_nt(g2, w_o[...]).astype(BF)
    outs.append(put(datt_ref, datt_h))
    advance(flows)
    outs.append(put(core, cores))
    smalls_ref[pl.ds(count, 8), :] = jnp.concatenate([gg3, gg4, gg5, jnp.zeros((5, width), F32)], axis=0)
    for flow in flows:
        flow.finish()
    for cp in outs:
        cp.wait()


class Butterfly:
    @staticmethod
    def scratch(devices, shape):
        n = devices.bit_length() - 1
        return [pltpu.VMEM((n,) + shape, F32), pltpu.SemaphoreType.DMA((n,)), pltpu.SemaphoreType.DMA((n,))]

    def __init__(self, pc, value, bufs):
        self.value, (self.got, self.ssem, self.rsem) = value, bufs
        self.devs = []
        for axis, me in (("tm", pc.tm), ("slot", pc.slot)):
            bit = 1
            while bit < lax.axis_size(axis):
                to = me + bit - 2 * bit * lax.rem(lax.div(me, bit), 2)
                self.devs.append((to, pc.slot) if axis == "tm" else (pc.tm, to))
                bit *= 2

    def copy(self, k):
        return pltpu.make_async_remote_copy(
            src_ref=self.value, dst_ref=self.got.at[k], send_sem=self.ssem.at[k], recv_sem=self.rsem.at[k],
            device_id=self.devs[k], device_id_type=MESH,
        )

    def stage(self, k):
        if k > 0:
            self.copy(k - 1).wait()
            self.value[...] = self.value[...] + self.got[k - 1]
        if k < len(self.devs):
            self.copy(k).start()


GROUP = 2048


class KeyGrads:
    @staticmethod
    def scratch(tms, rows):
        pairs, xs = H // 2, tms // 2
        sems = pltpu.SemaphoreType.DMA((pairs, xs + 1))
        return [
            pltpu.VMEM((pairs, 2, 2, tms, HD, rows), BF),
            pltpu.VMEM((pairs, 2, tms, HD, rows), BF),
            pltpu.VMEM((xs - 1, pairs, 2, 2, HD, rows), BF),
            pltpu.VMEM((pairs, 2, 2, HD, rows), BF),
            pltpu.VMEM((pairs, 2, HD, rows), BF),
            sems,
            sems,
        ]

    def __init__(self, pc, bufs):
        self.pc = pc
        self.mine, self.core, self.line, self.both, self.got, self.ssem, self.rsem = bufs

    def put(self, p, kind, e, value):
        rows = self.mine.shape[-1]
        for t in range(self.mine.shape[3]):
            self.mine[p, kind, e, t] = value[:, t * rows : (t + 1) * rows].astype(BF)

    def copy(self, p, k, src, dst, dev):
        return pltpu.make_async_remote_copy(
            src_ref=src, dst_ref=dst, send_sem=self.ssem.at[p, k], recv_sem=self.rsem.at[p, k], device_id=dev, device_id_type=MESH
        )

    def first(self, p):
        ((_, dev, _),) = self.pc.peers("c")
        return [self.copy(p, 0, self.mine.at[p, :, 1 - self.pc.at["c"]], self.core.at[p], dev)]

    def second(self, p):
        return [
            self.copy(p, off, self.core.at[p, :, pl.ds(2 * pos, 2)], self.line.at[off - 1, p], dev) for off, dev, pos in self.pc.peers("x")
        ]

    def third(self, p):
        ((_, dev, _),) = self.pc.peers("c")
        return [self.copy(p, self.pc.size["x"], self.both.at[p, :, 1 - self.pc.at["c"]], self.got.at[p], dev)]

    def step(self, p, i):
        c, x = self.pc.at["c"], self.pc.at["x"]
        if i == 1:
            for cp in self.first(p):
                cp.wait_recv()
            for kind in range(2):
                for t in range(self.core.shape[2]):
                    total = self.core[p, kind, t].astype(F32) + self.mine[p, kind, c, t].astype(F32)
                    self.core[p, kind, t] = total.astype(BF)
        if i == 2:
            for cp in self.second(p):
                cp.wait_recv()
            for kind in range(2):
                for t in range(2):
                    total = self.core[p, kind, 2 * x + t].astype(F32)
                    for j in range(self.line.shape[0]):
                        total = total + self.line[j, p, kind, t].astype(F32)
                    self.both[p, kind, t] = total.astype(BF)
        if i == 3:
            for cp in self.third(p):
                cp.wait_recv()
            for cp in self.first(p) + self.second(p):
                cp.wait_send()
            return
        for cp in (self.first, self.second, self.third)[i](p):
            cp.start()

    def sent(self, p):
        for cp in self.third(p):
            cp.wait_send()

    def collect(self, p, kind, dst):
        c = self.pc.at["c"]
        own = self.both[p, kind, c]
        other = self.got[p, kind]
        dst[pl.ds(pl.multiple_of(p * LANE + c * HD, HD), HD), :] = own
        dst[pl.ds(pl.multiple_of(p * LANE + (1 - c) * HD, HD), HD), :] = other


def late_body(
    qu_h, qv_h, kv_h, wn, trig_h, sin_h, cos_h, probs, datt_h, att_h, g_mid, cores_h, a2_h, x1_h, dx2_h, x_h, pre_h, smalls2, gain2, gain1,
    dx0_ref, flat, total_ref,
    qu, qv, kv, w_p, trig, sin, cos, datt, att, a2, x1_ref, dx2_ref, x_ref, wqkv, own, core, psem, fsem,
    dq_ref, dkt, dvt, gpost, qut, qvt, datt_t, g_low, *bufs,
):
    pc = Place()
    rows = qu.shape[0]
    half = sin.shape[1]
    fetch = Fetch(fsem)
    c = pc.at["c"]
    whole = [name for name in MID if name not in FRONT]
    met = pc.greet("cxyz")
    owns = [fetch(g_mid.at[rows_at(MID[name] + c * (GROUP // 2), GROUP // 2), :], own.at[i]) for i, name in enumerate(whole)]
    owns += [fetch(cores_h.at[i], core.at[i]) for i in range(len(FRONT))]
    needed = [fetch(s, d) for s, d in ((qu_h, qu), (datt_h, datt), (att_h, att), (kv_h, kv))]

    def copies(first, pairs):
        return lambda: [pltpu.make_async_copy(s, d, fsem.at[first + i]) for i, (s, d) in enumerate(pairs)]

    second = copies(fetch.n, ((qv_h, qv), (part_of(wn, "p"), w_p), (trig_h, trig), (sin_h, sin), (cos_h, cos)))
    later = copies(
        fetch.n + 5, ((a2_h, a2), (x1_h, x1_ref), (dx2_h, dx2_ref), (x_h, x_ref), (wn.at[pl.ds(FLAT["q"], 1536), :], wqkv))
    )
    last_in = lambda pre_ref, w1: copies(fetch.n + 10, ((pre_h, pre_ref), (wn.at[pl.ds(0, 4096), :], w1)))()
    taker = Taker(bufs)
    keys = KeyGrads(pc, taker(7))
    fly = Butterfly(pc, total_ref, taker(3))
    groups = {}
    for i, name in enumerate(FRONT):
        groups[name] = make_flows(pc, name, "back", None, None, core.at[i], flat, FLAT[name], taker)
    for i, name in enumerate(whole):
        mine = lambda o, n, lanes, i=i: own[i, pl.ds(o, n), lanes]
        src = g_mid.at[pl.ds(MID[name], GROUP), :]
        groups[name] = make_flows(pc, name, "whole", src, mine, core.at[len(FRONT) + i], flat, FLAT[name], taker)
    for i, name in enumerate(("q", "f1i", "f1o")):
        at = FLAT[name]
        mine = lambda o, n, lanes, at=at: g_low[pl.ds(pl.multiple_of(at + c * (GROUP // 2) + o, 16), n), lanes]
        groups[name] = make_flows(pc, name, "whole", g_low.at[pl.ds(at, GROUP), :], mine, core.at[3 + i], flat, at, taker)
    def run(point):
        picked = [(NAMES[token // 4], token % 4) for token in TURNS.get(point, ())]
        stages = [groups[name][i].take() for name, i in picked if i < len(groups[name])]
        return lambda: [stage() for stage in stages]

    first = run(-1)
    plan = {at: run(at) for at in range(2 * H)}
    after = lambda point: run(point)()
    scale = HD**-0.5

    def scores(p, pbuf, load):
        at = cols(p)
        for e in range(2):
            mine = lane_half(e)
            part = pl.ds(pl.multiple_of(p * LANE + e * HD, HD), HD)
            dm = jnp.where(mine, datt[:, at], jnp.zeros((), BF))
            inner = jnp.sum(dm.astype(F32) * att[:, at].astype(F32), axis=-1, keepdims=True)
            dp = dot_nt(dm, kv[p, 1].reshape(-1, LANE))
            load(2 * p + e).wait()
            low_p = pbuf[2 * p + e]
            ds = (low_p.astype(F32) * (dp - inner)).astype(BF)
            pbuf[2 * p + e] = ds
            keys.put(p, 0, e, dot(qut[part, :], ds))
            keys.put(p, 1, e, dot(datt_t[part, :], low_p))
            if e == 0:
                pl.when(p > 0)(lambda: keys.step(p - 1, 1))
            else:
                keys.step(p, 0)
            ticks(e, plan, p)

    def queries(p, pbuf):
        at = cols(p)
        dqu = dqv = None
        for e in range(2):
            mine = lane_half(e)
            part = pl.ds(pl.multiple_of(p * LANE + e * HD, HD), HD)
            ds = pbuf[2 * p + e]
            back = dot(ds, jnp.concatenate([trig[...], kv[p, 0].reshape(-1, LANE)], axis=1))
            db_s, db_c, part_u = back[:, :half], back[:, half : 2 * half], back[:, 2 * half :]
            da_s = (db_c * sin[...] - db_s * cos[...]).astype(BF)
            da_c = (db_c * cos[...] + db_s * sin[...]).astype(BF)
            turned = jnp.concatenate([da_s, da_c], axis=1)
            gpost[part, :] = dot(qvt[part, :], turned)
            part_v = dot(turned, w_p[:, at])
            dqu = part_u if e == 0 else jnp.where(mine, part_u, dqu)
            dqv = part_v if e == 0 else jnp.where(mine, part_v, dqv)
            if e == 0:
                pl.when(p == 0)(lambda: keys.step(last, 1))
            else:
                keys.step(p, 2)
            ticks(e, plan, p + H // 2)
        dqu = dqu * scale
        dqv = dqv * scale
        dq_ref[:, at] = (dqu + dqv).astype(BF)
        total_ref[pl.ds(37, 1), at] = jnp.sum(dqu, axis=0, keepdims=True)
        total_ref[pl.ds(38, 1), at] = jnp.sum(dqv, axis=0, keepdims=True)

    last = H // 2 - 1

    def attention(pbuf):
        load = lambda h: pltpu.make_async_copy(probs.at[h], pbuf.at[h], psem.at[h])
        for h in range(H):
            load(h).start()
        for cp in second() + later():
            cp.start()
        met()
        for cp in owns:
            cp.wait()
        first()
        for cp in needed:
            cp.wait()
        qut[...] = qu[...].T
        datt_t[...] = datt[...].T

        lax.fori_loop(0, H // 2, lambda p, t: (scores(p, pbuf, load), t)[1], 0)
        for cp in second():
            cp.wait()
        qvt[...] = qv[...].T
        lax.fori_loop(0, H // 2, lambda p, t: (queries(p, pbuf), t)[1], 0)

    pl.run_scoped(attention, pltpu.VMEM((H, rows, kv.shape[2] * rows), BF))

    def tail(pre_ref, w1, hid_ref, dpre_ref):
        for cp in last_in(pre_ref, w1):
            cp.start()
        g_low[pl.ds(FLAT["p"], 512), :] = gpost[...].T.astype(BF)
        for cp in later():
            cp.wait()
        a2t = a2[...].T
        g_low[pl.ds(FLAT["q"], 512), :] = dot(a2t, dq_ref[...]).astype(BF)
        da2 = dot_nt(dq_ref[...], wqkv[pl.ds(0, 512), :])
        after(16)
        for p in range(H // 2):
            keys.step(p, 3)
            keys.collect(p, 0, dkt)
            keys.collect(p, 1, dvt)
        g_low[pl.ds(FLAT["k"], 512), :] = dot_nt(a2t, dkt[...]).astype(BF)
        g_low[pl.ds(FLAT["v"], 512), :] = dot_nt(a2t, dvt[...]).astype(BF)
        advance(groups["q"])
        for cp in last_in(pre_ref, w1):
            cp.wait()
        ffn_hidden(pre_ref, hid_ref)
        after(17)
        da2 = da2 + dot_nt(dkt[...].T, wqkv[pl.ds(512, 512), :]) + dot_nt(dvt[...].T, wqkv[pl.ds(1024, 512), :])
        back, gg2 = norm_back(x1_ref[...], gain2[...], da2)
        dx1 = dx2_ref[...] + back
        g1 = (0.5 * dx1).astype(BF)
        x = x_ref[...].astype(F32)
        a1 = norm(x, gain1[...]).astype(BF)
        after(18)
        ffn_out_grad(g1, hid_ref, g_low.at[pl.ds(2048, 2048), :])
        advance(groups["f1o"])
        after(19)
        da1 = ffn_through(g1, w1.at[pl.ds(0, 2048), :], w1.at[pl.ds(2048, 2048), :], pre_ref, hid_ref, dpre_ref)
        after(20)
        ffn_in_grad(a1, dpre_ref, g_low.at[pl.ds(0, 2048), :])
        advance(groups["f1i"])
        back, gg1 = norm_back(x, gain1[...], da1)
        dx0_ref[...] = (dx1 + back).astype(BF)
        total_ref[pl.ds(smalls2.shape[0] - 5, 2), :] = jnp.concatenate([gg1, gg2], axis=0)

    pl.run_scoped(tail, pltpu.VMEM(pre_h.shape, F32), pltpu.VMEM((4096, 512), BF), pltpu.VMEM(pre_h.shape, BF), pltpu.VMEM(pre_h.shape, BF))
    count = smalls2.shape[0] - 8
    total_ref[pl.ds(0, count), :] = smalls2[pl.ds(0, count), :]
    total_ref[pl.ds(count, 3), :] = smalls2[pl.ds(count, 3), :]
    total_ref[pl.ds(count + 7, 1), :] = jnp.zeros((1, 512), F32)
    flows = flat_list(list(groups.values()))
    turns, steps = TURNS[21], len(fly.devs) + 1
    for i, token in enumerate(turns):
        if i * steps // len(turns) != (i - 1) * steps // len(turns):
            fly.stage(i * steps // len(turns))
        name, k = NAMES[token // 4], token % 4
        advance(groups[name][k : k + 1])
    while any(flow.now < flow.last for flow in flows):
        advance(flows)
    for p in range(H // 2):
        keys.sent(p)
    for flow in flows:
        flow.finish()


def widen_body(flat, total, bns, *refs):
    outs, smalls, (ibuf, obuf, rbuf, isem, osem, rsem) = refs[:11], refs[11:21], refs[21:]
    count = smalls[0].shape[0]
    lines = [pltpu.make_async_copy(total.at[pl.ds(0, count), :], smalls[0], rsem.at[0])]
    for i, ref in enumerate(smalls[1:]):
        rbuf[i] = total[pl.ds(count + i, 1), :] if i < 7 else bns[pl.ds(i - 7, 1), :]
        lines.append(pltpu.make_async_copy(rbuf.at[i], ref, rsem.at[1 + i]))
    for cp in lines:
        cp.start()
    step = 512
    n = FLAT_ROWS // step
    loads = [pltpu.make_async_copy(flat.at[pl.ds(i * step, step), :], ibuf.at[i], isem.at[i]) for i in range(n)]
    for cp in loads:
        cp.start()
    stores = []
    slots = obuf.shape[0]
    for i in range(n):
        name = [m for m in ORDER if FLAT[m] <= i * step][-1]
        out = outs[ORDER.index(name)]
        off = i * step - FLAT[name]
        fold = FOLDS.get(name, 1)
        if fold == 1:
            dst = out.at[pl.ds(off, step), :]
        else:
            dst = out.at[:, pl.ds(off, step)]
        loads[i].wait()
        if i >= slots:
            stores[i - slots].wait()
        obuf[i % slots] = ibuf[i].astype(F32)
        stores.append(pltpu.make_async_copy(obuf.at[i % slots], dst, osem.at[i % slots]))
        stores[-1].start()
    for cp in stores[-slots:] + lines:
        cp.wait()


def remote(body, cid, outs, ins, scratch, name):
    def space(x):
        if x is None:
            return pl.BlockSpec(memory_space=pl.ANY)
        return pl.BlockSpec(memory_space=x)

    return pl.pallas_call(
        body,
        out_shape=[jax.ShapeDtypeStruct(s, d) for s, d, _ in outs],
        in_specs=[space(m) for _, m in ins],
        out_specs=[space(m) for _, _, m in outs],
        scratch_shapes=list(scratch),
        compiler_params=pltpu.CompilerParams(collective_id=cid, has_side_effects=True, vmem_limit_bytes=VMEM_LIMIT),
        name=name,
    )(*[x for x, _ in ins])


def local(
    inputs, cotangent, lengths, weight_noise, ffn1_in, ffn1_out, query_w, key_w, value_w, pos_w, out_w,
    conv_in, conv_out, ffn2_in, ffn2_out, conv_kernel, ffn1_gain, attn_gain, conv_gain, ffn2_gain,
    final_gain, bn_gain, bn_bias, pos_u, pos_v,
):
    _, rows, width = inputs.shape
    tms, slots = lax.axis_size("tm"), lax.axis_size("slot")
    frames = rows * tms
    count = conv_kernel.shape[0]
    devices = tms * slots
    size = Place().size
    x = inputs[0]
    cot = cotangent[0]
    gains = [g.reshape(1, -1) for g in (ffn1_gain, attn_gain, conv_gain, ffn2_gain, final_gain)]
    bng, bnb, pu, pv = (g.reshape(1, -1) for g in (bn_gain, bn_bias, pos_u, pos_v))
    raws = (ffn1_in, ffn1_out, query_w, key_w, value_w, pos_w, out_w, conv_in, conv_out, ffn2_in, ffn2_out)
    VM, HB, SM = pltpu.VMEM, None, pltpu.SMEM
    DMA = pltpu.SemaphoreType.DMA
    V = lambda shape, dtype=BF: pltpu.VMEM(shape, dtype)
    shard_rows = weight_noise.shape[1] // width
    half, hidden = width // 2, 2048
    keys = (H // 2, 2, tms, rows, LANE)
    specs = [
        ((FLAT_ROWS, width), BF), ((rows, width), F32), ((rows, hidden), F32), ((rows, width), BF), ((rows, width), BF), ((rows, width), BF),
        (keys, BF), ((frames, width), BF), ((rows, half), F32), ((rows, half), F32), ((rows, width), BF), ((H, rows, frames), BF),
    ]
    wn, x1, pre1, a2, qu, qv, kv, trig, sin, cos, att, probs = remote(
        early_body, 0, [spec + (HB,) for spec in specs],
        [(lengths, SM), (weight_noise, VM)] + [(r, HB) for r in raws] + [(x, VM), (gains[0], VM), (gains[1], VM), (pu, VM), (pv, VM)],
        [V((FLAT_ROWS, width)), V((width // LANE, shard_rows, LANE), F32)]
        + [V(*spec) for spec in specs[1:10]]
        + [V((2, frames // 64, half), F32), V((2, 64, half), F32), V((rows, width)), V((2, rows, frames)), DMA((18,)), DMA((16,)), DMA((2,))]
        + Gather.scratch(size, shard_rows, width) + KeysAll.scratch(size["x"]),
        "early",
    )
    ext = pltpu.VMEM((width // LANE, rows + count, LANE), F32)
    output, dx2, datt, g_mid, smalls2, bns, cores = remote(
        middle_body, 1,
        [((rows, width), BF, HB), ((rows, width), F32, HB), ((rows, width), BF, HB), ((3 * GROUP, width), BF, HB),
         ((count + 8, width), F32, VM), ((8, width), F32, VM), ((max(1, len(FRONT)), GROUP // 2, width), BF, HB)],
        [(lengths, SM), (att, VM), (x1, VM), (cot, VM), (wn, HB), (conv_kernel, VM), (bng, VM), (bnb, VM)] + [(g, VM) for g in gains[2:]],
        [pltpu.VMEM((FLAT_SIZE[n], width), BF) for n in ("o", "ci", "co", "f2i", "f2o")]
        + [DMA((5,)), pltpu.VMEM((count, width), BF), pltpu.VMEM((count, width), BF), DMA((4,)),
           pltpu.VMEM((rows, width), BF), pltpu.VMEM((rows, width), BF), pltpu.VMEM((rows, 2 * width), F32), ext, ext,
           pltpu.VMEM((rows, width), F32), pltpu.VMEM((rows, hidden), F32), pltpu.VMEM((rows, width), F32),
           pltpu.VMEM((count, 8, LANE), F32), pltpu.VMEM((rows, width), F32), V((max(1, len(FRONT)), GROUP // 2, width)),
           V((rows, width)), V((rows, width), F32), V((rows, width)), V((3 * GROUP, width)),
           V((rows, hidden)), V((rows, hidden)), DMA((7,))]
        + Totals.scratch(tms, slots, 4 * width // LANE) + Totals.scratch(tms, slots, 2 * width // LANE) + flat_list([flat_list(flow_scratch(size, n, "front")) for n in FRONT]),
        "middle",
    )
    dx0, flat, total = remote(
        late_body, 2, [((rows, width), BF, VM), ((FLAT_ROWS, width), BF, HB), ((count + 8, width), F32, VM)],
        [(t, HB) for t in (qu, qv, kv, wn, trig, sin, cos, probs, datt, att, g_mid, cores, a2, x1, dx2, x, pre1)]
        + [(smalls2, VM), (gains[1], VM), (gains[0], VM)],
        [V((rows, width)), V((rows, width)), V(keys), V((width, width)), V((frames, width)),
         V((rows, half), F32), V((rows, half), F32), V((rows, width)), V((rows, width)), V((rows, width)),
         V((rows, width), F32), V((rows, width), F32), V((rows, width)), V((3 * width, width)),
         V((3 - len(FRONT), GROUP // 2, width)), V((6, GROUP // 2, width)), DMA((H,)), DMA((20,)),
         V((rows, width)), V((width, rows)), V((width, rows)), V((width, width), F32), V((width, rows)), V((width, rows)), V((width, rows)),
         V((FLAT_ROWS // 2, width))]
        + KeyGrads.scratch(tms, rows) + Butterfly.scratch(devices, (count + 8, width))
        + flat_list([flat_list(flow_scratch(size, n, "back")) for n in FRONT])
        + flat_list([flat_list(flow_scratch(size, n, "whole")) for n in MID if n not in FRONT])
        + flat_list([flat_list(flow_scratch(size, n, "whole")) for n in ("q", "f1i", "f1o")]),
        "late",
    )
    big = pl.pallas_call(
        widen_body,
        out_shape=[jax.ShapeDtypeStruct(r.shape, F32) for r in raws]
        + [jax.ShapeDtypeStruct((count, width), F32)] + [jax.ShapeDtypeStruct((1, width), F32)] * 9,
        in_specs=[pl.BlockSpec(memory_space=pl.ANY)] + [pl.BlockSpec(memory_space=pltpu.VMEM)] * 2,
        out_specs=[pl.BlockSpec(memory_space=pl.ANY)] * 21,
        scratch_shapes=[pltpu.VMEM((24, 512, width), BF), pltpu.VMEM((4, 512, width), F32), pltpu.VMEM((9, 1, width), F32), DMA((24,)), DMA((4,)), DMA((10,))],
        compiler_params=pltpu.CompilerParams(vmem_limit_bytes=VMEM_LIMIT),
        name="widen",
    )(flat, total, bns)
    t = [r[0] for r in big[12:]]
    return (output[None], dx0[None]) + tuple(big[:11]) + (
        big[11], t[3], t[4], t[0], t[1], t[2], t[7], t[8], t[5], t[6],
    )


def solution(mesh):
    split = P("slot", "tm", None)
    in_specs = (split, split, P("slot"), P(("tm", "slot"), None)) + (P(),) * 21
    out_specs = (split, split) + (P(),) * 21
    return jax.shard_map(local, mesh=mesh, in_specs=in_specs, out_specs=out_specs, check_vma=False)
```

```python
import math

import jax
import jax.numpy as jnp
from jax import lax
from jax.experimental import pallas as pl
from jax.experimental.pallas import tpu as pltpu
from jax.sharding import PartitionSpec as P

H = 8
HD = 64
LANE = 128
F32 = jnp.float32
BF = jnp.bfloat16
EPS = 1e-05
FILL = -1e30
VMEM_LIMIT = 60 * 2**20


def dot(a, b):
    return lax.dot_general(a, b, (((1,), (0,)), ((), ())), preferred_element_type=F32)


def dot_nt(a, b):
    return lax.dot_general(a, b, (((1,), (1,)), ((), ())), preferred_element_type=F32)


def dot_tn(a, b):
    return lax.dot_general(a, b, (((0,), (0,)), ((), ())), preferred_element_type=F32)


def norm_parts(v):
    mean = jnp.mean(v, axis=-1, keepdims=True)
    cen = v - mean
    r = lax.rsqrt(jnp.mean(cen * cen, axis=-1, keepdims=True) + EPS)
    return cen * r, r


def norm(v, gain):
    u, _ = norm_parts(v)
    return u * gain


def norm_back(v, gain, e):
    u, r = norm_parts(v)
    eg = e * gain
    back = r * (eg - jnp.mean(eg, axis=-1, keepdims=True) - u * jnp.mean(eg * u, axis=-1, keepdims=True))
    return back, jnp.sum(e * u, axis=0, keepdims=True)


def sigmoid(v):
    return 1.0 / (1.0 + jnp.exp(-v))


def swish_and_slope(v):
    s = sigmoid(v)
    sv = s * v
    return sv, s + sv * (1.0 - s)


def cols(p, width=LANE):
    return pl.ds(pl.multiple_of(p * width, width), width)


def lane_half(e):
    lane = lax.broadcasted_iota(jnp.int32, (1, LANE), 1)
    return (lane < HD) if e == 0 else (lane >= HD)


def call(body, outs, ins, scratch=(), name=None):
    return pl.pallas_call(
        body,
        out_shape=[jax.ShapeDtypeStruct(s, d) for s, d in outs],
        in_specs=[
            pl.BlockSpec(memory_space=pltpu.SMEM) if x.dtype == jnp.int32 else pl.BlockSpec(memory_space=pltpu.VMEM)
            for x in ins
        ],
        out_specs=[pl.BlockSpec(memory_space=pltpu.VMEM) for _ in outs],
        scratch_shapes=list(scratch),
        compiler_params=pltpu.CompilerParams(vmem_limit_bytes=VMEM_LIMIT),
        name=name,
    )(*ins)


MESH = pl.DeviceIdType.MESH


class Place:
    def __init__(self):
        tms, slots = lax.axis_size("tm"), lax.axis_size("slot")
        wide = 1 << ((slots.bit_length() - 1) // 2)
        self.size = {"c": 2, "x": tms // 2, "y": wide, "z": slots // wide}
        self.tm, self.slot = lax.axis_index("tm"), lax.axis_index("slot")
        self.at = {
            "c": lax.rem(self.tm, 2),
            "x": lax.div(self.tm, 2),
            "y": lax.rem(self.slot, wide),
            "z": lax.div(self.slot, wide),
        }

    def peer(self, axis, off):
        pos = dict(self.at)
        pos[axis] = lax.rem(pos[axis] + off, self.size[axis])
        return (pos["x"] * 2 + pos["c"], pos["z"] * self.size["y"] + pos["y"]), pos[axis]

    def peers(self, axis):
        return [(off,) + self.peer(axis, off) for off in range(1, self.size[axis])]

    def greet(self, axes):
        bar = pltpu.get_barrier_semaphore()
        count = 0
        for axis in axes:
            for _, dev, _ in self.peers(axis):
                pl.semaphore_signal(bar, inc=1, device_id=dev, device_id_type=MESH)
                count += 1
        return lambda: pl.semaphore_wait(bar, count)


def rows_at(start, size):
    return pl.ds(pl.multiple_of(start, 16), size)


def add_into(dst, start, lanes, terms, size):
    step = 64 if size % 64 == 0 else 16

    def one(i, carry):
        off = pl.multiple_of(i * step, step)
        total = terms[0](off, step).astype(F32)
        for term in terms[1:]:
            total = total + term(off, step).astype(F32)
        dst[pl.ds(pl.multiple_of(start + off, 16), step), lanes] = total.astype(dst.dtype)
        return carry

    lax.fori_loop(0, size // step, one, 0)


GROUP = 2048


class Flow:
    STAGES = 9

    @staticmethod
    def lane_parts(order, size):
        rows = GROUP // 2
        for axis in order[:2]:
            rows //= size[axis]
        return max(1, 16 * size[order[2]] // rows)

    @staticmethod
    def scratch(order, width, size, kind):
        shapes = []
        blk = GROUP // 2
        parts = Flow.lane_parts(order, size)
        for lv, axis in enumerate(order):
            n = size[axis]
            blk = blk * parts // n if lv == 2 else blk // n
            w = width // parts if lv == 2 else width
            if (kind != "front" or lv == 0) and (kind != "back" or lv > 0):
                shapes.append(pltpu.VMEM((n - 1, blk, w), BF))
        if kind != "front":
            shapes.append(pltpu.VMEM((blk, width // parts), BF))
        sems = pltpu.SemaphoreType.DMA
        return shapes + [sems((3,)), sems((2,)) if kind == "front" else sems((8,)), sems((1,))]

    def __init__(self, pc, order, lane, width, kind, src, own, core, out, first, bufs):
        self.ssem, self.rsem, self.lsem = bufs[-3:]
        bufs = list(bufs[:-3])
        self.now = 2 if kind == "back" else 0
        size = pc.size
        lanes = pl.ds(lane, width)
        c = pc.at["c"]
        top = GROUP // 2
        parts = self.lane_parts(order, size)
        blk, rel = [top], [0]
        for lv, axis in enumerate(order):
            if lv < 2:
                blk.append(blk[-1] // size[axis])
                rel.append(rel[-1] + pc.at[axis] * blk[-1])
        low = blk[2] * parts // size[order[2]]

        def share(pos):
            if parts == 1:
                return rel[2] + pos * low, lanes
            at = pl.multiple_of(lane + lax.rem(pos, parts) * (width // parts), LANE)
            return rel[2] + lax.div(pos, parts) * low, pl.ds(at, width // parts)

        ((_, cdev, _),) = pc.peers("c")
        into = [None] * 3
        if kind != "back":
            into[0] = bufs.pop(0)
        if kind != "front":
            into[1], into[2], fin = bufs
        copies = [[(lambda: src.at[rows_at((1 - c) * top, top), lanes], lambda: core.at[:, lanes], cdev)]]
        bytes_of = [lambda: core.at[:, lanes]]
        for lv, axis in enumerate(order):
            cps = []
            for off, dev, pos in pc.peers(axis):
                if lv < 2:
                    s = lambda lv=lv, pos=pos: core.at[rows_at(rel[lv] + pos * blk[lv + 1], blk[lv + 1]), lanes]
                else:
                    s = lambda pos=pos: core.at[rows_at(share(pos)[0], low), share(pos)[1]]
                cps.append((s, lambda lv=lv, off=off: into[lv].at[off - 1], dev))
            copies.append(cps)
            bytes_of.append(lambda lv=lv: into[lv])
        mine = share(pc.at[order[2]])
        out_share = lambda: out.at[rows_at(first + c * top + mine[0], low), mine[1]]
        out_at = lambda lv: out.at[rows_at(first + c * top + rel[lv], blk[lv]), lanes]
        copies.append([(lambda: fin, out_share, dev) for _, dev, _ in pc.peers(order[2])])
        bytes_of.append(
            lambda: out.at[rows_at(first + c * top + rel[2], (size[order[2]] - 1) * low), pl.ds(lane, width // parts)]
        )
        for lv in (2, 1):
            copies.append([(lambda lv=lv: out_at(lv), lambda lv=lv: out_at(lv), dev) for _, dev, _ in pc.peers(order[lv - 1])])
            bytes_of.append(
                lambda lv=lv: out.at[rows_at(first + c * top + rel[lv - 1], (size[order[lv - 1]] - 1) * blk[lv]), lanes]
            )
        copies.append([(lambda: out_at(0), lambda: out_at(0), cdev)])
        bytes_of.append(lambda: out_at(0))
        self.copies, self.bytes_of = copies, bytes_of

        def fold(lv):
            if lv == 0:
                add_into(core, 0, lanes, [lambda o, n: own(o, n, lanes), lambda o, n: core[pl.ds(o, n), lanes]], top)
                return
            row, ln, size_ = (mine + (low,)) if lv == 3 else (rel[lv], lanes, blk[lv])
            terms = [lambda o, n: core[pl.ds(pl.multiple_of(row + o, 16), n), ln]]
            for k in range(size[order[lv - 1]] - 1):
                terms.append(lambda o, n, k=k: into[lv - 1][k, pl.ds(o, n), :])
            if lv == 3:
                add_into(fin, 0, slice(None), terms, size_)
            else:
                add_into(core, row, lanes, terms, size_)

        keep = lambda: pltpu.make_async_copy(fin, out_share(), self.lsem.at[0])

        def s1():
            self.arrived(0)
            fold(0)
            self.start(1)

        def s2():
            if kind != "back":
                self.arrived(1)
                fold(1)
            if kind != "front":
                self.start(2)

        def s3():
            self.arrived(2)
            fold(2)
            self.start(3)

        def s4():
            self.arrived(3)
            fold(3)
            keep().start()
            self.start(4)

        def climb(i):
            def run():
                if i == 0:
                    keep().wait()
                self.arrived(4 + i)
                if i < 3:
                    self.start(5 + i)

            return run

        self.stages = [lambda: self.start(0), s1, s2, s3, s4] + [climb(i) for i in range(4)]
        self.last = 3 if kind == "front" else self.STAGES
        self.first = 2 if kind == "back" else 0

    def make(self, i, src, dst, dev):
        return pltpu.make_async_remote_copy(
            src_ref=src(), dst_ref=dst(), send_sem=self.ssem.at[i % 3], recv_sem=self.rsem.at[i], device_id=dev, device_id_type=MESH
        )

    def start(self, i):
        for src, dst, dev in self.copies[i]:
            self.make(i, src, dst, dev).start()

    def all_of(self, i):
        if len(self.copies[i]) == 1:
            return self.make(i, *self.copies[i][0])
        return self.make(i, self.bytes_of[i], self.bytes_of[i], self.copies[i][0][2])

    def arrived(self, i):
        self.all_of(i).wait_recv()

    def left(self, i):
        if i >= self.first:
            self.all_of(i).wait_send()

    def finish(self):
        self.left(self.last - 2)

    def take(self):
        if self.now >= self.last:
            return lambda: None
        i, self.now = self.now, self.now + 1

        def run():
            self.stages[i]()
            if i > 1:
                self.left(i - 2)

        return run


def advance(flows):
    for flow in flows:
        flow.take()()


MID = {"f2i": 2048, "f2o": 4096, "o": 0}
NAMES = ("f2i", "f2o", "o", "q", "f1o", "f1i")
AXES = {"A": ("y", "x", "z"), "B": ("x", "y", "z"), "X": ("z", "x", "y"), "Y": ("z", "y", "x")}
FRONT = ("f2i",)
LANES = {"f2i": "A2 B1 B1", "f2o": "A2 B1 X1", "o": "A2 B1 B1", "q": "A1 B1 B1 Y1", "f1o": "A1 B1 A1 X1", "f1i": "A1 B1 A1 B1"}
TURNS = {
    -1: (4, 5, 6, 8, 9, 10, 0, 1, 2,),
    0: (5, 6, 9,),
    1: (4, 8, 10,),
    2: (0, 1,),
    4: (5, 9, 2,),
    5: (6, 1,),
    6: (10, 0,),
    7: (2,),
    8: (6, 1, 5,),
    9: (4, 9,),
    10: (10, 6, 2,),
    11: (5,),
    12: (8, 9,),
    13: (10,),
    14: (0, 5, 6,),
    15: (4, 9, 1,),
    16: (10, 2,),
    17: (8, 5, 4,),
    18: (12, 13, 0,),
    19: (14, 15, 6,),
    20: (16, 17, 18,),
    21: (19, 12, 13, 8, 4, 0, 1, 2, 20, 21, 5, 22, 14, 1, 2, 12, 0, 5, 6, 23, 13, 16, 6, 17, 15, 18, 14, 12, 21, 8, 4, 13, 20, 16, 23, 17, 18, 19, 14, 22, 21, 15, 12, 20, 13, 9, 8, 23, 16, 15, 22, 17, 10, 19, 18, 12, 14, 4, 21, 13, 20, 9, 4, 19, 23, 16, 9, 10, 15, 22, 14, 18, 13, 10, 17, 21, 13, 23, 20, 15, 12, 16, 19, 8, 12, 18, 22, 17, 14, 8, 21, 20, 19, 14, 15, 22, 23, 15, 16, 17, 18, 21, 16, 19, 17, 20, 18, 23, 21, 19, 22, 20, 23, 22,),
}


def layout(name, size):
    words = LANES[name].split()
    if max(Flow.lane_parts(AXES[word[0]], size) for word in words) > 1:
        words = ["A2", "B2"]
    got, lane = [], 0
    for word in words:
        got.append((AXES[word[0]], lane, int(word[1]) * LANE))
        lane += got[-1][2]
    return got


def flow_scratch(size, name, kind):
    return [Flow.scratch(order, width, size, kind) for order, _, width in layout(name, size)]


def flat_list(lists):
    return [x for part in lists for x in part]


class Taker:
    def __init__(self, refs):
        self.refs = list(refs)

    def __call__(self, n):
        got, self.refs = self.refs[:n], self.refs[n:]
        return got


def make_flows(pc, name, kind, src, own, core, out, first, taker):
    flows = []
    for (order, lane, width), shapes in zip(layout(name, pc.size), flow_scratch(pc.size, name, kind)):
        flows.append(Flow(pc, order, lane, width, kind, src, own, core, out, first, taker(len(shapes))))
    return flows


FLAT = {"f1i": 0, "f1o": 2048, "q": 4096, "k": 4608, "v": 5120, "p": 5632, "o": 6144, "ci": 6656, "co": 7680, "f2i": 8192, "f2o": 10240}
FLAT_ROWS = 12288
ORDER = tuple(FLAT)
FOLDS = {"f1i": 4, "ci": 2, "f2i": 4}
FLAT_SIZE = {n: (list(FLAT.values()) + [FLAT_ROWS])[i + 1] - FLAT[n] for i, n in enumerate(FLAT)}


def ticks(point, plan, p):
    for at, run in plan.items():
        if at % 2 == point:
            pl.when(p == at // 2)(lambda run=run: (run(), None)[1])


class Gather:
    @staticmethod
    def scratch(size, shard_rows, width):
        part, pieces = Gather.cut(shard_rows)
        sems = pltpu.SemaphoreType.DMA((2 * pieces * (size["x"] + 6),))
        return [
            pltpu.VMEM((size["x"], 2, size["z"], size["y"], shard_rows, width), BF),
            pltpu.VMEM((width // LANE, 64, LANE), F32),
            sems,
            sems,
            pltpu.SemaphoreType.REGULAR,
        ]

    @staticmethod
    def cut(shard_rows):
        part = 64 if shard_rows % 64 == 0 else 16
        return part, shard_rows // part

    def __init__(self, pc, wf, bufs):
        self.pc, self.wf = pc, wf
        self.nb, self.scr, self.ssem, self.rsem, self.free = bufs
        self.shard_rows = self.nb.shape[4]
        self.part, self.pieces = self.cut(self.shard_rows)
        self.xs = pc.size["x"]
        self.used = 0
        self.stages = [self.plan(hx, q) for hx in range(2) for q in range(self.pieces)]

    def copies(self, ref, axis, only=None, total=None):
        out = []

        def make(ref, dev, k):
            return pltpu.make_async_remote_copy(
                src_ref=ref, dst_ref=ref, send_sem=self.ssem.at[k], recv_sem=self.rsem.at[k], device_id=dev, device_id_type=MESH
            )

        for off, dev, _ in self.pc.peers(axis):
            if only is not None and off != only:
                continue
            out.append((off, make(ref, dev, self.used)))
            if total is None:
                self.used += 1
        if total is None:
            return out, out
        self.used += 1
        return out, [(0, make(total, dev, self.used - 1))]

    def plan(self, hx, q):
        pc, nb = self.pc, self.nb
        x, c, z, y = (pc.at[a] for a in "xczy")
        rows = pl.ds(q * self.part, self.part)
        across = self.xs // 2
        side = pl.ds(hx * across, across)
        in_half = lambda pos: lax.div(pos, across) == hx
        width = nb.shape[5]
        wide, quarter = pl.ds(0, width // 2), width // 4
        away = pl.ds(3 * quarter, quarter)
        source = jnp.where(in_half(x), x, lax.rem(x + across, self.xs))
        lanes = pl.ds(pl.multiple_of(jnp.where(in_half(x), 2 * quarter, 3 * quarter), LANE), quarter)
        others = {axis: pl.ds(0, pc.size[axis] - 1) for axis in "xyz"}
        along = {
            "xa": self.copies(nb.at[x, c, z, y, rows, wide], "x"),
            "xd": self.copies(nb.at[x, c, z, y, rows, away], "x", across),
            "za": self.copies(nb.at[side, c, z, y, rows, wide], "z", None, nb.at[side, c, others["z"], y, rows, wide]),
            "zb": self.copies(nb.at[source, c, z, y, rows, lanes], "z", None, nb.at[source, c, others["z"], y, rows, lanes]),
            "ya": self.copies(nb.at[side, c, :, y, rows, wide], "y", None, nb.at[side, c, :, others["y"], rows, wide]),
            "yb": self.copies(nb.at[source, c, :, y, rows, lanes], "y", None, nb.at[source, c, :, others["y"], rows, lanes]),
            "xb": self.copies(nb.at[source, c, :, :, rows, lanes], "x", None, nb.at[others["x"], c, :, :, rows, lanes]),
            "c": self.copies(nb.at[side, c, :, :, rows], "c"),
        }

        def each(axis, what, cond=None):
            for off, cp in along[axis][0 if what == "start" else 1]:
                if cond is None:
                    getattr(cp, what)()
                else:
                    pl.when(cond(off))(lambda cp=cp: getattr(cp, what)())

        sends = lambda off: in_half(x)
        gets = lambda off: in_half(lax.rem(x - off + self.xs, self.xs))

        def end():
            each("c", "wait_recv")
            each("xa", "wait_send", sends)
            for axis in ("za", "zb", "ya", "yb", "xb"):
                each(axis, "wait_send")
            if self.part == 64:
                self.mix_half(hx, q)
            elif q == self.pieces - 1:
                self.mix_half(hx, None)

        def done():
            each("c", "wait_send")

        def then(*acts):
            return lambda: [each(*act) for act in acts]

        def let():
            @pl.when(in_half(x))
            def _():
                ((_, cp),) = along["xd"][0]
                cp.wait_send()
                ((_, dev, _),) = [peer for peer in pc.peers("x") if peer[0] == across]
                pl.semaphore_signal(self.free, inc=1, device_id=dev, device_id_type=MESH)

        def allowed():
            pl.when(jnp.logical_not(in_half(x)))(lambda: pl.semaphore_wait(self.free, 1))

        return {
            "X": then(("xa", "start", sends), ("xd", "start", sends)),
            "Z": then(("xa", "wait_recv", gets), ("xd", "wait_recv", gets), ("za", "start"), ("zb", "start")),
            "Y": lambda: (then(("za", "wait_recv"), ("zb", "wait_recv"), ("ya", "start"), ("yb", "start"))(), let()),
            "W": lambda: (each("yb", "wait_recv"), allowed(), each("xb", "start")),
            "C": then(("ya", "wait_recv"), ("xb", "wait_recv"), ("c", "start")),
            "E": end,
            "D": done,
        }

    def run(self, ops):
        for op in ops:
            if 0 <= op[1] < len(self.stages):
                self.stages[op[1]][op[0]]()

    def finish(self):
        for stages in self.stages:
            stages["D"]()

    def noise_at(self, row):
        pc = self.pc
        got = []
        sub = min(64, self.part)
        for i in range(64 // sub):
            at = row + i * sub
            d = lax.div(at, self.shard_rows)
            slots = pc.size["z"] * pc.size["y"]
            tm, sl = lax.div(d, slots), lax.rem(d, slots)
            off = pl.multiple_of(lax.rem(at, self.shard_rows), 16)
            got.append(
                self.nb[lax.div(tm, 2), lax.rem(tm, 2), lax.div(sl, pc.size["y"]), lax.rem(sl, pc.size["y"]), pl.ds(off, sub), :].astype(F32)
            )
        return got[0] if len(got) == 1 else jnp.concatenate(got, axis=0)

    def mix(self, row, base, size, fold):
        wf, scr = self.wf, self.scr
        value = self.noise_at(row)
        if fold == 1:
            at = rows_at(row, 64)
            wf[at, :] = (wf[at, :].astype(F32) + value).astype(BF)
            return
        for b in range(512 // LANE):
            scr[b] = value[:, b * LANE : (b + 1) * LANE]
        high = 64 // fold
        for j in range(fold):
            at = rows_at(base + j * (size // fold) + lax.div(row - base, fold), high)
            for b in range(512 // LANE):
                lanes = pl.ds(b * LANE, LANE)
                wf[at, lanes] = (wf[at, lanes].astype(F32) + scr[b, pl.ds(j, high, stride=fold), :]).astype(BF)

    def mix_half(self, hx, q):
        for name in ORDER:
            base, size, fold = FLAT[name], FLAT_SIZE[name], FOLDS.get(name, 1)
            if (base < FLAT_ROWS // 2) != (hx == 0):
                continue
            begin, end = base // 64, (base + size) // 64
            start, stride = (begin, 1) if q is None else (begin + (q - begin) % self.pieces, self.pieces)
            lax.fori_loop(
                0, (end - start + stride - 1) // stride,
                lambda i, t: (self.mix((start + i * stride) * 64, base, size, fold), t)[1], 0,
            )


class KeysAll:
    @staticmethod
    def scratch(xs):
        n = 2 * xs - 1
        sems = pltpu.SemaphoreType.DMA((H // 2, n))
        return [sems, sems]

    def __init__(self, pc, kv, bufs):
        self.pc, self.kv = pc, kv
        self.ssem, self.rsem = bufs

    def copy(self, p, k, tm, dev):
        ref = self.kv.at[p, :, tm]
        return pltpu.make_async_remote_copy(
            src_ref=ref, dst_ref=ref, send_sem=self.ssem.at[p, k], recv_sem=self.rsem.at[p, k], device_id=dev, device_id_type=MESH
        )

    def core(self, p):
        ((_, dev, _),) = self.pc.peers("c")
        return [self.copy(p, 0, self.pc.tm, dev)]

    def line(self, p):
        return [self.copy(p, off, self.pc.tm, dev) for off, dev, _ in self.pc.peers("x")]

    def relay(self, p):
        ((_, dev, _),) = self.pc.peers("c")
        xs = self.pc.size["x"]
        out = []
        for off in range(1, xs):
            source = lax.rem(self.pc.at["x"] - off + xs, xs) * 2 + self.pc.at["c"]
            out.append(self.copy(p, xs - 1 + off, source, dev))
        return out

    def send(self, p):
        for cp in self.core(p):
            cp.start()

    def send_line(self, p):
        for cp in self.line(p):
            cp.start()

    def forward(self, p):
        for come, on in zip(self.line(p), self.relay(p)):
            come.wait_recv()
            on.start()

    def ready(self, p):
        for cp in self.core(p) + self.relay(p):
            cp.wait_recv()

    def sent(self, p):
        for cp in self.line(p) + self.core(p) + self.relay(p):
            cp.wait_send()


def angle_tables(hi, lo, rates):
    for ref, step in ((hi, 64.0), (lo, 1.0)):
        count = ref.shape[1]
        angle = lax.broadcasted_iota(jnp.int32, (count, rates.shape[1]), 0).astype(F32) * step * rates
        ref[0] = jnp.sin(angle)
        ref[1] = jnp.cos(angle)


def angle_block(hi, lo, m):
    hs, hc = hi[0, pl.ds(m, 1), :], hi[1, pl.ds(m, 1), :]
    ls, lc = lo[0], lo[1]
    return hs * lc + hc * ls, hc * lc - hs * ls


def early_body(*refs):
    lens, noise, raws = refs[0], refs[1], refs[2:13]
    x_ref, gain1, gain2, pos_u, pos_v = refs[13:18]
    wn, x1_out, pre_out, a2_out, qu_out, qv_out, kv_out, trig_out, sin_out, cos_out, att_out, probs = refs[18:30]
    wf, flat, x1_ref, pre_ref, a2_ref, qu, qv, kv, trig, sin, cos, hi, lo, att, pbuf, wsem, osem, psem = refs[30:48]
    bufs = refs[48:]
    pc = Place()
    rows, width = x_ref.shape
    half = width // 2
    tms = lax.axis_size("tm")
    frames = rows * tms
    met = pc.greet("cxyz")
    loads = []
    for name, raw in zip(ORDER, raws):
        for j in range(FOLDS.get(name, 1)):
            size = FLAT_SIZE[name] // FOLDS.get(name, 1)
            dst = wf.at[pl.ds(FLAT[name] + j * size, size), :]
            loads.append(pltpu.make_async_copy(raw.at[:, pl.ds(j * 512, 512)], dst, wsem.at[len(loads)]))
            loads[-1].start()
    gather = Gather(pc, wf, bufs[:5])
    keys = KeysAll(pc, kv, bufs[5:7])

    def unfold(i, carry):
        for r in range(8):
            for b in range(width // LANE):
                at = pl.ds(pl.multiple_of((i * 8 + r) * width + b * LANE, LANE), LANE)
                flat[b, pl.ds(i * 8 + r, 1), :] = noise[:, at].astype(F32)
        return carry

    shard_rows = gather.shard_rows
    lax.fori_loop(0, shard_rows // 8, unfold, 0)
    for b in range(width // LANE):
        gather.nb[pc.at["x"], pc.at["c"], pc.at["z"], pc.at["y"], :, pl.ds(b * LANE, LANE)] = flat[b].astype(BF)
    rates = jnp.exp(lax.broadcasted_iota(jnp.int32, (1, half), 1).astype(F32) * (-2.0 * math.log(10000.0) / width))
    angle_tables(hi, lo, rates)

    def angles(m, carry):
        s, c = angle_block(hi, lo, m)
        at = rows_at(m * 64, 64)
        trig[at, pl.ds(0, half)] = s.astype(BF)
        trig[at, pl.ds(half, half)] = c.astype(BF)
        return carry

    def own_angles(m, carry):
        s, c = angle_block(hi, lo, pc.tm * (rows // 64) + m)
        sin[rows_at(m * 64, 64), :] = s
        cos[rows_at(m * 64, 64), :] = c
        return carry

    lax.fori_loop(0, frames // 64, angles, 0)
    lax.fori_loop(0, rows // 64, own_angles, 0)
    met()
    n = gather.pieces
    gather.run([("X", i) for i in range(2 * n)])
    gather.run([("Z", 0), ("Z", 1)])
    for cp in loads:
        cp.wait()
    outs = []

    def put(src, dst):
        cp = pltpu.make_async_copy(src, dst, osem.at[len(outs)])
        cp.start()
        outs.append(cp)

    x = x_ref[...].astype(F32)
    a1 = norm(x, gain1[...]).astype(BF)
    for t in range(2, n + 2):
        gather.run([("Z", t), ("Y", t - 2), ("W", t - 3), ("C", t - 4), ("E", t - 5)])
    gather.run([("W", n - 1), ("C", n - 2), ("E", n - 3), ("C", n - 1), ("E", n - 2), ("Z", n + 2), ("E", n - 1)])
    part = lambda name: wf.at[pl.ds(FLAT[name], FLAT_SIZE[name]), :]
    x1 = x + 0.5 * ffn_forward(a1, part("f1i"), part("f1o"), pre_ref)
    x1_ref[...] = x1
    a2 = norm(x1, gain2[...]).astype(BF)
    a2_ref[...] = a2
    k = dot(a2, part("k")[...]).astype(BF)
    v = dot(a2, part("v")[...]).astype(BF)
    for p in range(H // 2):
        kv[p, 0, pc.tm] = k[:, p * LANE : (p + 1) * LANE]
        kv[p, 1, pc.tm] = v[:, p * LANE : (p + 1) * LANE]
        if p == 0:
            keys.send_line(0)
        keys.send(p)
    gather.run([("Z", n + 3), ("Y", n), ("Y", n + 1)])
    q = dot(a2, part("q")[...])
    scale = HD**-0.5
    qu[...] = ((q + pos_u[...]).astype(BF).astype(F32) * scale).astype(BF)
    qv[...] = ((q + pos_v[...]).astype(BF).astype(F32) * scale).astype(BF)
    for src, dst in ((x1_ref, x1_out), (pre_ref, pre_out), (a2_ref, a2_out), (qu, qu_out), (qv, qv_out), (trig, trig_out), (sin, sin_out), (cos, cos_out)):
        put(src, dst)
    put(wf.at[pl.ds(0, FLAT_ROWS // 2), :], wn.at[pl.ds(0, FLAT_ROWS // 2), :])
    steps = {
        0: "W0 Y2 Z4", 1: "W1 Y3 Z5", 2: "C0 W2 Y4", 3: "E0 W3 Y5", 4: "C1 W4", 5: "E1 C2 W5", 6: "E2 C3", 7: "E3 C4 C5", 8: "E4 E5",
    }
    if n != 6:
        order = (("Z", 4), ("Y", 2), ("W", 0), ("C", 0), ("E", 0))
        steps = {8: " ".join("%s%d" % (op, i) for op, low in order for i in range(low, n))}
    steps = {at: [(op[0], n + int(op[1:])) for op in text.split()] for at, text in steps.items()}
    plan = {at: (lambda ops=ops: gather.run(ops)) for at, ops in steps.items() if at < H}
    ok = lax.broadcasted_iota(jnp.int32, (1, frames), 1) < lens[0]
    w_pos = part("p")
    store = lambda p, e: pltpu.make_async_copy(pbuf.at[e], probs.at[2 * p + e], psem.at[e])

    def pair(p, carry):
        at = cols(p)
        mixed = None
        for e in range(2):
            mine = lane_half(e)
            qve = jnp.where(mine, qv[:, at], jnp.zeros((), BF))
            que = jnp.where(mine, qu[:, at], jnp.zeros((), BF))
            turned = dot_nt(qve, w_pos[:, at])
            a_s, a_c = turned[:, :half], turned[:, half:]
            b_c = (a_s * sin[...] + a_c * cos[...]).astype(BF)
            b_s = (a_c * sin[...] - a_s * cos[...]).astype(BF)
            if e == 0:
                pl.when(p == 1)(lambda: keys.send_line(3))
                pl.when(p == 0)(lambda: (keys.forward(0), keys.send_line(1))[1])
                keys.ready(p)
            else:
                pl.when(p == 0)(lambda: keys.send_line(2))
            s = dot_nt(jnp.concatenate([b_s, b_c, que], axis=1), jnp.concatenate([trig[...], kv[p, 0].reshape(frames, LANE)], axis=1))
            s = jnp.where(ok, s, FILL)
            m = jnp.max(s, axis=-1, keepdims=True)
            ex = jnp.exp(s - m)
            tot = jnp.sum(ex, axis=-1, keepdims=True)
            low = (ex * (1.0 / tot)).astype(BF)
            pl.when(p > 0)(lambda: store(p - 1, e).wait())
            pbuf[e] = low
            store(p, e).start()
            got = dot(low, kv[p, 1].reshape(frames, LANE))
            mixed = got if e == 0 else jnp.where(mine, got, mixed)
            if e == 1:
                pl.when(p < H // 2 - 1)(lambda: keys.forward(p + 1))
            ticks(e, plan, p)
        att[:, at] = mixed.astype(BF)
        return carry

    lax.fori_loop(0, H // 2, pair, 0)
    put(kv, kv_out)
    put(att, att_out)
    gather.run(steps[8])
    put(wf.at[pl.ds(FLAT_ROWS // 2, FLAT_ROWS // 2), :], wn.at[pl.ds(FLAT_ROWS // 2, FLAT_ROWS // 2), :])
    for e in range(2):
        store(H // 2 - 1, e).wait()
    for p in range(H // 2):
        keys.sent(p)
    gather.finish()
    for cp in outs:
        cp.wait()


def chunk(c):
    return pl.ds(pl.multiple_of(c * 512, 512), 512)


def ffn_forward(normed, w_in, w_out, pre_ref):
    def one(c, acc):
        pre = dot(normed, w_in[chunk(c), :])
        pre_ref[:, chunk(c)] = pre
        return acc + dot((pre * sigmoid(pre)).astype(BF), w_out[chunk(c), :])

    return lax.fori_loop(0, w_in.shape[0] // 512, one, jnp.zeros((normed.shape[0], w_out.shape[1]), F32))


def ffn_through(g_low, w_in, w_out, pre_ref, hid_ref, dpre_ref):
    def one(c, acc):
        sw, slope = swish_and_slope(pre_ref[:, chunk(c)])
        hid_ref[:, chunk(c)] = sw.astype(BF)
        dpre = (dot_nt(g_low, w_out[chunk(c), :]) * slope).astype(BF)
        dpre_ref[:, chunk(c)] = dpre
        return acc + dot_nt(dpre, w_in[chunk(c), :])

    return lax.fori_loop(0, w_in.shape[0] // 512, one, jnp.zeros(g_low.shape, F32))


def ffn_in_grad(normed, dpre_ref, gin_ref):
    normed_t = normed.T

    def one(c, carry):
        gin_ref[chunk(c), :] = dot(normed_t, dpre_ref[:, chunk(c)]).astype(gin_ref.dtype)
        return carry

    lax.fori_loop(0, gin_ref.shape[0] // 512, one, 0)


def ffn_out_grad(g_low, hid_ref, gout_ref):
    def one(c, carry):
        gout_ref[chunk(c), :] = dot_tn(hid_ref[:, chunk(c)], g_low).astype(gout_ref.dtype)
        return carry

    lax.fori_loop(0, gout_ref.shape[0] // 512, one, 0)


def ffn_hidden(pre_ref, hid_ref):
    def one(c, carry):
        pre = pre_ref[:, chunk(c)]
        hid_ref[:, chunk(c)] = (pre * sigmoid(pre)).astype(BF)
        return carry

    lax.fori_loop(0, pre_ref.shape[1] // 512, one, 0)


class Fetch:
    def __init__(self, sems):
        self.sems, self.n = sems, 0

    def __call__(self, src, dst):
        cp = pltpu.make_async_copy(src, dst, self.sems.at[self.n])
        self.n += 1
        cp.start()
        return cp


def part_of(wn, name):
    return wn.at[pl.ds(FLAT[name], FLAT_SIZE[name]), :]


def valid_rows(lens, rows):
    first = lax.axis_index("tm") * rows
    return ((first + lax.broadcasted_iota(jnp.int32, (rows, 1), 0)) < lens[0]).astype(F32)


def spread(ext, start, value):
    value = value.astype(F32)
    for b in range(ext.shape[0]):
        ext[b, pl.ds(start, value.shape[0]), :] = value[:, b * LANE : (b + 1) * LANE]


def tap_sum(ext, taps, out_ref, offset):
    count = taps.shape[0]
    rows = out_ref.shape[0]
    block = 64 if rows % 64 == 0 else 16

    def one(i, carry):
        for b in range(ext.shape[0]):
            at = pl.ds(b * LANE, LANE)
            acc = jnp.zeros((block, LANE), F32)
            for k in range(count):
                acc = acc + taps[pl.ds(k, 1), at] * ext[b, pl.ds(i * block + offset(k), block), :]
            out_ref[pl.ds(pl.multiple_of(i * block, block), block), at] = acc
        return carry

    lax.fori_loop(0, rows // block, one, 0)


class Totals:
    @staticmethod
    def scratch(tms, slots, packed):
        n = tms + slots - 2
        return [
            pltpu.VMEM((tms, packed, LANE), F32),
            pltpu.VMEM((slots, packed, LANE), F32),
            pltpu.SemaphoreType.DMA((n,)),
            pltpu.SemaphoreType.DMA((n,)),
        ]

    def __init__(self, pc, bufs):
        self.pc, self.bufs = pc, bufs

    def begin(self, value):
        self.sent = []
        self.cps = self.send(0, value)

    def turn(self):
        self.cps = self.send(1, self.end(0))

    def done(self):
        value = self.end(1)
        for cp in self.sent:
            cp.wait_send()
        return value

    def send(self, i, value):
        pc, buf = self.pc, self.bufs[i]
        ssem, rsem = self.bufs[2:]
        me = (pc.tm, pc.slot)[i]
        buf[me] = value
        n = buf.shape[0]
        for off in range(1, n):
            to = lax.rem(me + off, n)
            k = off - 1 + i * (self.bufs[0].shape[0] - 1)
            cp = pltpu.make_async_remote_copy(
                src_ref=buf.at[me], dst_ref=buf.at[me], send_sem=ssem.at[k], recv_sem=rsem.at[k],
                device_id=(to, pc.slot) if i == 0 else (pc.tm, to), device_id_type=MESH,
            )
            cp.start()
            self.sent.append(cp)
        return self.sent[-(n - 1) :]

    def end(self, i):
        for cp in self.cps:
            cp.wait_recv()
        buf = self.bufs[i]
        value = buf[0]
        for j in range(1, buf.shape[0]):
            value = value + buf[j]
        return value


def packed(rows):
    return jnp.concatenate([row[:, at : at + LANE] for row in rows for at in range(0, row.shape[1], LANE)], axis=0)


def unpacked(value, row, width):
    n = width // LANE
    return jnp.concatenate([value[row * n + j : row * n + j + 1, :] for j in range(n)], axis=1)


def greet_rows(pc, tms, slots):
    bar = pltpu.get_barrier_semaphore()
    for off in range(1, tms):
        pl.semaphore_signal(bar, inc=1, device_id=(lax.rem(pc.tm + off, tms), pc.slot), device_id_type=MESH)
    for off in range(1, slots):
        pl.semaphore_signal(bar, inc=1, device_id=(pc.tm, lax.rem(pc.slot + off, slots)), device_id_type=MESH)
    pl.semaphore_wait(bar, tms + slots - 2)


def middle_body(
    lens, att, x1_ref, cot, wn, taps, bn_gain, bn_bias, gain3, gain4, gain5,
    out_h, dx2_h, datt_h, g_h, smalls_ref, bns_ref, cores,
    w_o, w_ci, w_co, w_f2i, w_f2o, fsem, early, late, hsem, gm_ref, ddwo_ref, z_ref, ext, ext2, dwo_ref, pre_ref, dgm_ref, acc, x2_ref, core, out_ref, dx2_ref, datt_ref, g_ref, hid_ref, dpre_ref, csem, *bufs,
):
    pc = Place()
    tms, slots = lax.axis_size("tm"), lax.axis_size("slot")
    rows, width = x1_ref.shape
    count = taps.shape[0]
    fetch, put = Fetch(fsem), Fetch(csem)
    outs = []
    got = {n: fetch(part_of(wn, n), d) for n, d in (("o", w_o), ("ci", w_ci), ("co", w_co), ("f2i", w_f2i), ("f2o", w_f2o))}
    greet_rows(pc, tms, slots)
    taker = Taker(bufs)
    totals = Totals(pc, taker(4)), Totals(pc, taker(4))
    flows = []
    for i, name in enumerate(FRONT):
        src = g_ref.at[pl.ds(MID[name], GROUP), :]
        half_rows = lambda o, n, lanes, src=src: src[pl.ds(pl.multiple_of(pc.at["c"] * (GROUP // 2) + o, 16), n), lanes]
        flows += make_flows(pc, name, "front", src, half_rows, core.at[i], None, 0, taker)

    def halo(src, dst, k, step):
        dev = (lax.rem(pc.tm + step + tms, tms), pc.slot)
        return pltpu.make_async_remote_copy(
            src_ref=src, dst_ref=dst, send_sem=hsem.at[2 * k], recv_sem=hsem.at[2 * k + 1], device_id=dev, device_id_type=MESH
        )

    got["o"].wait()
    x2 = x1_ref[...] + dot(att[...], w_o[...])
    x2_ref[...] = x2
    a3 = norm(x2, gain3[...]).astype(BF)
    got["ci"].wait()
    z1 = dot(a3, w_ci[pl.ds(0, width), :])
    z2 = dot(a3, w_ci[pl.ds(width, width), :])
    z_ref[:, pl.ds(0, width)] = z1
    z_ref[:, pl.ds(width, width)] = z2
    ok = valid_rows(lens, rows)
    gm_ref[...] = (z1 * sigmoid(z2) * ok).astype(BF)
    cp = halo(gm_ref.at[pl.ds(rows - count, count), :], early, 0, 1)
    cp.start()
    spread(ext, count, gm_ref[...])
    cp.wait()
    spread(ext, 0, jnp.where(pc.tm > 0, early[...], jnp.zeros((), BF)))
    tap_sum(ext, taps, dwo_ref, lambda k: k + 1)
    dwo = dwo_ref[...]
    dwv = dwo * ok
    totals[0].begin(
        packed(
            [
                jnp.sum(dwv, axis=0, keepdims=True),
                jnp.sum(dwv * dwv, axis=0, keepdims=True),
                jnp.zeros((1, 2 * width), F32) + jnp.sum(ok, axis=0, keepdims=True),
            ]
        )
    )
    totals[0].turn()
    sums = totals[0].done()
    total = sums[2 * width // LANE : 2 * width // LANE + 1, 0:1]
    mu = unpacked(sums, 0, width) / total
    inv = lax.rsqrt(unpacked(sums, 1, width) / total - mu * mu + EPS)
    xhat = (dwo_ref[...] - mu) * inv
    sw, slope = swish_and_slope(xhat * bn_gain[...] + bn_bias[...])
    sw = sw.astype(BF)
    got["co"].wait()
    x3 = x2_ref[...] + dot(sw, w_co[...])
    a4 = norm(x3, gain4[...]).astype(BF)
    got["f2i"].wait()
    got["f2o"].wait()
    x4 = x3 + 0.5 * ffn_forward(a4, w_f2i, w_f2o, pre_ref)
    out_ref[...] = norm(x4, gain5[...]).astype(BF)
    outs.append(put(out_ref, out_h))
    dx4, gg5 = norm_back(x4, gain5[...], cot[...].astype(F32))
    g4 = (0.5 * dx4).astype(BF)
    lo = FLAT["o"]
    da4 = ffn_through(g4, w_f2i, w_f2o, pre_ref, hid_ref, dpre_ref)
    back, gg4 = norm_back(x3, gain4[...], da4)
    dx3 = dx4 + back
    g3 = dx3.astype(BF)
    dbn = dot_nt(g3, w_co[...]) * slope
    totals[1].begin(packed([jnp.sum(dbn * xhat, axis=0, keepdims=True), jnp.sum(dbn, axis=0, keepdims=True)]))
    part = lambda name: g_ref.at[pl.ds(MID[name], GROUP), :]
    ffn_in_grad(a4, dpre_ref, part("f2i"))
    totals[1].turn()
    advance(flows)
    ffn_out_grad(g4, hid_ref, part("f2o"))
    g_ref[pl.ds(FLAT["co"] - lo, width), :] = dot_tn(sw, g3).astype(BF)
    for name in ("f2i", "f2o"):
        if name not in FRONT:
            outs.append(put(part(name), g_h.at[pl.ds(MID[name], GROUP), :]))
    sums2 = totals[1].done()
    gain_sum, bias_sum = unpacked(sums2, 0, width), unpacked(sums2, 1, width)
    bns_ref[0:1, :] = gain_sum
    bns_ref[1:2, :] = bias_sum
    bns_ref[2:8, :] = jnp.zeros((6, width), F32)
    ddwo_ref[...] = (bn_gain[...] * inv * (dbn - ok * (bias_sum + xhat * gain_sum) / total)).astype(BF)
    cp = halo(ddwo_ref.at[pl.ds(0, count), :], late, 1, -1)
    cp.start()
    advance(flows)
    spread(ext2, 0, ddwo_ref[...])
    cp.wait()
    spread(ext2, rows, jnp.where(pc.tm < tms - 1, late[...], jnp.zeros((), BF)))
    tap_sum(ext2, taps, dgm_ref, lambda k: count - 1 - k)
    block = 64 if rows % 64 == 0 else 16
    for b in range(ext.shape[0]):
        acc[...] = jnp.zeros(acc.shape, F32)

        def one(i, carry, b=b):
            mine = ext2[b, pl.ds(pl.multiple_of(i * block, block), block), :]
            for k in range(count):
                prod = mine * ext[b, pl.ds(i * block + k + 1, block), :]
                acc[k] = acc[k] + jnp.sum(prod.reshape(block // 8, 8, LANE), axis=0)
            return carry

        lax.fori_loop(0, rows // block, one, 0)
        smalls_ref[pl.ds(0, count), pl.ds(b * LANE, LANE)] = jnp.sum(acc[...], axis=1)
    z1 = z_ref[:, pl.ds(0, width)]
    sg = sigmoid(z_ref[:, pl.ds(width, width)])
    dg = dgm_ref[...] * ok
    dz1 = (dg * sg).astype(BF)
    dz2 = (dg * z1 * sg * (1.0 - sg)).astype(BF)
    a3t = norm(x2_ref[...], gain3[...]).astype(BF).T
    g_ref[pl.ds(FLAT["ci"] - lo, width), :] = dot(a3t, dz1).astype(BF)
    g_ref[pl.ds(FLAT["ci"] - lo + width, width), :] = dot(a3t, dz2).astype(BF)
    da3 = dot_nt(dz1, w_ci[pl.ds(0, width), :]) + dot_nt(dz2, w_ci[pl.ds(width, width), :])
    back, gg3 = norm_back(x2_ref[...], gain3[...], da3)
    dx2 = dx3 + back
    dx2_ref[...] = dx2
    outs.append(put(dx2_ref, dx2_h))
    g2 = dx2.astype(BF)
    g_ref[pl.ds(0, width), :] = dot_tn(att[...], g2).astype(BF)
    outs.append(put(g_ref.at[pl.ds(0, GROUP), :], g_h.at[pl.ds(0, GROUP), :]))
    datt_ref[...] = dot_nt(g2, w_o[...]).astype(BF)
    outs.append(put(datt_ref, datt_h))
    advance(flows)
    outs.append(put(core, cores))
    smalls_ref[pl.ds(count, 8), :] = jnp.concatenate([gg3, gg4, gg5, jnp.zeros((5, width), F32)], axis=0)
    for flow in flows:
        flow.finish()
    for cp in outs:
        cp.wait()


class Butterfly:
    @staticmethod
    def scratch(devices, shape):
        n = devices.bit_length() - 1
        return [pltpu.VMEM((n,) + shape, F32), pltpu.SemaphoreType.DMA((n,)), pltpu.SemaphoreType.DMA((n,))]

    def __init__(self, pc, value, bufs):
        self.value, (self.got, self.ssem, self.rsem) = value, bufs
        self.devs = []
        for axis, me in (("tm", pc.tm), ("slot", pc.slot)):
            bit = 1
            while bit < lax.axis_size(axis):
                to = me + bit - 2 * bit * lax.rem(lax.div(me, bit), 2)
                self.devs.append((to, pc.slot) if axis == "tm" else (pc.tm, to))
                bit *= 2

    def copy(self, k):
        return pltpu.make_async_remote_copy(
            src_ref=self.value, dst_ref=self.got.at[k], send_sem=self.ssem.at[k], recv_sem=self.rsem.at[k],
            device_id=self.devs[k], device_id_type=MESH,
        )

    def stage(self, k):
        if k > 0:
            self.copy(k - 1).wait()
            self.value[...] = self.value[...] + self.got[k - 1]
        if k < len(self.devs):
            self.copy(k).start()


GROUP = 2048


class KeyGrads:
    @staticmethod
    def scratch(tms, rows):
        pairs, xs = H // 2, tms // 2
        sems = pltpu.SemaphoreType.DMA((pairs, xs + 1))
        return [
            pltpu.VMEM((pairs, 2, 2, tms, HD, rows), BF),
            pltpu.VMEM((pairs, 2, tms, HD, rows), BF),
            pltpu.VMEM((xs - 1, pairs, 2, 2, HD, rows), BF),
            pltpu.VMEM((pairs, 2, 2, HD, rows), BF),
            pltpu.VMEM((pairs, 2, HD, rows), BF),
            sems,
            sems,
        ]

    def __init__(self, pc, bufs):
        self.pc = pc
        self.mine, self.core, self.line, self.both, self.got, self.ssem, self.rsem = bufs

    def put(self, p, kind, e, value):
        rows = self.mine.shape[-1]
        for t in range(self.mine.shape[3]):
            self.mine[p, kind, e, t] = value[:, t * rows : (t + 1) * rows].astype(BF)

    def copy(self, p, k, src, dst, dev):
        return pltpu.make_async_remote_copy(
            src_ref=src, dst_ref=dst, send_sem=self.ssem.at[p, k], recv_sem=self.rsem.at[p, k], device_id=dev, device_id_type=MESH
        )

    def first(self, p):
        ((_, dev, _),) = self.pc.peers("c")
        return [self.copy(p, 0, self.mine.at[p, :, 1 - self.pc.at["c"]], self.core.at[p], dev)]

    def second(self, p):
        return [
            self.copy(p, off, self.core.at[p, :, pl.ds(2 * pos, 2)], self.line.at[off - 1, p], dev) for off, dev, pos in self.pc.peers("x")
        ]

    def third(self, p):
        ((_, dev, _),) = self.pc.peers("c")
        return [self.copy(p, self.pc.size["x"], self.both.at[p, :, 1 - self.pc.at["c"]], self.got.at[p], dev)]

    def step(self, p, i):
        c, x = self.pc.at["c"], self.pc.at["x"]
        if i == 1:
            for cp in self.first(p):
                cp.wait_recv()
            for kind in range(2):
                for t in range(self.core.shape[2]):
                    total = self.core[p, kind, t].astype(F32) + self.mine[p, kind, c, t].astype(F32)
                    self.core[p, kind, t] = total.astype(BF)
        if i == 2:
            for cp in self.second(p):
                cp.wait_recv()
            for kind in range(2):
                for t in range(2):
                    total = self.core[p, kind, 2 * x + t].astype(F32)
                    for j in range(self.line.shape[0]):
                        total = total + self.line[j, p, kind, t].astype(F32)
                    self.both[p, kind, t] = total.astype(BF)
        if i == 3:
            for cp in self.third(p):
                cp.wait_recv()
            for cp in self.first(p) + self.second(p):
                cp.wait_send()
            return
        for cp in (self.first, self.second, self.third)[i](p):
            cp.start()

    def sent(self, p):
        for cp in self.third(p):
            cp.wait_send()

    def collect(self, p, kind, dst):
        c = self.pc.at["c"]
        own = self.both[p, kind, c]
        other = self.got[p, kind]
        dst[pl.ds(pl.multiple_of(p * LANE + c * HD, HD), HD), :] = own
        dst[pl.ds(pl.multiple_of(p * LANE + (1 - c) * HD, HD), HD), :] = other


def late_body(
    qu_h, qv_h, kv_h, wn, trig_h, sin_h, cos_h, probs, datt_h, att_h, g_mid, cores_h, a2_h, x1_h, dx2_h, x_h, pre_h, smalls2, gain2, gain1,
    dx0_ref, flat, total_ref,
    qu, qv, kv, w_p, trig, sin, cos, datt, att, a2, x1_ref, dx2_ref, x_ref, wqkv, own, core, psem, fsem,
    dq_ref, dkt, dvt, gpost, qut, qvt, datt_t, g_low, *bufs,
):
    pc = Place()
    rows = qu.shape[0]
    half = sin.shape[1]
    fetch = Fetch(fsem)
    c = pc.at["c"]
    whole = [name for name in MID if name not in FRONT]
    met = pc.greet("cxyz")
    owns = [fetch(g_mid.at[rows_at(MID[name] + c * (GROUP // 2), GROUP // 2), :], own.at[i]) for i, name in enumerate(whole)]
    owns += [fetch(cores_h.at[i], core.at[i]) for i in range(len(FRONT))]
    needed = [fetch(s, d) for s, d in ((qu_h, qu), (datt_h, datt), (att_h, att), (kv_h, kv))]

    def copies(first, pairs):
        return lambda: [pltpu.make_async_copy(s, d, fsem.at[first + i]) for i, (s, d) in enumerate(pairs)]

    second = copies(fetch.n, ((qv_h, qv), (part_of(wn, "p"), w_p), (trig_h, trig), (sin_h, sin), (cos_h, cos)))
    later = copies(
        fetch.n + 5, ((a2_h, a2), (x1_h, x1_ref), (dx2_h, dx2_ref), (x_h, x_ref), (wn.at[pl.ds(FLAT["q"], 1536), :], wqkv))
    )
    last_in = lambda pre_ref, w1: copies(fetch.n + 10, ((pre_h, pre_ref), (wn.at[pl.ds(0, 4096), :], w1)))()
    taker = Taker(bufs)
    keys = KeyGrads(pc, taker(7))
    fly = Butterfly(pc, total_ref, taker(3))
    groups = {}
    for i, name in enumerate(FRONT):
        groups[name] = make_flows(pc, name, "back", None, None, core.at[i], flat, FLAT[name], taker)
    for i, name in enumerate(whole):
        mine = lambda o, n, lanes, i=i: own[i, pl.ds(o, n), lanes]
        src = g_mid.at[pl.ds(MID[name], GROUP), :]
        groups[name] = make_flows(pc, name, "whole", src, mine, core.at[len(FRONT) + i], flat, FLAT[name], taker)
    for i, name in enumerate(("q", "f1i", "f1o")):
        at = FLAT[name]
        mine = lambda o, n, lanes, at=at: g_low[pl.ds(pl.multiple_of(at + c * (GROUP // 2) + o, 16), n), lanes]
        groups[name] = make_flows(pc, name, "whole", g_low.at[pl.ds(at, GROUP), :], mine, core.at[3 + i], flat, at, taker)
    def run(point):
        picked = [(NAMES[token // 4], token % 4) for token in TURNS.get(point, ())]
        stages = [groups[name][i].take() for name, i in picked if i < len(groups[name])]
        return lambda: [stage() for stage in stages]

    first = run(-1)
    plan = {at: run(at) for at in range(2 * H)}
    after = lambda point: run(point)()
    scale = HD**-0.5

    def scores(p, pbuf, load):
        at = cols(p)
        for e in range(2):
            mine = lane_half(e)
            part = pl.ds(pl.multiple_of(p * LANE + e * HD, HD), HD)
            dm = jnp.where(mine, datt[:, at], jnp.zeros((), BF))
            inner = jnp.sum(dm.astype(F32) * att[:, at].astype(F32), axis=-1, keepdims=True)
            dp = dot_nt(dm, kv[p, 1].reshape(-1, LANE))
            load(2 * p + e).wait()
            low_p = pbuf[2 * p + e]
            ds = (low_p.astype(F32) * (dp - inner)).astype(BF)
            pbuf[2 * p + e] = ds
            keys.put(p, 0, e, dot(qut[part, :], ds))
            keys.put(p, 1, e, dot(datt_t[part, :], low_p))
            if e == 0:
                pl.when(p > 0)(lambda: keys.step(p - 1, 1))
            else:
                keys.step(p, 0)
            ticks(e, plan, p)

    def queries(p, pbuf):
        at = cols(p)
        dqu = dqv = None
        for e in range(2):
            mine = lane_half(e)
            part = pl.ds(pl.multiple_of(p * LANE + e * HD, HD), HD)
            ds = pbuf[2 * p + e]
            back = dot(ds, jnp.concatenate([trig[...], kv[p, 0].reshape(-1, LANE)], axis=1))
            db_s, db_c, part_u = back[:, :half], back[:, half : 2 * half], back[:, 2 * half :]
            da_s = (db_c * sin[...] - db_s * cos[...]).astype(BF)
            da_c = (db_c * cos[...] + db_s * sin[...]).astype(BF)
            turned = jnp.concatenate([da_s, da_c], axis=1)
            gpost[part, :] = dot(qvt[part, :], turned)
            part_v = dot(turned, w_p[:, at])
            dqu = part_u if e == 0 else jnp.where(mine, part_u, dqu)
            dqv = part_v if e == 0 else jnp.where(mine, part_v, dqv)
            if e == 0:
                pl.when(p == 0)(lambda: keys.step(last, 1))
            else:
                keys.step(p, 2)
            ticks(e, plan, p + H // 2)
        dqu = dqu * scale
        dqv = dqv * scale
        dq_ref[:, at] = (dqu + dqv).astype(BF)
        total_ref[pl.ds(37, 1), at] = jnp.sum(dqu, axis=0, keepdims=True)
        total_ref[pl.ds(38, 1), at] = jnp.sum(dqv, axis=0, keepdims=True)

    last = H // 2 - 1

    def attention(pbuf):
        load = lambda h: pltpu.make_async_copy(probs.at[h], pbuf.at[h], psem.at[h])
        for h in range(H):
            load(h).start()
        for cp in second() + later():
            cp.start()
        met()
        for cp in owns:
            cp.wait()
        first()
        for cp in needed:
            cp.wait()
        qut[...] = qu[...].T
        datt_t[...] = datt[...].T

        lax.fori_loop(0, H // 2, lambda p, t: (scores(p, pbuf, load), t)[1], 0)
        for cp in second():
            cp.wait()
        qvt[...] = qv[...].T
        lax.fori_loop(0, H // 2, lambda p, t: (queries(p, pbuf), t)[1], 0)

    pl.run_scoped(attention, pltpu.VMEM((H, rows, kv.shape[2] * rows), BF))

    def tail(pre_ref, w1, hid_ref, dpre_ref):
        for cp in last_in(pre_ref, w1):
            cp.start()
        g_low[pl.ds(FLAT["p"], 512), :] = gpost[...].T.astype(BF)
        for cp in later():
            cp.wait()
        a2t = a2[...].T
        g_low[pl.ds(FLAT["q"], 512), :] = dot(a2t, dq_ref[...]).astype(BF)
        da2 = dot_nt(dq_ref[...], wqkv[pl.ds(0, 512), :])
        after(16)
        for p in range(H // 2):
            keys.step(p, 3)
            keys.collect(p, 0, dkt)
            keys.collect(p, 1, dvt)
        g_low[pl.ds(FLAT["k"], 512), :] = dot_nt(a2t, dkt[...]).astype(BF)
        g_low[pl.ds(FLAT["v"], 512), :] = dot_nt(a2t, dvt[...]).astype(BF)
        advance(groups["q"])
        for cp in last_in(pre_ref, w1):
            cp.wait()
        ffn_hidden(pre_ref, hid_ref)
        after(17)
        da2 = da2 + dot_nt(dkt[...].T, wqkv[pl.ds(512, 512), :]) + dot_nt(dvt[...].T, wqkv[pl.ds(1024, 512), :])
        back, gg2 = norm_back(x1_ref[...], gain2[...], da2)
        dx1 = dx2_ref[...] + back
        g1 = (0.5 * dx1).astype(BF)
        x = x_ref[...].astype(F32)
        a1 = norm(x, gain1[...]).astype(BF)
        after(18)
        ffn_out_grad(g1, hid_ref, g_low.at[pl.ds(2048, 2048), :])
        advance(groups["f1o"])
        after(19)
        da1 = ffn_through(g1, w1.at[pl.ds(0, 2048), :], w1.at[pl.ds(2048, 2048), :], pre_ref, hid_ref, dpre_ref)
        after(20)
        ffn_in_grad(a1, dpre_ref, g_low.at[pl.ds(0, 2048), :])
        advance(groups["f1i"])
        back, gg1 = norm_back(x, gain1[...], da1)
        dx0_ref[...] = (dx1 + back).astype(BF)
        total_ref[pl.ds(smalls2.shape[0] - 5, 2), :] = jnp.concatenate([gg1, gg2], axis=0)

    pl.run_scoped(tail, pltpu.VMEM(pre_h.shape, F32), pltpu.VMEM((4096, 512), BF), pltpu.VMEM(pre_h.shape, BF), pltpu.VMEM(pre_h.shape, BF))
    count = smalls2.shape[0] - 8
    total_ref[pl.ds(0, count), :] = smalls2[pl.ds(0, count), :]
    total_ref[pl.ds(count, 3), :] = smalls2[pl.ds(count, 3), :]
    total_ref[pl.ds(count + 7, 1), :] = jnp.zeros((1, 512), F32)
    flows = flat_list(list(groups.values()))
    turns, steps = TURNS[21], len(fly.devs) + 1
    for i, token in enumerate(turns):
        if i * steps // len(turns) != (i - 1) * steps // len(turns):
            fly.stage(i * steps // len(turns))
        name, k = NAMES[token // 4], token % 4
        advance(groups[name][k : k + 1])
    while any(flow.now < flow.last for flow in flows):
        advance(flows)
    for p in range(H // 2):
        keys.sent(p)
    for flow in flows:
        flow.finish()


def widen_body(flat, total, bns, *refs):
    outs, smalls, (ibuf, obuf, rbuf, isem, osem, rsem) = refs[:11], refs[11:21], refs[21:]
    count = smalls[0].shape[0]
    lines = [pltpu.make_async_copy(total.at[pl.ds(0, count), :], smalls[0], rsem.at[0])]
    for i, ref in enumerate(smalls[1:]):
        rbuf[i] = total[pl.ds(count + i, 1), :] if i < 7 else bns[pl.ds(i - 7, 1), :]
        lines.append(pltpu.make_async_copy(rbuf.at[i], ref, rsem.at[1 + i]))
    for cp in lines:
        cp.start()
    step = 512
    n = FLAT_ROWS // step
    loads = [pltpu.make_async_copy(flat.at[pl.ds(i * step, step), :], ibuf.at[i], isem.at[i]) for i in range(n)]
    for cp in loads:
        cp.start()
    stores = []
    slots = obuf.shape[0]
    for i in range(n):
        name = [m for m in ORDER if FLAT[m] <= i * step][-1]
        out = outs[ORDER.index(name)]
        off = i * step - FLAT[name]
        fold = FOLDS.get(name, 1)
        if fold == 1:
            dst = out.at[pl.ds(off, step), :]
        else:
            dst = out.at[:, pl.ds(off, step)]
        loads[i].wait()
        if i >= slots:
            stores[i - slots].wait()
        obuf[i % slots] = ibuf[i].astype(F32)
        stores.append(pltpu.make_async_copy(obuf.at[i % slots], dst, osem.at[i % slots]))
        stores[-1].start()
    for cp in stores[-slots:] + lines:
        cp.wait()


def remote(body, cid, outs, ins, scratch, name):
    def space(x):
        if x is None:
            return pl.BlockSpec(memory_space=pl.ANY)
        return pl.BlockSpec(memory_space=x)

    return pl.pallas_call(
        body,
        out_shape=[jax.ShapeDtypeStruct(s, d) for s, d, _ in outs],
        in_specs=[space(m) for _, m in ins],
        out_specs=[space(m) for _, _, m in outs],
        scratch_shapes=list(scratch),
        compiler_params=pltpu.CompilerParams(collective_id=cid, has_side_effects=True, vmem_limit_bytes=VMEM_LIMIT),
        name=name,
    )(*[x for x, _ in ins])


def local(
    inputs, cotangent, lengths, weight_noise, ffn1_in, ffn1_out, query_w, key_w, value_w, pos_w, out_w,
    conv_in, conv_out, ffn2_in, ffn2_out, conv_kernel, ffn1_gain, attn_gain, conv_gain, ffn2_gain,
    final_gain, bn_gain, bn_bias, pos_u, pos_v,
):
    _, rows, width = inputs.shape
    tms, slots = lax.axis_size("tm"), lax.axis_size("slot")
    frames = rows * tms
    count = conv_kernel.shape[0]
    devices = tms * slots
    size = Place().size
    x = inputs[0]
    cot = cotangent[0]
    gains = [g.reshape(1, -1) for g in (ffn1_gain, attn_gain, conv_gain, ffn2_gain, final_gain)]
    bng, bnb, pu, pv = (g.reshape(1, -1) for g in (bn_gain, bn_bias, pos_u, pos_v))
    raws = (ffn1_in, ffn1_out, query_w, key_w, value_w, pos_w, out_w, conv_in, conv_out, ffn2_in, ffn2_out)
    VM, HB, SM = pltpu.VMEM, None, pltpu.SMEM
    DMA = pltpu.SemaphoreType.DMA
    V = lambda shape, dtype=BF: pltpu.VMEM(shape, dtype)
    shard_rows = weight_noise.shape[1] // width
    half, hidden = width // 2, 2048
    keys = (H // 2, 2, tms, rows, LANE)
    specs = [
        ((FLAT_ROWS, width), BF), ((rows, width), F32), ((rows, hidden), F32), ((rows, width), BF), ((rows, width), BF), ((rows, width), BF),
        (keys, BF), ((frames, width), BF), ((rows, half), F32), ((rows, half), F32), ((rows, width), BF), ((H, rows, frames), BF),
    ]
    wn, x1, pre1, a2, qu, qv, kv, trig, sin, cos, att, probs = remote(
        early_body, 0, [spec + (HB,) for spec in specs],
        [(lengths, SM), (weight_noise, VM)] + [(r, HB) for r in raws] + [(x, VM), (gains[0], VM), (gains[1], VM), (pu, VM), (pv, VM)],
        [V((FLAT_ROWS, width)), V((width // LANE, shard_rows, LANE), F32)]
        + [V(*spec) for spec in specs[1:10]]
        + [V((2, frames // 64, half), F32), V((2, 64, half), F32), V((rows, width)), V((2, rows, frames)), DMA((18,)), DMA((16,)), DMA((2,))]
        + Gather.scratch(size, shard_rows, width) + KeysAll.scratch(size["x"]),
        "early",
    )
    ext = pltpu.VMEM((width // LANE, rows + count, LANE), F32)
    output, dx2, datt, g_mid, smalls2, bns, cores = remote(
        middle_body, 1,
        [((rows, width), BF, HB), ((rows, width), F32, HB), ((rows, width), BF, HB), ((3 * GROUP, width), BF, HB),
         ((count + 8, width), F32, VM), ((8, width), F32, VM), ((max(1, len(FRONT)), GROUP // 2, width), BF, HB)],
        [(lengths, SM), (att, VM), (x1, VM), (cot, VM), (wn, HB), (conv_kernel, VM), (bng, VM), (bnb, VM)] + [(g, VM) for g in gains[2:]],
        [pltpu.VMEM((FLAT_SIZE[n], width), BF) for n in ("o", "ci", "co", "f2i", "f2o")]
        + [DMA((5,)), pltpu.VMEM((count, width), BF), pltpu.VMEM((count, width), BF), DMA((4,)),
           pltpu.VMEM((rows, width), BF), pltpu.VMEM((rows, width), BF), pltpu.VMEM((rows, 2 * width), F32), ext, ext,
           pltpu.VMEM((rows, width), F32), pltpu.VMEM((rows, hidden), F32), pltpu.VMEM((rows, width), F32),
           pltpu.VMEM((count, 8, LANE), F32), pltpu.VMEM((rows, width), F32), V((max(1, len(FRONT)), GROUP // 2, width)),
           V((rows, width)), V((rows, width), F32), V((rows, width)), V((3 * GROUP, width)),
           V((rows, hidden)), V((rows, hidden)), DMA((7,))]
        + Totals.scratch(tms, slots, 4 * width // LANE) + Totals.scratch(tms, slots, 2 * width // LANE) + flat_list([flat_list(flow_scratch(size, n, "front")) for n in FRONT]),
        "middle",
    )
    dx0, flat, total = remote(
        late_body, 2, [((rows, width), BF, VM), ((FLAT_ROWS, width), BF, HB), ((count + 8, width), F32, VM)],
        [(t, HB) for t in (qu, qv, kv, wn, trig, sin, cos, probs, datt, att, g_mid, cores, a2, x1, dx2, x, pre1)]
        + [(smalls2, VM), (gains[1], VM), (gains[0], VM)],
        [V((rows, width)), V((rows, width)), V(keys), V((width, width)), V((frames, width)),
         V((rows, half), F32), V((rows, half), F32), V((rows, width)), V((rows, width)), V((rows, width)),
         V((rows, width), F32), V((rows, width), F32), V((rows, width)), V((3 * width, width)),
         V((3 - len(FRONT), GROUP // 2, width)), V((6, GROUP // 2, width)), DMA((H,)), DMA((20,)),
         V((rows, width)), V((width, rows)), V((width, rows)), V((width, width), F32), V((width, rows)), V((width, rows)), V((width, rows)),
         V((FLAT_ROWS // 2, width))]
        + KeyGrads.scratch(tms, rows) + Butterfly.scratch(devices, (count + 8, width))
        + flat_list([flat_list(flow_scratch(size, n, "back")) for n in FRONT])
        + flat_list([flat_list(flow_scratch(size, n, "whole")) for n in MID if n not in FRONT])
        + flat_list([flat_list(flow_scratch(size, n, "whole")) for n in ("q", "f1i", "f1o")]),
        "late",
    )
    big = pl.pallas_call(
        widen_body,
        out_shape=[jax.ShapeDtypeStruct(r.shape, F32) for r in raws]
        + [jax.ShapeDtypeStruct((count, width), F32)] + [jax.ShapeDtypeStruct((1, width), F32)] * 9,
        in_specs=[pl.BlockSpec(memory_space=pl.ANY)] + [pl.BlockSpec(memory_space=pltpu.VMEM)] * 2,
        out_specs=[pl.BlockSpec(memory_space=pl.ANY)] * 21,
        scratch_shapes=[pltpu.VMEM((24, 512, width), BF), pltpu.VMEM((4, 512, width), F32), pltpu.VMEM((9, 1, width), F32), DMA((24,)), DMA((4,)), DMA((10,))],
        compiler_params=pltpu.CompilerParams(vmem_limit_bytes=VMEM_LIMIT),
        name="widen",
    )(flat, total, bns)
    t = [r[0] for r in big[12:]]
    return (output[None], dx0[None]) + tuple(big[:11]) + (
        big[11], t[3], t[4], t[0], t[1], t[2], t[7], t[8], t[5], t[6],
    )


def solution(mesh):
    split = P("slot", "tm", None)
    in_specs = (split, split, P("slot"), P(("tm", "slot"), None)) + (P(),) * 21
    out_specs = (split, split) + (P(),) * 21
    return jax.shard_map(local, mesh=mesh, in_specs=in_specs, out_specs=out_specs, check_vma=False)
```

```python
import math

import jax
import jax.numpy as jnp
from jax import lax
from jax.experimental import pallas as pl
from jax.experimental.pallas import tpu as pltpu
from jax.sharding import PartitionSpec as P

H = 8
HD = 64
LANE = 128
F32 = jnp.float32
BF = jnp.bfloat16
EPS = 1e-05
FILL = -1e30
VMEM_LIMIT = 60 * 2**20


def dot(a, b):
    return lax.dot_general(a, b, (((1,), (0,)), ((), ())), preferred_element_type=F32)


def dot_nt(a, b):
    return lax.dot_general(a, b, (((1,), (1,)), ((), ())), preferred_element_type=F32)


def dot_tn(a, b):
    return lax.dot_general(a, b, (((0,), (0,)), ((), ())), preferred_element_type=F32)


def norm_parts(v):
    mean = jnp.mean(v, axis=-1, keepdims=True)
    cen = v - mean
    r = lax.rsqrt(jnp.mean(cen * cen, axis=-1, keepdims=True) + EPS)
    return cen * r, r


def norm(v, gain):
    u, _ = norm_parts(v)
    return u * gain


def norm_back(v, gain, e):
    u, r = norm_parts(v)
    eg = e * gain
    back = r * (eg - jnp.mean(eg, axis=-1, keepdims=True) - u * jnp.mean(eg * u, axis=-1, keepdims=True))
    return back, jnp.sum(e * u, axis=0, keepdims=True)


def sigmoid(v):
    return 1.0 / (1.0 + jnp.exp(-v))


def swish_and_slope(v):
    s = sigmoid(v)
    sv = s * v
    return sv, s + sv * (1.0 - s)


def cols(p, width=LANE):
    return pl.ds(pl.multiple_of(p * width, width), width)


def lane_half(e):
    lane = lax.broadcasted_iota(jnp.int32, (1, LANE), 1)
    return (lane < HD) if e == 0 else (lane >= HD)


def call(body, outs, ins, scratch=(), name=None):
    return pl.pallas_call(
        body,
        out_shape=[jax.ShapeDtypeStruct(s, d) for s, d in outs],
        in_specs=[
            pl.BlockSpec(memory_space=pltpu.SMEM) if x.dtype == jnp.int32 else pl.BlockSpec(memory_space=pltpu.VMEM)
            for x in ins
        ],
        out_specs=[pl.BlockSpec(memory_space=pltpu.VMEM) for _ in outs],
        scratch_shapes=list(scratch),
        compiler_params=pltpu.CompilerParams(vmem_limit_bytes=VMEM_LIMIT),
        name=name,
    )(*ins)


MESH = pl.DeviceIdType.MESH


class Place:
    def __init__(self):
        tms, slots = lax.axis_size("tm"), lax.axis_size("slot")
        wide = 1 << ((slots.bit_length() - 1) // 2)
        self.size = {"c": 2, "x": tms // 2, "y": wide, "z": slots // wide}
        self.tm, self.slot = lax.axis_index("tm"), lax.axis_index("slot")
        self.at = {
            "c": lax.rem(self.tm, 2),
            "x": lax.div(self.tm, 2),
            "y": lax.rem(self.slot, wide),
            "z": lax.div(self.slot, wide),
        }

    def peer(self, axis, off):
        pos = dict(self.at)
        pos[axis] = lax.rem(pos[axis] + off, self.size[axis])
        return (pos["x"] * 2 + pos["c"], pos["z"] * self.size["y"] + pos["y"]), pos[axis]

    def peers(self, axis):
        return [(off,) + self.peer(axis, off) for off in range(1, self.size[axis])]

    def greet(self, axes):
        bar = pltpu.get_barrier_semaphore()
        count = 0
        for axis in axes:
            for _, dev, _ in self.peers(axis):
                pl.semaphore_signal(bar, inc=1, device_id=dev, device_id_type=MESH)
                count += 1
        return lambda: pl.semaphore_wait(bar, count)


def rows_at(start, size):
    return pl.ds(pl.multiple_of(start, 16), size)


def add_into(dst, start, lanes, terms, size):
    step = 64 if size % 64 == 0 else 16

    def one(i, carry):
        off = pl.multiple_of(i * step, step)
        total = terms[0](off, step).astype(F32)
        for term in terms[1:]:
            total = total + term(off, step).astype(F32)
        dst[pl.ds(pl.multiple_of(start + off, 16), step), lanes] = total.astype(dst.dtype)
        return carry

    lax.fori_loop(0, size // step, one, 0)


GROUP = 2048


class Flow:
    STAGES = 9

    @staticmethod
    def lane_parts(order, size):
        rows = GROUP // 2
        for axis in order[:2]:
            rows //= size[axis]
        return max(1, 16 * size[order[2]] // rows)

    @staticmethod
    def scratch(order, width, size, kind):
        shapes = []
        blk = GROUP // 2
        parts = Flow.lane_parts(order, size)
        for lv, axis in enumerate(order):
            n = size[axis]
            blk = blk * parts // n if lv == 2 else blk // n
            w = width // parts if lv == 2 else width
            if (kind != "front" or lv == 0) and (kind != "back" or lv > 0):
                shapes.append(pltpu.VMEM((n - 1, blk, w), BF))
        if kind != "front":
            shapes.append(pltpu.VMEM((blk, width // parts), BF))
        sems = pltpu.SemaphoreType.DMA
        return shapes + [sems((3,)), sems((2,)) if kind == "front" else sems((8,)), sems((1,))]

    def __init__(self, pc, order, lane, width, kind, src, own, core, out, first, bufs):
        self.ssem, self.rsem, self.lsem = bufs[-3:]
        bufs = list(bufs[:-3])
        self.now = 2 if kind == "back" else 0
        size = pc.size
        lanes = pl.ds(lane, width)
        c = pc.at["c"]
        top = GROUP // 2
        parts = self.lane_parts(order, size)
        blk, rel = [top], [0]
        for lv, axis in enumerate(order):
            if lv < 2:
                blk.append(blk[-1] // size[axis])
                rel.append(rel[-1] + pc.at[axis] * blk[-1])
        low = blk[2] * parts // size[order[2]]

        def share(pos):
            if parts == 1:
                return rel[2] + pos * low, lanes
            at = pl.multiple_of(lane + lax.rem(pos, parts) * (width // parts), LANE)
            return rel[2] + lax.div(pos, parts) * low, pl.ds(at, width // parts)

        ((_, cdev, _),) = pc.peers("c")
        into = [None] * 3
        if kind != "back":
            into[0] = bufs.pop(0)
        if kind != "front":
            into[1], into[2], fin = bufs
        copies = [[(lambda: src.at[rows_at((1 - c) * top, top), lanes], lambda: core.at[:, lanes], cdev)]]
        bytes_of = [lambda: core.at[:, lanes]]
        for lv, axis in enumerate(order):
            cps = []
            for off, dev, pos in pc.peers(axis):
                if lv < 2:
                    s = lambda lv=lv, pos=pos: core.at[rows_at(rel[lv] + pos * blk[lv + 1], blk[lv + 1]), lanes]
                else:
                    s = lambda pos=pos: core.at[rows_at(share(pos)[0], low), share(pos)[1]]
                cps.append((s, lambda lv=lv, off=off: into[lv].at[off - 1], dev))
            copies.append(cps)
            bytes_of.append(lambda lv=lv: into[lv])
        mine = share(pc.at[order[2]])
        out_share = lambda: out.at[rows_at(first + c * top + mine[0], low), mine[1]]
        out_at = lambda lv: out.at[rows_at(first + c * top + rel[lv], blk[lv]), lanes]
        copies.append([(lambda: fin, out_share, dev) for _, dev, _ in pc.peers(order[2])])
        bytes_of.append(
            lambda: out.at[rows_at(first + c * top + rel[2], (size[order[2]] - 1) * low), pl.ds(lane, width // parts)]
        )
        for lv in (2, 1):
            copies.append([(lambda lv=lv: out_at(lv), lambda lv=lv: out_at(lv), dev) for _, dev, _ in pc.peers(order[lv - 1])])
            bytes_of.append(
                lambda lv=lv: out.at[rows_at(first + c * top + rel[lv - 1], (size[order[lv - 1]] - 1) * blk[lv]), lanes]
            )
        copies.append([(lambda: out_at(0), lambda: out_at(0), cdev)])
        bytes_of.append(lambda: out_at(0))
        self.copies, self.bytes_of = copies, bytes_of

        def fold(lv):
            if lv == 0:
                add_into(core, 0, lanes, [lambda o, n: own(o, n, lanes), lambda o, n: core[pl.ds(o, n), lanes]], top)
                return
            row, ln, size_ = (mine + (low,)) if lv == 3 else (rel[lv], lanes, blk[lv])
            terms = [lambda o, n: core[pl.ds(pl.multiple_of(row + o, 16), n), ln]]
            for k in range(size[order[lv - 1]] - 1):
                terms.append(lambda o, n, k=k: into[lv - 1][k, pl.ds(o, n), :])
            if lv == 3:
                add_into(fin, 0, slice(None), terms, size_)
            else:
                add_into(core, row, lanes, terms, size_)

        keep = lambda: pltpu.make_async_copy(fin, out_share(), self.lsem.at[0])

        def s1():
            self.arrived(0)
            fold(0)
            self.start(1)

        def s2():
            if kind != "back":
                self.arrived(1)
                fold(1)
            if kind != "front":
                self.start(2)

        def s3():
            self.arrived(2)
            fold(2)
            self.start(3)

        def s4():
            self.arrived(3)
            fold(3)
            keep().start()
            self.start(4)

        def climb(i):
            def run():
                if i == 0:
                    keep().wait()
                self.arrived(4 + i)
                if i < 3:
                    self.start(5 + i)

            return run

        self.stages = [lambda: self.start(0), s1, s2, s3, s4] + [climb(i) for i in range(4)]
        self.last = 3 if kind == "front" else self.STAGES
        self.first = 2 if kind == "back" else 0

    def make(self, i, src, dst, dev):
        return pltpu.make_async_remote_copy(
            src_ref=src(), dst_ref=dst(), send_sem=self.ssem.at[i % 3], recv_sem=self.rsem.at[i], device_id=dev, device_id_type=MESH
        )

    def start(self, i):
        for src, dst, dev in self.copies[i]:
            self.make(i, src, dst, dev).start()

    def all_of(self, i):
        if len(self.copies[i]) == 1:
            return self.make(i, *self.copies[i][0])
        return self.make(i, self.bytes_of[i], self.bytes_of[i], self.copies[i][0][2])

    def arrived(self, i):
        self.all_of(i).wait_recv()

    def left(self, i):
        if i >= self.first:
            self.all_of(i).wait_send()

    def finish(self):
        self.left(self.last - 2)

    def take(self):
        if self.now >= self.last:
            return lambda: None
        i, self.now = self.now, self.now + 1

        def run():
            self.stages[i]()
            if i > 1:
                self.left(i - 2)

        return run


def advance(flows):
    for flow in flows:
        flow.take()()


MID = {"f2i": 2048, "f2o": 4096, "o": 0}
NAMES = ("f2i", "f2o", "o", "q", "f1o", "f1i")
AXES = {"A": ("y", "x", "z"), "B": ("x", "y", "z"), "X": ("z", "x", "y"), "Y": ("z", "y", "x")}
FRONT = ("f2i",)
LANES = {"f2i": "A2 B1 B1", "f2o": "A2 B1 X1", "o": "A2 B1 B1", "q": "A1 B1 B1 Y1", "f1o": "A1 B1 A1 X1", "f1i": "A1 B1 A1 B1"}
TURNS = {
    -1: (4, 5, 6, 8, 9, 10, 0, 1, 2,),
    0: (5, 6, 9,),
    1: (4, 8, 10,),
    2: (0, 1,),
    4: (5, 9, 2,),
    5: (6, 1,),
    6: (10, 0,),
    7: (2,),
    8: (6, 1, 5,),
    9: (4, 9,),
    10: (10, 6, 2,),
    11: (5,),
    12: (8, 9,),
    13: (10,),
    14: (0, 5, 6,),
    15: (4, 9, 1,),
    16: (10, 2,),
    17: (8, 5, 4,),
    18: (12, 13, 0,),
    19: (14, 15, 6,),
    20: (16, 17, 18,),
    21: (19, 12, 13, 8, 4, 0, 1, 2, 20, 21, 5, 22, 14, 1, 2, 12, 0, 5, 6, 23, 13, 16, 6, 17, 15, 18, 14, 12, 21, 8, 4, 13, 20, 16, 23, 17, 18, 19, 14, 22, 21, 15, 12, 20, 13, 9, 8, 23, 16, 15, 22, 17, 10, 19, 18, 12, 14, 4, 21, 13, 20, 9, 4, 19, 23, 16, 9, 10, 15, 22, 14, 18, 13, 10, 17, 21, 13, 23, 20, 15, 12, 16, 19, 8, 12, 18, 22, 17, 14, 8, 21, 20, 19, 14, 15, 22, 23, 15, 16, 17, 18, 21, 16, 19, 17, 20, 18, 23, 21, 19, 22, 20, 23, 22,),
}


def layout(name, size):
    words = LANES[name].split()
    if max(Flow.lane_parts(AXES[word[0]], size) for word in words) > 1:
        words = ["A2", "B2"]
    got, lane = [], 0
    for word in words:
        got.append((AXES[word[0]], lane, int(word[1]) * LANE))
        lane += got[-1][2]
    return got


def flow_scratch(size, name, kind):
    return [Flow.scratch(order, width, size, kind) for order, _, width in layout(name, size)]


def flat_list(lists):
    return [x for part in lists for x in part]


class Taker:
    def __init__(self, refs):
        self.refs = list(refs)

    def __call__(self, n):
        got, self.refs = self.refs[:n], self.refs[n:]
        return got


def make_flows(pc, name, kind, src, own, core, out, first, taker):
    flows = []
    for (order, lane, width), shapes in zip(layout(name, pc.size), flow_scratch(pc.size, name, kind)):
        flows.append(Flow(pc, order, lane, width, kind, src, own, core, out, first, taker(len(shapes))))
    return flows


FLAT = {"f1i": 0, "f1o": 2048, "q": 4096, "k": 4608, "v": 5120, "p": 5632, "o": 6144, "ci": 6656, "co": 7680, "f2i": 8192, "f2o": 10240}
FLAT_ROWS = 12288
ORDER = tuple(FLAT)
FOLDS = {"f1i": 4, "ci": 2, "f2i": 4}
FLAT_SIZE = {n: (list(FLAT.values()) + [FLAT_ROWS])[i + 1] - FLAT[n] for i, n in enumerate(FLAT)}


def ticks(point, plan, p):
    for at, run in plan.items():
        if at % 2 == point:
            pl.when(p == at // 2)(lambda run=run: (run(), None)[1])


class Gather:
    @staticmethod
    def scratch(size, shard_rows, width):
        part, pieces = Gather.cut(shard_rows)
        sems = pltpu.SemaphoreType.DMA((2 * pieces * (size["x"] + 6),))
        return [
            pltpu.VMEM((size["x"], 2, size["z"], size["y"], shard_rows, width), BF),
            pltpu.VMEM((width // LANE, 64, LANE), F32),
            sems,
            sems,
            pltpu.SemaphoreType.REGULAR,
        ]

    @staticmethod
    def cut(shard_rows):
        part = 64 if shard_rows % 64 == 0 else 16
        return part, shard_rows // part

    def __init__(self, pc, wf, bufs):
        self.pc, self.wf = pc, wf
        self.nb, self.scr, self.ssem, self.rsem, self.free = bufs
        self.shard_rows = self.nb.shape[4]
        self.part, self.pieces = self.cut(self.shard_rows)
        self.xs = pc.size["x"]
        self.used = 0
        self.stages = [self.plan(hx, q) for hx in range(2) for q in range(self.pieces)]

    def copies(self, ref, axis, only=None, total=None):
        out = []

        def make(ref, dev, k):
            return pltpu.make_async_remote_copy(
                src_ref=ref, dst_ref=ref, send_sem=self.ssem.at[k], recv_sem=self.rsem.at[k], device_id=dev, device_id_type=MESH
            )

        for off, dev, _ in self.pc.peers(axis):
            if only is not None and off != only:
                continue
            out.append((off, make(ref, dev, self.used)))
            if total is None:
                self.used += 1
        if total is None:
            return out, out
        self.used += 1
        return out, [(0, make(total, dev, self.used - 1))]

    def plan(self, hx, q):
        pc, nb = self.pc, self.nb
        x, c, z, y = (pc.at[a] for a in "xczy")
        rows = pl.ds(q * self.part, self.part)
        across = self.xs // 2
        side = pl.ds(hx * across, across)
        in_half = lambda pos: lax.div(pos, across) == hx
        width = nb.shape[5]
        wide, quarter = pl.ds(0, width // 2), width // 4
        away = pl.ds(3 * quarter, quarter)
        source = jnp.where(in_half(x), x, lax.rem(x + across, self.xs))
        lanes = pl.ds(pl.multiple_of(jnp.where(in_half(x), 2 * quarter, 3 * quarter), LANE), quarter)
        others = {axis: pl.ds(0, pc.size[axis] - 1) for axis in "xyz"}
        along = {
            "xa": self.copies(nb.at[x, c, z, y, rows, wide], "x"),
            "xd": self.copies(nb.at[x, c, z, y, rows, away], "x", across),
            "za": self.copies(nb.at[side, c, z, y, rows, wide], "z", None, nb.at[side, c, others["z"], y, rows, wide]),
            "zb": self.copies(nb.at[source, c, z, y, rows, lanes], "z", None, nb.at[source, c, others["z"], y, rows, lanes]),
            "ya": self.copies(nb.at[side, c, :, y, rows, wide], "y", None, nb.at[side, c, :, others["y"], rows, wide]),
            "yb": self.copies(nb.at[source, c, :, y, rows, lanes], "y", None, nb.at[source, c, :, others["y"], rows, lanes]),
            "xb": self.copies(nb.at[source, c, :, :, rows, lanes], "x", None, nb.at[others["x"], c, :, :, rows, lanes]),
            "c": self.copies(nb.at[side, c, :, :, rows], "c"),
        }

        def each(axis, what, cond=None):
            for off, cp in along[axis][0 if what == "start" else 1]:
                if cond is None:
                    getattr(cp, what)()
                else:
                    pl.when(cond(off))(lambda cp=cp: getattr(cp, what)())

        sends = lambda off: in_half(x)
        gets = lambda off: in_half(lax.rem(x - off + self.xs, self.xs))

        def end():
            each("c", "wait_recv")
            each("xa", "wait_send", sends)
            for axis in ("za", "zb", "ya", "yb", "xb"):
                each(axis, "wait_send")
            if self.part == 64:
                self.mix_half(hx, q)
            elif q == self.pieces - 1:
                self.mix_half(hx, None)

        def done():
            each("c", "wait_send")

        def then(*acts):
            return lambda: [each(*act) for act in acts]

        def let():
            @pl.when(in_half(x))
            def _():
                ((_, cp),) = along["xd"][0]
                cp.wait_send()
                ((_, dev, _),) = [peer for peer in pc.peers("x") if peer[0] == across]
                pl.semaphore_signal(self.free, inc=1, device_id=dev, device_id_type=MESH)

        def allowed():
            pl.when(jnp.logical_not(in_half(x)))(lambda: pl.semaphore_wait(self.free, 1))

        return {
            "X": then(("xa", "start", sends), ("xd", "start", sends)),
            "Z": then(("xa", "wait_recv", gets), ("xd", "wait_recv", gets), ("za", "start"), ("zb", "start")),
            "Y": lambda: (then(("za", "wait_recv"), ("zb", "wait_recv"), ("ya", "start"), ("yb", "start"))(), let()),
            "W": lambda: (each("yb", "wait_recv"), allowed(), each("xb", "start")),
            "C": then(("ya", "wait_recv"), ("xb", "wait_recv"), ("c", "start")),
            "E": end,
            "D": done,
        }

    def run(self, ops):
        for op in ops:
            if 0 <= op[1] < len(self.stages):
                self.stages[op[1]][op[0]]()

    def finish(self):
        for stages in self.stages:
            stages["D"]()

    def noise_at(self, row):
        pc = self.pc
        got = []
        sub = min(64, self.part)
        for i in range(64 // sub):
            at = row + i * sub
            d = lax.div(at, self.shard_rows)
            slots = pc.size["z"] * pc.size["y"]
            tm, sl = lax.div(d, slots), lax.rem(d, slots)
            off = pl.multiple_of(lax.rem(at, self.shard_rows), 16)
            got.append(
                self.nb[lax.div(tm, 2), lax.rem(tm, 2), lax.div(sl, pc.size["y"]), lax.rem(sl, pc.size["y"]), pl.ds(off, sub), :].astype(F32)
            )
        return got[0] if len(got) == 1 else jnp.concatenate(got, axis=0)

    def mix(self, row, base, size, fold):
        wf, scr = self.wf, self.scr
        value = self.noise_at(row)
        if fold == 1:
            at = rows_at(row, 64)
            wf[at, :] = (wf[at, :].astype(F32) + value).astype(BF)
            return
        for b in range(512 // LANE):
            scr[b] = value[:, b * LANE : (b + 1) * LANE]
        high = 64 // fold
        for j in range(fold):
            at = rows_at(base + j * (size // fold) + lax.div(row - base, fold), high)
            for b in range(512 // LANE):
                lanes = pl.ds(b * LANE, LANE)
                wf[at, lanes] = (wf[at, lanes].astype(F32) + scr[b, pl.ds(j, high, stride=fold), :]).astype(BF)

    def mix_half(self, hx, q):
        for name in ORDER:
            base, size, fold = FLAT[name], FLAT_SIZE[name], FOLDS.get(name, 1)
            if (base < FLAT_ROWS // 2) != (hx == 0):
                continue
            begin, end = base // 64, (base + size) // 64
            start, stride = (begin, 1) if q is None else (begin + (q - begin) % self.pieces, self.pieces)
            lax.fori_loop(
                0, (end - start + stride - 1) // stride,
                lambda i, t: (self.mix((start + i * stride) * 64, base, size, fold), t)[1], 0,
            )


class KeysAll:
    @staticmethod
    def scratch(xs):
        n = 2 * xs - 1
        sems = pltpu.SemaphoreType.DMA((H // 2, n))
        return [sems, sems]

    def __init__(self, pc, kv, bufs):
        self.pc, self.kv = pc, kv
        self.ssem, self.rsem = bufs

    def copy(self, p, k, tm, dev):
        ref = self.kv.at[p, :, tm]
        return pltpu.make_async_remote_copy(
            src_ref=ref, dst_ref=ref, send_sem=self.ssem.at[p, k], recv_sem=self.rsem.at[p, k], device_id=dev, device_id_type=MESH
        )

    def core(self, p):
        ((_, dev, _),) = self.pc.peers("c")
        return [self.copy(p, 0, self.pc.tm, dev)]

    def line(self, p):
        return [self.copy(p, off, self.pc.tm, dev) for off, dev, _ in self.pc.peers("x")]

    def relay(self, p):
        ((_, dev, _),) = self.pc.peers("c")
        xs = self.pc.size["x"]
        out = []
        for off in range(1, xs):
            source = lax.rem(self.pc.at["x"] - off + xs, xs) * 2 + self.pc.at["c"]
            out.append(self.copy(p, xs - 1 + off, source, dev))
        return out

    def send(self, p):
        for cp in self.core(p):
            cp.start()

    def send_line(self, p):
        for cp in self.line(p):
            cp.start()

    def forward(self, p):
        for come, on in zip(self.line(p), self.relay(p)):
            come.wait_recv()
            on.start()

    def ready(self, p):
        for cp in self.core(p) + self.relay(p):
            cp.wait_recv()

    def sent(self, p):
        for cp in self.line(p) + self.core(p) + self.relay(p):
            cp.wait_send()


def angle_tables(hi, lo, rates):
    for ref, step in ((hi, 64.0), (lo, 1.0)):
        count = ref.shape[1]
        angle = lax.broadcasted_iota(jnp.int32, (count, rates.shape[1]), 0).astype(F32) * step * rates
        ref[0] = jnp.sin(angle)
        ref[1] = jnp.cos(angle)


def angle_block(hi, lo, m):
    hs, hc = hi[0, pl.ds(m, 1), :], hi[1, pl.ds(m, 1), :]
    ls, lc = lo[0], lo[1]
    return hs * lc + hc * ls, hc * lc - hs * ls


def early_body(*refs):
    lens, noise, raws = refs[0], refs[1], refs[2:13]
    x_ref, gain1, gain2, pos_u, pos_v = refs[13:18]
    wn, x1_out, pre_out, a2_out, qu_out, qv_out, kv_out, trig_out, sin_out, cos_out, att_out, probs = refs[18:30]
    wf, flat, x1_ref, pre_ref, a2_ref, qu, qv, kv, trig, sin, cos, hi, lo, att, pbuf, wsem, osem, psem = refs[30:48]
    bufs = refs[48:]
    pc = Place()
    rows, width = x_ref.shape
    half = width // 2
    tms = lax.axis_size("tm")
    frames = rows * tms
    met = pc.greet("cxyz")
    loads = []
    for name, raw in zip(ORDER, raws):
        for j in range(FOLDS.get(name, 1)):
            size = FLAT_SIZE[name] // FOLDS.get(name, 1)
            dst = wf.at[pl.ds(FLAT[name] + j * size, size), :]
            loads.append(pltpu.make_async_copy(raw.at[:, pl.ds(j * 512, 512)], dst, wsem.at[len(loads)]))
            loads[-1].start()
    gather = Gather(pc, wf, bufs[:5])
    keys = KeysAll(pc, kv, bufs[5:7])

    def unfold(i, carry):
        for r in range(8):
            for b in range(width // LANE):
                at = pl.ds(pl.multiple_of((i * 8 + r) * width + b * LANE, LANE), LANE)
                flat[b, pl.ds(i * 8 + r, 1), :] = noise[:, at].astype(F32)
        return carry

    shard_rows = gather.shard_rows
    lax.fori_loop(0, shard_rows // 8, unfold, 0)
    for b in range(width // LANE):
        gather.nb[pc.at["x"], pc.at["c"], pc.at["z"], pc.at["y"], :, pl.ds(b * LANE, LANE)] = flat[b].astype(BF)
    rates = jnp.exp(lax.broadcasted_iota(jnp.int32, (1, half), 1).astype(F32) * (-2.0 * math.log(10000.0) / width))
    angle_tables(hi, lo, rates)

    def angles(m, carry):
        s, c = angle_block(hi, lo, m)
        at = rows_at(m * 64, 64)
        trig[at, pl.ds(0, half)] = s.astype(BF)
        trig[at, pl.ds(half, half)] = c.astype(BF)
        return carry

    def own_angles(m, carry):
        s, c = angle_block(hi, lo, pc.tm * (rows // 64) + m)
        sin[rows_at(m * 64, 64), :] = s
        cos[rows_at(m * 64, 64), :] = c
        return carry

    lax.fori_loop(0, frames // 64, angles, 0)
    lax.fori_loop(0, rows // 64, own_angles, 0)
    met()
    n = gather.pieces
    gather.run([("X", i) for i in range(2 * n)])
    gather.run([("Z", 0), ("Z", 1)])
    for cp in loads:
        cp.wait()
    outs = []

    def put(src, dst):
        cp = pltpu.make_async_copy(src, dst, osem.at[len(outs)])
        cp.start()
        outs.append(cp)

    x = x_ref[...].astype(F32)
    a1 = norm(x, gain1[...]).astype(BF)
    for t in range(2, n + 2):
        gather.run([("Z", t), ("Y", t - 2), ("W", t - 3), ("C", t - 4), ("E", t - 5)])
    gather.run([("W", n - 1), ("C", n - 2), ("E", n - 3), ("C", n - 1), ("E", n - 2), ("Z", n + 2), ("E", n - 1)])
    part = lambda name: wf.at[pl.ds(FLAT[name], FLAT_SIZE[name]), :]
    x1 = x + 0.5 * ffn_forward(a1, part("f1i"), part("f1o"), pre_ref)
    x1_ref[...] = x1
    a2 = norm(x1, gain2[...]).astype(BF)
    a2_ref[...] = a2
    k = dot(a2, part("k")[...]).astype(BF)
    v = dot(a2, part("v")[...]).astype(BF)
    for p in range(H // 2):
        kv[p, 0, pc.tm] = k[:, p * LANE : (p + 1) * LANE]
        kv[p, 1, pc.tm] = v[:, p * LANE : (p + 1) * LANE]
        if p == 0:
            keys.send_line(0)
        keys.send(p)
    gather.run([("Z", n + 3), ("Y", n), ("Y", n + 1)])
    q = dot(a2, part("q")[...])
    scale = HD**-0.5
    qu[...] = ((q + pos_u[...]).astype(BF).astype(F32) * scale).astype(BF)
    qv[...] = ((q + pos_v[...]).astype(BF).astype(F32) * scale).astype(BF)
    for src, dst in ((x1_ref, x1_out), (pre_ref, pre_out), (a2_ref, a2_out), (qu, qu_out), (qv, qv_out), (trig, trig_out), (sin, sin_out), (cos, cos_out)):
        put(src, dst)
    put(wf.at[pl.ds(0, FLAT_ROWS // 2), :], wn.at[pl.ds(0, FLAT_ROWS // 2), :])
    steps = {
        0: "W0 Y2 Z4", 1: "W1 Y3 Z5", 2: "C0 W2 Y4", 3: "E0 W3 Y5", 4: "C1 W4", 5: "E1 C2 W5", 6: "E2 C3", 7: "E3 C4 C5", 8: "E4 E5",
    }
    if n != 6:
        order = (("Z", 4), ("Y", 2), ("W", 0), ("C", 0), ("E", 0))
        steps = {8: " ".join("%s%d" % (op, i) for op, low in order for i in range(low, n))}
    steps = {at: [(op[0], n + int(op[1:])) for op in text.split()] for at, text in steps.items()}
    plan = {at: (lambda ops=ops: gather.run(ops)) for at, ops in steps.items() if at < H}
    ok = lax.broadcasted_iota(jnp.int32, (1, frames), 1) < lens[0]
    w_pos = part("p")
    store = lambda p, e: pltpu.make_async_copy(pbuf.at[e], probs.at[2 * p + e], psem.at[e])

    def pair(p, carry):
        at = cols(p)
        mixed = None
        for e in range(2):
            mine = lane_half(e)
            qve = jnp.where(mine, qv[:, at], jnp.zeros((), BF))
            que = jnp.where(mine, qu[:, at], jnp.zeros((), BF))
            turned = dot_nt(qve, w_pos[:, at])
            a_s, a_c = turned[:, :half], turned[:, half:]
            b_c = (a_s * sin[...] + a_c * cos[...]).astype(BF)
            b_s = (a_c * sin[...] - a_s * cos[...]).astype(BF)
            if e == 0:
                pl.when(p == 1)(lambda: keys.send_line(3))
                pl.when(p == 0)(lambda: (keys.forward(0), keys.send_line(1))[1])
                keys.ready(p)
            else:
                pl.when(p == 0)(lambda: keys.send_line(2))
            s = dot_nt(jnp.concatenate([b_s, b_c, que], axis=1), jnp.concatenate([trig[...], kv[p, 0].reshape(frames, LANE)], axis=1))
            s = jnp.where(ok, s, FILL)
            m = jnp.max(s, axis=-1, keepdims=True)
            ex = jnp.exp(s - m)
            tot = jnp.sum(ex, axis=-1, keepdims=True)
            low = (ex * (1.0 / tot)).astype(BF)
            pl.when(p > 0)(lambda: store(p - 1, e).wait())
            pbuf[e] = low
            store(p, e).start()
            got = dot(low, kv[p, 1].reshape(frames, LANE))
            mixed = got if e == 0 else jnp.where(mine, got, mixed)
            if e == 1:
                pl.when(p < H // 2 - 1)(lambda: keys.forward(p + 1))
            ticks(e, plan, p)
        att[:, at] = mixed.astype(BF)
        return carry

    lax.fori_loop(0, H // 2, pair, 0)
    put(kv, kv_out)
    put(att, att_out)
    gather.run(steps[8])
    put(wf.at[pl.ds(FLAT_ROWS // 2, FLAT_ROWS // 2), :], wn.at[pl.ds(FLAT_ROWS // 2, FLAT_ROWS // 2), :])
    for e in range(2):
        store(H // 2 - 1, e).wait()
    for p in range(H // 2):
        keys.sent(p)
    gather.finish()
    for cp in outs:
        cp.wait()


def chunk(c):
    return pl.ds(pl.multiple_of(c * 512, 512), 512)


def ffn_forward(normed, w_in, w_out, pre_ref):
    def one(c, acc):
        pre = dot(normed, w_in[chunk(c), :])
        pre_ref[:, chunk(c)] = pre
        return acc + dot((pre * sigmoid(pre)).astype(BF), w_out[chunk(c), :])

    return lax.fori_loop(0, w_in.shape[0] // 512, one, jnp.zeros((normed.shape[0], w_out.shape[1]), F32))


def ffn_through(g_low, w_in, w_out, pre_ref, hid_ref, dpre_ref):
    def one(c, acc):
        sw, slope = swish_and_slope(pre_ref[:, chunk(c)])
        hid_ref[:, chunk(c)] = sw.astype(BF)
        dpre = (dot_nt(g_low, w_out[chunk(c), :]) * slope).astype(BF)
        dpre_ref[:, chunk(c)] = dpre
        return acc + dot_nt(dpre, w_in[chunk(c), :])

    return lax.fori_loop(0, w_in.shape[0] // 512, one, jnp.zeros(g_low.shape, F32))


def ffn_in_grad(normed, dpre_ref, gin_ref):
    normed_t = normed.T

    def one(c, carry):
        gin_ref[chunk(c), :] = dot(normed_t, dpre_ref[:, chunk(c)]).astype(gin_ref.dtype)
        return carry

    lax.fori_loop(0, gin_ref.shape[0] // 512, one, 0)


def ffn_out_grad(g_low, hid_ref, gout_ref):
    def one(c, carry):
        gout_ref[chunk(c), :] = dot_tn(hid_ref[:, chunk(c)], g_low).astype(gout_ref.dtype)
        return carry

    lax.fori_loop(0, gout_ref.shape[0] // 512, one, 0)


def ffn_hidden(pre_ref, hid_ref):
    def one(c, carry):
        pre = pre_ref[:, chunk(c)]
        hid_ref[:, chunk(c)] = (pre * sigmoid(pre)).astype(BF)
        return carry

    lax.fori_loop(0, pre_ref.shape[1] // 512, one, 0)


class Fetch:
    def __init__(self, sems):
        self.sems, self.n = sems, 0

    def __call__(self, src, dst):
        cp = pltpu.make_async_copy(src, dst, self.sems.at[self.n])
        self.n += 1
        cp.start()
        return cp


def part_of(wn, name):
    return wn.at[pl.ds(FLAT[name], FLAT_SIZE[name]), :]


def valid_rows(lens, rows):
    first = lax.axis_index("tm") * rows
    return ((first + lax.broadcasted_iota(jnp.int32, (rows, 1), 0)) < lens[0]).astype(F32)


def spread(ext, start, value):
    value = value.astype(F32)
    for b in range(ext.shape[0]):
        ext[b, pl.ds(start, value.shape[0]), :] = value[:, b * LANE : (b + 1) * LANE]


def tap_sum(ext, taps, out_ref, offset):
    count = taps.shape[0]
    rows = out_ref.shape[0]
    block = 64 if rows % 64 == 0 else 16

    def one(i, carry):
        for b in range(ext.shape[0]):
            at = pl.ds(b * LANE, LANE)
            acc = jnp.zeros((block, LANE), F32)
            for k in range(count):
                acc = acc + taps[pl.ds(k, 1), at] * ext[b, pl.ds(i * block + offset(k), block), :]
            out_ref[pl.ds(pl.multiple_of(i * block, block), block), at] = acc
        return carry

    lax.fori_loop(0, rows // block, one, 0)


class Totals:
    @staticmethod
    def scratch(tms, slots, packed):
        n = tms + slots - 2
        return [
            pltpu.VMEM((tms, packed, LANE), F32),
            pltpu.VMEM((slots, packed, LANE), F32),
            pltpu.SemaphoreType.DMA((n,)),
            pltpu.SemaphoreType.DMA((n,)),
        ]

    def __init__(self, pc, bufs):
        self.pc, self.bufs = pc, bufs

    def begin(self, value):
        self.sent = []
        self.cps = self.send(0, value)

    def turn(self):
        self.cps = self.send(1, self.end(0))

    def done(self):
        value = self.end(1)
        for cp in self.sent:
            cp.wait_send()
        return value

    def send(self, i, value):
        pc, buf = self.pc, self.bufs[i]
        ssem, rsem = self.bufs[2:]
        me = (pc.tm, pc.slot)[i]
        buf[me] = value
        n = buf.shape[0]
        for off in range(1, n):
            to = lax.rem(me + off, n)
            k = off - 1 + i * (self.bufs[0].shape[0] - 1)
            cp = pltpu.make_async_remote_copy(
                src_ref=buf.at[me], dst_ref=buf.at[me], send_sem=ssem.at[k], recv_sem=rsem.at[k],
                device_id=(to, pc.slot) if i == 0 else (pc.tm, to), device_id_type=MESH,
            )
            cp.start()
            self.sent.append(cp)
        return self.sent[-(n - 1) :]

    def end(self, i):
        for cp in self.cps:
            cp.wait_recv()
        buf = self.bufs[i]
        value = buf[0]
        for j in range(1, buf.shape[0]):
            value = value + buf[j]
        return value


def packed(rows):
    return jnp.concatenate([row[:, at : at + LANE] for row in rows for at in range(0, row.shape[1], LANE)], axis=0)


def unpacked(value, row, width):
    n = width // LANE
    return jnp.concatenate([value[row * n + j : row * n + j + 1, :] for j in range(n)], axis=1)


def greet_rows(pc, tms, slots):
    bar = pltpu.get_barrier_semaphore()
    for off in range(1, tms):
        pl.semaphore_signal(bar, inc=1, device_id=(lax.rem(pc.tm + off, tms), pc.slot), device_id_type=MESH)
    for off in range(1, slots):
        pl.semaphore_signal(bar, inc=1, device_id=(pc.tm, lax.rem(pc.slot + off, slots)), device_id_type=MESH)
    pl.semaphore_wait(bar, tms + slots - 2)


def middle_body(
    lens, att, x1_ref, cot, wn, taps, bn_gain, bn_bias, gain3, gain4, gain5,
    out_h, dx2_h, datt_h, g_h, smalls_ref, bns_ref, cores,
    w_o, w_ci, w_co, w_f2i, w_f2o, fsem, early, late, hsem, gm_ref, ddwo_ref, z_ref, ext, ext2, dwo_ref, pre_ref, dgm_ref, acc, x2_ref, core, out_ref, dx2_ref, datt_ref, g_ref, hid_ref, dpre_ref, csem, *bufs,
):
    pc = Place()
    tms, slots = lax.axis_size("tm"), lax.axis_size("slot")
    rows, width = x1_ref.shape
    count = taps.shape[0]
    fetch, put = Fetch(fsem), Fetch(csem)
    outs = []
    got = {n: fetch(part_of(wn, n), d) for n, d in (("o", w_o), ("ci", w_ci), ("co", w_co), ("f2i", w_f2i), ("f2o", w_f2o))}
    greet_rows(pc, tms, slots)
    taker = Taker(bufs)
    totals = Totals(pc, taker(4)), Totals(pc, taker(4))
    flows = []
    for i, name in enumerate(FRONT):
        src = g_ref.at[pl.ds(MID[name], GROUP), :]
        half_rows = lambda o, n, lanes, src=src: src[pl.ds(pl.multiple_of(pc.at["c"] * (GROUP // 2) + o, 16), n), lanes]
        flows += make_flows(pc, name, "front", src, half_rows, core.at[i], None, 0, taker)

    def halo(src, dst, k, step):
        dev = (lax.rem(pc.tm + step + tms, tms), pc.slot)
        return pltpu.make_async_remote_copy(
            src_ref=src, dst_ref=dst, send_sem=hsem.at[2 * k], recv_sem=hsem.at[2 * k + 1], device_id=dev, device_id_type=MESH
        )

    got["o"].wait()
    x2 = x1_ref[...] + dot(att[...], w_o[...])
    x2_ref[...] = x2
    a3 = norm(x2, gain3[...]).astype(BF)
    got["ci"].wait()
    z1 = dot(a3, w_ci[pl.ds(0, width), :])
    z2 = dot(a3, w_ci[pl.ds(width, width), :])
    z_ref[:, pl.ds(0, width)] = z1
    z_ref[:, pl.ds(width, width)] = z2
    ok = valid_rows(lens, rows)
    gm_ref[...] = (z1 * sigmoid(z2) * ok).astype(BF)
    cp = halo(gm_ref.at[pl.ds(rows - count, count), :], early, 0, 1)
    cp.start()
    spread(ext, count, gm_ref[...])
    cp.wait()
    spread(ext, 0, jnp.where(pc.tm > 0, early[...], jnp.zeros((), BF)))
    tap_sum(ext, taps, dwo_ref, lambda k: k + 1)
    dwo = dwo_ref[...]
    dwv = dwo * ok
    totals[0].begin(
        packed(
            [
                jnp.sum(dwv, axis=0, keepdims=True),
                jnp.sum(dwv * dwv, axis=0, keepdims=True),
                jnp.zeros((1, 2 * width), F32) + jnp.sum(ok, axis=0, keepdims=True),
            ]
        )
    )
    totals[0].turn()
    sums = totals[0].done()
    total = sums[2 * width // LANE : 2 * width // LANE + 1, 0:1]
    mu = unpacked(sums, 0, width) / total
    inv = lax.rsqrt(unpacked(sums, 1, width) / total - mu * mu + EPS)
    xhat = (dwo_ref[...] - mu) * inv
    sw, slope = swish_and_slope(xhat * bn_gain[...] + bn_bias[...])
    sw = sw.astype(BF)
    got["co"].wait()
    x3 = x2_ref[...] + dot(sw, w_co[...])
    a4 = norm(x3, gain4[...]).astype(BF)
    got["f2i"].wait()
    got["f2o"].wait()
    x4 = x3 + 0.5 * ffn_forward(a4, w_f2i, w_f2o, pre_ref)
    out_ref[...] = norm(x4, gain5[...]).astype(BF)
    outs.append(put(out_ref, out_h))
    dx4, gg5 = norm_back(x4, gain5[...], cot[...].astype(F32))
    g4 = (0.5 * dx4).astype(BF)
    lo = FLAT["o"]
    da4 = ffn_through(g4, w_f2i, w_f2o, pre_ref, hid_ref, dpre_ref)
    back, gg4 = norm_back(x3, gain4[...], da4)
    dx3 = dx4 + back
    g3 = dx3.astype(BF)
    dbn = dot_nt(g3, w_co[...]) * slope
    totals[1].begin(packed([jnp.sum(dbn * xhat, axis=0, keepdims=True), jnp.sum(dbn, axis=0, keepdims=True)]))
    part = lambda name: g_ref.at[pl.ds(MID[name], GROUP), :]
    ffn_in_grad(a4, dpre_ref, part("f2i"))
    totals[1].turn()
    advance(flows)
    ffn_out_grad(g4, hid_ref, part("f2o"))
    g_ref[pl.ds(FLAT["co"] - lo, width), :] = dot_tn(sw, g3).astype(BF)
    for name in ("f2i", "f2o"):
        if name not in FRONT:
            outs.append(put(part(name), g_h.at[pl.ds(MID[name], GROUP), :]))
    sums2 = totals[1].done()
    gain_sum, bias_sum = unpacked(sums2, 0, width), unpacked(sums2, 1, width)
    bns_ref[0:1, :] = gain_sum
    bns_ref[1:2, :] = bias_sum
    bns_ref[2:8, :] = jnp.zeros((6, width), F32)
    ddwo_ref[...] = (bn_gain[...] * inv * (dbn - ok * (bias_sum + xhat * gain_sum) / total)).astype(BF)
    cp = halo(ddwo_ref.at[pl.ds(0, count), :], late, 1, -1)
    cp.start()
    advance(flows)
    spread(ext2, 0, ddwo_ref[...])
    cp.wait()
    spread(ext2, rows, jnp.where(pc.tm < tms - 1, late[...], jnp.zeros((), BF)))
    tap_sum(ext2, taps, dgm_ref, lambda k: count - 1 - k)
    block = 64 if rows % 64 == 0 else 16
    for b in range(ext.shape[0]):
        acc[...] = jnp.zeros(acc.shape, F32)

        def one(i, carry, b=b):
            mine = ext2[b, pl.ds(pl.multiple_of(i * block, block), block), :]
            for k in range(count):
                prod = mine * ext[b, pl.ds(i * block + k + 1, block), :]
                acc[k] = acc[k] + jnp.sum(prod.reshape(block // 8, 8, LANE), axis=0)
            return carry

        lax.fori_loop(0, rows // block, one, 0)
        smalls_ref[pl.ds(0, count), pl.ds(b * LANE, LANE)] = jnp.sum(acc[...], axis=1)
    z1 = z_ref[:, pl.ds(0, width)]
    sg = sigmoid(z_ref[:, pl.ds(width, width)])
    dg = dgm_ref[...] * ok
    dz1 = (dg * sg).astype(BF)
    dz2 = (dg * z1 * sg * (1.0 - sg)).astype(BF)
    a3t = norm(x2_ref[...], gain3[...]).astype(BF).T
    g_ref[pl.ds(FLAT["ci"] - lo, width), :] = dot(a3t, dz1).astype(BF)
    g_ref[pl.ds(FLAT["ci"] - lo + width, width), :] = dot(a3t, dz2).astype(BF)
    da3 = dot_nt(dz1, w_ci[pl.ds(0, width), :]) + dot_nt(dz2, w_ci[pl.ds(width, width), :])
    back, gg3 = norm_back(x2_ref[...], gain3[...], da3)
    dx2 = dx3 + back
    dx2_ref[...] = dx2
    outs.append(put(dx2_ref, dx2_h))
    g2 = dx2.astype(BF)
    g_ref[pl.ds(0, width), :] = dot_tn(att[...], g2).astype(BF)
    outs.append(put(g_ref.at[pl.ds(0, GROUP), :], g_h.at[pl.ds(0, GROUP), :]))
    datt_ref[...] = dot_nt(g2, w_o[...]).astype(BF)
    outs.append(put(datt_ref, datt_h))
    advance(flows)
    outs.append(put(core, cores))
    smalls_ref[pl.ds(count, 8), :] = jnp.concatenate([gg3, gg4, gg5, jnp.zeros((5, width), F32)], axis=0)
    for flow in flows:
        flow.finish()
    for cp in outs:
        cp.wait()


class Butterfly:
    @staticmethod
    def scratch(devices, shape):
        n = devices.bit_length() - 1
        return [pltpu.VMEM((n,) + shape, F32), pltpu.SemaphoreType.DMA((n,)), pltpu.SemaphoreType.DMA((n,))]

    def __init__(self, pc, value, bufs):
        self.value, (self.got, self.ssem, self.rsem) = value, bufs
        self.devs = []
        for axis, me in (("tm", pc.tm), ("slot", pc.slot)):
            bit = 1
            while bit < lax.axis_size(axis):
                to = me + bit - 2 * bit * lax.rem(lax.div(me, bit), 2)
                self.devs.append((to, pc.slot) if axis == "tm" else (pc.tm, to))
                bit *= 2

    def copy(self, k):
        return pltpu.make_async_remote_copy(
            src_ref=self.value, dst_ref=self.got.at[k], send_sem=self.ssem.at[k], recv_sem=self.rsem.at[k],
            device_id=self.devs[k], device_id_type=MESH,
        )

    def stage(self, k):
        if k > 0:
            self.copy(k - 1).wait()
            self.value[...] = self.value[...] + self.got[k - 1]
        if k < len(self.devs):
            self.copy(k).start()


GROUP = 2048


class KeyGrads:
    @staticmethod
    def scratch(tms, rows):
        pairs, xs = H // 2, tms // 2
        sems = pltpu.SemaphoreType.DMA((pairs, xs + 1))
        return [
            pltpu.VMEM((pairs, 2, 2, tms, HD, rows), BF),
            pltpu.VMEM((pairs, 2, tms, HD, rows), BF),
            pltpu.VMEM((xs - 1, pairs, 2, 2, HD, rows), BF),
            pltpu.VMEM((pairs, 2, 2, HD, rows), BF),
            pltpu.VMEM((pairs, 2, HD, rows), BF),
            sems,
            sems,
        ]

    def __init__(self, pc, bufs):
        self.pc = pc
        self.mine, self.core, self.line, self.both, self.got, self.ssem, self.rsem = bufs

    def put(self, p, kind, e, value):
        rows = self.mine.shape[-1]
        for t in range(self.mine.shape[3]):
            self.mine[p, kind, e, t] = value[:, t * rows : (t + 1) * rows].astype(BF)

    def copy(self, p, k, src, dst, dev):
        return pltpu.make_async_remote_copy(
            src_ref=src, dst_ref=dst, send_sem=self.ssem.at[p, k], recv_sem=self.rsem.at[p, k], device_id=dev, device_id_type=MESH
        )

    def first(self, p):
        ((_, dev, _),) = self.pc.peers("c")
        return [self.copy(p, 0, self.mine.at[p, :, 1 - self.pc.at["c"]], self.core.at[p], dev)]

    def second(self, p):
        return [
            self.copy(p, off, self.core.at[p, :, pl.ds(2 * pos, 2)], self.line.at[off - 1, p], dev) for off, dev, pos in self.pc.peers("x")
        ]

    def third(self, p):
        ((_, dev, _),) = self.pc.peers("c")
        return [self.copy(p, self.pc.size["x"], self.both.at[p, :, 1 - self.pc.at["c"]], self.got.at[p], dev)]

    def step(self, p, i):
        c, x = self.pc.at["c"], self.pc.at["x"]
        if i == 1:
            for cp in self.first(p):
                cp.wait_recv()
            for kind in range(2):
                for t in range(self.core.shape[2]):
                    total = self.core[p, kind, t].astype(F32) + self.mine[p, kind, c, t].astype(F32)
                    self.core[p, kind, t] = total.astype(BF)
        if i == 2:
            for cp in self.second(p):
                cp.wait_recv()
            for kind in range(2):
                for t in range(2):
                    total = self.core[p, kind, 2 * x + t].astype(F32)
                    for j in range(self.line.shape[0]):
                        total = total + self.line[j, p, kind, t].astype(F32)
                    self.both[p, kind, t] = total.astype(BF)
        if i == 3:
            for cp in self.third(p):
                cp.wait_recv()
            for cp in self.first(p) + self.second(p):
                cp.wait_send()
            return
        for cp in (self.first, self.second, self.third)[i](p):
            cp.start()

    def sent(self, p):
        for cp in self.third(p):
            cp.wait_send()

    def collect(self, p, kind, dst):
        c = self.pc.at["c"]
        own = self.both[p, kind, c]
        other = self.got[p, kind]
        dst[pl.ds(pl.multiple_of(p * LANE + c * HD, HD), HD), :] = own
        dst[pl.ds(pl.multiple_of(p * LANE + (1 - c) * HD, HD), HD), :] = other


def late_body(
    qu_h, qv_h, kv_h, wn, trig_h, sin_h, cos_h, probs, datt_h, att_h, g_mid, cores_h, a2_h, x1_h, dx2_h, x_h, pre_h, smalls2, gain2, gain1,
    dx0_ref, flat, total_ref,
    qu, qv, kv, w_p, trig, sin, cos, datt, att, a2, x1_ref, dx2_ref, x_ref, wqkv, own, core, psem, fsem,
    dq_ref, dkt, dvt, gpost, qut, qvt, datt_t, g_low, *bufs,
):
    pc = Place()
    rows = qu.shape[0]
    half = sin.shape[1]
    fetch = Fetch(fsem)
    c = pc.at["c"]
    whole = [name for name in MID if name not in FRONT]
    met = pc.greet("cxyz")
    owns = [fetch(g_mid.at[rows_at(MID[name] + c * (GROUP // 2), GROUP // 2), :], own.at[i]) for i, name in enumerate(whole)]
    owns += [fetch(cores_h.at[i], core.at[i]) for i in range(len(FRONT))]
    needed = [fetch(s, d) for s, d in ((qu_h, qu), (datt_h, datt), (att_h, att), (kv_h, kv))]

    def copies(first, pairs):
        return lambda: [pltpu.make_async_copy(s, d, fsem.at[first + i]) for i, (s, d) in enumerate(pairs)]

    second = copies(fetch.n, ((qv_h, qv), (part_of(wn, "p"), w_p), (trig_h, trig), (sin_h, sin), (cos_h, cos)))
    later = copies(
        fetch.n + 5, ((a2_h, a2), (x1_h, x1_ref), (dx2_h, dx2_ref), (x_h, x_ref), (wn.at[pl.ds(FLAT["q"], 1536), :], wqkv))
    )
    last_in = lambda pre_ref, w1: copies(fetch.n + 10, ((pre_h, pre_ref), (wn.at[pl.ds(0, 4096), :], w1)))()
    taker = Taker(bufs)
    keys = KeyGrads(pc, taker(7))
    fly = Butterfly(pc, total_ref, taker(3))
    groups = {}
    for i, name in enumerate(FRONT):
        groups[name] = make_flows(pc, name, "back", None, None, core.at[i], flat, FLAT[name], taker)
    for i, name in enumerate(whole):
        mine = lambda o, n, lanes, i=i: own[i, pl.ds(o, n), lanes]
        src = g_mid.at[pl.ds(MID[name], GROUP), :]
        groups[name] = make_flows(pc, name, "whole", src, mine, core.at[len(FRONT) + i], flat, FLAT[name], taker)
    for i, name in enumerate(("q", "f1i", "f1o")):
        at = FLAT[name]
        mine = lambda o, n, lanes, at=at: g_low[pl.ds(pl.multiple_of(at + c * (GROUP // 2) + o, 16), n), lanes]
        groups[name] = make_flows(pc, name, "whole", g_low.at[pl.ds(at, GROUP), :], mine, core.at[3 + i], flat, at, taker)
    def run(point):
        picked = [(NAMES[token // 4], token % 4) for token in TURNS.get(point, ())]
        stages = [groups[name][i].take() for name, i in picked if i < len(groups[name])]
        return lambda: [stage() for stage in stages]

    first = run(-1)
    plan = {at: run(at) for at in range(2 * H)}
    after = lambda point: run(point)()
    scale = HD**-0.5

    def scores(p, pbuf, load):
        at = cols(p)
        for e in range(2):
            mine = lane_half(e)
            part = pl.ds(pl.multiple_of(p * LANE + e * HD, HD), HD)
            dm = jnp.where(mine, datt[:, at], jnp.zeros((), BF))
            inner = jnp.sum(dm.astype(F32) * att[:, at].astype(F32), axis=-1, keepdims=True)
            dp = dot_nt(dm, kv[p, 1].reshape(-1, LANE))
            load(2 * p + e).wait()
            low_p = pbuf[2 * p + e]
            ds = (low_p.astype(F32) * (dp - inner)).astype(BF)
            pbuf[2 * p + e] = ds
            keys.put(p, 0, e, dot(qut[part, :], ds))
            keys.put(p, 1, e, dot(datt_t[part, :], low_p))
            if e == 0:
                pl.when(p > 0)(lambda: keys.step(p - 1, 1))
            else:
                keys.step(p, 0)
            ticks(e, plan, p)

    def queries(p, pbuf):
        at = cols(p)
        dqu = dqv = None
        for e in range(2):
            mine = lane_half(e)
            part = pl.ds(pl.multiple_of(p * LANE + e * HD, HD), HD)
            ds = pbuf[2 * p + e]
            back = dot(ds, jnp.concatenate([trig[...], kv[p, 0].reshape(-1, LANE)], axis=1))
            db_s, db_c, part_u = back[:, :half], back[:, half : 2 * half], back[:, 2 * half :]
            da_s = (db_c * sin[...] - db_s * cos[...]).astype(BF)
            da_c = (db_c * cos[...] + db_s * sin[...]).astype(BF)
            turned = jnp.concatenate([da_s, da_c], axis=1)
            gpost[part, :] = dot(qvt[part, :], turned)
            part_v = dot(turned, w_p[:, at])
            dqu = part_u if e == 0 else jnp.where(mine, part_u, dqu)
            dqv = part_v if e == 0 else jnp.where(mine, part_v, dqv)
            if e == 0:
                pl.when(p == 0)(lambda: keys.step(last, 1))
            else:
                keys.step(p, 2)
            ticks(e, plan, p + H // 2)
        dqu = dqu * scale
        dqv = dqv * scale
        dq_ref[:, at] = (dqu + dqv).astype(BF)
        total_ref[pl.ds(37, 1), at] = jnp.sum(dqu, axis=0, keepdims=True)
        total_ref[pl.ds(38, 1), at] = jnp.sum(dqv, axis=0, keepdims=True)

    last = H // 2 - 1

    def attention(pbuf):
        load = lambda h: pltpu.make_async_copy(probs.at[h], pbuf.at[h], psem.at[h])
        for h in range(H):
            load(h).start()
        for cp in second() + later():
            cp.start()
        met()
        for cp in owns:
            cp.wait()
        first()
        for cp in needed:
            cp.wait()
        qut[...] = qu[...].T
        datt_t[...] = datt[...].T

        lax.fori_loop(0, H // 2, lambda p, t: (scores(p, pbuf, load), t)[1], 0)
        for cp in second():
            cp.wait()
        qvt[...] = qv[...].T
        lax.fori_loop(0, H // 2, lambda p, t: (queries(p, pbuf), t)[1], 0)

    pl.run_scoped(attention, pltpu.VMEM((H, rows, kv.shape[2] * rows), BF))

    def tail(pre_ref, w1, hid_ref, dpre_ref):
        for cp in last_in(pre_ref, w1):
            cp.start()
        g_low[pl.ds(FLAT["p"], 512), :] = gpost[...].T.astype(BF)
        for cp in later():
            cp.wait()
        a2t = a2[...].T
        g_low[pl.ds(FLAT["q"], 512), :] = dot(a2t, dq_ref[...]).astype(BF)
        da2 = dot_nt(dq_ref[...], wqkv[pl.ds(0, 512), :])
        after(16)
        for p in range(H // 2):
            keys.step(p, 3)
            keys.collect(p, 0, dkt)
            keys.collect(p, 1, dvt)
        g_low[pl.ds(FLAT["k"], 512), :] = dot_nt(a2t, dkt[...]).astype(BF)
        g_low[pl.ds(FLAT["v"], 512), :] = dot_nt(a2t, dvt[...]).astype(BF)
        advance(groups["q"])
        for cp in last_in(pre_ref, w1):
            cp.wait()
        ffn_hidden(pre_ref, hid_ref)
        after(17)
        da2 = da2 + dot_nt(dkt[...].T, wqkv[pl.ds(512, 512), :]) + dot_nt(dvt[...].T, wqkv[pl.ds(1024, 512), :])
        back, gg2 = norm_back(x1_ref[...], gain2[...], da2)
        dx1 = dx2_ref[...] + back
        g1 = (0.5 * dx1).astype(BF)
        x = x_ref[...].astype(F32)
        a1 = norm(x, gain1[...]).astype(BF)
        after(18)
        ffn_out_grad(g1, hid_ref, g_low.at[pl.ds(2048, 2048), :])
        advance(groups["f1o"])
        after(19)
        da1 = ffn_through(g1, w1.at[pl.ds(0, 2048), :], w1.at[pl.ds(2048, 2048), :], pre_ref, hid_ref, dpre_ref)
        after(20)
        ffn_in_grad(a1, dpre_ref, g_low.at[pl.ds(0, 2048), :])
        advance(groups["f1i"])
        back, gg1 = norm_back(x, gain1[...], da1)
        dx0_ref[...] = (dx1 + back).astype(BF)
        total_ref[pl.ds(smalls2.shape[0] - 5, 2), :] = jnp.concatenate([gg1, gg2], axis=0)

    pl.run_scoped(tail, pltpu.VMEM(pre_h.shape, F32), pltpu.VMEM((4096, 512), BF), pltpu.VMEM(pre_h.shape, BF), pltpu.VMEM(pre_h.shape, BF))
    count = smalls2.shape[0] - 8
    total_ref[pl.ds(0, count), :] = smalls2[pl.ds(0, count), :]
    total_ref[pl.ds(count, 3), :] = smalls2[pl.ds(count, 3), :]
    total_ref[pl.ds(count + 7, 1), :] = jnp.zeros((1, 512), F32)
    flows = flat_list(list(groups.values()))
    turns, steps = TURNS[21], len(fly.devs) + 1
    for i, token in enumerate(turns):
        if i * steps // len(turns) != (i - 1) * steps // len(turns):
            fly.stage(i * steps // len(turns))
        name, k = NAMES[token // 4], token % 4
        advance(groups[name][k : k + 1])
    while any(flow.now < flow.last for flow in flows):
        advance(flows)
    for p in range(H // 2):
        keys.sent(p)
    for flow in flows:
        flow.finish()


def widen_body(flat, total, bns, *refs):
    outs, smalls, (ibuf, obuf, rbuf, isem, osem, rsem) = refs[:11], refs[11:21], refs[21:]
    count = smalls[0].shape[0]
    lines = [pltpu.make_async_copy(total.at[pl.ds(0, count), :], smalls[0], rsem.at[0])]
    for i, ref in enumerate(smalls[1:]):
        rbuf[i] = total[pl.ds(count + i, 1), :] if i < 7 else bns[pl.ds(i - 7, 1), :]
        lines.append(pltpu.make_async_copy(rbuf.at[i], ref, rsem.at[1 + i]))
    for cp in lines:
        cp.start()
    step = 512
    n = FLAT_ROWS // step
    loads = [pltpu.make_async_copy(flat.at[pl.ds(i * step, step), :], ibuf.at[i], isem.at[i]) for i in range(n)]
    for cp in loads:
        cp.start()
    stores = []
    slots = obuf.shape[0]
    for i in range(n):
        name = [m for m in ORDER if FLAT[m] <= i * step][-1]
        out = outs[ORDER.index(name)]
        off = i * step - FLAT[name]
        fold = FOLDS.get(name, 1)
        if fold == 1:
            dst = out.at[pl.ds(off, step), :]
        else:
            dst = out.at[:, pl.ds(off, step)]
        loads[i].wait()
        if i >= slots:
            stores[i - slots].wait()
        obuf[i % slots] = ibuf[i].astype(F32)
        stores.append(pltpu.make_async_copy(obuf.at[i % slots], dst, osem.at[i % slots]))
        stores[-1].start()
    for cp in stores[-slots:] + lines:
        cp.wait()


def remote(body, cid, outs, ins, scratch, name):
    def space(x):
        if x is None:
            return pl.BlockSpec(memory_space=pl.ANY)
        return pl.BlockSpec(memory_space=x)

    return pl.pallas_call(
        body,
        out_shape=[jax.ShapeDtypeStruct(s, d) for s, d, _ in outs],
        in_specs=[space(m) for _, m in ins],
        out_specs=[space(m) for _, _, m in outs],
        scratch_shapes=list(scratch),
        compiler_params=pltpu.CompilerParams(collective_id=cid, has_side_effects=True, vmem_limit_bytes=VMEM_LIMIT),
        name=name,
    )(*[x for x, _ in ins])


def local(
    inputs, cotangent, lengths, weight_noise, ffn1_in, ffn1_out, query_w, key_w, value_w, pos_w, out_w,
    conv_in, conv_out, ffn2_in, ffn2_out, conv_kernel, ffn1_gain, attn_gain, conv_gain, ffn2_gain,
    final_gain, bn_gain, bn_bias, pos_u, pos_v,
):
    _, rows, width = inputs.shape
    tms, slots = lax.axis_size("tm"), lax.axis_size("slot")
    frames = rows * tms
    count = conv_kernel.shape[0]
    devices = tms * slots
    size = Place().size
    x = inputs[0]
    cot = cotangent[0]
    gains = [g.reshape(1, -1) for g in (ffn1_gain, attn_gain, conv_gain, ffn2_gain, final_gain)]
    bng, bnb, pu, pv = (g.reshape(1, -1) for g in (bn_gain, bn_bias, pos_u, pos_v))
    raws = (ffn1_in, ffn1_out, query_w, key_w, value_w, pos_w, out_w, conv_in, conv_out, ffn2_in, ffn2_out)
    VM, HB, SM = pltpu.VMEM, None, pltpu.SMEM
    DMA = pltpu.SemaphoreType.DMA
    V = lambda shape, dtype=BF: pltpu.VMEM(shape, dtype)
    shard_rows = weight_noise.shape[1] // width
    half, hidden = width // 2, 2048
    keys = (H // 2, 2, tms, rows, LANE)
    specs = [
        ((FLAT_ROWS, width), BF), ((rows, width), F32), ((rows, hidden), F32), ((rows, width), BF), ((rows, width), BF), ((rows, width), BF),
        (keys, BF), ((frames, width), BF), ((rows, half), F32), ((rows, half), F32), ((rows, width), BF), ((H, rows, frames), BF),
    ]
    wn, x1, pre1, a2, qu, qv, kv, trig, sin, cos, att, probs = remote(
        early_body, 0, [spec + (HB,) for spec in specs],
        [(lengths, SM), (weight_noise, VM)] + [(r, HB) for r in raws] + [(x, VM), (gains[0], VM), (gains[1], VM), (pu, VM), (pv, VM)],
        [V((FLAT_ROWS, width)), V((width // LANE, shard_rows, LANE), F32)]
        + [V(*spec) for spec in specs[1:10]]
        + [V((2, frames // 64, half), F32), V((2, 64, half), F32), V((rows, width)), V((2, rows, frames)), DMA((18,)), DMA((16,)), DMA((2,))]
        + Gather.scratch(size, shard_rows, width) + KeysAll.scratch(size["x"]),
        "early",
    )
    ext = pltpu.VMEM((width // LANE, rows + count, LANE), F32)
    output, dx2, datt, g_mid, smalls2, bns, cores = remote(
        middle_body, 1,
        [((rows, width), BF, HB), ((rows, width), F32, HB), ((rows, width), BF, HB), ((3 * GROUP, width), BF, HB),
         ((count + 8, width), F32, VM), ((8, width), F32, VM), ((max(1, len(FRONT)), GROUP // 2, width), BF, HB)],
        [(lengths, SM), (att, VM), (x1, VM), (cot, VM), (wn, HB), (conv_kernel, VM), (bng, VM), (bnb, VM)] + [(g, VM) for g in gains[2:]],
        [pltpu.VMEM((FLAT_SIZE[n], width), BF) for n in ("o", "ci", "co", "f2i", "f2o")]
        + [DMA((5,)), pltpu.VMEM((count, width), BF), pltpu.VMEM((count, width), BF), DMA((4,)),
           pltpu.VMEM((rows, width), BF), pltpu.VMEM((rows, width), BF), pltpu.VMEM((rows, 2 * width), F32), ext, ext,
           pltpu.VMEM((rows, width), F32), pltpu.VMEM((rows, hidden), F32), pltpu.VMEM((rows, width), F32),
           pltpu.VMEM((count, 8, LANE), F32), pltpu.VMEM((rows, width), F32), V((max(1, len(FRONT)), GROUP // 2, width)),
           V((rows, width)), V((rows, width), F32), V((rows, width)), V((3 * GROUP, width)),
           V((rows, hidden)), V((rows, hidden)), DMA((7,))]
        + Totals.scratch(tms, slots, 4 * width // LANE) + Totals.scratch(tms, slots, 2 * width // LANE) + flat_list([flat_list(flow_scratch(size, n, "front")) for n in FRONT]),
        "middle",
    )
    dx0, flat, total = remote(
        late_body, 2, [((rows, width), BF, VM), ((FLAT_ROWS, width), BF, HB), ((count + 8, width), F32, VM)],
        [(t, HB) for t in (qu, qv, kv, wn, trig, sin, cos, probs, datt, att, g_mid, cores, a2, x1, dx2, x, pre1)]
        + [(smalls2, VM), (gains[1], VM), (gains[0], VM)],
        [V((rows, width)), V((rows, width)), V(keys), V((width, width)), V((frames, width)),
         V((rows, half), F32), V((rows, half), F32), V((rows, width)), V((rows, width)), V((rows, width)),
         V((rows, width), F32), V((rows, width), F32), V((rows, width)), V((3 * width, width)),
         V((3 - len(FRONT), GROUP // 2, width)), V((6, GROUP // 2, width)), DMA((H,)), DMA((20,)),
         V((rows, width)), V((width, rows)), V((width, rows)), V((width, width), F32), V((width, rows)), V((width, rows)), V((width, rows)),
         V((FLAT_ROWS // 2, width))]
        + KeyGrads.scratch(tms, rows) + Butterfly.scratch(devices, (count + 8, width))
        + flat_list([flat_list(flow_scratch(size, n, "back")) for n in FRONT])
        + flat_list([flat_list(flow_scratch(size, n, "whole")) for n in MID if n not in FRONT])
        + flat_list([flat_list(flow_scratch(size, n, "whole")) for n in ("q", "f1i", "f1o")]),
        "late",
    )
    big = pl.pallas_call(
        widen_body,
        out_shape=[jax.ShapeDtypeStruct(r.shape, F32) for r in raws]
        + [jax.ShapeDtypeStruct((count, width), F32)] + [jax.ShapeDtypeStruct((1, width), F32)] * 9,
        in_specs=[pl.BlockSpec(memory_space=pl.ANY)] + [pl.BlockSpec(memory_space=pltpu.VMEM)] * 2,
        out_specs=[pl.BlockSpec(memory_space=pl.ANY)] * 21,
        scratch_shapes=[pltpu.VMEM((24, 512, width), BF), pltpu.VMEM((12, 512, width), F32), pltpu.VMEM((9, 1, width), F32), DMA((24,)), DMA((12,)), DMA((10,))],
        compiler_params=pltpu.CompilerParams(vmem_limit_bytes=VMEM_LIMIT),
        name="widen",
    )(flat, total, bns)
    t = [r[0] for r in big[12:]]
    return (output[None], dx0[None]) + tuple(big[:11]) + (
        big[11], t[3], t[4], t[0], t[1], t[2], t[7], t[8], t[5], t[6],
    )


def solution(mesh):
    split = P("slot", "tm", None)
    in_specs = (split, split, P("slot"), P(("tm", "slot"), None)) + (P(),) * 21
    out_specs = (split, split) + (P(),) * 21
    return jax.shard_map(local, mesh=mesh, in_specs=in_specs, out_specs=out_specs, check_vma=False)
```
